32 devices in a mesh: seq: 8 (over y, x, core), head: 4 (over z).
Axes of the slice: x: 2, y: 2, z: 4, core: 2. Of those that a mesh axis runs over, the one named last changes fastest.
Arguments:
- mixer_input: bfloat16 [4096, 8192], P('seq', 'head'), may hold values from -0.54 to 0.54
- output_grad: bfloat16 [4096, 8192], P('seq', 'head'), may hold values from -6.5 to 6.5
- input_map: bfloat16 [4096, 128], P('seq'), may hold values from -1 to 1
- output_map: bfloat16 [4096, 128], P('seq'), may hold values from -1 to 1
- decays: float32 [128, 4096], P('head', 'seq'), may hold values from 0.25 to 1
Outputs:
- input_grad: bfloat16 [4096, 8192], P('seq', 'head')
- input_map_grad: float32 [4096, 128], P(('seq', 'head'))
- output_map_grad: float32 [4096, 128], P(('seq', 'head'))
The draws below stay inside these ranges and needn't reach their ends.
All inputs are finite; a program needn't handle non-finite values.
Results may differ from the reference program's by a relative error of at most 0.0012.
Values sent between devices are 32-bit elements; how exact they have to be, the bound alone decides.
No kernel may reach another device: no remote copies, remote signals or barrier semaphores. Data moves between devices by JAX's collectives and lax.ppermute only.
A program may use at most 128 MiB of HBM per device.

```python
import jax
import jax.numpy as jnp
from jax import lax

H = 128
P_SIZE = 64
N = 128
Q = 128
TOK_DEV = 512
TOKENS = 4096


def head_rates(key, sudden_count, quick_count, middle_count, gradual_count):
    subkeys = jax.random.split(key, 6)
    ordering = jax.random.permutation(subkeys[0], H)
    positions = lax.iota(jnp.int32, H)
    bound_one = sudden_count
    bound_two = bound_one + quick_count
    bound_three = bound_two + middle_count
    bound_four = bound_three + gradual_count
    by_position = (positions >= bound_one).astype(jnp.int32) + (positions >= bound_two).astype(jnp.int32)
    by_position = by_position + (positions >= bound_three).astype(jnp.int32) + (positions >= bound_four).astype(jnp.int32)
    head_kind = jnp.zeros((H,), jnp.int32).at[ordering].set(by_position)
    sudden = 1.0 / jax.random.uniform(subkeys[1], (H,), minval=3.5, maxval=5.0)
    quick = 1.0 / jax.random.uniform(subkeys[2], (H,), minval=30.0, maxval=50.0)
    middle = jax.random.uniform(subkeys[3], (H,), minval=4.4, maxval=5.2) / TOK_DEV
    gradual = jax.random.uniform(subkeys[4], (H,), minval=0.08, maxval=0.17) / TOK_DEV
    lasting = jax.random.uniform(subkeys[5], (H,), minval=0.3, maxval=0.7) * (2.302585 / TOKENS)
    stacked = jnp.stack([sudden, quick, middle, gradual, lasting])
    chosen = lax.broadcasted_iota(jnp.int32, (5, H), 0) == head_kind[None, :]
    return jnp.sum(jnp.where(chosen, stacked, 0.0), axis=0)


def draw_decays(key, part):
    head_rate = head_rates(key, H // 16, H // 16, H // 8, H // 4)
    key = jax.random.fold_in(key, 7)
    subkeys = jax.random.split(key, 4)
    roughness = jnp.exp(jax.random.uniform(subkeys[0], (H, TOKENS), minval=-0.693, maxval=0.693))
    device_scale = jnp.exp(jax.random.uniform(subkeys[1], (H, TOKENS // TOK_DEV), minval=-0.35, maxval=0.35))
    roughness = roughness * jnp.repeat(device_scale, TOK_DEV, axis=1)
    strike_spots = jax.random.randint(subkeys[2], (H, 2), 0, TOKENS)
    places = lax.broadcasted_iota(jnp.int32, (H, TOKENS), 1)
    struck = (places == strike_spots[:, 0:1]) | (places == strike_spots[:, 1:2])
    drop_sizes = jax.random.uniform(subkeys[3], (H, TOKENS), minval=0.6, maxval=0.8)
    return jnp.where(struck, drop_sizes, 1.0) * jnp.exp(-head_rate[:, None] * roughness)


def draw_mixer_input(key, part):
    key = jax.random.fold_in(key, 11)
    subkeys = jax.random.split(key, 2)
    entries = jnp.clip(jax.random.normal(subkeys[0], (TOKENS, H * P_SIZE)), -6.0, 6.0)
    loudness = jnp.exp(jax.random.uniform(subkeys[1], (TOKENS // TOK_DEV, 1), minval=-1.5, maxval=1.5))
    return (0.02 * entries * jnp.repeat(loudness, TOK_DEV, axis=0)).astype(jnp.bfloat16)


def draw_output_grad(key, part):
    head_rate = head_rates(key, H // 16, H // 16, H // 8, H // 4)
    head_gain = jnp.clip(jnp.sqrt(0.5 * head_rate * TOKENS), 1.0, 12.0)
    column_gain = jnp.repeat(head_gain, P_SIZE)[None, :]
    key = jax.random.fold_in(key, 13)
    subkeys = jax.random.split(key, 2)
    entries = jnp.clip(jax.random.normal(subkeys[0], (TOKENS, H * P_SIZE)), -6.0, 6.0)
    loudness = jnp.exp(jax.random.uniform(subkeys[1], (TOKENS // TOK_DEV, 1), minval=-1.5, maxval=1.5))
    return (0.02 * entries * jnp.repeat(loudness, TOK_DEV, axis=0) * column_gain).astype(jnp.bfloat16)


def steps_of(own_key, extent, shards, smallest, high):
    factor_of = 1.0
    for dim, parts in shards:
        steps = jax.random.uniform(jax.random.fold_in(jax.random.fold_in(own_key, 6), dim), (parts,), jnp.float32, smallest / len(shards), high / len(shards))
        factor_of = factor_of * jnp.repeat(jnp.exp(steps), extent[dim] // parts).reshape((-1,) + (1,) * (len(extent) - 1 - dim))
    return factor_of


def bell_draw(rng, extent, spread, most, cuts=(), held_as=jnp.bfloat16):
    array = jax.random.normal(rng, extent, jnp.float32) * spread
    if len(cuts) > 0:
        array = steps_of(rng, extent, cuts, -0.22, 0.18) * array
    return jnp.clip(array, min=-most, max=most).astype(held_as)


def setup_inputs(seed: int = 0) -> dict:
    keys = jax.random.split(jax.random.key(seed), 6)
    mixer_input = draw_mixer_input(jax.random.fold_in(keys[5], 71), 0)
    output_grad = draw_output_grad(jax.random.fold_in(keys[5], 71), 0)
    input_map = bell_draw(keys[2], (TOKENS, N), 0.16, 1.0, ((0, 8),))
    output_map = bell_draw(keys[3], (TOKENS, N), 0.16, 1.0, ((0, 8),))
    decays = draw_decays(jax.random.fold_in(keys[5], 71), 0)
    return {"mixer_input": mixer_input, "output_grad": output_grad, "input_map": input_map, "output_map": output_map, "decays": decays}


highest = lax.Precision.HIGHEST


def causal_table(logs_group):
    width = logs_group.shape[1]
    rows = lax.broadcasted_iota(jnp.int32, (width, width), 0)
    columns = lax.broadcasted_iota(jnp.int32, (width, width), 1)
    later = logs_group[:, :, None] - logs_group[:, None, :]
    return jnp.where((columns <= rows)[None], jnp.exp(jnp.minimum(later, 0.0)), 0.0)


def mixing(table, grad_group, input_group):
    return jnp.einsum('hts,thp,shp->ts', table, grad_group, input_group, precision=highest)


def reference(mixer_input, output_grad, input_map, output_map, decays):
    tokens = mixer_input.shape[0]
    groups = tokens // Q
    inputs = mixer_input.astype(jnp.float32).reshape(groups, Q, H, P_SIZE)
    grads = output_grad.astype(jnp.float32).reshape(groups, Q, H, P_SIZE)
    in_maps = input_map.astype(jnp.float32).reshape(groups, Q, N)
    out_maps = output_map.astype(jnp.float32).reshape(groups, Q, N)
    cumulative = jnp.cumsum(jnp.log(decays).reshape(H, groups, Q), axis=2).transpose(1, 0, 2)

    def forward_step(state, pieces):
        input_group, grad_group, in_group, logs_group = pieces
        table = causal_table(logs_group)
        mixed = mixing(table, grad_group, input_group)
        gathered = jnp.dot(mixed, in_group, precision=highest)
        gathered = gathered + jnp.einsum('ht,thp,hpn->tn', jnp.exp(logs_group), grad_group, state, precision=highest)
        ending = logs_group[:, -1]
        weights = jnp.exp(ending[:, None] - logs_group)
        state = jnp.exp(ending)[:, None, None] * state + jnp.einsum('hs,shp,sn->hpn', weights, input_group, in_group, precision=highest)
        return state, gathered

    def backward_step(carry, pieces):
        input_group, grad_group, in_group, out_group, logs_group = pieces
        table = causal_table(logs_group)
        mixed = mixing(table, grad_group, input_group)
        scores = jnp.dot(out_group, in_group.T, precision=highest)
        ending = logs_group[:, -1]
        weights = jnp.exp(ending[:, None] - logs_group)
        input_part = jnp.einsum('hst,st,shp->thp', table, scores, grad_group, precision=highest)
        input_part = input_part + jnp.einsum('ht,hpn,tn->thp', weights, carry, in_group, precision=highest)
        map_part = jnp.dot(mixed.T, out_group, precision=highest)
        map_part = map_part + jnp.einsum('ht,thp,hpn->tn', weights, input_group, carry, precision=highest)
        carry = jnp.exp(ending)[:, None, None] * carry + jnp.einsum('hs,shp,sn->hpn', jnp.exp(logs_group), grad_group, out_group, precision=highest)
        return carry, (input_part, map_part)

    empty = jnp.zeros((H, P_SIZE, N), jnp.float32)
    out_grads = lax.scan(forward_step, empty, (inputs, grads, in_maps, cumulative))[1]
    input_parts, map_parts = lax.scan(backward_step, empty, (inputs, grads, in_maps, out_maps, cumulative), reverse=True)[1]
    input_grad = input_parts.reshape(tokens, H * P_SIZE).astype(jnp.bfloat16)
    return input_grad, map_parts.reshape(tokens, N), out_grads.reshape(tokens, N)
```

```python
import functools

import jax
import jax.numpy as jnp
from jax import lax
from jax.experimental import pallas as pl
from jax.experimental.pallas import tpu as pltpu
from jax.sharding import PartitionSpec as P

P_SIZE = 64
N = 128
SUB = 64
TILE = 256
EXTRA = 8
F32 = jnp.float32
BF16 = jnp.bfloat16

NN = (((1,), (0,)), ((), ()))
NT = (((1,), (1,)), ((), ()))


def dot(a, b, dims=NN):
    return lax.dot_general(a, b, dims, preferred_element_type=F32)


def halves(v):
    hi = v.astype(BF16)
    return hi, (v - hi.astype(F32)).astype(BF16)


def dot21(pair, b, dims=NN):
    return dot(pair[0], b, dims) + dot(pair[1], b, dims)


def dot12(a, pair, dims=NN):
    return dot(a, pair[0], dims) + dot(a, pair[1], dims)


def dot22(p, q, dims=NN):
    return dot(p[0], q[0], dims) + (dot(p[0], q[1], dims) + dot(p[1], q[0], dims))


def thirds(v):
    hi = v.astype(BF16)
    rest = v - hi.astype(F32)
    mid = rest.astype(BF16)
    return hi, mid, (rest - mid.astype(F32)).astype(BF16)


def packed_thirds(v, heads):
    hi, mid, lo = thirds(v)
    group = lax.broadcasted_iota(jnp.int32, v.shape, 1) // heads
    picked = jnp.where(group == 0, hi.astype(F32), jnp.where(group == 1, mid.astype(F32), lo.astype(F32)))
    return picked.astype(BF16)


def spread(heads, first, width):
    rows = lax.broadcasted_iota(jnp.int32, (3 * heads, width), 0)
    columns = lax.broadcasted_iota(jnp.int32, (3 * heads, width), 1)
    return (rows % heads == first + columns // P_SIZE).astype(F32).astype(BF16)


def summed_logs(table, logs3):
    return dot(table, logs3[0], NT) + (dot(table, logs3[1], NT) + dot(table, logs3[2], NT))


def log_parts(decays):
    logs = jnp.log(decays)
    return tuple(jnp.concatenate([part.astype(F32)] * 3, axis=0).astype(BF16) for part in thirds(logs))


def factors_kernel(decays_ref, pre_ref, suf_ref):
    heads, local = decays_ref.shape
    logs3 = log_parts(decays_ref[...])
    rows = lax.broadcasted_iota(jnp.int32, (local, local), 0)
    columns = lax.broadcasted_iota(jnp.int32, (local, local), 1)
    upto = (columns <= rows).astype(F32).astype(BF16)
    after = (columns > rows).astype(F32).astype(BF16)
    pre_ref[...] = packed_thirds(jnp.exp(summed_logs(upto, logs3)), heads)
    suf_ref[...] = packed_thirds(jnp.exp(summed_logs(after, logs3)), heads)


def factors(decays):
    heads, local = decays.shape
    shape = jax.ShapeDtypeStruct((local, 3 * heads), BF16)
    return pl.pallas_call(
        factors_kernel,
        out_shape=(shape, shape),
        name="decay_factors",
        cost_estimate=pl.CostEstimate(flops=6 * local * local * 128 * 2, bytes_accessed=300000, transcendentals=0),
    )(decays)


def totals_kernel(heads, first_tile, pick_ref, x_ref, dy_ref, bt_ref, ct_ref, pre_ref, suf_ref, out_ref):
    tile = x_ref.shape[1]
    at = pick_ref[0] * first_tile + pl.program_id(0)
    table = spread(heads, at * (tile // P_SIZE), tile)
    before = dot(pre_ref[...], table)
    after = dot(suf_ref[...], table)
    ended = before[before.shape[0] - 1 :, :]
    out_ref[0, :N, :] = dot12(bt_ref[...], halves(x_ref[...].astype(F32) * after))
    out_ref[1, :N, :] = dot12(ct_ref[...], halves(dy_ref[...].astype(F32) * before))
    out_ref[0, N:, :] = jnp.broadcast_to(ended, (EXTRA, tile))
    out_ref[1, N:, :] = jnp.broadcast_to(ended, (EXTRA, tile))


def totals(half, x, dy, bt, ct, pre, suf):
    local, width = x.shape
    heads = width // P_SIZE
    count = width // 2 // TILE
    whole = lambda a: pl.BlockSpec(a.shape, lambda j, pick: (0, 0))
    column = pl.BlockSpec((local, TILE), lambda j, pick: (0, pick[0] * count + j))
    return pl.pallas_call(
        functools.partial(totals_kernel, heads, count),
        grid_spec=pltpu.PrefetchScalarGridSpec(
            num_scalar_prefetch=1,
            grid=(count,),
            in_specs=[column, column, whole(bt), whole(ct), whole(pre), whole(suf)],
            out_specs=pl.BlockSpec((2, N + EXTRA, TILE), lambda j, pick: (0, 0, j)),
        ),
        out_shape=jax.ShapeDtypeStruct((2, N + EXTRA, width // 2), F32),
        name="state_totals",
        cost_estimate=pl.CostEstimate(flops=8 * local * N * width // 2, bytes_accessed=4 * local * width, transcendentals=0),
    )(half, x, dy, bt, ct, pre, suf)


def ordered(core, mine, recv):
    return jnp.where(core == 0, mine, recv), jnp.where(core == 0, recv, mine)


def chip_kernel(core_ref, mine_ref, recv_ref, state_ref, grad_ref):
    core = core_ref[0]
    early, late = ordered(core, mine_ref[0], recv_ref[0])
    early_decay, late_decay = early[N : N + 1], late[N : N + 1]
    both = jnp.broadcast_to(early_decay * late_decay, (EXTRA, early.shape[1]))
    state_ref[:N, :] = late_decay * early[:N] + late[:N]
    state_ref[N:, :] = both
    early, late = ordered(core, mine_ref[1], recv_ref[1])
    grad_ref[:N, :] = early[:N] + early_decay * late[:N]
    grad_ref[N:, :] = both


def chip_totals(core, mine, recv):
    width = mine.shape[2]
    tile = min(512, width)
    block = pl.BlockSpec((2, N + EXTRA, tile), lambda j, pick: (0, 0, j))
    out = pl.BlockSpec((N + EXTRA, tile), lambda j, pick: (0, j))
    shape = jax.ShapeDtypeStruct((N + EXTRA, width), F32)
    return pl.pallas_call(
        chip_kernel,
        grid_spec=pltpu.PrefetchScalarGridSpec(
            num_scalar_prefetch=1, grid=(width // tile,), in_specs=[block, block], out_specs=(out, out)
        ),
        out_shape=(shape, shape),
        name="chip_totals",
        cost_estimate=pl.CostEstimate(flops=6 * N * width, bytes_accessed=24 * N * width, transcendentals=0),
    )(core, mine, recv)


def carried_kernel(forward, core_ref, mine_ref, recv_ref, *refs):
    others, (own_ref, peer_ref) = refs[:-2], refs[-2:]
    core = core_ref[0]
    carried = None
    weight = None
    for ref in others:
        if carried is None:
            carried, weight = ref[:N, :], ref[N : N + 1, :]
        else:
            carried, weight = carried + weight * ref[:N, :], weight * ref[N : N + 1, :]
    if carried is None:
        carried = jnp.zeros(own_ref.shape, F32)
    early, late = ordered(core, mine_ref[0], recv_ref[0])
    if forward:
        at_early = carried
        at_late = early[N : N + 1] * carried + early[:N]
    else:
        at_late = carried
        at_early = late[:N] + late[N : N + 1] * carried
    own_ref[...] = jnp.where(core == 0, at_early, at_late)
    peer_ref[...] = jnp.where(core == 0, at_late, at_early)


def carried(forward, core, mine, recv, others):
    width = mine.shape[2]
    tile = min(512, width)
    which = 0 if forward else 1
    pair = pl.BlockSpec((1, N + EXTRA, tile), lambda j, pick: (which, 0, j))
    other = pl.BlockSpec((N + EXTRA, tile), lambda j, pick: (0, j))
    out = pl.BlockSpec((N, tile), lambda j, pick: (0, j))
    shape = jax.ShapeDtypeStruct((N, width), F32)
    return pl.pallas_call(
        functools.partial(carried_kernel, forward),
        grid_spec=pltpu.PrefetchScalarGridSpec(
            num_scalar_prefetch=1,
            grid=(width // tile,),
            in_specs=[pair, pair] + [other] * len(others),
            out_specs=(out, out),
        ),
        out_shape=(shape, shape),
        name="carried_states" if forward else "carried_grads",
        cost_estimate=pl.CostEstimate(flops=10 * N * width, bytes_accessed=28 * N * width, transcendentals=0),
    )(core, mine, recv, *others)


def local_kernel(
    heads, x_ref, dy_ref, b_ref, c_ref, bt_ref, ct_ref, decays_ref, part_ref, map_ref, out_ref,
    lift_ref, drop_ref, rows_ref, mixed_ref, scores_ref, dys_ref, xs_ref,
):
    local, tile = x_ref.shape
    chunks = local // SUB
    step = pl.program_id(0)

    @pl.when(step == 0)
    def _():
        logs3 = log_parts(decays_ref[...])
        rows = lax.broadcasted_iota(jnp.int32, (local, local), 0)
        columns = lax.broadcasted_iota(jnp.int32, (local, local), 1)
        middle = (rows // SUB) * SUB + SUB // 2
        same = rows // SUB == columns // SUB
        later = same & (columns > middle) & (columns <= rows)
        sooner = same & (columns > rows) & (columns <= middle)
        signed = (later.astype(F32) - sooner.astype(F32)).astype(BF16)
        offset = summed_logs(signed, logs3)
        lift_ref[...] = packed_thirds(jnp.exp(offset), heads)
        drop_ref[...] = packed_thirds(jnp.exp(-offset), heads)
        chunk = lax.broadcasted_iota(jnp.int32, (2 * chunks, local), 0)
        token = lax.broadcasted_iota(jnp.int32, (2 * chunks, local), 1)
        inside = (token // SUB) == (chunk % chunks)
        first = token % SUB <= SUB // 2
        taken = inside & (first == (chunk < chunks))
        rows_ref[...] = packed_thirds(jnp.exp(summed_logs(taken.astype(F32).astype(BF16), logs3)), heads)
        mixed_ref[...] = jnp.zeros(mixed_ref.shape, F32)
        out_ref[...] = jnp.zeros(out_ref.shape, F32)
        map_ref[...] = jnp.zeros(map_ref.shape, F32)
        earlier = lax.broadcasted_iota(jnp.int32, (SUB, SUB), 0) <= lax.broadcasted_iota(jnp.int32, (SUB, SUB), 1)
        for k in range(chunks):
            at = pl.ds(k * SUB, SUB)
            score = jnp.where(earlier, dot(b_ref[at, :], c_ref[at, :], NT), 0.0)
            scores_ref[0, at, :], scores_ref[1, at, :] = halves(score)

    table = spread(heads, step * (tile // P_SIZE), tile)
    dys_ref[0], dys_ref[1] = halves(dy_ref[...].astype(F32) * dot(lift_ref[...], table))
    drop = dot(drop_ref[...], table)
    xs_ref[0], xs_ref[1] = halves(x_ref[...].astype(F32) * drop)
    row = dot(rows_ref[...], table)

    state = None
    for k in range(chunks):
        at = pl.ds(k * SUB, SUB)
        dys = dys_ref[0, at, :], dys_ref[1, at, :]
        xs = xs_ref[0, at, :], xs_ref[1, at, :]
        to_middle, to_end = row[k : k + 1], row[chunks + k : chunks + k + 1]
        mixed_ref[at, :] += dot22(dys, xs, NT)
        if state is not None:
            out_ref[at, :] += dot22(dys, halves(state * to_middle), NT)
        if k < chunks - 1:
            gained = to_end * dot12(bt_ref[:, k * SUB : (k + 1) * SUB], xs)
            state = gained if state is None else (to_middle * to_end) * state + gained
    grad = None
    for k in reversed(range(chunks)):
        at = pl.ds(k * SUB, SUB)
        dys = dys_ref[0, at, :], dys_ref[1, at, :]
        xs = xs_ref[0, at, :], xs_ref[1, at, :]
        to_middle, to_end = row[k : k + 1], row[chunks + k : chunks + k + 1]
        scores = scores_ref[0, at, :], scores_ref[1, at, :]
        summed = dot22(scores, dys)
        if grad is not None:
            scaled = halves(grad * to_end)
            summed = summed + dot12(b_ref[at, :], scaled)
            map_ref[at, :] += dot22(xs, scaled, NT)
        part_ref[at, :] = drop[k * SUB : (k + 1) * SUB] * summed
        if k > 0:
            gained = to_middle * dot12(ct_ref[:, k * SUB : (k + 1) * SUB], dys)
            grad = gained if grad is None else (to_middle * to_end) * grad + gained

    @pl.when(step == pl.num_programs(0) - 1)
    def _():
        causal = lax.broadcasted_iota(jnp.int32, (SUB, SUB), 0) >= lax.broadcasted_iota(jnp.int32, (SUB, SUB), 1)
        for k in range(chunks):
            at = pl.ds(k * SUB, SUB)
            mixed = jnp.where(causal, mixed_ref[at, :], 0.0)
            out_ref[at, :] += dot21(halves(mixed), b_ref[at, :])
            map_ref[at, :] += dot21(halves(mixed.T), c_ref[at, :])


def local_part(x, dy, b, c, bt, ct, decays):
    local, width = x.shape
    heads = width // P_SIZE
    count = width // TILE
    chunks = local // SUB
    whole = lambda a: pl.BlockSpec(a.shape, lambda j: (0, 0))
    column = pl.BlockSpec((local, TILE), lambda j: (0, j))
    tokens = pl.BlockSpec((local, N), lambda j: (0, 0))
    return pl.pallas_call(
        functools.partial(local_kernel, heads),
        grid=(count,),
        in_specs=[column, column, whole(b), whole(c), whole(bt), whole(ct), whole(decays)],
        out_specs=(column, tokens, tokens),
        out_shape=(
            jax.ShapeDtypeStruct((local, width), F32),
            jax.ShapeDtypeStruct((local, N), F32),
            jax.ShapeDtypeStruct((local, N), F32),
        ),
        scratch_shapes=[
            pltpu.VMEM((local, 3 * heads), BF16),
            pltpu.VMEM((local, 3 * heads), BF16),
            pltpu.VMEM((2 * chunks, 3 * heads), BF16),
            pltpu.VMEM((local, SUB), F32),
            pltpu.VMEM((2, local, SUB), BF16),
            pltpu.VMEM((2, local, TILE), BF16),
            pltpu.VMEM((2, local, TILE), BF16),
        ],
        compiler_params=pltpu.CompilerParams(vmem_limit_bytes=32 * 1024 * 1024),
        name="local_part",
        cost_estimate=pl.CostEstimate(flops=40 * local * N * width, bytes_accessed=8 * local * width, transcendentals=0),
    )(x, dy, b, c, bt, ct, decays)


def out_kernel(heads, count, pick_ref, dy_ref, pre_ref, state_ref, before_ref, out_ref):
    tile = dy_ref.shape[1]

    @pl.when(pl.program_id(0) == 0)
    def _():
        out_ref[...] = before_ref[...]

    table = spread(heads, (pick_ref[0] * count + pl.program_id(0)) * (tile // P_SIZE), tile)
    scaled = halves(dy_ref[...].astype(F32) * dot(pre_ref[...], table))
    out_ref[...] += dot22(scaled, halves(state_ref[...]), NT)


def out_terms(half, dy, pre, state, before):
    local, width = dy.shape
    heads = width // P_SIZE
    count = width // 2 // TILE
    tokens = pl.BlockSpec((local, N), lambda j, pick: (0, 0))
    return pl.pallas_call(
        functools.partial(out_kernel, heads, count),
        grid_spec=pltpu.PrefetchScalarGridSpec(
            num_scalar_prefetch=1,
            grid=(count,),
            in_specs=[
                pl.BlockSpec((local, TILE), lambda j, pick: (0, pick[0] * count + j)),
                pl.BlockSpec(pre.shape, lambda j, pick: (0, 0)),
                pl.BlockSpec((N, TILE), lambda j, pick: (0, j)),
                tokens,
            ],
            out_specs=tokens,
        ),
        out_shape=jax.ShapeDtypeStruct((local, N), F32),
        name="out_terms",
        cost_estimate=pl.CostEstimate(flops=6 * local * N * width // 2, bytes_accessed=2 * local * width, transcendentals=0),
    )(half, dy, pre, state, before)


def in_kernel(heads, count, pick_ref, x_ref, suf_ref, b_ref, grad_ref, part_ref, before_ref, *refs):
    input_ref, map_ref = refs[-2:]
    tile = x_ref.shape[1]

    @pl.when(pl.program_id(0) == 0)
    def _():
        map_ref[...] = before_ref[...]

    table = spread(heads, (pick_ref[0] * count + pl.program_id(0)) * (tile // P_SIZE), tile)
    after = dot(suf_ref[...], table)
    scaled = halves(x_ref[...].astype(F32) * after)
    grad = halves(grad_ref[...])
    map_ref[...] += dot22(scaled, grad, NT)
    input_ref[...] = (part_ref[...] + after * dot12(b_ref[...], grad)).astype(BF16)


def in_terms(half, x, suf, b, grad, part, before, filled=None):
    local, width = x.shape
    heads = width // P_SIZE
    count = width // 2 // TILE
    whole = lambda a: pl.BlockSpec(a.shape, lambda j, pick: (0, 0))
    column = pl.BlockSpec((local, TILE), lambda j, pick: (0, pick[0] * count + j))
    tokens = pl.BlockSpec((local, N), lambda j, pick: (0, 0))
    in_specs = [column, whole(suf), whole(b), pl.BlockSpec((N, TILE), lambda j, pick: (0, j)), column, tokens]
    args = [half, x, suf, b, grad, part, before]
    aliases = {}
    if filled is not None:
        in_specs.append(pl.BlockSpec(memory_space=pl.ANY))
        args.append(filled)
        aliases = {7: 0}
    return pl.pallas_call(
        functools.partial(in_kernel, heads, count),
        grid_spec=pltpu.PrefetchScalarGridSpec(
            num_scalar_prefetch=1, grid=(count,), in_specs=in_specs, out_specs=(column, tokens)
        ),
        out_shape=(jax.ShapeDtypeStruct((local, width), BF16), jax.ShapeDtypeStruct((local, N), F32)),
        input_output_aliases=aliases,
        name="in_terms",
        cost_estimate=pl.CostEstimate(flops=10 * local * N * width // 2, bytes_accessed=4 * local * width, transcendentals=0),
    )(*args)


def swap_cores(v, length):
    return lax.ppermute(v, "seq", [(i, i ^ 1) for i in range(length)])


def shifted(v, length, by):
    pairs = [(i, i + 2 * by) for i in range(length) if 0 <= i + 2 * by < length]
    return lax.ppermute(v, "seq", pairs)


def head_sum(v):
    return lax.psum_scatter(v, "head", scatter_dimension=0, tiled=True)


def per_device(mixer_input, output_grad, input_map, output_map, decays):
    length = lax.axis_size("seq")
    chips = length // 2
    core = jnp.reshape(lax.axis_index("seq") % 2, (1,)).astype(jnp.int32)
    other = 1 - core
    bt, ct = input_map.T, output_map.T
    pre, suf = factors(decays)
    sent = totals(other, mixer_input, output_grad, bt, ct, pre, suf)
    recv = swap_cores(sent, length)
    mine = totals(core, mixer_input, output_grad, bt, ct, pre, suf)
    state_total, grad_total = chip_totals(core, mine, recv)
    states = [shifted(state_total, length, r) for r in range(1, chips)]
    grads = [shifted(grad_total, length, -r) for r in range(1, chips)]
    part, map_part, out_part = local_part(mixer_input, output_grad, input_map, output_map, bt, ct, decays)

    state_own, state_peer = carried(True, core, mine, recv, states)
    state_other = swap_cores(state_peer, length)
    out_part = out_terms(core, output_grad, pre, state_own, out_part)
    out_part = out_terms(other, output_grad, pre, state_other, out_part)
    output_map_grad = head_sum(out_part)

    grad_own, grad_peer = carried(False, core, mine, recv, grads)
    grad_other = swap_cores(grad_peer, length)
    input_grad, map_part = in_terms(core, mixer_input, suf, input_map, grad_own, part, map_part)
    input_grad, map_part = in_terms(other, mixer_input, suf, input_map, grad_other, part, map_part, input_grad)
    input_map_grad = head_sum(map_part)
    return input_grad, input_map_grad, output_map_grad


def solution(mesh):
    in_specs = (
        P("seq", "head"),
        P("seq", "head"),
        P("seq", None),
        P("seq", None),
        P("head", "seq"),
    )
    out_specs = (P("seq", "head"), P(("seq", "head"), None), P(("seq", "head"), None))
    return jax.shard_map(
        per_device, mesh=mesh, in_specs=in_specs, out_specs=out_specs, check_vma=False
    )
```

```python
import functools

import jax
import jax.numpy as jnp
from jax import lax
from jax.experimental import pallas as pl
from jax.experimental.pallas import tpu as pltpu
from jax.sharding import PartitionSpec as P

P_SIZE = 64
N = 128
SUB = 64
TILE = 256
EXTRA = 8
PARAMS = pltpu.CompilerParams(vmem_limit_bytes=56 * 1024 * 1024)
F32 = jnp.float32
BF16 = jnp.bfloat16

NN = (((1,), (0,)), ((), ()))
NT = (((1,), (1,)), ((), ()))


def dot(a, b, dims=NN):
    return lax.dot_general(a, b, dims, preferred_element_type=F32)


def halves(v):
    hi = v.astype(BF16)
    return hi, (v - hi.astype(F32)).astype(BF16)


def dot21(pair, b, dims=NN):
    return dot(pair[0], b, dims) + dot(pair[1], b, dims)


def dot12(a, pair, dims=NN):
    return dot(a, pair[0], dims) + dot(a, pair[1], dims)


def dot22(p, q, dims=NN):
    return dot(p[0], q[0], dims) + (dot(p[0], q[1], dims) + dot(p[1], q[0], dims))


def thirds(v):
    hi = v.astype(BF16)
    rest = v - hi.astype(F32)
    mid = rest.astype(BF16)
    return hi, mid, (rest - mid.astype(F32)).astype(BF16)


def packed_thirds(v, heads):
    hi, mid, lo = thirds(v)
    group = lax.broadcasted_iota(jnp.int32, v.shape, 1) // heads
    picked = jnp.where(group == 0, hi.astype(F32), jnp.where(group == 1, mid.astype(F32), lo.astype(F32)))
    return picked.astype(BF16)


def spread(heads, first, width):
    rows = lax.broadcasted_iota(jnp.int32, (3 * heads, width), 0)
    columns = lax.broadcasted_iota(jnp.int32, (3 * heads, width), 1)
    return (rows % heads == first + columns // P_SIZE).astype(F32).astype(BF16)


def stacked(*parts):
    return jnp.concatenate(parts, axis=0)


def transposed(v):
    return v.astype(F32).T.astype(BF16)


def summed_logs(table, logs3):
    return dot(table, logs3[0], NT) + (dot(table, logs3[1], NT) + dot(table, logs3[2], NT))


def log_parts(decays):
    logs = jnp.log(decays)
    return tuple(jnp.concatenate([part.astype(F32)] * 3, axis=0).astype(BF16) for part in thirds(logs))


def device_factors(decays, pre_ref, suf_ref):
    heads, local = decays.shape
    logs3 = log_parts(decays)
    rows = lax.broadcasted_iota(jnp.int32, (local, local), 0)
    columns = lax.broadcasted_iota(jnp.int32, (local, local), 1)
    upto = (columns <= rows).astype(F32).astype(BF16)
    after = (columns > rows).astype(F32).astype(BF16)
    pre_ref[...] = packed_thirds(jnp.exp(summed_logs(upto, logs3)), heads)
    suf_ref[...] = packed_thirds(jnp.exp(summed_logs(after, logs3)), heads)


def totals_kernel(heads, count, pick_ref, x_ref, dy_ref, b_ref, c_ref, *refs):
    if len(refs) == 6:
        decays_ref, out_ref, pre_ref, suf_ref, bt_ref, ct_ref = refs
    else:
        pre_ref, suf_ref, out_ref, bt_ref, ct_ref = refs
        decays_ref = None
    step = pl.program_id(0)

    @pl.when(step == 0)
    def _():
        bt_ref[...] = transposed(b_ref[...])
        ct_ref[...] = transposed(c_ref[...])
        if decays_ref is not None:
            device_factors(decays_ref[...], pre_ref, suf_ref)

    tile = x_ref.shape[1]
    table = spread(heads, (pick_ref[0] * count + step) * (tile // P_SIZE), tile)
    before = dot(pre_ref[...], table)
    after = dot(suf_ref[...], table)
    ended = before[before.shape[0] - 1 :, :]
    out_ref[0, :N, :] = dot12(bt_ref[...], halves(x_ref[...].astype(F32) * after))
    out_ref[1, :N, :] = dot12(ct_ref[...], halves(dy_ref[...].astype(F32) * before))
    out_ref[0, N:, :] = jnp.broadcast_to(ended, (EXTRA, tile))
    out_ref[1, N:, :] = jnp.broadcast_to(ended, (EXTRA, tile))


def totals(half, x, dy, b, c, decays=None, pre=None, suf=None):
    local, width = x.shape
    heads = width // P_SIZE
    count = width // 2 // TILE
    whole = lambda a: pl.BlockSpec(a.shape, lambda j, pick: (0, 0))
    column = pl.BlockSpec((local, TILE), lambda j, pick: (0, pick[0] * count + j))
    factor = jax.ShapeDtypeStruct((local, 3 * heads), BF16)
    rest = (pre, suf) if decays is None else (decays,)
    out_specs = [pl.BlockSpec((2, N + EXTRA, TILE), lambda j, pick: (0, 0, j))]
    out_shape = [jax.ShapeDtypeStruct((2, N + EXTRA, width // 2), F32)]
    if decays is not None:
        out_specs += [whole(factor), whole(factor)]
        out_shape += [factor, factor]
    return pl.pallas_call(
        functools.partial(totals_kernel, heads, count),
        grid_spec=pltpu.PrefetchScalarGridSpec(
            num_scalar_prefetch=1,
            grid=(count,),
            in_specs=[column, column, whole(b), whole(c)] + [whole(a) for a in rest],
            out_specs=out_specs,
            scratch_shapes=[pltpu.VMEM((N, local), BF16), pltpu.VMEM((N, local), BF16)],
        ),
        out_shape=out_shape,
        compiler_params=PARAMS,
        name="state_totals",
        cost_estimate=pl.CostEstimate(flops=8 * local * N * width // 2, bytes_accessed=4 * local * width, transcendentals=0),
    )(half, x, dy, b, c, *rest)


def ordered(core, mine, recv):
    return jnp.where(core == 0, mine, recv), jnp.where(core == 0, recv, mine)


def chip_kernel(chips, place_ref, mine_ref, recv_ref, *out_refs):
    core, chip = place_ref[0], place_ref[1]
    early, late = ordered(core, mine_ref[0], recv_ref[0])
    early_decay, late_decay = early[N : N + 1], late[N : N + 1]
    both = jnp.broadcast_to(early_decay * late_decay, (EXTRA, early.shape[1]))
    state = late_decay * early[:N] + late[:N]
    early, late = ordered(core, mine_ref[1], recv_ref[1])
    grad = early[:N] + early_decay * late[:N]
    for r, out_ref in enumerate(out_refs, 1):
        out_ref[:N, :] = jnp.where(chip + r < chips, state, grad)
        out_ref[N:, :] = both


def chip_totals(chips, place, mine, recv):
    width = mine.shape[2]
    tile = min(512, width)
    block = pl.BlockSpec((2, N + EXTRA, tile), lambda j, pick: (0, 0, j))
    out = pl.BlockSpec((N + EXTRA, tile), lambda j, pick: (0, j))
    shape = jax.ShapeDtypeStruct((N + EXTRA, width), F32)
    return pl.pallas_call(
        functools.partial(chip_kernel, chips),
        grid_spec=pltpu.PrefetchScalarGridSpec(
            num_scalar_prefetch=1, grid=(width // tile,), in_specs=[block, block], out_specs=[out] * (chips - 1)
        ),
        out_shape=[shape] * (chips - 1),
        compiler_params=PARAMS,
        name="chip_totals",
        cost_estimate=pl.CostEstimate(flops=6 * N * width, bytes_accessed=24 * N * width, transcendentals=0),
    )(place, mine, recv)


def carried_kernel(chips, place_ref, mine_ref, recv_ref, *refs):
    others, (own_ref, peer_ref) = refs[:-2], refs[-2:]
    core, chip = place_ref[0], place_ref[1]
    state = grad = jnp.zeros((N, own_ref.shape[2]), F32)
    state_weight = grad_weight = jnp.ones((1, own_ref.shape[2]), F32)
    for r, ref in enumerate(others, 1):
        earlier = chip >= r
        state = jnp.where(earlier, state + state_weight * ref[:N, :], state)
        state_weight = state_weight * ref[N : N + 1, :]
    for r in range(1, chips):
        later = chip + r < chips
        ref = others[chips - r - 1]
        grad = jnp.where(later, grad + grad_weight * ref[:N, :], grad)
        grad_weight = grad_weight * ref[N : N + 1, :]
    early, late = ordered(core, mine_ref[0], recv_ref[0])
    at_late = early[N : N + 1] * state + early[:N]
    own_ref[0] = jnp.where(core == 0, state, at_late)
    peer_ref[0] = jnp.where(core == 0, at_late, state)
    early, late = ordered(core, mine_ref[1], recv_ref[1])
    at_early = late[:N] + late[N : N + 1] * grad
    own_ref[1] = jnp.where(core == 0, at_early, grad)
    peer_ref[1] = jnp.where(core == 0, grad, at_early)


def carried(chips, place, mine, recv, others):
    width = mine.shape[2]
    tile = min(512, width)
    pair = pl.BlockSpec((2, N + EXTRA, tile), lambda j, pick: (0, 0, j))
    other = pl.BlockSpec((N + EXTRA, tile), lambda j, pick: (0, j))
    out = pl.BlockSpec((2, N, tile), lambda j, pick: (0, 0, j))
    shape = jax.ShapeDtypeStruct((2, N, width), F32)
    return pl.pallas_call(
        functools.partial(carried_kernel, chips),
        grid_spec=pltpu.PrefetchScalarGridSpec(
            num_scalar_prefetch=1,
            grid=(width // tile,),
            in_specs=[pair, pair] + [other] * len(others),
            out_specs=(out, out),
        ),
        out_shape=(shape, shape),
        compiler_params=PARAMS,
        name="carried_in",
        cost_estimate=pl.CostEstimate(flops=20 * N * width, bytes_accessed=44 * N * width, transcendentals=0),
    )(place, mine, recv, *others)


def local_kernel(
    heads, x_ref, dy_ref, b_ref, c_ref, decays_ref, part_ref, out_ref, map_ref,
    lift_ref, drop_ref, rows_ref, sums_ref, scores_ref, twice_ref, bt_ref, ct_ref, dys_ref, xs_ref,
):
    local, tile = x_ref.shape
    chunks = local // SUB
    step = pl.program_id(0)

    @pl.when(step == 0)
    def _():
        logs3 = log_parts(decays_ref[...])
        rows = lax.broadcasted_iota(jnp.int32, (local, local), 0)
        columns = lax.broadcasted_iota(jnp.int32, (local, local), 1)
        middle = (rows // SUB) * SUB + SUB // 2
        same = rows // SUB == columns // SUB
        later = same & (columns > middle) & (columns <= rows)
        sooner = same & (columns > rows) & (columns <= middle)
        signed = (later.astype(F32) - sooner.astype(F32)).astype(BF16)
        offset = summed_logs(signed, logs3)
        lift_ref[...] = packed_thirds(jnp.exp(offset), heads)
        drop_ref[...] = packed_thirds(jnp.exp(-offset), heads)
        chunk = lax.broadcasted_iota(jnp.int32, (2 * chunks, local), 0)
        token = lax.broadcasted_iota(jnp.int32, (2 * chunks, local), 1)
        inside = (token // SUB) == (chunk % chunks)
        first = token % SUB <= SUB // 2
        taken = inside & (first == (chunk < chunks))
        rows_ref[...] = packed_thirds(jnp.exp(summed_logs(taken.astype(F32).astype(BF16), logs3)), heads)
        sums_ref[...] = jnp.zeros(sums_ref.shape, F32)
        map_ref[...] = jnp.zeros(map_ref.shape, F32)
        twice_ref[:, :N] = b_ref[...]
        twice_ref[:, N:] = b_ref[...]
        sooner = lax.broadcasted_iota(jnp.int32, (SUB, SUB), 0) <= lax.broadcasted_iota(jnp.int32, (SUB, SUB), 1)
        for k in range(chunks):
            at = pl.ds(k * SUB, SUB)
            hi, lo = halves(jnp.where(sooner, dot(b_ref[at, :], c_ref[at, :], NT), 0.0))
            scores_ref[at, :SUB] = hi
            scores_ref[at, SUB : 2 * SUB] = lo
            scores_ref[at, 2 * SUB :] = hi
            bt_ref[k] = transposed(stacked(b_ref[at, :], b_ref[at, :]))
            ct_ref[k] = transposed(stacked(c_ref[at, :], c_ref[at, :]))

    table = spread(heads, step * (tile // P_SIZE), tile)
    dys_ref[0], dys_ref[1] = halves(dy_ref[...].astype(F32) * dot(lift_ref[...], table))
    drop = dot(drop_ref[...], table)
    xs_ref[0], xs_ref[1] = halves(x_ref[...].astype(F32) * drop)
    row = dot(rows_ref[...], table)

    state = None
    for k in range(chunks):
        at = pl.ds(k * SUB, SUB)
        dys, xs = (dys_ref[0, at, :], dys_ref[1, at, :]), (xs_ref[0, at, :], xs_ref[1, at, :])
        to_middle, to_end = row[k : k + 1], row[chunks + k : chunks + k + 1]
        if state is None:
            against = xs
        else:
            scaled = halves(state * to_middle)
            against = stacked(scaled[0], xs[0]), stacked(scaled[1], xs[1])
        both = dot(stacked(*dys), against[0], NT)
        summed = both[:SUB] + (both[SUB:] + dot(dys[0], against[1], NT))
        if state is None:
            sums_ref[at, N:] += summed
        else:
            sums_ref[at, :] += summed
        if k < chunks - 1:
            gained = to_end * dot(bt_ref[k], stacked(*xs))
            state = gained if state is None else (to_middle * to_end) * state + gained
    grad = None
    for k in reversed(range(chunks)):
        at = pl.ds(k * SUB, SUB)
        dys, xs = (dys_ref[0, at, :], dys_ref[1, at, :]), (xs_ref[0, at, :], xs_ref[1, at, :])
        to_middle, to_end = row[k : k + 1], row[chunks + k : chunks + k + 1]
        summed = dot(scores_ref[at, :], stacked(dys[0], dys[0], dys[1]))
        if grad is not None:
            scaled = halves(grad * to_end)
            summed = summed + dot(twice_ref[at, :], stacked(*scaled))
            both = dot(stacked(*xs), scaled[0], NT)
            map_ref[at, :] += both[:SUB] + (both[SUB:] + dot(xs[0], scaled[1], NT))
        part_ref[at, :] = drop[k * SUB : (k + 1) * SUB] * summed
        if k > 0:
            gained = to_middle * dot(ct_ref[k], stacked(*dys))
            grad = gained if grad is None else (to_middle * to_end) * grad + gained

    @pl.when(step == pl.num_programs(0) - 1)
    def _():
        causal = lax.broadcasted_iota(jnp.int32, (SUB, SUB), 0) >= lax.broadcasted_iota(jnp.int32, (SUB, SUB), 1)
        for k in range(chunks):
            at = pl.ds(k * SUB, SUB)
            mixed = jnp.where(causal, sums_ref[at, N:], 0.0)
            out_ref[at, :] = sums_ref[at, :N] + dot21(halves(mixed), b_ref[at, :])
            map_ref[at, :] += dot21(halves(mixed.T), c_ref[at, :])


def local_part(x, dy, b, c, decays):
    local, width = x.shape
    heads = width // P_SIZE
    count = width // TILE
    chunks = local // SUB
    whole = lambda a: pl.BlockSpec(a.shape, lambda j: (0, 0))
    column = pl.BlockSpec((local, TILE), lambda j: (0, j))
    tokens = pl.BlockSpec((local, N), lambda j: (0, 0))
    return pl.pallas_call(
        functools.partial(local_kernel, heads),
        grid=(count,),
        in_specs=[column, column, whole(b), whole(c), whole(decays)],
        out_specs=(column, tokens, tokens),
        out_shape=(
            jax.ShapeDtypeStruct((local, width), F32),
            jax.ShapeDtypeStruct((local, N), F32),
            jax.ShapeDtypeStruct((local, N), F32),
        ),
        scratch_shapes=[
            pltpu.VMEM((local, 3 * heads), BF16),
            pltpu.VMEM((local, 3 * heads), BF16),
            pltpu.VMEM((2 * chunks, 3 * heads), BF16),
            pltpu.VMEM((local, N + SUB), F32),
            pltpu.VMEM((local, 3 * SUB), BF16),
            pltpu.VMEM((local, 2 * N), BF16),
            pltpu.VMEM((chunks, N, 2 * SUB), BF16),
            pltpu.VMEM((chunks, N, 2 * SUB), BF16),
            pltpu.VMEM((2, local, TILE), BF16),
            pltpu.VMEM((2, local, TILE), BF16),
        ],
        compiler_params=PARAMS,
        name="local_part",
        cost_estimate=pl.CostEstimate(flops=40 * local * N * width, bytes_accessed=8 * local * width, transcendentals=0),
    )(x, dy, b, c, decays)


def map_kernel(heads, count, ranks, pick_ref, x_ref, dy_ref, pre_ref, suf_ref, carry_ref, out_before_ref, map_before_ref, *refs):
    messages, (out_ref, map_ref) = refs[:-2], refs[-2:]
    step = pl.program_id(0)
    tile = dy_ref.shape[1]

    @pl.when(step == 0)
    def _():
        out_ref[...] = out_before_ref[...]
        map_ref[...] = map_before_ref[...]

    table = spread(heads, (pick_ref[0] * count + step) * (tile // P_SIZE), tile)
    scaled = halves(dy_ref[...].astype(F32) * dot(pre_ref[...], table))
    out_ref[...] += dot22(scaled, halves(carry_ref[0]), NT)
    scaled = halves(x_ref[...].astype(F32) * dot(suf_ref[...], table))
    map_ref[...] += dot22(scaled, halves(carry_ref[1]), NT)

    if messages:

        @pl.when(step == count - 1)
        def _():
            rows = messages[0].shape[1]
            for r, message in enumerate(messages):
                at = pl.ds(pl.multiple_of(((pick_ref[1] + r) % ranks) * rows, rows), rows)
                message[0] = out_ref[at, :]
                message[1] = map_ref[at, :]


def map_terms(pick, x, dy, pre, suf, carry, out_before, map_before, ranks=0):
    local, width = dy.shape
    heads = width // P_SIZE
    count = width // 2 // TILE
    whole = lambda a: pl.BlockSpec(a.shape, lambda j, pick: (0,) * len(a.shape))
    tokens = jax.ShapeDtypeStruct((local, N), F32)
    column = pl.BlockSpec((local, TILE), lambda j, pick: (0, pick[0] * count + j))
    if ranks:
        out_shape = [jax.ShapeDtypeStruct((2, local // ranks, N), F32)] * ranks
        scratch = [pltpu.VMEM((local, N), F32), pltpu.VMEM((local, N), F32)]
    else:
        out_shape, scratch = [tokens, tokens], []
    return pl.pallas_call(
        functools.partial(map_kernel, heads, count, ranks),
        grid_spec=pltpu.PrefetchScalarGridSpec(
            num_scalar_prefetch=1,
            grid=(count,),
            in_specs=[
                column,
                column,
                whole(pre),
                whole(suf),
                pl.BlockSpec((2, N, TILE), lambda j, pick: (0, 0, j)),
                whole(tokens),
                whole(tokens),
            ],
            out_specs=[whole(shape) for shape in out_shape],
            scratch_shapes=scratch,
        ),
        out_shape=out_shape,
        compiler_params=PARAMS,
        name="map_terms",
        cost_estimate=pl.CostEstimate(flops=12 * local * N * width // 2, bytes_accessed=4 * local * width, transcendentals=0),
    )(pick, x, dy, pre, suf, carry, out_before, map_before)


def input_kernel(heads, count, pick_ref, part_ref, suf_ref, b_ref, own_ref, other_ref, input_ref):
    tile = part_ref.shape[1]
    step = pl.program_id(0)
    after = dot(suf_ref[...], spread(heads, step * (tile // P_SIZE), tile))
    grad = jnp.where(step // count == pick_ref[0], own_ref[0], other_ref[0])
    input_ref[...] = (part_ref[...] + after * dot12(b_ref[...], halves(grad))).astype(BF16)


def input_terms(core, part, suf, b, own, other):
    local, width = part.shape
    heads = width // P_SIZE
    count = width // 2 // TILE
    whole = lambda a: pl.BlockSpec(a.shape, lambda j, pick: (0, 0))
    column = pl.BlockSpec((local, TILE), lambda j, pick: (0, j))
    carry = pl.BlockSpec((1, N, TILE), lambda j, pick: (1, 0, j % count))
    return pl.pallas_call(
        functools.partial(input_kernel, heads, count),
        grid_spec=pltpu.PrefetchScalarGridSpec(
            num_scalar_prefetch=1,
            grid=(2 * count,),
            in_specs=[column, whole(suf), whole(b), carry, carry],
            out_specs=column,
        ),
        out_shape=jax.ShapeDtypeStruct((local, width), BF16),
        compiler_params=PARAMS,
        name="input_terms",
        cost_estimate=pl.CostEstimate(flops=4 * local * N * width, bytes_accessed=8 * local * width, transcendentals=0),
    )(core, part, suf, b, own, other)


def swap_cores(v, length):
    return lax.ppermute(v, "seq", [(i, i ^ 1) for i in range(length)])


def turned(v, axis, length, by):
    return lax.ppermute(v, axis, [(i, (i + by) % length) for i in range(length)])


def per_device(mixer_input, output_grad, input_map, output_map, decays):
    length, ranks = lax.axis_size("seq"), lax.axis_size("head")
    chips = length // 2
    index, rank = lax.axis_index("seq"), lax.axis_index("head")
    core, chip = index % 2, index // 2
    place = jnp.stack([core, chip]).astype(jnp.int32)
    here = jnp.stack([core, rank]).astype(jnp.int32)
    there = jnp.stack([1 - core, rank]).astype(jnp.int32)
    sent, pre, suf = totals(there, mixer_input, output_grad, input_map, output_map, decays=decays)
    recv = swap_cores(sent, length)
    (mine,) = totals(here, mixer_input, output_grad, input_map, output_map, pre=pre, suf=suf)
    messages = chip_totals(chips, place, mine, recv)
    others = [turned(message, "seq", length, 2 * r) for r, message in enumerate(messages, 1)]
    part, out_part, map_part = local_part(mixer_input, output_grad, input_map, output_map, decays)
    others, part, out_part, map_part = lax.optimization_barrier((others, part, out_part, map_part))
    own, peer = carried(chips, place, mine, recv, others)
    other = swap_cores(peer, length)
    out_part, map_part = map_terms(here, mixer_input, output_grad, pre, suf, own, out_part, map_part)
    shares = map_terms(there, mixer_input, output_grad, pre, suf, other, out_part, map_part, ranks)
    total = shares[0]
    own, other, shares = lax.optimization_barrier((own, other, shares))
    for r in range(1, ranks):
        total = total + turned(shares[r], "head", ranks, r)
    input_grad = input_terms(place, part, suf, input_map, own, other)
    return input_grad, total[1], total[0]


def solution(mesh):
    in_specs = (
        P("seq", "head"),
        P("seq", "head"),
        P("seq", None),
        P("seq", None),
        P("head", "seq"),
    )
    out_specs = (P("seq", "head"), P(("seq", "head"), None), P(("seq", "head"), None))
    return jax.shard_map(
        per_device, mesh=mesh, in_specs=in_specs, out_specs=out_specs, check_vma=False
    )
```

```python
import functools

import jax
import jax.numpy as jnp
from jax import lax
from jax.experimental import pallas as pl
from jax.experimental.pallas import tpu as pltpu
from jax.sharding import PartitionSpec as P

P_SIZE = 64
N = 128
SUB = 64
TILE = 256
EXTRA = 8
LANES = 128
CORE, OTHER, CHIP, RANK = range(4)
PARAMS = pltpu.CompilerParams(vmem_limit_bytes=24 * 1024 * 1024)
F32 = jnp.float32
BF16 = jnp.bfloat16

NN = (((1,), (0,)), ((), ()))
NT = (((1,), (1,)), ((), ()))


def dot(a, b, dims=NN):
    return lax.dot_general(a, b, dims, preferred_element_type=F32)


def halves(v):
    hi = v.astype(BF16)
    return hi, (v - hi.astype(F32)).astype(BF16)


def dot21(pair, b, dims=NN):
    return dot(pair[0], b, dims) + dot(pair[1], b, dims)


def dot12(a, pair, dims=NN):
    return dot(a, pair[0], dims) + dot(a, pair[1], dims)


def dot22(p, q, dims=NN):
    return dot(p[0], q[0], dims) + (dot(p[0], q[1], dims) + dot(p[1], q[0], dims))


def thirds(v):
    hi = v.astype(BF16)
    rest = v - hi.astype(F32)
    mid = rest.astype(BF16)
    return hi, mid, (rest - mid.astype(F32)).astype(BF16)


def spread(heads, first, width):
    rows = lax.broadcasted_iota(jnp.int32, (heads, width), 0)
    columns = lax.broadcasted_iota(jnp.int32, (heads, width), 1)
    offset = columns - (rows - first) * P_SIZE
    picked = ((offset >= 0) & (offset < P_SIZE)).astype(F32)
    rest = jnp.zeros((LANES - 3 * heads, width), F32)
    return jnp.concatenate([picked, picked, picked, rest], axis=0).astype(BF16)


def stacked(*parts):
    return jnp.concatenate(parts, axis=0)


def transposed(v):
    return v.astype(F32).T.astype(BF16)


def log_parts(decays):
    return jnp.concatenate([part.astype(F32) for part in thirds(jnp.log(decays))], axis=0).astype(BF16)


def summed_logs(logs, table):
    heads = logs.shape[0] // 3
    sums = dot(logs, table.astype(F32).astype(BF16))
    return sums[:heads] + (sums[heads : 2 * heads] + sums[2 * heads :])


def packed(v):
    parts = [part.astype(F32) for part in thirds(v)]
    rest = jnp.zeros((LANES - 3 * v.shape[0], v.shape[1]), F32)
    return jnp.concatenate(parts + [rest], axis=0).T.astype(BF16)


def device_factors(decays, pre_ref, suf_ref):
    local = decays.shape[1]
    logs = log_parts(decays)
    rows = lax.broadcasted_iota(jnp.int32, (local, local), 0)
    columns = lax.broadcasted_iota(jnp.int32, (local, local), 1)
    pre_ref[...] = packed(jnp.exp(summed_logs(logs, rows <= columns)))
    suf_ref[...] = packed(jnp.exp(summed_logs(logs, rows > columns)))


def totals_kernel(heads, count, half, place_ref, x_ref, dy_ref, b_ref, c_ref, *refs):
    if len(refs) == 7:
        decays_ref, out_ref, scaled_ref, pre_ref, suf_ref, bt_ref, ct_ref = refs
    else:
        pre_ref, suf_ref, out_ref, scaled_ref, bt_ref, ct_ref = refs
        decays_ref = None
    step = pl.program_id(0)

    @pl.when(step == 0)
    def _():
        bt_ref[...] = transposed(b_ref[...])
        ct_ref[...] = transposed(c_ref[...])
        if decays_ref is not None:
            device_factors(decays_ref[...], pre_ref, suf_ref)

    tile = x_ref.shape[1]
    table = spread(heads, (place_ref[half] * count + step) * (tile // P_SIZE), tile)
    before = dot(pre_ref[...], table)
    after = dot(suf_ref[...], table)
    ended = before[before.shape[0] - 1 :, :]
    for i, (source, factor, other) in enumerate(((x_ref, after, bt_ref), (dy_ref, before, ct_ref))):
        scaled = halves(source[...].astype(F32) * factor)
        scaled_ref[i, 0], scaled_ref[i, 1] = scaled
        out_ref[i, :N, :] = dot12(other[...], scaled)
    out_ref[0, N:, :] = jnp.broadcast_to(ended, (EXTRA, tile))
    out_ref[1, N:, :] = jnp.broadcast_to(ended, (EXTRA, tile))


def totals(half, place, x, dy, b, c, decays=None, pre=None, suf=None):
    local, width = x.shape
    heads = width // P_SIZE
    count = width // 2 // TILE
    whole = lambda a: pl.BlockSpec(a.shape, lambda j, pick: (0, 0))
    column = pl.BlockSpec((local, TILE), lambda j, pick: (0, pick[half] * count + j))
    factor = jax.ShapeDtypeStruct((local, LANES), BF16)
    rest = (pre, suf) if decays is None else (decays,)
    out_specs = [
        pl.BlockSpec((2, N + EXTRA, TILE), lambda j, pick: (0, 0, j)),
        pl.BlockSpec((2, 2, local, TILE), lambda j, pick: (0, 0, 0, j)),
    ]
    out_shape = [
        jax.ShapeDtypeStruct((2, N + EXTRA, width // 2), F32),
        jax.ShapeDtypeStruct((2, 2, local, width // 2), BF16),
    ]
    if decays is not None:
        out_specs += [whole(factor), whole(factor)]
        out_shape += [factor, factor]
    return pl.pallas_call(
        functools.partial(totals_kernel, heads, count, half),
        grid_spec=pltpu.PrefetchScalarGridSpec(
            num_scalar_prefetch=1,
            grid=(count,),
            in_specs=[column, column, whole(b), whole(c)] + [whole(a) for a in rest],
            out_specs=out_specs,
            scratch_shapes=[pltpu.VMEM((N, local), BF16), pltpu.VMEM((N, local), BF16)],
        ),
        out_shape=out_shape,
        compiler_params=PARAMS,
        name="state_totals",
        cost_estimate=pl.CostEstimate(flops=8 * local * N * width // 2, bytes_accessed=4 * local * width, transcendentals=0),
    )(place, x, dy, b, c, *rest)


def ordered(core, mine, recv):
    return jnp.where(core == 0, mine, recv), jnp.where(core == 0, recv, mine)


def chip_kernel(chips, place_ref, mine_ref, recv_ref, *out_refs):
    core, chip = place_ref[CORE], place_ref[CHIP]
    early, late = ordered(core, mine_ref[0], recv_ref[0])
    early_decay, late_decay = early[N : N + 1], late[N : N + 1]
    both = jnp.broadcast_to(early_decay * late_decay, (EXTRA, early.shape[1]))
    state = late_decay * early[:N] + late[:N]
    early, late = ordered(core, mine_ref[1], recv_ref[1])
    grad = early[:N] + early_decay * late[:N]
    for r, out_ref in enumerate(out_refs, 1):
        out_ref[:N, :] = jnp.where(chip + r < chips, state, grad)
        out_ref[N:, :] = both


def chip_totals(chips, place, mine, recv):
    width = mine.shape[2]
    tile = min(512, width)
    block = pl.BlockSpec((2, N + EXTRA, tile), lambda j, pick: (0, 0, j))
    out = pl.BlockSpec((N + EXTRA, tile), lambda j, pick: (0, j))
    shape = jax.ShapeDtypeStruct((N + EXTRA, width), F32)
    return pl.pallas_call(
        functools.partial(chip_kernel, chips),
        grid_spec=pltpu.PrefetchScalarGridSpec(
            num_scalar_prefetch=1, grid=(width // tile,), in_specs=[block, block], out_specs=[out] * (chips - 1)
        ),
        out_shape=[shape] * (chips - 1),
        compiler_params=PARAMS,
        name="chip_totals",
        cost_estimate=pl.CostEstimate(flops=6 * N * width, bytes_accessed=24 * N * width, transcendentals=0),
    )(place, mine, recv)


def carried_kernel(chips, place_ref, mine_ref, recv_ref, *refs):
    others, (own_ref, peer_ref) = refs[:-2], refs[-2:]
    core, chip = place_ref[CORE], place_ref[CHIP]
    state = grad = jnp.zeros((N, own_ref.shape[2]), F32)
    state_weight = grad_weight = jnp.ones((1, own_ref.shape[2]), F32)
    for r, ref in enumerate(others, 1):
        earlier = chip >= r
        state = jnp.where(earlier, state + state_weight * ref[:N, :], state)
        state_weight = state_weight * ref[N : N + 1, :]
    for r in range(1, chips):
        later = chip + r < chips
        ref = others[chips - r - 1]
        grad = jnp.where(later, grad + grad_weight * ref[:N, :], grad)
        grad_weight = grad_weight * ref[N : N + 1, :]
    early, late = ordered(core, mine_ref[0], recv_ref[0])
    at_late = early[N : N + 1] * state + early[:N]
    own_ref[0] = jnp.where(core == 0, state, at_late)
    peer_ref[0] = jnp.where(core == 0, at_late, state)
    early, late = ordered(core, mine_ref[1], recv_ref[1])
    at_early = late[:N] + late[N : N + 1] * grad
    own_ref[1] = jnp.where(core == 0, at_early, grad)
    peer_ref[1] = jnp.where(core == 0, grad, at_early)


def carried(chips, place, mine, recv, others):
    width = mine.shape[2]
    tile = min(512, width)
    pair = pl.BlockSpec((2, N + EXTRA, tile), lambda j, pick: (0, 0, j))
    other = pl.BlockSpec((N + EXTRA, tile), lambda j, pick: (0, j))
    out = pl.BlockSpec((2, N, tile), lambda j, pick: (0, 0, j))
    shape = jax.ShapeDtypeStruct((2, N, width), F32)
    return pl.pallas_call(
        functools.partial(carried_kernel, chips),
        grid_spec=pltpu.PrefetchScalarGridSpec(
            num_scalar_prefetch=1,
            grid=(width // tile,),
            in_specs=[pair, pair] + [other] * len(others),
            out_specs=(out, out),
        ),
        out_shape=(shape, shape),
        compiler_params=PARAMS,
        name="carried_in",
        cost_estimate=pl.CostEstimate(flops=20 * N * width, bytes_accessed=44 * N * width, transcendentals=0),
    )(place, mine, recv, *others)


def local_kernel(
    heads, x_ref, dy_ref, b_ref, c_ref, decays_ref, part_ref, out_ref, map_ref,
    lift_ref, drop_ref, rows_ref, sums_ref, scores_ref, twice_ref, bt_ref, ct_ref, dys_ref, xs_ref,
):
    local, tile = x_ref.shape
    chunks = local // SUB
    step = pl.program_id(0)

    @pl.when(step == 0)
    def _():
        logs = log_parts(decays_ref[...])
        rows = lax.broadcasted_iota(jnp.int32, (local, local), 0)
        columns = lax.broadcasted_iota(jnp.int32, (local, local), 1)
        start = columns & -SUB
        middle = start + SUB // 2
        later = (rows > middle) & (rows <= columns)
        sooner = (rows > columns) & (rows <= middle)
        offset = summed_logs(logs, later.astype(F32) - sooner.astype(F32))
        lift_ref[...] = packed(jnp.exp(offset))
        drop_ref[...] = packed(jnp.exp(-offset))
        rows = lax.broadcasted_iota(jnp.int32, (local, LANES), 0)
        columns = lax.broadcasted_iota(jnp.int32, (local, LANES), 1)
        start = rows & -SUB
        first = (rows - start <= SUB // 2) & (start == columns * SUB)
        second = (rows - start > SUB // 2) & (start == (columns - chunks) * SUB)
        rows_ref[...] = packed(jnp.exp(summed_logs(logs, first | second)))
        sums_ref[...] = jnp.zeros(sums_ref.shape, F32)
        map_ref[...] = jnp.zeros(map_ref.shape, F32)
        twice_ref[:, :N] = b_ref[...]
        twice_ref[:, N:] = b_ref[...]
        sooner = lax.broadcasted_iota(jnp.int32, (SUB, SUB), 0) <= lax.broadcasted_iota(jnp.int32, (SUB, SUB), 1)
        for k in range(chunks):
            at = pl.ds(k * SUB, SUB)
            hi, lo = halves(jnp.where(sooner, dot(b_ref[at, :], c_ref[at, :], NT), 0.0))
            scores_ref[at, :SUB] = hi
            scores_ref[at, SUB : 2 * SUB] = lo
            scores_ref[at, 2 * SUB :] = hi
            bt_ref[k] = transposed(stacked(b_ref[at, :], b_ref[at, :]))
            ct_ref[k] = transposed(stacked(c_ref[at, :], c_ref[at, :]))

    table = spread(heads, step * (tile // P_SIZE), tile)
    dys_ref[0], dys_ref[1] = halves(dy_ref[...].astype(F32) * dot(lift_ref[...], table))
    drop = dot(drop_ref[...], table)
    xs_ref[0], xs_ref[1] = halves(x_ref[...].astype(F32) * drop)
    row = dot(rows_ref[: 2 * chunks, :], table)

    state = None
    for k in range(chunks):
        at = pl.ds(k * SUB, SUB)
        dys, xs = (dys_ref[0, at, :], dys_ref[1, at, :]), (xs_ref[0, at, :], xs_ref[1, at, :])
        to_middle, to_end = row[k : k + 1], row[chunks + k : chunks + k + 1]
        if state is None:
            against = xs
        else:
            scaled = halves(state * to_middle)
            against = stacked(scaled[0], xs[0]), stacked(scaled[1], xs[1])
        both = dot(stacked(*dys), against[0], NT)
        summed = both[:SUB] + (both[SUB:] + dot(dys[0], against[1], NT))
        if state is None:
            sums_ref[at, N:] += summed
        else:
            sums_ref[at, :] += summed
        if k < chunks - 1:
            gained = to_end * dot(bt_ref[k], stacked(*xs))
            state = gained if state is None else (to_middle * to_end) * state + gained
    grad = None
    for k in reversed(range(chunks)):
        at = pl.ds(k * SUB, SUB)
        dys, xs = (dys_ref[0, at, :], dys_ref[1, at, :]), (xs_ref[0, at, :], xs_ref[1, at, :])
        to_middle, to_end = row[k : k + 1], row[chunks + k : chunks + k + 1]
        summed = dot(scores_ref[at, :], stacked(dys[0], dys[0], dys[1]))
        if grad is not None:
            scaled = halves(grad * to_end)
            summed = summed + dot(twice_ref[at, :], stacked(*scaled))
            both = dot(stacked(*xs), scaled[0], NT)
            map_ref[at, :] += both[:SUB] + (both[SUB:] + dot(xs[0], scaled[1], NT))
        part_ref[at, :] = drop[k * SUB : (k + 1) * SUB] * summed
        if k > 0:
            gained = to_middle * dot(ct_ref[k], stacked(*dys))
            grad = gained if grad is None else (to_middle * to_end) * grad + gained

    @pl.when(step == pl.num_programs(0) - 1)
    def _():
        causal = lax.broadcasted_iota(jnp.int32, (SUB, SUB), 0) >= lax.broadcasted_iota(jnp.int32, (SUB, SUB), 1)
        for k in range(chunks):
            at = pl.ds(k * SUB, SUB)
            mixed = jnp.where(causal, sums_ref[at, N:], 0.0)
            out_ref[at, :] = sums_ref[at, :N] + dot21(halves(mixed), b_ref[at, :])
            map_ref[at, :] += dot21(halves(mixed.T), c_ref[at, :])


def local_part(x, dy, b, c, decays):
    local, width = x.shape
    heads = width // P_SIZE
    count = width // TILE
    chunks = local // SUB
    whole = lambda a: pl.BlockSpec(a.shape, lambda j: (0, 0))
    column = pl.BlockSpec((local, TILE), lambda j: (0, j))
    tokens = pl.BlockSpec((local, N), lambda j: (0, 0))
    return pl.pallas_call(
        functools.partial(local_kernel, heads),
        grid=(count,),
        in_specs=[column, column, whole(b), whole(c), whole(decays)],
        out_specs=(column, tokens, tokens),
        out_shape=(
            jax.ShapeDtypeStruct((local, width), F32),
            jax.ShapeDtypeStruct((local, N), F32),
            jax.ShapeDtypeStruct((local, N), F32),
        ),
        scratch_shapes=[
            pltpu.VMEM((local, LANES), BF16),
            pltpu.VMEM((local, LANES), BF16),
            pltpu.VMEM((LANES, LANES), BF16),
            pltpu.VMEM((local, N + SUB), F32),
            pltpu.VMEM((local, 3 * SUB), BF16),
            pltpu.VMEM((local, 2 * N), BF16),
            pltpu.VMEM((chunks, N, 2 * SUB), BF16),
            pltpu.VMEM((chunks, N, 2 * SUB), BF16),
            pltpu.VMEM((2, local, TILE), BF16),
            pltpu.VMEM((2, local, TILE), BF16),
        ],
        compiler_params=PARAMS,
        name="local_part",
        cost_estimate=pl.CostEstimate(flops=40 * local * N * width, bytes_accessed=8 * local * width, transcendentals=0),
    )(x, dy, b, c, decays)


def map_kernel(count, ranks, place_ref, scaled_ref, carry_ref, out_before_ref, map_before_ref, *refs):
    messages, (out_ref, map_ref) = refs[:-2], refs[-2:]
    step = pl.program_id(0)

    @pl.when(step == 0)
    def _():
        out_ref[...] = out_before_ref[...]
        map_ref[...] = map_before_ref[...]

    for i, sum_ref in enumerate((map_ref, out_ref)):
        carry = halves(carry_ref[1 - i])
        both = dot(scaled_ref[i, 0], stacked(*carry), NT)
        sum_ref[...] += both[:, :N] + (both[:, N:] + dot(scaled_ref[i, 1], carry[0], NT))

    if messages:

        @pl.when(step == count - 1)
        def _():
            rows = messages[0].shape[1]
            for r, message in enumerate(messages):
                at = pl.ds(pl.multiple_of(((place_ref[RANK] + r) % ranks) * rows, rows), rows)
                message[0] = out_ref[at, :]
                message[1] = map_ref[at, :]


def map_terms(place, scaled, carry, out_before, map_before, ranks=0):
    local, width = scaled.shape[2:]
    count = width // TILE
    whole = lambda a: pl.BlockSpec(a.shape, lambda j, pick: (0,) * len(a.shape))
    tokens = jax.ShapeDtypeStruct((local, N), F32)
    if ranks:
        out_shape = [jax.ShapeDtypeStruct((2, local // ranks, N), F32)] * ranks
        scratch = [pltpu.VMEM((local, N), F32), pltpu.VMEM((local, N), F32)]
    else:
        out_shape, scratch = [tokens, tokens], []
    return pl.pallas_call(
        functools.partial(map_kernel, count, ranks),
        grid_spec=pltpu.PrefetchScalarGridSpec(
            num_scalar_prefetch=1,
            grid=(count,),
            in_specs=[
                pl.BlockSpec((2, 2, local, TILE), lambda j, pick: (0, 0, 0, j)),
                pl.BlockSpec((2, N, TILE), lambda j, pick: (0, 0, j)),
                whole(tokens),
                whole(tokens),
            ],
            out_specs=[whole(shape) for shape in out_shape],
            scratch_shapes=scratch,
        ),
        out_shape=out_shape,
        compiler_params=PARAMS,
        name="map_terms",
        cost_estimate=pl.CostEstimate(flops=12 * local * N * width, bytes_accessed=8 * local * width, transcendentals=0),
    )(place, scaled, carry, out_before, map_before)


def input_kernel(heads, count, pick_ref, part_ref, suf_ref, b_ref, own_ref, other_ref, input_ref):
    tile = part_ref.shape[1]
    step = pl.program_id(0)
    after = dot(suf_ref[...], spread(heads, step * (tile // P_SIZE), tile))
    grad = jnp.where(step // count == pick_ref[CORE], own_ref[0], other_ref[0])
    input_ref[...] = (part_ref[...] + after * dot12(b_ref[...], halves(grad))).astype(BF16)


def input_terms(core, part, suf, b, own, other):
    local, width = part.shape
    heads = width // P_SIZE
    count = width // 2 // TILE
    whole = lambda a: pl.BlockSpec(a.shape, lambda j, pick: (0, 0))
    column = pl.BlockSpec((local, TILE), lambda j, pick: (0, j))
    carry = pl.BlockSpec((1, N, TILE), lambda j, pick: (1, 0, j % count))
    return pl.pallas_call(
        functools.partial(input_kernel, heads, count),
        grid_spec=pltpu.PrefetchScalarGridSpec(
            num_scalar_prefetch=1,
            grid=(2 * count,),
            in_specs=[column, whole(suf), whole(b), carry, carry],
            out_specs=column,
        ),
        out_shape=jax.ShapeDtypeStruct((local, width), BF16),
        compiler_params=PARAMS,
        name="input_terms",
        cost_estimate=pl.CostEstimate(flops=4 * local * N * width, bytes_accessed=8 * local * width, transcendentals=0),
    )(core, part, suf, b, own, other)


def swap_cores(v, length):
    return lax.ppermute(v, "seq", [(i, i ^ 1) for i in range(length)])


def turned(v, axis, length, by):
    return lax.ppermute(v, axis, [(i, (i + by) % length) for i in range(length)])


def per_device(mixer_input, output_grad, input_map, output_map, decays):
    length, ranks = lax.axis_size("seq"), lax.axis_size("head")
    chips = length // 2
    index, rank = lax.axis_index("seq"), lax.axis_index("head")
    core, chip = index % 2, index // 2
    place = jnp.stack([core, 1 - core, chip, rank]).astype(jnp.int32)
    args = mixer_input, output_grad, input_map, output_map
    sent, scaled_other, pre, suf = totals(OTHER, place, *args, decays=decays)
    recv = swap_cores(sent, length)
    mine, scaled_mine = totals(CORE, place, *args, pre=pre, suf=suf)
    messages = chip_totals(chips, place, mine, recv)
    others = [turned(message, "seq", length, 2 * r) for r, message in enumerate(messages, 1)]
    part, out_part, map_part = local_part(*args, decays)
    others, part, out_part, map_part = lax.optimization_barrier((others, part, out_part, map_part))
    own, peer = carried(chips, place, mine, recv, others)
    other = swap_cores(peer, length)
    out_part, map_part = map_terms(place, scaled_mine, own, out_part, map_part)
    shares = map_terms(place, scaled_other, other, out_part, map_part, ranks)
    total = shares[0]
    own, other, shares = lax.optimization_barrier((own, other, shares))
    for r in range(1, ranks):
        total = total + turned(shares[r], "head", ranks, r)
    input_grad = input_terms(place, part, suf, input_map, own, other)
    return input_grad, total[1], total[0]


def solution(mesh):
    in_specs = (
        P("seq", "head"),
        P("seq", "head"),
        P("seq", None),
        P("seq", None),
        P("head", "seq"),
    )
    out_specs = (P("seq", "head"), P(("seq", "head"), None), P(("seq", "head"), None))
    return jax.shard_map(
        per_device, mesh=mesh, in_specs=in_specs, out_specs=out_specs, check_vma=False
    )
```

```python
import functools

import jax
import jax.numpy as jnp
from jax import lax
from jax.experimental import pallas as pl
from jax.experimental.pallas import tpu as pltpu
from jax.sharding import PartitionSpec as P

P_SIZE = 64
N = 128
SUB = 64
TILE = 256
EXTRA = 8
LANES = 128
CORE, OTHER, CHIP, RANK = range(4)
PARAMS = pltpu.CompilerParams(vmem_limit_bytes=24 * 1024 * 1024)
FIRST = pltpu.CompilerParams(vmem_limit_bytes=60 * 1024 * 1024)
F32 = jnp.float32
BF16 = jnp.bfloat16

NN = (((1,), (0,)), ((), ()))
NT = (((1,), (1,)), ((), ()))


def dot(a, b, dims=NN):
    return lax.dot_general(a, b, dims, preferred_element_type=F32)


def halves(v):
    hi = v.astype(BF16)
    return hi, (v - hi.astype(F32)).astype(BF16)


def dot21(pair, b, dims=NN):
    return dot(pair[0], b, dims) + dot(pair[1], b, dims)


def dot12(a, pair, dims=NN):
    return dot(a, pair[0], dims) + dot(a, pair[1], dims)


def dot22(p, q, dims=NN):
    return dot(p[0], q[0], dims) + (dot(p[0], q[1], dims) + dot(p[1], q[0], dims))


def thirds(v):
    hi = v.astype(BF16)
    rest = v - hi.astype(F32)
    mid = rest.astype(BF16)
    return hi, mid, (rest - mid.astype(F32)).astype(BF16)


def spread(heads, first, width):
    rows = lax.broadcasted_iota(jnp.int32, (heads, width), 0)
    columns = lax.broadcasted_iota(jnp.int32, (heads, width), 1)
    offset = columns - (rows - first) * P_SIZE
    picked = ((offset >= 0) & (offset < P_SIZE)).astype(F32)
    rest = jnp.zeros((LANES - 3 * heads, width), F32)
    return jnp.concatenate([picked, picked, picked, rest], axis=0).astype(BF16)


def stacked(*parts):
    return jnp.concatenate(parts, axis=0)


def transposed(v):
    return v.astype(F32).T.astype(BF16)


def log_parts(decays):
    return jnp.concatenate([part.astype(F32) for part in thirds(jnp.log(decays))], axis=0).astype(BF16)


def summed_logs(logs, table):
    heads = logs.shape[0] // 3
    sums = dot(logs, table.astype(F32).astype(BF16))
    return sums[:heads] + (sums[heads : 2 * heads] + sums[2 * heads :])


def packed(v):
    parts = [part.astype(F32) for part in thirds(v)]
    rest = jnp.zeros((LANES - 3 * v.shape[0], v.shape[1]), F32)
    return jnp.concatenate(parts + [rest], axis=0).T.astype(BF16)


def device_factors(decays, pre_ref, suf_ref):
    local = decays.shape[1]
    logs = log_parts(decays)
    rows = lax.broadcasted_iota(jnp.int32, (local, local), 0)
    columns = lax.broadcasted_iota(jnp.int32, (local, local), 1)
    pre_ref[...] = packed(jnp.exp(summed_logs(logs, rows <= columns)))
    suf_ref[...] = packed(jnp.exp(summed_logs(logs, rows > columns)))


def totals_kernel(heads, count, half, place_ref, x_ref, dy_ref, b_ref, c_ref, *refs):
    if len(refs) == 7:
        decays_ref, out_ref, scaled_ref, pre_ref, suf_ref, bt_ref, ct_ref = refs
    else:
        pre_ref, suf_ref, out_ref, scaled_ref, bt_ref, ct_ref = refs
        decays_ref = None
    step = pl.program_id(0)

    @pl.when(step == 0)
    def _():
        bt_ref[...] = transposed(b_ref[...])
        ct_ref[...] = transposed(c_ref[...])
        if decays_ref is not None:
            device_factors(decays_ref[...], pre_ref, suf_ref)

    tile = x_ref.shape[1]
    table = spread(heads, (place_ref[half] * count + step) * (tile // P_SIZE), tile)
    before = dot(pre_ref[...], table)
    after = dot(suf_ref[...], table)
    ended = before[before.shape[0] - 1 :, :]
    for i, (source, factor, other) in enumerate(((x_ref, after, bt_ref), (dy_ref, before, ct_ref))):
        scaled = halves(source[...].astype(F32) * factor)
        scaled_ref[i, 0], scaled_ref[i, 1] = scaled
        out_ref[i, :N, :] = dot12(other[...], scaled)
    out_ref[0, N:, :] = jnp.broadcast_to(ended, (EXTRA, tile))
    out_ref[1, N:, :] = jnp.broadcast_to(ended, (EXTRA, tile))


def totals(half, place, x, dy, b, c, decays=None, pre=None, suf=None):
    local, width = x.shape
    heads = width // P_SIZE
    count = width // 2 // TILE
    whole = lambda a: pl.BlockSpec(a.shape, lambda j, pick: (0, 0))
    column = pl.BlockSpec((local, TILE), lambda j, pick: (0, pick[half] * count + j))
    factor = jax.ShapeDtypeStruct((local, LANES), BF16)
    rest = (pre, suf) if decays is None else (decays,)
    out_specs = [
        pl.BlockSpec((2, N + EXTRA, TILE), lambda j, pick: (0, 0, j)),
        pl.BlockSpec((2, 2, local, TILE), lambda j, pick: (0, 0, 0, j)),
    ]
    out_shape = [
        jax.ShapeDtypeStruct((2, N + EXTRA, width // 2), F32),
        jax.ShapeDtypeStruct((2, 2, local, width // 2), BF16),
    ]
    if decays is not None:
        out_specs += [whole(factor), whole(factor)]
        out_shape += [factor, factor]
    return pl.pallas_call(
        functools.partial(totals_kernel, heads, count, half),
        grid_spec=pltpu.PrefetchScalarGridSpec(
            num_scalar_prefetch=1,
            grid=(count,),
            in_specs=[column, column, whole(b), whole(c)] + [whole(a) for a in rest],
            out_specs=out_specs,
            scratch_shapes=[pltpu.VMEM((N, local), BF16), pltpu.VMEM((N, local), BF16)],
        ),
        out_shape=out_shape,
        compiler_params=FIRST,
        name="state_totals",
        cost_estimate=pl.CostEstimate(flops=8 * local * N * width // 2, bytes_accessed=4 * local * width, transcendentals=0),
    )(place, x, dy, b, c, *rest)


def ordered(core, mine, recv):
    return jnp.where(core == 0, mine, recv), jnp.where(core == 0, recv, mine)


def chip_kernel(chips, place_ref, mine_ref, recv_ref, *out_refs):
    core, chip = place_ref[CORE], place_ref[CHIP]
    early, late = ordered(core, mine_ref[0], recv_ref[0])
    early_decay, late_decay = early[N : N + 1], late[N : N + 1]
    both = jnp.broadcast_to(early_decay * late_decay, (EXTRA, early.shape[1]))
    state = late_decay * early[:N] + late[:N]
    early, late = ordered(core, mine_ref[1], recv_ref[1])
    grad = early[:N] + early_decay * late[:N]
    for r, out_ref in enumerate(out_refs, 1):
        out_ref[:N, :] = jnp.where(chip + r < chips, state, grad)
        out_ref[N:, :] = both


def chip_totals(chips, place, mine, recv):
    width = mine.shape[2]
    tile = min(512, width)
    block = pl.BlockSpec((2, N + EXTRA, tile), lambda j, pick: (0, 0, j))
    out = pl.BlockSpec((N + EXTRA, tile), lambda j, pick: (0, j))
    shape = jax.ShapeDtypeStruct((N + EXTRA, width), F32)
    return pl.pallas_call(
        functools.partial(chip_kernel, chips),
        grid_spec=pltpu.PrefetchScalarGridSpec(
            num_scalar_prefetch=1, grid=(width // tile,), in_specs=[block, block], out_specs=[out] * (chips - 1)
        ),
        out_shape=[shape] * (chips - 1),
        compiler_params=PARAMS,
        name="chip_totals",
        cost_estimate=pl.CostEstimate(flops=6 * N * width, bytes_accessed=24 * N * width, transcendentals=0),
    )(place, mine, recv)


def carried_kernel(chips, place_ref, mine_ref, recv_ref, *refs):
    others, (own_ref, peer_ref) = refs[:-2], refs[-2:]
    core, chip = place_ref[CORE], place_ref[CHIP]
    state = grad = jnp.zeros((N, own_ref.shape[2]), F32)
    state_weight = grad_weight = jnp.ones((1, own_ref.shape[2]), F32)
    for r, ref in enumerate(others, 1):
        earlier = chip >= r
        state = jnp.where(earlier, state + state_weight * ref[:N, :], state)
        state_weight = state_weight * ref[N : N + 1, :]
    for r in range(1, chips):
        later = chip + r < chips
        ref = others[chips - r - 1]
        grad = jnp.where(later, grad + grad_weight * ref[:N, :], grad)
        grad_weight = grad_weight * ref[N : N + 1, :]
    early, late = ordered(core, mine_ref[0], recv_ref[0])
    at_late = early[N : N + 1] * state + early[:N]
    own_ref[0] = jnp.where(core == 0, state, at_late)
    peer_ref[0] = jnp.where(core == 0, at_late, state)
    early, late = ordered(core, mine_ref[1], recv_ref[1])
    at_early = late[:N] + late[N : N + 1] * grad
    own_ref[1] = jnp.where(core == 0, at_early, grad)
    peer_ref[1] = jnp.where(core == 0, grad, at_early)


def carried(chips, place, mine, recv, others):
    width = mine.shape[2]
    tile = min(512, width)
    pair = pl.BlockSpec((2, N + EXTRA, tile), lambda j, pick: (0, 0, j))
    other = pl.BlockSpec((N + EXTRA, tile), lambda j, pick: (0, j))
    out = pl.BlockSpec((2, N, tile), lambda j, pick: (0, 0, j))
    shape = jax.ShapeDtypeStruct((2, N, width), F32)
    return pl.pallas_call(
        functools.partial(carried_kernel, chips),
        grid_spec=pltpu.PrefetchScalarGridSpec(
            num_scalar_prefetch=1,
            grid=(width // tile,),
            in_specs=[pair, pair] + [other] * len(others),
            out_specs=(out, out),
        ),
        out_shape=(shape, shape),
        compiler_params=PARAMS,
        name="carried_in",
        cost_estimate=pl.CostEstimate(flops=20 * N * width, bytes_accessed=44 * N * width, transcendentals=0),
    )(place, mine, recv, *others)


def blocks(chunks):
    span = 1
    while span < chunks:
        yield span, [at for at in range(span, chunks, 2 * span)]
        span *= 2


def row_bounds(chunks):
    for span, _ in blocks(chunks):
        for k in range(chunks):
            middle = k * SUB + SUB // 2
            boundary = (k // span + 1 - (k // span) % 2) * span * SUB
            yield (boundary, middle + 1) if middle >= boundary else (middle + 1, boundary)


def local_factors(decays, lift_ref, drop_ref, rows_ref):
    local = decays.shape[1]
    logs = log_parts(decays)
    rows = lax.broadcasted_iota(jnp.int32, (local, local), 0)
    columns = lax.broadcasted_iota(jnp.int32, (local, local), 1)
    middle = (columns & -SUB) + SUB // 2
    later = (rows > middle) & (rows <= columns)
    sooner = (rows > columns) & (rows <= middle)
    offset = summed_logs(logs, later.astype(F32) - sooner.astype(F32))
    lift_ref[...] = packed(jnp.exp(offset))
    drop_ref[...] = packed(jnp.exp(-offset))
    width = rows_ref.shape[0]
    lane = lax.broadcasted_iota(jnp.int32, (1, width), 1)
    first = last = jnp.zeros((1, width), jnp.int32)
    for i, (start, end) in enumerate(row_bounds(local // SUB)):
        first, last = jnp.where(lane == i, start, first), jnp.where(lane == i, end, last)
    rows = lax.broadcasted_iota(jnp.int32, (local, width), 0)
    rows_ref[...] = packed(jnp.exp(summed_logs(logs, (rows >= first) & (rows < last))))


def score_parts(b, c, ref, at, causal):
    score = dot(b, c, NT)
    if causal:
        rows = lax.broadcasted_iota(jnp.int32, score.shape, 0)
        columns = lax.broadcasted_iota(jnp.int32, score.shape, 1)
        score = jnp.where(rows <= columns, score, 0.0)
    hi, lo = halves(score)
    width = score.shape[1]
    ref[at, :width] = hi
    ref[at, width : 2 * width] = lo
    if ref.shape[1] > 2 * width:
        ref[at, 2 * width :] = hi


def scored(ref, at, dys):
    width = dys[0].shape[0]
    if ref.shape[1] > 2 * width:
        return dot(ref[at, :], stacked(dys[0], dys[0], dys[1]))
    return dot(ref[at, :], stacked(dys[0], dys[0])) + dot(ref[at, :width], dys[1])


def add_mixed(ref, at, dys, xs):
    width = xs[0].shape[0]
    both = dot(dys[0], stacked(*xs), NT)
    if width < LANES:
        ref[at, :] += both
        ref[at, :width] += dot(dys[1], xs[0], NT)
    else:
        ref[at, :] += both[:, :width] + (both[:, width:] + dot(dys[1], xs[0], NT))


def added_up(v, width):
    return v[:, :width] + v[:, width:] if v.shape[1] > width else v


def local_kernel(
    heads, x_ref, dy_ref, b_ref, c_ref, decays_ref, part_ref, out_ref, map_ref,
    lift_ref, drop_ref, rows_ref, full_ref, dys_ref, xs_ref, back_ref, sums_ref, scores_ref, *level_refs,
):
    local, tile = x_ref.shape
    chunks = local // SUB
    step = pl.program_id(0)
    levels = [(span, at, level_refs[2 * i], level_refs[2 * i + 1]) for i, (span, at) in enumerate(blocks(chunks))]

    @pl.when(step == 0)
    def _():
        local_factors(decays_ref[...], lift_ref, drop_ref, rows_ref)
        sums_ref[...] = jnp.zeros(sums_ref.shape, F32)
        for k in range(chunks):
            at = pl.ds(k * SUB, SUB)
            score_parts(b_ref[at, :], c_ref[at, :], scores_ref, at, True)
        for span, boundaries, mixed_ref, level_scores_ref in levels:
            mixed_ref[...] = jnp.zeros(mixed_ref.shape, F32)
            size = span * SUB
            for i, boundary in enumerate(boundaries):
                before, after = pl.ds((boundary - span) * SUB, size), pl.ds(boundary * SUB, size)
                score_parts(b_ref[before, :], c_ref[after, :], level_scores_ref, pl.ds(i * size, size), False)

    table = spread(heads, step * (tile // P_SIZE), tile)
    dys_ref[...] = dy_ref[...].astype(F32) * dot(lift_ref[...], table)
    back_ref[...] = dot(drop_ref[...], table)
    xs_ref[...] = x_ref[...].astype(F32) * back_ref[...]
    row = dot(rows_ref[...], table)

    for k in range(chunks):
        at = pl.ds(k * SUB, SUB)
        dys, xs = halves(dys_ref[at, :]), halves(xs_ref[at, :])
        add_mixed(sums_ref, at, dys, xs)
        part_ref[at, :] = back_ref[at, :] * scored(scores_ref, at, dys)

    for level, (span, boundaries, mixed_ref, level_scores_ref) in enumerate(levels):
        size = span * SUB
        for i, boundary in enumerate(boundaries):
            at = pl.ds(i * size, size)
            factor = lambda k: row[level * chunks + k : level * chunks + k + 1]
            take = lambda ref, first: halves(
                stacked(*[ref[k * SUB : (k + 1) * SUB, :] * factor(k) for k in range(first, first + span)])
            )
            dys, xs = take(dys_ref, boundary), take(xs_ref, boundary - span)
            add_mixed(mixed_ref, at, dys, xs)
            gained = scored(level_scores_ref, at, dys)
            for q in range(span):
                k = boundary - span + q
                rows = pl.ds(k * SUB, SUB)
                part_ref[rows, :] += (back_ref[rows, :] * factor(k)) * gained[q * SUB : (q + 1) * SUB]

    @pl.when(step == pl.num_programs(0) - 1)
    def _():
        full_ref[...] = jnp.zeros(full_ref.shape, F32)
        rows = lax.broadcasted_iota(jnp.int32, (SUB, SUB), 0)
        columns = lax.broadcasted_iota(jnp.int32, (SUB, SUB), 1)
        for k in range(chunks):
            at = pl.ds(k * SUB, SUB)
            full_ref[at, k * SUB : (k + 1) * SUB] = jnp.where(rows >= columns, added_up(sums_ref[at, :], SUB), 0.0)
        for span, boundaries, mixed_ref, _ in levels:
            size = span * SUB
            for i, boundary in enumerate(boundaries):
                block = added_up(mixed_ref[pl.ds(i * size, size), :], size)
                full_ref[pl.ds(boundary * SUB, size), (boundary - span) * SUB : boundary * SUB] = block
        map_ref[...] = jnp.zeros(map_ref.shape, F32)
        for k in range(0, local, LANES):
            at = pl.ds(k, LANES)
            mixed = full_ref[at, :]
            out_ref[at, :] = dot21(halves(mixed), b_ref[...])
            map_ref[...] += dot21(halves(mixed.T), c_ref[at, :])


def local_part(x, dy, b, c, decays):
    local, width = x.shape
    heads = width // P_SIZE
    count = width // TILE
    chunks = local // SUB
    whole = lambda a: pl.BlockSpec(a.shape, lambda j: (0, 0))
    column = pl.BlockSpec((local, TILE), lambda j: (0, j))
    tokens = pl.BlockSpec((local, N), lambda j: (0, 0))
    scratch = [
        pltpu.VMEM((local, LANES), BF16),
        pltpu.VMEM((local, LANES), BF16),
        pltpu.VMEM((LANES, LANES), BF16),
        pltpu.VMEM((local, local), F32),
        pltpu.VMEM((local, TILE), F32),
        pltpu.VMEM((local, TILE), F32),
        pltpu.VMEM((local, TILE), F32),
        pltpu.VMEM((local, 2 * SUB), F32),
        pltpu.VMEM((local, 3 * SUB), BF16),
    ]
    for span, _ in blocks(chunks):
        size = span * SUB
        scratch.append(pltpu.VMEM((local // 2, max(size, LANES)), F32))
        scratch.append(pltpu.VMEM((local // 2, (3 if size < LANES else 2) * size), BF16))
    return pl.pallas_call(
        functools.partial(local_kernel, heads),
        grid=(count,),
        in_specs=[column, column, whole(b), whole(c), whole(decays)],
        out_specs=(column, tokens, tokens),
        out_shape=(
            jax.ShapeDtypeStruct((local, width), F32),
            jax.ShapeDtypeStruct((local, N), F32),
            jax.ShapeDtypeStruct((local, N), F32),
        ),
        scratch_shapes=scratch,
        compiler_params=PARAMS,
        name="local_part",
        cost_estimate=pl.CostEstimate(flops=40 * local * N * width, bytes_accessed=8 * local * width, transcendentals=0),
    )(x, dy, b, c, decays)


def map_kernel(count, ranks, place_ref, scaled_ref, carry_ref, out_before_ref, map_before_ref, *refs):
    messages, (out_ref, map_ref) = refs[:-2], refs[-2:]
    step = pl.program_id(0)

    @pl.when(step == 0)
    def _():
        out_ref[...] = out_before_ref[...]
        map_ref[...] = map_before_ref[...]

    for i, sum_ref in enumerate((map_ref, out_ref)):
        carry = halves(carry_ref[1 - i])
        both = dot(scaled_ref[i, 0], stacked(*carry), NT)
        sum_ref[...] += both[:, :N] + (both[:, N:] + dot(scaled_ref[i, 1], carry[0], NT))

    if messages:

        @pl.when(step == count - 1)
        def _():
            rows = messages[0].shape[1]
            for r, message in enumerate(messages):
                at = pl.ds(pl.multiple_of(((place_ref[RANK] + r) % ranks) * rows, rows), rows)
                message[0] = out_ref[at, :]
                message[1] = map_ref[at, :]


def map_terms(place, scaled, carry, out_before, map_before, ranks=0):
    local, width = scaled.shape[2:]
    count = width // TILE
    whole = lambda a: pl.BlockSpec(a.shape, lambda j, pick: (0,) * len(a.shape))
    tokens = jax.ShapeDtypeStruct((local, N), F32)
    if ranks:
        out_shape = [jax.ShapeDtypeStruct((2, local // ranks, N), F32)] * ranks
        scratch = [pltpu.VMEM((local, N), F32), pltpu.VMEM((local, N), F32)]
    else:
        out_shape, scratch = [tokens, tokens], []
    return pl.pallas_call(
        functools.partial(map_kernel, count, ranks),
        grid_spec=pltpu.PrefetchScalarGridSpec(
            num_scalar_prefetch=1,
            grid=(count,),
            in_specs=[
                pl.BlockSpec((2, 2, local, TILE), lambda j, pick: (0, 0, 0, j)),
                pl.BlockSpec((2, N, TILE), lambda j, pick: (0, 0, j)),
                whole(tokens),
                whole(tokens),
            ],
            out_specs=[whole(shape) for shape in out_shape],
            scratch_shapes=scratch,
        ),
        out_shape=out_shape,
        compiler_params=PARAMS,
        name="map_terms",
        cost_estimate=pl.CostEstimate(flops=12 * local * N * width, bytes_accessed=8 * local * width, transcendentals=0),
    )(place, scaled, carry, out_before, map_before)


def input_kernel(heads, count, pick_ref, part_ref, suf_ref, b_ref, own_ref, other_ref, input_ref):
    tile = part_ref.shape[1]
    step = pl.program_id(0)
    after = dot(suf_ref[...], spread(heads, step * (tile // P_SIZE), tile))
    grad = jnp.where(step // count == pick_ref[CORE], own_ref[0], other_ref[0])
    input_ref[...] = (part_ref[...] + after * dot12(b_ref[...], halves(grad))).astype(BF16)


def input_terms(core, part, suf, b, own, other):
    local, width = part.shape
    heads = width // P_SIZE
    count = width // 2 // TILE
    whole = lambda a: pl.BlockSpec(a.shape, lambda j, pick: (0, 0))
    column = pl.BlockSpec((local, TILE), lambda j, pick: (0, j))
    carry = pl.BlockSpec((1, N, TILE), lambda j, pick: (1, 0, j % count))
    return pl.pallas_call(
        functools.partial(input_kernel, heads, count),
        grid_spec=pltpu.PrefetchScalarGridSpec(
            num_scalar_prefetch=1,
            grid=(2 * count,),
            in_specs=[column, whole(suf), whole(b), carry, carry],
            out_specs=column,
        ),
        out_shape=jax.ShapeDtypeStruct((local, width), BF16),
        compiler_params=PARAMS,
        name="input_terms",
        cost_estimate=pl.CostEstimate(flops=4 * local * N * width, bytes_accessed=8 * local * width, transcendentals=0),
    )(core, part, suf, b, own, other)


def swap_cores(v, length):
    return lax.ppermute(v, "seq", [(i, i ^ 1) for i in range(length)])


def turned(v, axis, length, by):
    return lax.ppermute(v, axis, [(i, (i + by) % length) for i in range(length)])


def per_device(mixer_input, output_grad, input_map, output_map, decays):
    length, ranks = lax.axis_size("seq"), lax.axis_size("head")
    chips = length // 2
    index, rank = lax.axis_index("seq"), lax.axis_index("head")
    core, chip = index % 2, index // 2
    place = jnp.stack([core, 1 - core, chip, rank]).astype(jnp.int32)
    args = mixer_input, output_grad, input_map, output_map
    sent, scaled_other, pre, suf = totals(OTHER, place, *args, decays=decays)
    recv = swap_cores(sent, length)
    mine, scaled_mine = totals(CORE, place, *args, pre=pre, suf=suf)
    messages = chip_totals(chips, place, mine, recv)
    others = [turned(message, "seq", length, 2 * r) for r, message in enumerate(messages, 1)]
    part, out_part, map_part = local_part(*args, decays)
    others, part, out_part, map_part = lax.optimization_barrier((others, part, out_part, map_part))
    own, peer = carried(chips, place, mine, recv, others)
    other = swap_cores(peer, length)
    out_part, map_part = map_terms(place, scaled_mine, own, out_part, map_part)
    shares = map_terms(place, scaled_other, other, out_part, map_part, ranks)
    total = shares[0]
    own, other, shares = lax.optimization_barrier((own, other, shares))
    for r in range(1, ranks):
        total = total + turned(shares[r], "head", ranks, r)
    input_grad = input_terms(place, part, suf, input_map, own, other)
    return input_grad, total[1], total[0]


def solution(mesh):
    in_specs = (
        P("seq", "head"),
        P("seq", "head"),
        P("seq", None),
        P("seq", None),
        P("head", "seq"),
    )
    out_specs = (P("seq", "head"), P(("seq", "head"), None), P(("seq", "head"), None))
    return jax.shard_map(
        per_device, mesh=mesh, in_specs=in_specs, out_specs=out_specs, check_vma=False
    )
```

```python
import functools

import jax
import jax.numpy as jnp
from jax import lax
from jax.experimental import pallas as pl
from jax.experimental.pallas import tpu as pltpu
from jax.sharding import PartitionSpec as P

P_SIZE = 64
N = 128
SUB = 64
TILE = 256
EXTRA = 8
LANES = 128
CORE, OTHER, CHIP, RANK = range(4)
PARAMS = pltpu.CompilerParams(vmem_limit_bytes=24 * 1024 * 1024)
FIRST = pltpu.CompilerParams(vmem_limit_bytes=60 * 1024 * 1024)
F32 = jnp.float32
BF16 = jnp.bfloat16

NN = (((1,), (0,)), ((), ()))
NT = (((1,), (1,)), ((), ()))


def dot(a, b, dims=NN):
    return lax.dot_general(a, b, dims, preferred_element_type=F32)


def halves(v):
    hi = v.astype(BF16)
    return hi, (v - hi.astype(F32)).astype(BF16)


def dot21(pair, b, dims=NN):
    return dot(pair[0], b, dims) + dot(pair[1], b, dims)


def dot12(a, pair, dims=NN):
    return dot(a, pair[0], dims) + dot(a, pair[1], dims)


def dot22(p, q, dims=NN):
    return dot(p[0], q[0], dims) + (dot(p[0], q[1], dims) + dot(p[1], q[0], dims))


def thirds(v):
    hi = v.astype(BF16)
    rest = v - hi.astype(F32)
    mid = rest.astype(BF16)
    return hi, mid, (rest - mid.astype(F32)).astype(BF16)


def spread(heads, first, width):
    rows = lax.broadcasted_iota(jnp.int32, (heads, width), 0)
    columns = lax.broadcasted_iota(jnp.int32, (heads, width), 1)
    offset = columns - (rows - first) * P_SIZE
    picked = ((offset >= 0) & (offset < P_SIZE)).astype(F32)
    rest = jnp.zeros((LANES - 3 * heads, width), F32)
    return jnp.concatenate([picked, picked, picked, rest], axis=0).astype(BF16)


def stacked(*parts):
    return jnp.concatenate(parts, axis=0)


def transposed(v):
    return v.astype(F32).T.astype(BF16)


def log_parts(decays):
    return jnp.concatenate([part.astype(F32) for part in thirds(jnp.log(decays))], axis=0).astype(BF16)


def summed_logs(logs, table):
    heads = logs.shape[0] // 3
    sums = dot(logs, table.astype(F32).astype(BF16))
    return sums[:heads] + (sums[heads : 2 * heads] + sums[2 * heads :])


def packed(v):
    parts = [part.astype(F32) for part in thirds(v)]
    rest = jnp.zeros((LANES - 3 * v.shape[0], v.shape[1]), F32)
    return jnp.concatenate(parts + [rest], axis=0).T.astype(BF16)


def device_factors(decays, pre_ref, suf_ref):
    local = decays.shape[1]
    logs = log_parts(decays)
    rows = lax.broadcasted_iota(jnp.int32, (local, local), 0)
    columns = lax.broadcasted_iota(jnp.int32, (local, local), 1)
    pre_ref[...] = packed(jnp.exp(summed_logs(logs, rows <= columns)))
    suf_ref[...] = packed(jnp.exp(summed_logs(logs, rows > columns)))


def totals_kernel(heads, count, half, place_ref, x_ref, dy_ref, b_ref, c_ref, *refs):
    if len(refs) == 6:
        decays_ref, out_ref, pre_ref, suf_ref, bt_ref, ct_ref = refs
    else:
        pre_ref, suf_ref, out_ref, bt_ref, ct_ref = refs
        decays_ref = None
    step = pl.program_id(0)

    @pl.when(step == 0)
    def _():
        bt_ref[...] = transposed(b_ref[...])
        ct_ref[...] = transposed(c_ref[...])
        if decays_ref is not None:
            device_factors(decays_ref[...], pre_ref, suf_ref)

    tile = x_ref.shape[1]
    table = spread(heads, (place_ref[half] * count + step) * (tile // P_SIZE), tile)
    before = dot(pre_ref[...], table)
    after = dot(suf_ref[...], table)
    ended = before[before.shape[0] - 1 :, :]
    for i, (source, factor, other) in enumerate(((x_ref, after, bt_ref), (dy_ref, before, ct_ref))):
        out_ref[i, :N, :] = dot12(other[...], halves(source[...].astype(F32) * factor))
    out_ref[0, N:, :] = jnp.broadcast_to(ended, (EXTRA, tile))
    out_ref[1, N:, :] = jnp.broadcast_to(ended, (EXTRA, tile))


def totals(half, place, x, dy, b, c, decays=None, pre=None, suf=None):
    local, width = x.shape
    heads = width // P_SIZE
    count = width // 2 // TILE
    whole = lambda a: pl.BlockSpec(a.shape, lambda j, pick: (0, 0))
    column = pl.BlockSpec((local, TILE), lambda j, pick: (0, pick[half] * count + j))
    factor = jax.ShapeDtypeStruct((local, LANES), BF16)
    rest = (pre, suf) if decays is None else (decays,)
    out_specs = [pl.BlockSpec((2, N + EXTRA, TILE), lambda j, pick: (0, 0, j))]
    out_shape = [jax.ShapeDtypeStruct((2, N + EXTRA, width // 2), F32)]
    if decays is not None:
        out_specs += [whole(factor), whole(factor)]
        out_shape += [factor, factor]
    return pl.pallas_call(
        functools.partial(totals_kernel, heads, count, half),
        grid_spec=pltpu.PrefetchScalarGridSpec(
            num_scalar_prefetch=1,
            grid=(count,),
            in_specs=[column, column, whole(b), whole(c)] + [whole(a) for a in rest],
            out_specs=out_specs,
            scratch_shapes=[pltpu.VMEM((N, local), BF16), pltpu.VMEM((N, local), BF16)],
        ),
        out_shape=out_shape,
        compiler_params=FIRST,
        name="state_totals",
        cost_estimate=pl.CostEstimate(flops=8 * local * N * width // 2, bytes_accessed=4 * local * width, transcendentals=0),
    )(place, x, dy, b, c, *rest)


def ordered(core, mine, recv):
    return jnp.where(core == 0, mine, recv), jnp.where(core == 0, recv, mine)


def chip_kernel(chips, place_ref, mine_ref, recv_ref, *out_refs):
    core, chip = place_ref[CORE], place_ref[CHIP]
    early, late = ordered(core, mine_ref[0], recv_ref[0])
    early_decay, late_decay = early[N : N + 1], late[N : N + 1]
    both = jnp.broadcast_to(early_decay * late_decay, (EXTRA, early.shape[1]))
    state = late_decay * early[:N] + late[:N]
    early, late = ordered(core, mine_ref[1], recv_ref[1])
    grad = early[:N] + early_decay * late[:N]
    for r, out_ref in enumerate(out_refs, 1):
        out_ref[:N, :] = jnp.where(chip + r < chips, state, grad)
        out_ref[N:, :] = both


def chip_totals(chips, place, mine, recv):
    width = mine.shape[2]
    tile = min(512, width)
    block = pl.BlockSpec((2, N + EXTRA, tile), lambda j, pick: (0, 0, j))
    out = pl.BlockSpec((N + EXTRA, tile), lambda j, pick: (0, j))
    shape = jax.ShapeDtypeStruct((N + EXTRA, width), F32)
    return pl.pallas_call(
        functools.partial(chip_kernel, chips),
        grid_spec=pltpu.PrefetchScalarGridSpec(
            num_scalar_prefetch=1, grid=(width // tile,), in_specs=[block, block], out_specs=[out] * (chips - 1)
        ),
        out_shape=[shape] * (chips - 1),
        compiler_params=PARAMS,
        name="chip_totals",
        cost_estimate=pl.CostEstimate(flops=6 * N * width, bytes_accessed=24 * N * width, transcendentals=0),
    )(place, mine, recv)


def sides(place_ref):
    chip = place_ref[CHIP]
    return chip < 2, (chip == 1) | (chip == 2)


def first_kernel(place_ref, mine_ref, recv_ref, same_ref, cross_ref, back_ref, decay_ref):
    left, inner = sides(place_ref)
    core = place_ref[CORE]
    width = mine_ref.shape[2] // 2
    early, late = ordered(core, mine_ref[0], recv_ref[0])
    early_decay, late_decay = early[N : N + 1], late[N : N + 1]
    state = late_decay * early[:N] + late[:N]
    decay = early_decay * late_decay
    early, late = ordered(core, mine_ref[1], recv_ref[1])
    grad = early[:N] + early_decay * late[:N]
    out, back = jnp.where(left, state, grad), jnp.where(left, grad, state)
    same_ref[:N, :] = out[:, :width]
    same_ref[N : 2 * N, :] = jnp.where(inner, back[:, :width], out[:, width:])
    rows = lax.broadcasted_iota(jnp.int32, (EXTRA, width), 0)
    same_ref[2 * N :, :] = jnp.where(rows == 0, decay[:, :width], decay[:, width:])
    cross_ref[...] = out[:, width:]
    back_ref[...] = back[:, width:]
    decay_ref[...] = jnp.broadcast_to(decay[:, width:], (EXTRA, width))


def second_kernel(place_ref, own_ref, back_ref, same_ref, cross_ref, decay_ref, cross2_ref, same2_ref):
    _, inner = sides(place_ref)
    own, other = own_ref[:N, :], same_ref[:N, :]
    own_decay, other_decay = own_ref[2 * N : 2 * N + 1, :], same_ref[2 * N : 2 * N + 1, :]
    cross2_ref[...] = jnp.where(inner, own + own_decay * other, other + other_decay * own)
    weight = own_ref[2 * N + 1 : 2 * N + 2, :] * decay_ref[:1, :]
    same2_ref[...] = jnp.where(inner, back_ref[...] + weight * cross_ref[...], cross_ref[...])


def plain_call(kernel, name, out_shape, place, *args):
    whole = lambda a: pl.BlockSpec(a.shape, lambda j, pick: (0,) * len(a.shape))
    return pl.pallas_call(
        kernel,
        grid_spec=pltpu.PrefetchScalarGridSpec(
            num_scalar_prefetch=1,
            grid=(1,),
            in_specs=[whole(a) for a in args],
            out_specs=[whole(a) for a in out_shape],
        ),
        out_shape=out_shape,
        compiler_params=PARAMS,
        name=name,
        cost_estimate=pl.CostEstimate(
            flops=8 * sum(a.size for a in args), bytes_accessed=4 * sum(a.size for a in args), transcendentals=0
        ),
    )(place, *args)


def crossed(v, length, bit):
    return lax.ppermute(v, "seq", [(i, i ^ bit) for i in range(length)])


def first_phase(place, length, mine, recv):
    half = mine.shape[2] // 2
    shapes = [jax.ShapeDtypeStruct((rows, half), F32) for rows in (2 * N + EXTRA, N, N, EXTRA)]
    own, cross, back, decay = plain_call(first_kernel, "first_messages", shapes, place, mine, recv)
    return own, back, crossed(own, length, 2), crossed(cross, length, 4), crossed(decay, length, 6)


def second_phase(place, own, back, same, cross, decay):
    shape = jax.ShapeDtypeStruct(back.shape, F32)
    return plain_call(second_kernel, "second_messages", [shape, shape], place, own, back, same, cross, decay)


def carried4_kernel(
    place_ref, mine_ref, recv_ref, same_ref, cross_ref, decay_ref, cross2_ref, same2_ref, own_ref, peer_ref
):
    left, inner = sides(place_ref)
    width = cross_ref.shape[1]
    decay_a, decay_b = same_ref[2 * N : 2 * N + 1, :], same_ref[2 * N + 1 : 2 * N + 2, :]
    for part in range(2):
        at = slice(part * width, (part + 1) * width)
        out = jnp.where(inner, same_ref[part * N : (part + 1) * N, :], 0.0)
        if part == 0:
            back = jnp.where(inner, cross2_ref[...], same_ref[N : 2 * N, :] + decay_a * cross2_ref[...])
        else:
            back = same2_ref[...] + jnp.where(inner, decay_ref[:1, :], decay_b) * cross_ref[...]
        carried_cores(
            place_ref[CORE], jnp.where(left, out, back), jnp.where(left, back, out), mine_ref, recv_ref, own_ref, peer_ref, at
        )


def carried4(place, mine, recv, *others):
    shape = jax.ShapeDtypeStruct((2, N, mine.shape[2]), F32)
    return plain_call(carried4_kernel, "carried_in", [shape, shape], place, mine, recv, *others)


def carried_cores(core, state, grad, mine_ref, recv_ref, own_ref, peer_ref, at):
    early, late = ordered(core, mine_ref[0, :, at], recv_ref[0, :, at])
    at_late = early[N : N + 1] * state + early[:N]
    own_ref[0, :, at] = jnp.where(core == 0, state, at_late)
    peer_ref[0, :, at] = jnp.where(core == 0, at_late, state)
    early, late = ordered(core, mine_ref[1, :, at], recv_ref[1, :, at])
    at_early = late[:N] + late[N : N + 1] * grad
    own_ref[1, :, at] = jnp.where(core == 0, at_early, grad)
    peer_ref[1, :, at] = jnp.where(core == 0, grad, at_early)


def carried_kernel(chips, place_ref, mine_ref, recv_ref, *refs):
    others, (own_ref, peer_ref) = refs[:-2], refs[-2:]
    core, chip = place_ref[CORE], place_ref[CHIP]
    state = grad = jnp.zeros((N, own_ref.shape[2]), F32)
    state_weight = grad_weight = jnp.ones((1, own_ref.shape[2]), F32)
    for r, ref in enumerate(others, 1):
        earlier = chip >= r
        state = jnp.where(earlier, state + state_weight * ref[:N, :], state)
        state_weight = state_weight * ref[N : N + 1, :]
    for r in range(1, chips):
        later = chip + r < chips
        ref = others[chips - r - 1]
        grad = jnp.where(later, grad + grad_weight * ref[:N, :], grad)
        grad_weight = grad_weight * ref[N : N + 1, :]
    carried_cores(core, state, grad, mine_ref, recv_ref, own_ref, peer_ref, slice(None))


def carried(chips, place, mine, recv, others):
    width = mine.shape[2]
    tile = min(512, width)
    pair = pl.BlockSpec((2, N + EXTRA, tile), lambda j, pick: (0, 0, j))
    other = pl.BlockSpec((N + EXTRA, tile), lambda j, pick: (0, j))
    out = pl.BlockSpec((2, N, tile), lambda j, pick: (0, 0, j))
    shape = jax.ShapeDtypeStruct((2, N, width), F32)
    return pl.pallas_call(
        functools.partial(carried_kernel, chips),
        grid_spec=pltpu.PrefetchScalarGridSpec(
            num_scalar_prefetch=1,
            grid=(width // tile,),
            in_specs=[pair, pair] + [other] * len(others),
            out_specs=(out, out),
        ),
        out_shape=(shape, shape),
        compiler_params=PARAMS,
        name="carried_in",
        cost_estimate=pl.CostEstimate(flops=20 * N * width, bytes_accessed=44 * N * width, transcendentals=0),
    )(place, mine, recv, *others)


def blocks(chunks):
    span = 1
    while span < chunks:
        yield span, [at for at in range(span, chunks, 2 * span)]
        span *= 2


def row_bounds(chunks):
    for span, _ in blocks(chunks):
        for k in range(chunks):
            middle = k * SUB + SUB // 2
            boundary = (k // span + 1 - (k // span) % 2) * span * SUB
            yield (boundary, middle + 1) if middle >= boundary else (middle + 1, boundary)


def local_factors(decays, lift_ref, drop_ref, rows_ref):
    local = decays.shape[1]
    logs = log_parts(decays)
    rows = lax.broadcasted_iota(jnp.int32, (local, local), 0)
    columns = lax.broadcasted_iota(jnp.int32, (local, local), 1)
    middle = (columns & -SUB) + SUB // 2
    later = (rows > middle) & (rows <= columns)
    sooner = (rows > columns) & (rows <= middle)
    offset = summed_logs(logs, later.astype(F32) - sooner.astype(F32))
    lift_ref[...] = packed(jnp.exp(offset))
    drop_ref[...] = packed(jnp.exp(-offset))
    width = rows_ref.shape[0]
    lane = lax.broadcasted_iota(jnp.int32, (1, width), 1)
    first = last = jnp.zeros((1, width), jnp.int32)
    for i, (start, end) in enumerate(row_bounds(local // SUB)):
        first, last = jnp.where(lane == i, start, first), jnp.where(lane == i, end, last)
    rows = lax.broadcasted_iota(jnp.int32, (local, width), 0)
    rows_ref[...] = packed(jnp.exp(summed_logs(logs, (rows >= first) & (rows < last))))


def score_parts(b, c, ref, at, causal):
    score = dot(b, c, NT)
    if causal:
        rows = lax.broadcasted_iota(jnp.int32, score.shape, 0)
        columns = lax.broadcasted_iota(jnp.int32, score.shape, 1)
        score = jnp.where(rows <= columns, score, 0.0)
    hi, lo = halves(score)
    width = score.shape[1]
    ref[at, :width] = hi
    ref[at, width : 2 * width] = lo
    if ref.shape[1] > 2 * width:
        ref[at, 2 * width :] = hi


def scored(ref, at, dys):
    width = dys[0].shape[0]
    if ref.shape[1] > 2 * width:
        return dot(ref[at, :], stacked(dys[0], dys[0], dys[1]))
    return dot(ref[at, :], stacked(dys[0], dys[0])) + dot(ref[at, :width], dys[1])


def add_mixed(ref, at, dys, xs):
    width = xs[0].shape[0]
    both = dot(dys[0], stacked(*xs), NT)
    if width < LANES:
        ref[at, :] += both
        ref[at, :width] += dot(dys[1], xs[0], NT)
    else:
        ref[at, :] += both[:, :width] + (both[:, width:] + dot(dys[1], xs[0], NT))


def added_up(v, width):
    return v[:, :width] + v[:, width:] if v.shape[1] > width else v


def local_kernel(
    heads, x_ref, dy_ref, b_ref, c_ref, decays_ref, part_ref, out_ref, map_ref,
    lift_ref, drop_ref, rows_ref, full_ref, dys_ref, xs_ref, back_ref, sums_ref, scores_ref, *level_refs,
):
    local, tile = x_ref.shape
    chunks = local // SUB
    step = pl.program_id(0)
    levels = [(span, at, level_refs[2 * i], level_refs[2 * i + 1]) for i, (span, at) in enumerate(blocks(chunks))]

    @pl.when(step == 0)
    def _():
        local_factors(decays_ref[...], lift_ref, drop_ref, rows_ref)
        sums_ref[...] = jnp.zeros(sums_ref.shape, F32)
        for k in range(chunks):
            at = pl.ds(k * SUB, SUB)
            score_parts(b_ref[at, :], c_ref[at, :], scores_ref, at, True)
        for span, boundaries, mixed_ref, level_scores_ref in levels:
            mixed_ref[...] = jnp.zeros(mixed_ref.shape, F32)
            size = span * SUB
            for i, boundary in enumerate(boundaries):
                before, after = pl.ds((boundary - span) * SUB, size), pl.ds(boundary * SUB, size)
                score_parts(b_ref[before, :], c_ref[after, :], level_scores_ref, pl.ds(i * size, size), False)

    table = spread(heads, step * (tile // P_SIZE), tile)
    dys_ref[...] = dy_ref[...].astype(F32) * dot(lift_ref[...], table)
    back_ref[...] = dot(drop_ref[...], table)
    xs_ref[...] = x_ref[...].astype(F32) * back_ref[...]
    row = dot(rows_ref[...], table)

    for k in range(chunks):
        at = pl.ds(k * SUB, SUB)
        dys, xs = halves(dys_ref[at, :]), halves(xs_ref[at, :])
        add_mixed(sums_ref, at, dys, xs)
        part_ref[at, :] = back_ref[at, :] * scored(scores_ref, at, dys)

    for level, (span, boundaries, mixed_ref, level_scores_ref) in enumerate(levels):
        size = span * SUB
        for i, boundary in enumerate(boundaries):
            at = pl.ds(i * size, size)
            factor = lambda k: row[level * chunks + k : level * chunks + k + 1]
            take = lambda ref, first: halves(
                stacked(*[ref[k * SUB : (k + 1) * SUB, :] * factor(k) for k in range(first, first + span)])
            )
            dys, xs = take(dys_ref, boundary), take(xs_ref, boundary - span)
            add_mixed(mixed_ref, at, dys, xs)
            gained = scored(level_scores_ref, at, dys)
            for q in range(span):
                k = boundary - span + q
                rows = pl.ds(k * SUB, SUB)
                part_ref[rows, :] += (back_ref[rows, :] * factor(k)) * gained[q * SUB : (q + 1) * SUB]

    @pl.when(step == pl.num_programs(0) - 1)
    def _():
        full_ref[...] = jnp.zeros(full_ref.shape, F32)
        rows = lax.broadcasted_iota(jnp.int32, (SUB, SUB), 0)
        columns = lax.broadcasted_iota(jnp.int32, (SUB, SUB), 1)
        for k in range(chunks):
            at = pl.ds(k * SUB, SUB)
            full_ref[at, k * SUB : (k + 1) * SUB] = jnp.where(rows >= columns, added_up(sums_ref[at, :], SUB), 0.0)
        for span, boundaries, mixed_ref, _ in levels:
            size = span * SUB
            for i, boundary in enumerate(boundaries):
                block = added_up(mixed_ref[pl.ds(i * size, size), :], size)
                full_ref[pl.ds(boundary * SUB, size), (boundary - span) * SUB : boundary * SUB] = block
        map_ref[...] = jnp.zeros(map_ref.shape, F32)
        for k in range(0, local, LANES):
            at = pl.ds(k, LANES)
            mixed = full_ref[at, :]
            out_ref[at, :] = dot21(halves(mixed), b_ref[...])
            map_ref[...] += dot21(halves(mixed.T), c_ref[at, :])


def local_part(x, dy, b, c, decays):
    local, width = x.shape
    heads = width // P_SIZE
    count = width // TILE
    chunks = local // SUB
    whole = lambda a: pl.BlockSpec(a.shape, lambda j: (0, 0))
    column = pl.BlockSpec((local, TILE), lambda j: (0, j))
    tokens = pl.BlockSpec((local, N), lambda j: (0, 0))
    scratch = [
        pltpu.VMEM((local, LANES), BF16),
        pltpu.VMEM((local, LANES), BF16),
        pltpu.VMEM((LANES, LANES), BF16),
        pltpu.VMEM((local, local), F32),
        pltpu.VMEM((local, TILE), F32),
        pltpu.VMEM((local, TILE), F32),
        pltpu.VMEM((local, TILE), F32),
        pltpu.VMEM((local, 2 * SUB), F32),
        pltpu.VMEM((local, 3 * SUB), BF16),
    ]
    for span, _ in blocks(chunks):
        size = span * SUB
        scratch.append(pltpu.VMEM((local // 2, max(size, LANES)), F32))
        scratch.append(pltpu.VMEM((local // 2, (3 if size < LANES else 2) * size), BF16))
    return pl.pallas_call(
        functools.partial(local_kernel, heads),
        grid=(count,),
        in_specs=[column, column, whole(b), whole(c), whole(decays)],
        out_specs=(column, tokens, tokens),
        out_shape=(
            jax.ShapeDtypeStruct((local, width), F32),
            jax.ShapeDtypeStruct((local, N), F32),
            jax.ShapeDtypeStruct((local, N), F32),
        ),
        scratch_shapes=scratch,
        compiler_params=PARAMS,
        name="local_part",
        cost_estimate=pl.CostEstimate(flops=40 * local * N * width, bytes_accessed=8 * local * width, transcendentals=0),
    )(x, dy, b, c, decays)


def scaled_kernel(heads, x_ref, dy_ref, pre_ref, suf_ref, out_ref):
    tile = x_ref.shape[1]
    table = spread(heads, pl.program_id(0) * (tile // P_SIZE), tile)
    for i, (source, factor) in enumerate(((x_ref, suf_ref), (dy_ref, pre_ref))):
        out_ref[i, 0], out_ref[i, 1] = halves(source[...].astype(F32) * dot(factor[...], table))


def scaled_pairs(x, dy, pre, suf):
    local, width = x.shape
    whole = lambda a: pl.BlockSpec(a.shape, lambda j: (0, 0))
    column = pl.BlockSpec((local, TILE), lambda j: (0, j))
    return pl.pallas_call(
        functools.partial(scaled_kernel, width // P_SIZE),
        grid=(width // TILE,),
        in_specs=[column, column, whole(pre), whole(suf)],
        out_specs=pl.BlockSpec((2, 2, local, TILE), lambda j: (0, 0, 0, j)),
        out_shape=jax.ShapeDtypeStruct((2, 2, local, width), BF16),
        compiler_params=PARAMS,
        name="scaled_pairs",
        cost_estimate=pl.CostEstimate(flops=4 * local * LANES * width, bytes_accessed=12 * local * width, transcendentals=0),
    )(x, dy, pre, suf)


def map_kernel(count, ranks, place_ref, scaled_ref, carry_ref, out_before_ref, map_before_ref, *refs):
    messages, (out_ref, map_ref) = refs[:-2], refs[-2:]
    step = pl.program_id(0)

    @pl.when(step == 0)
    def _():
        out_ref[...] = out_before_ref[...]
        map_ref[...] = map_before_ref[...]

    for i, sum_ref in enumerate((map_ref, out_ref)):
        carry = halves(carry_ref[1 - i])
        both = dot(scaled_ref[i, 0], stacked(*carry), NT)
        sum_ref[...] += both[:, :N] + (both[:, N:] + dot(scaled_ref[i, 1], carry[0], NT))

    if messages:

        @pl.when(step == count - 1)
        def _():
            rows = messages[0].shape[1]
            for r, message in enumerate(messages):
                at = pl.ds(pl.multiple_of(((place_ref[RANK] + r) % ranks) * rows, rows), rows)
                message[0] = out_ref[at, :]
                message[1] = map_ref[at, :]


def map_terms(half, place, scaled, carry, out_before, map_before, ranks=0):
    local, width = scaled.shape[2], carry.shape[2]
    tile = min(512, width)
    count = width // tile
    whole = lambda a: pl.BlockSpec(a.shape, lambda j, pick: (0,) * len(a.shape))
    tokens = jax.ShapeDtypeStruct((local, N), F32)
    if ranks:
        out_shape = [jax.ShapeDtypeStruct((2, local // ranks, N), F32)] * ranks
        scratch = [pltpu.VMEM((local, N), F32), pltpu.VMEM((local, N), F32)]
    else:
        out_shape, scratch = [tokens, tokens], []
    return pl.pallas_call(
        functools.partial(map_kernel, count, ranks),
        grid_spec=pltpu.PrefetchScalarGridSpec(
            num_scalar_prefetch=1,
            grid=(count,),
            in_specs=[
                pl.BlockSpec((2, 2, local, tile), lambda j, pick: (0, 0, 0, pick[half] * count + j)),
                pl.BlockSpec((2, N, tile), lambda j, pick: (0, 0, j)),
                whole(tokens),
                whole(tokens),
            ],
            out_specs=[whole(shape) for shape in out_shape],
            scratch_shapes=scratch,
        ),
        out_shape=out_shape,
        compiler_params=PARAMS,
        name="map_terms",
        cost_estimate=pl.CostEstimate(flops=12 * local * N * width, bytes_accessed=8 * local * width, transcendentals=0),
    )(place, scaled, carry, out_before, map_before)


def input_kernel(heads, count, pick_ref, part_ref, suf_ref, b_ref, own_ref, other_ref, input_ref):
    tile = part_ref.shape[1]
    step = pl.program_id(0)
    after = dot(suf_ref[...], spread(heads, step * (tile // P_SIZE), tile))
    grad = jnp.where(step // count == pick_ref[CORE], own_ref[0], other_ref[0])
    input_ref[...] = (part_ref[...] + after * dot12(b_ref[...], halves(grad))).astype(BF16)


def input_terms(core, part, suf, b, own, other):
    local, width = part.shape
    heads = width // P_SIZE
    count = width // 2 // TILE
    whole = lambda a: pl.BlockSpec(a.shape, lambda j, pick: (0, 0))
    column = pl.BlockSpec((local, TILE), lambda j, pick: (0, j))
    carry = pl.BlockSpec((1, N, TILE), lambda j, pick: (1, 0, j % count))
    return pl.pallas_call(
        functools.partial(input_kernel, heads, count),
        grid_spec=pltpu.PrefetchScalarGridSpec(
            num_scalar_prefetch=1,
            grid=(2 * count,),
            in_specs=[column, whole(suf), whole(b), carry, carry],
            out_specs=column,
        ),
        out_shape=jax.ShapeDtypeStruct((local, width), BF16),
        compiler_params=PARAMS,
        name="input_terms",
        cost_estimate=pl.CostEstimate(flops=4 * local * N * width, bytes_accessed=8 * local * width, transcendentals=0),
    )(core, part, suf, b, own, other)


def swap_cores(v, length):
    return lax.ppermute(v, "seq", [(i, i ^ 1) for i in range(length)])


def turned(v, axis, length, by):
    return lax.ppermute(v, axis, [(i, (i + by) % length) for i in range(length)])


def per_device(mixer_input, output_grad, input_map, output_map, decays):
    length, ranks = lax.axis_size("seq"), lax.axis_size("head")
    chips = length // 2
    index, rank = lax.axis_index("seq"), lax.axis_index("head")
    core, chip = index % 2, index // 2
    place = jnp.stack([core, 1 - core, chip, rank]).astype(jnp.int32)
    args = mixer_input, output_grad, input_map, output_map
    sent, pre, suf = totals(OTHER, place, *args, decays=decays)
    recv = swap_cores(sent, length)
    (mine,) = totals(CORE, place, *args, pre=pre, suf=suf)
    if chips == 4:
        own, back, *others = first_phase(place, length, mine, recv)
        part, out_part, map_part = local_part(*args, decays)
        others, part, out_part, map_part = lax.optimization_barrier((others, part, out_part, map_part))
        cross, same = second_phase(place, own, back, *others)
        others += [crossed(cross, length, 4), crossed(same, length, 2)]
        pre, suf, _, _ = lax.optimization_barrier((pre, suf, cross, same))
        scaled = scaled_pairs(mixer_input, output_grad, pre, suf)
        others, scaled = lax.optimization_barrier((others, scaled))
        own, peer = carried4(place, mine, recv, *others)
    else:
        messages = chip_totals(chips, place, mine, recv)
        others = [turned(message, "seq", length, 2 * r) for r, message in enumerate(messages, 1)]
        part, out_part, map_part = local_part(*args, decays)
        scaled = scaled_pairs(mixer_input, output_grad, pre, suf)
        own, peer = carried(chips, place, mine, recv, others)
    other = swap_cores(peer, length)
    out_part, map_part = map_terms(CORE, place, scaled, own, out_part, map_part)
    shares = map_terms(OTHER, place, scaled, other, out_part, map_part, ranks)
    total = shares[0]
    own, other, shares = lax.optimization_barrier((own, other, shares))
    for r in range(1, ranks):
        total = total + turned(shares[r], "head", ranks, r)
    input_grad = input_terms(place, part, suf, input_map, own, other)
    return input_grad, total[1], total[0]


def solution(mesh):
    in_specs = (
        P("seq", "head"),
        P("seq", "head"),
        P("seq", None),
        P("seq", None),
        P("head", "seq"),
    )
    out_specs = (P("seq", "head"), P(("seq", "head"), None), P(("seq", "head"), None))
    return jax.shard_map(
        per_device, mesh=mesh, in_specs=in_specs, out_specs=out_specs, check_vma=False
    )
```

```python
import functools

import jax
import jax.numpy as jnp
from jax import lax
from jax.experimental import pallas as pl
from jax.experimental.pallas import tpu as pltpu
from jax.sharding import PartitionSpec as P

P_SIZE = 64
N = 128
SUB = 64
TILE = 256
EXTRA = 8
LANES = 128
CORE, OTHER = range(2)
PARAMS = pltpu.CompilerParams(vmem_limit_bytes=24 * 1024 * 1024)
FIRST = pltpu.CompilerParams(vmem_limit_bytes=60 * 1024 * 1024)
F32 = jnp.float32
BF16 = jnp.bfloat16

NN = (((1,), (0,)), ((), ()))
NT = (((1,), (1,)), ((), ()))


def dot(a, b, dims=NN):
    return lax.dot_general(a, b, dims, preferred_element_type=F32)


def halves(v):
    hi = v.astype(BF16)
    return hi, (v - hi.astype(F32)).astype(BF16)


def dot21(pair, b, dims=NN):
    return dot(pair[0], b, dims) + dot(pair[1], b, dims)


def dot12(a, pair, dims=NN):
    return dot(a, pair[0], dims) + dot(a, pair[1], dims)


def dot22(p, q, dims=NN):
    return dot(p[0], q[0], dims) + (dot(p[0], q[1], dims) + dot(p[1], q[0], dims))


def thirds(v):
    hi = v.astype(BF16)
    rest = v - hi.astype(F32)
    mid = rest.astype(BF16)
    return hi, mid, (rest - mid.astype(F32)).astype(BF16)


def spread(by_head, first, width):
    lanes = lax.broadcasted_iota(jnp.int32, by_head.shape, 1)
    step = LANES // P_SIZE
    shift = P_SIZE.bit_length() - 1
    taken = [
        jnp.take_along_axis(by_head, first + step * k + (lanes >> shift), axis=1) for k in range(width // LANES)
    ]
    return jnp.concatenate(taken, axis=1)


def place(half):
    core = lax.axis_index("seq") % 2
    return core if half == CORE else 1 - core


def stacked(*parts):
    return jnp.concatenate(parts, axis=0)


def transposed(v):
    return v.astype(F32).T.astype(BF16)


def log_parts(decays):
    return jnp.concatenate([part.astype(F32) for part in thirds(jnp.log(decays))], axis=0).astype(BF16)


def summed_logs(logs, table):
    heads = logs.shape[0] // 3
    sums = dot(logs, table.astype(F32).astype(BF16))
    return sums[:heads] + (sums[heads : 2 * heads] + sums[2 * heads :])


def by_token(v):
    rest = jnp.zeros((LANES - v.shape[0], v.shape[1]), F32)
    return jnp.concatenate([v, rest], axis=0).T


def device_factors(decays, pre_ref, suf_ref):
    local = decays.shape[1]
    logs = log_parts(decays)
    rows = lax.broadcasted_iota(jnp.int32, (local, local), 0)
    columns = lax.broadcasted_iota(jnp.int32, (local, local), 1)
    pre_ref[...] = by_token(jnp.exp(summed_logs(logs, rows <= columns)))
    suf_ref[...] = by_token(jnp.exp(summed_logs(logs, rows > columns)))


def totals_kernel(count, half, x_ref, dy_ref, b_ref, c_ref, *refs):
    if len(refs) == 6:
        decays_ref, out_ref, pre_ref, suf_ref, bt_ref, ct_ref = refs
    else:
        pre_ref, suf_ref, out_ref, bt_ref, ct_ref = refs
        decays_ref = None
    step = pl.program_id(0)

    @pl.when(step == 0)
    def _():
        bt_ref[...] = transposed(b_ref[...])
        ct_ref[...] = transposed(c_ref[...])
        if decays_ref is not None:
            device_factors(decays_ref[...], pre_ref, suf_ref)

    tile = x_ref.shape[1]
    first = (place(half) * count + step) * (tile // P_SIZE)
    before = spread(pre_ref[...], first, tile)
    after = spread(suf_ref[...], first, tile)
    ended = before[before.shape[0] - 1 :, :]
    for i, (source, factor, other) in enumerate(((x_ref, after, bt_ref), (dy_ref, before, ct_ref))):
        out_ref[i, :N, :] = dot12(other[...], halves(source[...].astype(F32) * factor))
    out_ref[0, N:, :] = jnp.broadcast_to(ended, (EXTRA, tile))
    out_ref[1, N:, :] = jnp.broadcast_to(ended, (EXTRA, tile))


def totals(half, x, dy, b, c, decays=None, pre=None, suf=None):
    local, width = x.shape
    count = width // 2 // TILE
    whole = lambda a: pl.BlockSpec(a.shape, lambda j: (0, 0))
    column = pl.BlockSpec((local, TILE), lambda j: (0, place(half) * count + j))
    factor = jax.ShapeDtypeStruct((local, LANES), F32)
    rest = (pre, suf) if decays is None else (decays,)
    out_specs = [pl.BlockSpec((2, N + EXTRA, TILE), lambda j: (0, 0, j))]
    out_shape = [jax.ShapeDtypeStruct((2, N + EXTRA, width // 2), F32)]
    if decays is not None:
        out_specs += [whole(factor), whole(factor)]
        out_shape += [factor, factor]
    return pl.pallas_call(
        functools.partial(totals_kernel, count, half),
        grid=(count,),
        in_specs=[column, column, whole(b), whole(c)] + [whole(a) for a in rest],
        out_specs=out_specs,
        scratch_shapes=[pltpu.VMEM((N, local), BF16), pltpu.VMEM((N, local), BF16)],
        out_shape=out_shape,
        compiler_params=FIRST,
        name="state_totals",
        cost_estimate=pl.CostEstimate(flops=8 * local * N * width // 2, bytes_accessed=4 * local * width, transcendentals=0),
    )(x, dy, b, c, *rest)


def ordered(core, mine, recv):
    return jnp.where(core == 0, mine, recv), jnp.where(core == 0, recv, mine)


def chip_kernel(chips, mine_ref, recv_ref, *out_refs):
    core, chip = place(CORE), lax.axis_index("seq") // 2
    early, late = ordered(core, mine_ref[0], recv_ref[0])
    early_decay, late_decay = early[N : N + 1], late[N : N + 1]
    both = jnp.broadcast_to(early_decay * late_decay, (EXTRA, early.shape[1]))
    state = late_decay * early[:N] + late[:N]
    early, late = ordered(core, mine_ref[1], recv_ref[1])
    grad = early[:N] + early_decay * late[:N]
    for r, out_ref in enumerate(out_refs, 1):
        out_ref[:N, :] = jnp.where(chip + r < chips, state, grad)
        out_ref[N:, :] = both


def chip_totals(chips, mine, recv):
    width = mine.shape[2]
    tile = min(512, width)
    block = pl.BlockSpec((2, N + EXTRA, tile), lambda j: (0, 0, j))
    out = pl.BlockSpec((N + EXTRA, tile), lambda j: (0, j))
    shape = jax.ShapeDtypeStruct((N + EXTRA, width), F32)
    return pl.pallas_call(
        functools.partial(chip_kernel, chips),
        grid=(width // tile,),
        in_specs=[block, block],
        out_specs=[out] * (chips - 1),
        out_shape=[shape] * (chips - 1),
        compiler_params=PARAMS,
        name="chip_totals",
        cost_estimate=pl.CostEstimate(flops=6 * N * width, bytes_accessed=24 * N * width, transcendentals=0),
    )(mine, recv)


def sides():
    chip = lax.axis_index("seq") // 2
    return chip < 2, (chip == 1) | (chip == 2)


def first_kernel(mine_ref, recv_ref, same_ref, cross_ref, back_ref, decay_ref):
    left, inner = sides()
    core = place(CORE)
    width = mine_ref.shape[2] // 2
    early, late = ordered(core, mine_ref[0], recv_ref[0])
    early_decay, late_decay = early[N : N + 1], late[N : N + 1]
    state = late_decay * early[:N] + late[:N]
    decay = early_decay * late_decay
    early, late = ordered(core, mine_ref[1], recv_ref[1])
    grad = early[:N] + early_decay * late[:N]
    out, back = jnp.where(left, state, grad), jnp.where(left, grad, state)
    same_ref[:N, :] = out[:, :width]
    same_ref[N : 2 * N, :] = jnp.where(inner, back[:, :width], out[:, width:])
    rows = lax.broadcasted_iota(jnp.int32, (EXTRA, width), 0)
    same_ref[2 * N :, :] = jnp.where(rows == 0, decay[:, :width], decay[:, width:])
    cross_ref[...] = out[:, width:]
    back_ref[...] = back[:, width:]
    decay_ref[...] = jnp.broadcast_to(decay[:, width:], (EXTRA, width))


def second_kernel(own_ref, back_ref, same_ref, cross_ref, decay_ref, cross2_ref, same2_ref):
    _, inner = sides()
    own, other = own_ref[:N, :], same_ref[:N, :]
    own_decay, other_decay = own_ref[2 * N : 2 * N + 1, :], same_ref[2 * N : 2 * N + 1, :]
    cross2_ref[...] = jnp.where(inner, own + own_decay * other, other + other_decay * own)
    weight = own_ref[2 * N + 1 : 2 * N + 2, :] * decay_ref[:1, :]
    same2_ref[...] = jnp.where(inner, back_ref[...] + weight * cross_ref[...], cross_ref[...])


def plain_call(kernel, name, out_shape, *args):
    whole = lambda a: pl.BlockSpec(a.shape, lambda j: (0,) * len(a.shape))
    size = sum(a.size for a in args)
    return pl.pallas_call(
        kernel,
        grid=(1,),
        in_specs=[whole(a) for a in args],
        out_specs=[whole(a) for a in out_shape],
        out_shape=out_shape,
        compiler_params=PARAMS,
        name=name,
        cost_estimate=pl.CostEstimate(flops=8 * size, bytes_accessed=4 * size, transcendentals=0),
    )(*args)


def crossed(v, length, bit):
    return lax.ppermute(v, "seq", [(i, i ^ bit) for i in range(length)])


def first_phase(length, mine, recv):
    half = mine.shape[2] // 2
    shapes = [jax.ShapeDtypeStruct((rows, half), F32) for rows in (2 * N + EXTRA, N, N, EXTRA)]
    own, cross, back, decay = plain_call(first_kernel, "first_messages", shapes, mine, recv)
    return own, back, crossed(own, length, 2), crossed(cross, length, 4), crossed(decay, length, 6)


def second_phase(own, back, same, cross, decay):
    shape = jax.ShapeDtypeStruct(back.shape, F32)
    return plain_call(second_kernel, "second_messages", [shape, shape], own, back, same, cross, decay)


def carried4_kernel(mine_ref, recv_ref, same_ref, cross_ref, decay_ref, cross2_ref, same2_ref, own_ref, peer_ref):
    left, inner = sides()
    width = cross_ref.shape[1]
    decay_a, decay_b = same_ref[2 * N : 2 * N + 1, :], same_ref[2 * N + 1 : 2 * N + 2, :]
    for part in range(2):
        at = slice(part * width, (part + 1) * width)
        out = jnp.where(inner, same_ref[part * N : (part + 1) * N, :], 0.0)
        if part == 0:
            back = jnp.where(inner, cross2_ref[...], same_ref[N : 2 * N, :] + decay_a * cross2_ref[...])
        else:
            back = same2_ref[...] + jnp.where(inner, decay_ref[:1, :], decay_b) * cross_ref[...]
        carried_cores(
            place(CORE), jnp.where(left, out, back), jnp.where(left, back, out), mine_ref, recv_ref, own_ref, peer_ref, at
        )


def carried4(mine, recv, *others):
    shape = jax.ShapeDtypeStruct((2, N, mine.shape[2]), F32)
    return plain_call(carried4_kernel, "carried_in", [shape, shape], mine, recv, *others)


def carried_cores(core, state, grad, mine_ref, recv_ref, own_ref, peer_ref, at):
    early, late = ordered(core, mine_ref[0, :, at], recv_ref[0, :, at])
    at_late = early[N : N + 1] * state + early[:N]
    own_ref[0, :, at] = jnp.where(core == 0, state, at_late)
    peer_ref[0, :, at] = jnp.where(core == 0, at_late, state)
    early, late = ordered(core, mine_ref[1, :, at], recv_ref[1, :, at])
    at_early = late[:N] + late[N : N + 1] * grad
    own_ref[1, :, at] = jnp.where(core == 0, at_early, grad)
    peer_ref[1, :, at] = jnp.where(core == 0, grad, at_early)


def carried_kernel(chips, mine_ref, recv_ref, *refs):
    others, (own_ref, peer_ref) = refs[:-2], refs[-2:]
    core, chip = place(CORE), lax.axis_index("seq") // 2
    state = grad = jnp.zeros((N, own_ref.shape[2]), F32)
    state_weight = grad_weight = jnp.ones((1, own_ref.shape[2]), F32)
    for r, ref in enumerate(others, 1):
        earlier = chip >= r
        state = jnp.where(earlier, state + state_weight * ref[:N, :], state)
        state_weight = state_weight * ref[N : N + 1, :]
    for r in range(1, chips):
        later = chip + r < chips
        ref = others[chips - r - 1]
        grad = jnp.where(later, grad + grad_weight * ref[:N, :], grad)
        grad_weight = grad_weight * ref[N : N + 1, :]
    carried_cores(core, state, grad, mine_ref, recv_ref, own_ref, peer_ref, slice(None))


def carried(chips, mine, recv, others):
    width = mine.shape[2]
    tile = min(512, width)
    pair = pl.BlockSpec((2, N + EXTRA, tile), lambda j: (0, 0, j))
    other = pl.BlockSpec((N + EXTRA, tile), lambda j: (0, j))
    out = pl.BlockSpec((2, N, tile), lambda j: (0, 0, j))
    shape = jax.ShapeDtypeStruct((2, N, width), F32)
    return pl.pallas_call(
        functools.partial(carried_kernel, chips),
        grid=(width // tile,),
        in_specs=[pair, pair] + [other] * len(others),
        out_specs=(out, out),
        out_shape=(shape, shape),
        compiler_params=PARAMS,
        name="carried_in",
        cost_estimate=pl.CostEstimate(flops=20 * N * width, bytes_accessed=44 * N * width, transcendentals=0),
    )(mine, recv, *others)


def blocks(chunks):
    span = 2
    while span < chunks:
        yield span, [at for at in range(span, chunks, 2 * span)]
        span *= 2


def row_bounds(chunks):
    middles = [k * SUB + SUB // 2 + 1 for k in range(chunks)]
    for span in [1] + [span for span, _ in blocks(chunks)]:
        for k, middle in enumerate(middles):
            boundary = (k // span + 1 - (k // span) % 2) * span * SUB
            yield min(boundary, middle), max(boundary, middle)
    yield from ((0, middle) for middle in middles)
    yield from ((middle, chunks * SUB) for middle in middles)


def local_factors(decays, lift_ref, drop_ref, rows_ref):
    local = decays.shape[1]
    logs = log_parts(decays)
    rows = lax.broadcasted_iota(jnp.int32, (local, local), 0)
    columns = lax.broadcasted_iota(jnp.int32, (local, local), 1)
    middle = (columns & -SUB) + SUB // 2
    later = (rows > middle) & (rows <= columns)
    sooner = (rows > columns) & (rows <= middle)
    offset = summed_logs(logs, later.astype(F32) - sooner.astype(F32))
    lift_ref[...] = by_token(jnp.exp(offset))
    drop_ref[...] = by_token(jnp.exp(-offset))
    lane = lax.broadcasted_iota(jnp.int32, (1, LANES), 1)
    first = last = jnp.zeros((1, LANES), jnp.int32)
    for i, (start, end) in enumerate(row_bounds(local // SUB)):
        first, last = jnp.where(lane == i, start, first), jnp.where(lane == i, end, last)
    rows = lax.broadcasted_iota(jnp.int32, (local, LANES), 0)
    decay = by_token(jnp.exp(summed_logs(logs, (rows >= first) & (rows < last))))
    rows_ref[...] = decay[: rows_ref.shape[0]]


def score_parts(b, c, ref, at, times, ahead=None):
    score = dot(b, c, NT)
    if ahead is not None:
        rows = lax.broadcasted_iota(jnp.int32, score.shape, 0)
        columns = lax.broadcasted_iota(jnp.int32, score.shape, 1)
        score = jnp.where(rows <= columns + ahead, score, 0.0)
    hi, lo = halves(score)
    width = score.shape[1]
    ref[at, :width] = hi
    ref[at, width : 2 * width] = lo
    if times == 3:
        ref[at, 2 * width :] = hi


def added_up(v):
    width = v.shape[1] // 2
    return v[:, :width] + v[:, width:]


def local_kernel(first_tile, continued, *refs):
    x_ref, dy_ref, b_ref, c_ref, decays_ref = refs[:5]
    refs = refs[5:]
    if continued:
        out_before_ref, map_before_ref = refs[:2]
        refs = refs[4:]
    part_ref, scaled_ref, out_ref, map_ref = refs[:4]
    lift_ref, drop_ref, rows_ref, full_ref, dys_ref, xs_ref, back_ref, sums_ref, even_ref, odd_ref = refs[4:14]
    level_refs = refs[14:]
    local, tile = x_ref.shape
    chunks = local // SUB
    step = pl.program_id(0)
    levels = [(span, at, level_refs[2 * i], level_refs[2 * i + 1]) for i, (span, at) in enumerate(blocks(chunks))]

    @pl.when(step == 0)
    def _():
        local_factors(decays_ref[...], lift_ref, drop_ref, rows_ref)
        sums_ref[...] = jnp.zeros(sums_ref.shape, F32)
        for k in range(0, chunks, 2):
            pair, even, odd = pl.ds(k * SUB, 2 * SUB), pl.ds(k * SUB, SUB), pl.ds((k + 1) * SUB, SUB)
            score_parts(b_ref[even, :], c_ref[even, :], even_ref, pl.ds(k // 2 * SUB, SUB), 3, 0)
            score_parts(b_ref[pair, :], c_ref[odd, :], odd_ref, pair, 3, SUB)
        for span, boundaries, mixed_ref, scores_ref in levels:
            mixed_ref[...] = jnp.zeros(mixed_ref.shape, F32)
            size = span * SUB
            for i, boundary in enumerate(boundaries):
                before, after = pl.ds((boundary - span) * SUB, size), pl.ds(boundary * SUB, size)
                score_parts(b_ref[before, :], c_ref[after, :], scores_ref, pl.ds(i * size, size), 2)

    first = (first_tile + step) * (tile // P_SIZE)
    dys_ref[...] = dy_ref[...].astype(F32) * spread(lift_ref[...], first, tile)
    back_ref[...] = spread(drop_ref[...], first, tile)
    xs_ref[...] = x_ref[...].astype(F32) * back_ref[...]
    row = spread(rows_ref[...], first, tile)
    factor = lambda kind, k: row[kind * chunks + k : kind * chunks + k + 1]

    for k in range(0, chunks, 2):
        even, odd, pair = pl.ds(k * SUB, SUB), pl.ds((k + 1) * SUB, SUB), pl.ds(k * SUB, 2 * SUB)
        dys, xs = halves(dys_ref[even, :]), halves(xs_ref[even, :])
        sums_ref[even, :] += dot(dys[0], stacked(*xs), NT)
        sums_ref[even, :SUB] += dot(dys[1], xs[0], NT)
        gained_even = dot(even_ref[pl.ds(k // 2 * SUB, SUB), :], stacked(dys[0], dys[0], dys[1]))
        joint = factor(0, k) * factor(0, k + 1)
        crossing = halves(xs_ref[even, :] * joint)
        dys, xs = halves(dys_ref[odd, :]), halves(xs_ref[odd, :])
        high = stacked(xs[0], crossing[0])
        both = dot(dys[0], stacked(high, xs[1], crossing[1]), NT)
        sums_ref[odd, :] += added_up(both) + dot(dys[1], high, NT)
        gained_odd = dot(odd_ref[pair, :], stacked(dys[0], dys[0], dys[1]))
        part_ref[even, :] = back_ref[even, :] * (gained_even + joint * gained_odd[:SUB])
        part_ref[odd, :] = back_ref[odd, :] * gained_odd[SUB:]

    for level, (span, boundaries, mixed_ref, scores_ref) in enumerate(levels, 1):
        size = span * SUB
        for i, boundary in enumerate(boundaries):
            at = pl.ds(i * size, size)
            take = lambda ref, start: halves(
                stacked(*[ref[k * SUB : (k + 1) * SUB, :] * factor(level, k) for k in range(start, start + span)])
            )
            dys, xs = take(dys_ref, boundary), take(xs_ref, boundary - span)
            both = dot(dys[0], stacked(*xs), NT)
            mixed_ref[at, :] += added_up(both) + dot(dys[1], xs[0], NT)
            gained = dot(scores_ref[at, :], stacked(dys[0], dys[0])) + dot(scores_ref[at, :size], dys[1])
            for q in range(span):
                k = boundary - span + q
                rows = pl.ds(k * SUB, SUB)
                part_ref[rows, :] += (back_ref[rows, :] * factor(level, k)) * gained[q * SUB : (q + 1) * SUB]

    for k in range(chunks):
        at = pl.ds(k * SUB, SUB)
        kind = len(levels) + 1
        scaled_ref[1, 0, at, :], scaled_ref[1, 1, at, :] = halves(dys_ref[at, :] * factor(kind, k))
        scaled_ref[0, 0, at, :], scaled_ref[0, 1, at, :] = halves(xs_ref[at, :] * factor(kind + 1, k))

    @pl.when(step == pl.num_programs(0) - 1)
    def _():
        full_ref[...] = jnp.zeros(full_ref.shape, F32)
        rows = lax.broadcasted_iota(jnp.int32, (SUB, SUB), 0)
        columns = lax.broadcasted_iota(jnp.int32, (SUB, SUB), 1)
        for k in range(0, chunks, 2):
            even, odd = pl.ds(k * SUB, SUB), pl.ds((k + 1) * SUB, SUB)
            full_ref[even, k * SUB : (k + 1) * SUB] = jnp.where(rows >= columns, added_up(sums_ref[even, :]), 0.0)
            full_ref[odd, (k + 1) * SUB : (k + 2) * SUB] = jnp.where(rows >= columns, sums_ref[odd, :SUB], 0.0)
            full_ref[odd, k * SUB : (k + 1) * SUB] = sums_ref[odd, SUB:]
        for span, boundaries, mixed_ref, _ in levels:
            size = span * SUB
            for i, boundary in enumerate(boundaries):
                block = mixed_ref[pl.ds(i * size, size), :]
                full_ref[pl.ds(boundary * SUB, size), (boundary - span) * SUB : boundary * SUB] = block
        map_ref[...] = map_before_ref[...] if continued else jnp.zeros(map_ref.shape, F32)
        for k in range(0, local, LANES):
            at = pl.ds(k, LANES)
            mixed = full_ref[at, :]
            gained = dot21(halves(mixed), b_ref[...])
            out_ref[at, :] = out_before_ref[at, :] + gained if continued else gained
            map_ref[...] += dot21(halves(mixed.T), c_ref[at, :])


def local_part(first_tile, count, x, dy, b, c, decays, before=None):
    local, width = x.shape
    chunks = local // SUB
    whole = lambda a: pl.BlockSpec(a.shape, lambda j: (0, 0))
    column = pl.BlockSpec((local, TILE), lambda j: (0, first_tile + j))
    tokens = pl.BlockSpec((local, N), lambda j: (0, 0))
    scratch = [
        pltpu.VMEM((local, LANES), F32),
        pltpu.VMEM((local, LANES), F32),
        pltpu.VMEM((-(-len(list(row_bounds(chunks))) // 8) * 8, LANES), F32),
        pltpu.VMEM((local, local), F32),
        pltpu.VMEM((local, TILE), F32),
        pltpu.VMEM((local, TILE), F32),
        pltpu.VMEM((local, TILE), F32),
        pltpu.VMEM((local, 2 * SUB), F32),
        pltpu.VMEM((local // 2, 3 * SUB), BF16),
        pltpu.VMEM((local, 3 * SUB), BF16),
    ]
    for span, _ in blocks(chunks):
        scratch.append(pltpu.VMEM((local // 2, span * SUB), F32))
        scratch.append(pltpu.VMEM((local // 2, 2 * span * SUB), BF16))
    in_specs = [column, column, whole(b), whole(c), whole(decays)]
    args, aliases = [x, dy, b, c, decays], {}
    if before is not None:
        part, scaled, out_part, map_part = before
        in_specs += [tokens, tokens, pl.BlockSpec(memory_space=pl.ANY), pl.BlockSpec(memory_space=pl.ANY)]
        args += [out_part, map_part, part, scaled]
        aliases = {7: 0, 8: 1}
    return pl.pallas_call(
        functools.partial(local_kernel, first_tile, before is not None),
        grid=(count,),
        in_specs=in_specs,
        out_specs=(column, pl.BlockSpec((2, 2, local, TILE), lambda j: (0, 0, 0, first_tile + j)), tokens, tokens),
        out_shape=(
            jax.ShapeDtypeStruct((local, width), F32),
            jax.ShapeDtypeStruct((2, 2, local, width), BF16),
            jax.ShapeDtypeStruct((local, N), F32),
            jax.ShapeDtypeStruct((local, N), F32),
        ),
        scratch_shapes=scratch,
        input_output_aliases=aliases,
        compiler_params=PARAMS,
        name="local_part",
        cost_estimate=pl.CostEstimate(
            flops=40 * local * N * TILE * count, bytes_accessed=8 * local * TILE * count, transcendentals=0
        ),
    )(*args)


def map_kernel(count, ranks, scaled_ref, carry_ref, out_before_ref, map_before_ref, *refs):
    messages, (out_ref, map_ref) = refs[:-2], refs[-2:]
    step = pl.program_id(0)

    @pl.when(step == 0)
    def _():
        out_ref[...] = out_before_ref[...]
        map_ref[...] = map_before_ref[...]

    for i, sum_ref in enumerate((map_ref, out_ref)):
        carry = halves(carry_ref[1 - i])
        both = dot(scaled_ref[i, 0], stacked(*carry), NT)
        sum_ref[...] += both[:, :N] + (both[:, N:] + dot(scaled_ref[i, 1], carry[0], NT))

    if messages:

        @pl.when(step == count - 1)
        def _():
            rows = messages[0].shape[1]
            for r, message in enumerate(messages):
                at = pl.ds(pl.multiple_of(((lax.axis_index("head") + r) % ranks) * rows, rows), rows)
                message[0] = out_ref[at, :]
                message[1] = map_ref[at, :]


def map_terms(half, scaled, carry, out_before, map_before, ranks=0):
    local, width = scaled.shape[2], carry.shape[2]
    tile = min(512, width)
    count = width // tile
    whole = lambda a: pl.BlockSpec(a.shape, lambda j: (0,) * len(a.shape))
    tokens = jax.ShapeDtypeStruct((local, N), F32)
    if ranks:
        out_shape = [jax.ShapeDtypeStruct((2, local // ranks, N), F32)] * ranks
        scratch = [pltpu.VMEM((local, N), F32), pltpu.VMEM((local, N), F32)]
    else:
        out_shape, scratch = [tokens, tokens], []
    return pl.pallas_call(
        functools.partial(map_kernel, count, ranks),
        grid=(count,),
        in_specs=[
            pl.BlockSpec((2, 2, local, tile), lambda j: (0, 0, 0, place(half) * count + j)),
            pl.BlockSpec((2, N, tile), lambda j: (0, 0, j)),
            whole(tokens),
            whole(tokens),
        ],
        out_specs=[whole(shape) for shape in out_shape],
        scratch_shapes=scratch,
        out_shape=out_shape,
        compiler_params=PARAMS,
        name="map_terms",
        cost_estimate=pl.CostEstimate(flops=12 * local * N * width, bytes_accessed=8 * local * width, transcendentals=0),
    )(scaled, carry, out_before, map_before)


def input_kernel(count, part_ref, suf_ref, b_ref, own_ref, other_ref, input_ref):
    tile = part_ref.shape[1]
    step = pl.program_id(0)
    after = spread(suf_ref[...], step * (tile // P_SIZE), tile)
    grad = jnp.where(step // count == place(CORE), own_ref[0], other_ref[0])
    input_ref[...] = (part_ref[...] + after * dot12(b_ref[...], halves(grad))).astype(BF16)


def input_terms(part, suf, b, own, other):
    local, width = part.shape
    count = width // 2 // TILE
    whole = lambda a: pl.BlockSpec(a.shape, lambda j: (0, 0))
    column = pl.BlockSpec((local, TILE), lambda j: (0, j))
    carry = pl.BlockSpec((1, N, TILE), lambda j: (1, 0, j % count))
    return pl.pallas_call(
        functools.partial(input_kernel, count),
        grid=(2 * count,),
        in_specs=[column, whole(suf), whole(b), carry, carry],
        out_specs=column,
        out_shape=jax.ShapeDtypeStruct((local, width), BF16),
        compiler_params=PARAMS,
        name="input_terms",
        cost_estimate=pl.CostEstimate(flops=4 * local * N * width, bytes_accessed=8 * local * width, transcendentals=0),
    )(part, suf, b, own, other)


def swap_cores(v, length):
    return lax.ppermute(v, "seq", [(i, i ^ 1) for i in range(length)])


def turned(v, axis, length, by):
    return lax.ppermute(v, axis, [(i, (i + by) % length) for i in range(length)])


def per_device(mixer_input, output_grad, input_map, output_map, decays):
    length, ranks = lax.axis_size("seq"), lax.axis_size("head")
    chips = length // 2
    args = mixer_input, output_grad, input_map, output_map
    sent, pre, suf = totals(OTHER, *args, decays=decays)
    recv = swap_cores(sent, length)
    (mine,) = totals(CORE, *args, pre=pre, suf=suf)
    tiles = mixer_input.shape[1] // TILE
    if chips == 4:
        ahead = tiles * 3 // 4
        own, back, *others = first_phase(length, mine, recv)
        result = local_part(0, ahead, *args, decays)
        others, result = lax.optimization_barrier((others, result))
        cross, same = second_phase(own, back, *others)
        others += [crossed(cross, length, 4), crossed(same, length, 2)]
        result, _, _ = lax.optimization_barrier((result, cross, same))
        result = local_part(ahead, tiles - ahead, *args, decays, result)
        others, result = lax.optimization_barrier((others, result))
        own, peer = carried4(mine, recv, *others)
    else:
        messages = chip_totals(chips, mine, recv)
        others = [turned(message, "seq", length, 2 * r) for r, message in enumerate(messages, 1)]
        result = local_part(0, tiles, *args, decays)
        own, peer = carried(chips, mine, recv, others)
    part, scaled, out_part, map_part = result
    other = swap_cores(peer, length)
    out_part, map_part = map_terms(CORE, scaled, own, out_part, map_part)
    shares = map_terms(OTHER, scaled, other, out_part, map_part, ranks)
    total = shares[0]
    own, other, shares = lax.optimization_barrier((own, other, shares))
    for r in range(1, ranks):
        total = total + turned(shares[r], "head", ranks, r)
    input_grad = input_terms(part, suf, input_map, own, other)
    return input_grad, total[1], total[0]


def solution(mesh):
    in_specs = (
        P("seq", "head"),
        P("seq", "head"),
        P("seq", None),
        P("seq", None),
        P("head", "seq"),
    )
    out_specs = (P("seq", "head"), P(("seq", "head"), None), P(("seq", "head"), None))
    return jax.shard_map(
        per_device, mesh=mesh, in_specs=in_specs, out_specs=out_specs, check_vma=False
    )
```

```python
import functools

import jax
import jax.numpy as jnp
from jax import lax
from jax.experimental import pallas as pl
from jax.experimental.pallas import tpu as pltpu
from jax.sharding import PartitionSpec as P

P_SIZE = 64
N = 128
SUB = 64
TILE = 256
EXTRA = 8
LANES = 128
CORE, OTHER = range(2)
PARAMS = pltpu.CompilerParams(vmem_limit_bytes=24 * 1024 * 1024)
FIRST = pltpu.CompilerParams(vmem_limit_bytes=56 * 1024 * 1024)
F32 = jnp.float32
BF16 = jnp.bfloat16

NN = (((1,), (0,)), ((), ()))
NT = (((1,), (1,)), ((), ()))


def dot(a, b, dims=NN):
    return lax.dot_general(a, b, dims, preferred_element_type=F32)


def halves(v):
    hi = v.astype(BF16)
    return hi, (v - hi.astype(F32)).astype(BF16)


def dot21(pair, b, dims=NN):
    return dot(pair[0], b, dims) + dot(pair[1], b, dims)


def dot12(a, pair, dims=NN):
    return dot(a, pair[0], dims) + dot(a, pair[1], dims)


def dot22(p, q, dims=NN):
    return dot(p[0], q[0], dims) + (dot(p[0], q[1], dims) + dot(p[1], q[0], dims))


def thirds(v):
    hi = v.astype(BF16)
    rest = v - hi.astype(F32)
    mid = rest.astype(BF16)
    return hi, mid, (rest - mid.astype(F32)).astype(BF16)


def spread(by_head, first, width):
    lanes = lax.broadcasted_iota(jnp.int32, by_head.shape, 1)
    step = LANES // P_SIZE
    shift = P_SIZE.bit_length() - 1
    taken = [
        jnp.take_along_axis(by_head, first + step * k + (lanes >> shift), axis=1) for k in range(width // LANES)
    ]
    return jnp.concatenate(taken, axis=1)


def place(half):
    core = lax.axis_index("seq") % 2
    return core if half == CORE else 1 - core


def stacked(*parts):
    return jnp.concatenate(parts, axis=0)


def transposed(v):
    return v.astype(F32).T.astype(BF16)


def log_parts(decays):
    return jnp.concatenate([part.astype(F32) for part in thirds(jnp.log(decays))], axis=0).astype(BF16)


def summed_logs(logs, table):
    heads = logs.shape[0] // 3
    sums = dot(logs, table.astype(F32).astype(BF16))
    return sums[:heads] + (sums[heads : 2 * heads] + sums[2 * heads :])


def by_token(v):
    rest = jnp.zeros((LANES - v.shape[0], v.shape[1]), F32)
    return jnp.concatenate([v, rest], axis=0).T


def device_factors(decays, pre_ref, suf_ref):
    local = decays.shape[1]
    logs = log_parts(decays)
    rows = lax.broadcasted_iota(jnp.int32, (local, local), 0)
    columns = lax.broadcasted_iota(jnp.int32, (local, local), 1)
    pre_ref[...] = by_token(jnp.exp(summed_logs(logs, rows <= columns)))
    suf_ref[...] = by_token(jnp.exp(summed_logs(logs, rows > columns)))


def totals_kernel(half, x_ref, dy_ref, b_ref, c_ref, decays_ref, out_ref, pre_ref, suf_ref):
    rows, width = x_ref.shape
    step = pl.program_id(0)

    @pl.when(step == 0)
    def _():
        device_factors(decays_ref[...], pre_ref, suf_ref)

    first = place(half) * (width // P_SIZE)
    at = pl.ds(pl.multiple_of(step * rows, rows), rows)
    for i, (source, factor, other) in enumerate(((x_ref, suf_ref, b_ref), (dy_ref, pre_ref, c_ref))):
        scaled = halves(source[...].astype(F32) * spread(factor[at, :], first, width))
        turned_map = transposed(other[at, :])
        gained = dot(jnp.concatenate([turned_map, turned_map], axis=1), stacked(*scaled))

        @pl.when(step == 0)
        def _():
            out_ref[i, :N, :] = gained

        @pl.when(step > 0)
        def _():
            out_ref[i, :N, :] += gained

    @pl.when(step == pl.num_programs(0) - 1)
    def _():
        last = pre_ref[pre_ref.shape[0] - EXTRA :, :]
        ended = jnp.broadcast_to(spread(last, first, width)[EXTRA - 1 :], (EXTRA, width))
        out_ref[0, N:, :] = ended
        out_ref[1, N:, :] = ended


def totals(half, x, dy, b, c, decays, params):
    local, width = x.shape
    width //= 2
    whole = lambda a: pl.BlockSpec(a.shape, lambda j: (0, 0))
    rows = pl.BlockSpec((LANES, width), lambda j: (j, place(half)))
    factor = jax.ShapeDtypeStruct((local, LANES), F32)
    return pl.pallas_call(
        functools.partial(totals_kernel, half),
        grid=(local // LANES,),
        in_specs=[rows, rows, whole(b), whole(c), whole(decays)],
        out_specs=[pl.BlockSpec((2, N + EXTRA, width), lambda j: (0, 0, 0)), whole(factor), whole(factor)],
        out_shape=[jax.ShapeDtypeStruct((2, N + EXTRA, width), F32), factor, factor],
        compiler_params=params,
        name="state_totals",
        cost_estimate=pl.CostEstimate(flops=8 * local * N * width, bytes_accessed=4 * local * width, transcendentals=0),
    )(x, dy, b, c, decays)


def ordered(core, mine, recv):
    return jnp.where(core == 0, mine, recv), jnp.where(core == 0, recv, mine)


def chip_kernel(chips, mine_ref, recv_ref, *out_refs):
    core, chip = place(CORE), lax.axis_index("seq") // 2
    early, late = ordered(core, mine_ref[0], recv_ref[0])
    early_decay, late_decay = early[N : N + 1], late[N : N + 1]
    both = jnp.broadcast_to(early_decay * late_decay, (EXTRA, early.shape[1]))
    state = late_decay * early[:N] + late[:N]
    early, late = ordered(core, mine_ref[1], recv_ref[1])
    grad = early[:N] + early_decay * late[:N]
    for r, out_ref in enumerate(out_refs, 1):
        out_ref[:N, :] = jnp.where(chip + r < chips, state, grad)
        out_ref[N:, :] = both


def chip_totals(chips, mine, recv):
    width = mine.shape[2]
    tile = min(512, width)
    block = pl.BlockSpec((2, N + EXTRA, tile), lambda j: (0, 0, j))
    out = pl.BlockSpec((N + EXTRA, tile), lambda j: (0, j))
    shape = jax.ShapeDtypeStruct((N + EXTRA, width), F32)
    return pl.pallas_call(
        functools.partial(chip_kernel, chips),
        grid=(width // tile,),
        in_specs=[block, block],
        out_specs=[out] * (chips - 1),
        out_shape=[shape] * (chips - 1),
        compiler_params=PARAMS,
        name="chip_totals",
        cost_estimate=pl.CostEstimate(flops=6 * N * width, bytes_accessed=24 * N * width, transcendentals=0),
    )(mine, recv)


def sides():
    chip = lax.axis_index("seq") // 2
    return chip < 2, (chip == 1) | (chip == 2)


def first_kernel(mine_ref, recv_ref, same_ref, cross_ref, back_ref, decay_ref):
    left, inner = sides()
    core = place(CORE)
    width = mine_ref.shape[2] // 2
    early, late = ordered(core, mine_ref[0], recv_ref[0])
    early_decay, late_decay = early[N : N + 1], late[N : N + 1]
    state = late_decay * early[:N] + late[:N]
    decay = early_decay * late_decay
    early, late = ordered(core, mine_ref[1], recv_ref[1])
    grad = early[:N] + early_decay * late[:N]
    out, back = jnp.where(left, state, grad), jnp.where(left, grad, state)
    same_ref[:N, :] = out[:, :width]
    same_ref[N : 2 * N, :] = jnp.where(inner, back[:, :width], out[:, width:])
    rows = lax.broadcasted_iota(jnp.int32, (EXTRA, width), 0)
    same_ref[2 * N :, :] = jnp.where(rows == 0, decay[:, :width], decay[:, width:])
    cross_ref[...] = out[:, width:]
    back_ref[...] = back[:, width:]
    decay_ref[...] = jnp.broadcast_to(decay[:, width:], (EXTRA, width))


def second_kernel(own_ref, back_ref, same_ref, cross_ref, decay_ref, cross2_ref, same2_ref):
    _, inner = sides()
    own, other = own_ref[:N, :], same_ref[:N, :]
    own_decay, other_decay = own_ref[2 * N : 2 * N + 1, :], same_ref[2 * N : 2 * N + 1, :]
    cross2_ref[...] = jnp.where(inner, own + own_decay * other, other + other_decay * own)
    weight = own_ref[2 * N + 1 : 2 * N + 2, :] * decay_ref[:1, :]
    same2_ref[...] = jnp.where(inner, back_ref[...] + weight * cross_ref[...], cross_ref[...])


def plain_call(kernel, name, out_shape, *args):
    whole = lambda a: pl.BlockSpec(a.shape, lambda j: (0,) * len(a.shape))
    size = sum(a.size for a in args)
    return pl.pallas_call(
        kernel,
        grid=(1,),
        in_specs=[whole(a) for a in args],
        out_specs=[whole(a) for a in out_shape],
        out_shape=out_shape,
        compiler_params=PARAMS,
        name=name,
        cost_estimate=pl.CostEstimate(flops=8 * size, bytes_accessed=4 * size, transcendentals=0),
    )(*args)


def crossed(v, length, bit):
    return lax.ppermute(v, "seq", [(i, i ^ bit) for i in range(length)])


def first_phase(length, mine, recv):
    half = mine.shape[2] // 2
    shapes = [jax.ShapeDtypeStruct((rows, half), F32) for rows in (2 * N + EXTRA, N, N, EXTRA)]
    own, cross, back, decay = plain_call(first_kernel, "first_messages", shapes, mine, recv)
    return own, back, crossed(own, length, 2), crossed(cross, length, 4), crossed(decay, length, 6)


def second_phase(own, back, same, cross, decay):
    shape = jax.ShapeDtypeStruct(back.shape, F32)
    return plain_call(second_kernel, "second_messages", [shape, shape], own, back, same, cross, decay)


def carried4_kernel(mine_ref, recv_ref, same_ref, cross_ref, decay_ref, cross2_ref, same2_ref, own_ref, peer_ref):
    left, inner = sides()
    width = cross_ref.shape[1]
    decay_a, decay_b = same_ref[2 * N : 2 * N + 1, :], same_ref[2 * N + 1 : 2 * N + 2, :]
    for part in range(2):
        at = slice(part * width, (part + 1) * width)
        out = jnp.where(inner, same_ref[part * N : (part + 1) * N, :], 0.0)
        if part == 0:
            back = jnp.where(inner, cross2_ref[...], same_ref[N : 2 * N, :] + decay_a * cross2_ref[...])
        else:
            back = same2_ref[...] + jnp.where(inner, decay_ref[:1, :], decay_b) * cross_ref[...]
        carried_cores(
            place(CORE), jnp.where(left, out, back), jnp.where(left, back, out), mine_ref, recv_ref, own_ref, peer_ref, at
        )


def carried4(mine, recv, *others):
    shape = jax.ShapeDtypeStruct((2, N, mine.shape[2]), F32)
    return plain_call(carried4_kernel, "carried_in", [shape, shape], mine, recv, *others)


def carried_cores(core, state, grad, mine_ref, recv_ref, own_ref, peer_ref, at):
    early, late = ordered(core, mine_ref[0, :, at], recv_ref[0, :, at])
    at_late = early[N : N + 1] * state + early[:N]
    own_ref[0, :, at] = jnp.where(core == 0, state, at_late)
    peer_ref[0, :, at] = jnp.where(core == 0, at_late, state)
    early, late = ordered(core, mine_ref[1, :, at], recv_ref[1, :, at])
    at_early = late[:N] + late[N : N + 1] * grad
    own_ref[1, :, at] = jnp.where(core == 0, at_early, grad)
    peer_ref[1, :, at] = jnp.where(core == 0, grad, at_early)


def carried_kernel(chips, mine_ref, recv_ref, *refs):
    others, (own_ref, peer_ref) = refs[:-2], refs[-2:]
    core, chip = place(CORE), lax.axis_index("seq") // 2
    state = grad = jnp.zeros((N, own_ref.shape[2]), F32)
    state_weight = grad_weight = jnp.ones((1, own_ref.shape[2]), F32)
    for r, ref in enumerate(others, 1):
        earlier = chip >= r
        state = jnp.where(earlier, state + state_weight * ref[:N, :], state)
        state_weight = state_weight * ref[N : N + 1, :]
    for r in range(1, chips):
        later = chip + r < chips
        ref = others[chips - r - 1]
        grad = jnp.where(later, grad + grad_weight * ref[:N, :], grad)
        grad_weight = grad_weight * ref[N : N + 1, :]
    carried_cores(core, state, grad, mine_ref, recv_ref, own_ref, peer_ref, slice(None))


def carried(chips, mine, recv, others):
    width = mine.shape[2]
    tile = min(512, width)
    pair = pl.BlockSpec((2, N + EXTRA, tile), lambda j: (0, 0, j))
    other = pl.BlockSpec((N + EXTRA, tile), lambda j: (0, j))
    out = pl.BlockSpec((2, N, tile), lambda j: (0, 0, j))
    shape = jax.ShapeDtypeStruct((2, N, width), F32)
    return pl.pallas_call(
        functools.partial(carried_kernel, chips),
        grid=(width // tile,),
        in_specs=[pair, pair] + [other] * len(others),
        out_specs=(out, out),
        out_shape=(shape, shape),
        compiler_params=PARAMS,
        name="carried_in",
        cost_estimate=pl.CostEstimate(flops=20 * N * width, bytes_accessed=44 * N * width, transcendentals=0),
    )(mine, recv, *others)


def blocks(chunks):
    span = 2
    while span < chunks:
        yield span, [at for at in range(span, chunks, 2 * span)]
        span *= 2


def row_bounds(chunks):
    middles = [k * SUB + SUB // 2 + 1 for k in range(chunks)]
    for span in [1] + [span for span, _ in blocks(chunks)]:
        for k, middle in enumerate(middles):
            boundary = (k // span + 1 - (k // span) % 2) * span * SUB
            yield min(boundary, middle), max(boundary, middle)
    yield from ((0, middle) for middle in middles)
    yield from ((middle, chunks * SUB) for middle in middles)


def local_factors(decays, lift_ref, drop_ref, rows_ref):
    local = decays.shape[1]
    logs = log_parts(decays)
    rows = lax.broadcasted_iota(jnp.int32, (local, local), 0)
    columns = lax.broadcasted_iota(jnp.int32, (local, local), 1)
    middle = (columns & -SUB) + SUB // 2
    later = (rows > middle) & (rows <= columns)
    sooner = (rows > columns) & (rows <= middle)
    offset = summed_logs(logs, later.astype(F32) - sooner.astype(F32))
    lift_ref[...] = by_token(jnp.exp(offset))
    drop_ref[...] = by_token(jnp.exp(-offset))
    lane = lax.broadcasted_iota(jnp.int32, (1, LANES), 1)
    first = last = jnp.zeros((1, LANES), jnp.int32)
    for i, (start, end) in enumerate(row_bounds(local // SUB)):
        first, last = jnp.where(lane == i, start, first), jnp.where(lane == i, end, last)
    rows = lax.broadcasted_iota(jnp.int32, (local, LANES), 0)
    decay = by_token(jnp.exp(summed_logs(logs, (rows >= first) & (rows < last))))
    rows_ref[...] = decay[: rows_ref.shape[0]]


def score_parts(b, c, ref, at, times, ahead=None):
    score = dot(b, c, NT)
    if ahead is not None:
        rows = lax.broadcasted_iota(jnp.int32, score.shape, 0)
        columns = lax.broadcasted_iota(jnp.int32, score.shape, 1)
        score = jnp.where(rows <= columns + ahead, score, 0.0)
    hi, lo = halves(score)
    width = score.shape[1]
    ref[at, :width] = hi
    ref[at, width : 2 * width] = lo
    if times == 3:
        ref[at, 2 * width :] = hi


def added_up(v):
    width = v.shape[1] // 2
    return v[:, :width] + v[:, width:]


def local_kernel(first_tile, continued, *refs):
    x_ref, dy_ref, b_ref, c_ref, decays_ref = refs[:5]
    refs = refs[5:]
    if continued:
        out_before_ref, map_before_ref = refs[:2]
        refs = refs[4:]
    part_ref, scaled_ref, out_ref, map_ref = refs[:4]
    lift_ref, drop_ref, rows_ref, full_ref, dys_ref, xs_ref, back_ref, sums_ref, even_ref, odd_ref = refs[4:14]
    level_refs = refs[14:]
    local, tile = x_ref.shape
    chunks = local // SUB
    step = pl.program_id(0)
    levels = [(span, at, level_refs[2 * i], level_refs[2 * i + 1]) for i, (span, at) in enumerate(blocks(chunks))]

    @pl.when(step == 0)
    def _():
        local_factors(decays_ref[...], lift_ref, drop_ref, rows_ref)
        sums_ref[...] = jnp.zeros(sums_ref.shape, F32)
        for k in range(0, chunks, 2):
            pair, even, odd = pl.ds(k * SUB, 2 * SUB), pl.ds(k * SUB, SUB), pl.ds((k + 1) * SUB, SUB)
            score_parts(b_ref[even, :], c_ref[even, :], even_ref, pl.ds(k // 2 * SUB, SUB), 3, 0)
            score_parts(b_ref[pair, :], c_ref[odd, :], odd_ref, pair, 3, SUB)
        for span, boundaries, mixed_ref, scores_ref in levels:
            mixed_ref[...] = jnp.zeros(mixed_ref.shape, F32)
            size = span * SUB
            for i, boundary in enumerate(boundaries):
                before, after = pl.ds((boundary - span) * SUB, size), pl.ds(boundary * SUB, size)
                score_parts(b_ref[before, :], c_ref[after, :], scores_ref, pl.ds(i * size, size), 2)

    first = (first_tile + step) * (tile // P_SIZE)
    dys_ref[...] = dy_ref[...].astype(F32) * spread(lift_ref[...], first, tile)
    back_ref[...] = spread(drop_ref[...], first, tile)
    xs_ref[...] = x_ref[...].astype(F32) * back_ref[...]
    row = spread(rows_ref[...], first, tile)
    factor = lambda kind, k: row[kind * chunks + k : kind * chunks + k + 1]

    for k in range(0, chunks, 2):
        even, odd, pair = pl.ds(k * SUB, SUB), pl.ds((k + 1) * SUB, SUB), pl.ds(k * SUB, 2 * SUB)
        dys, xs = halves(dys_ref[even, :]), halves(xs_ref[even, :])
        sums_ref[even, :] += dot(dys[0], stacked(*xs), NT)
        sums_ref[even, :SUB] += dot(dys[1], xs[0], NT)
        gained_even = dot(even_ref[pl.ds(k // 2 * SUB, SUB), :], stacked(dys[0], dys[0], dys[1]))
        joint = factor(0, k) * factor(0, k + 1)
        crossing = halves(xs_ref[even, :] * joint)
        dys, xs = halves(dys_ref[odd, :]), halves(xs_ref[odd, :])
        high = stacked(xs[0], crossing[0])
        both = dot(dys[0], stacked(high, xs[1], crossing[1]), NT)
        sums_ref[odd, :] += added_up(both) + dot(dys[1], high, NT)
        gained_odd = dot(odd_ref[pair, :], stacked(dys[0], dys[0], dys[1]))
        part_ref[even, :] = back_ref[even, :] * (gained_even + joint * gained_odd[:SUB])
        part_ref[odd, :] = back_ref[odd, :] * gained_odd[SUB:]

    for level, (span, boundaries, mixed_ref, scores_ref) in enumerate(levels, 1):
        size = span * SUB
        for i, boundary in enumerate(boundaries):
            at = pl.ds(i * size, size)
            take = lambda ref, start: halves(
                stacked(*[ref[k * SUB : (k + 1) * SUB, :] * factor(level, k) for k in range(start, start + span)])
            )
            dys, xs = take(dys_ref, boundary), take(xs_ref, boundary - span)
            both = dot(dys[0], stacked(*xs), NT)
            mixed_ref[at, :] += added_up(both) + dot(dys[1], xs[0], NT)
            gained = dot(scores_ref[at, :], stacked(dys[0], dys[0])) + dot(scores_ref[at, :size], dys[1])
            for q in range(span):
                k = boundary - span + q
                rows = pl.ds(k * SUB, SUB)
                part_ref[rows, :] += (back_ref[rows, :] * factor(level, k)) * gained[q * SUB : (q + 1) * SUB]

    for k in range(chunks):
        at = pl.ds(k * SUB, SUB)
        kind = len(levels) + 1
        scaled_ref[1, 0, at, :], scaled_ref[1, 1, at, :] = halves(dys_ref[at, :] * factor(kind, k))
        scaled_ref[0, 0, at, :], scaled_ref[0, 1, at, :] = halves(xs_ref[at, :] * factor(kind + 1, k))

    @pl.when(step == pl.num_programs(0) - 1)
    def _():
        full_ref[...] = jnp.zeros(full_ref.shape, F32)
        rows = lax.broadcasted_iota(jnp.int32, (SUB, SUB), 0)
        columns = lax.broadcasted_iota(jnp.int32, (SUB, SUB), 1)
        for k in range(0, chunks, 2):
            even, odd = pl.ds(k * SUB, SUB), pl.ds((k + 1) * SUB, SUB)
            full_ref[even, k * SUB : (k + 1) * SUB] = jnp.where(rows >= columns, added_up(sums_ref[even, :]), 0.0)
            full_ref[odd, (k + 1) * SUB : (k + 2) * SUB] = jnp.where(rows >= columns, sums_ref[odd, :SUB], 0.0)
            full_ref[odd, k * SUB : (k + 1) * SUB] = sums_ref[odd, SUB:]
        for span, boundaries, mixed_ref, _ in levels:
            size = span * SUB
            for i, boundary in enumerate(boundaries):
                block = mixed_ref[pl.ds(i * size, size), :]
                full_ref[pl.ds(boundary * SUB, size), (boundary - span) * SUB : boundary * SUB] = block
        map_ref[...] = map_before_ref[...] if continued else jnp.zeros(map_ref.shape, F32)
        for k in range(0, local, LANES):
            at = pl.ds(k, LANES)
            mixed = full_ref[at, :]
            gained = dot21(halves(mixed), b_ref[...])
            out_ref[at, :] = out_before_ref[at, :] + gained if continued else gained
            map_ref[...] += dot21(halves(mixed.T), c_ref[at, :])


def local_part(first_tile, count, x, dy, b, c, decays, before=None):
    local, width = x.shape
    chunks = local // SUB
    whole = lambda a: pl.BlockSpec(a.shape, lambda j: (0, 0))
    column = pl.BlockSpec((local, TILE), lambda j: (0, first_tile + j))
    tokens = pl.BlockSpec((local, N), lambda j: (0, 0))
    scratch = [
        pltpu.VMEM((local, LANES), F32),
        pltpu.VMEM((local, LANES), F32),
        pltpu.VMEM((-(-len(list(row_bounds(chunks))) // 8) * 8, LANES), F32),
        pltpu.VMEM((local, local), F32),
        pltpu.VMEM((local, TILE), F32),
        pltpu.VMEM((local, TILE), F32),
        pltpu.VMEM((local, TILE), F32),
        pltpu.VMEM((local, 2 * SUB), F32),
        pltpu.VMEM((local // 2, 3 * SUB), BF16),
        pltpu.VMEM((local, 3 * SUB), BF16),
    ]
    for span, _ in blocks(chunks):
        scratch.append(pltpu.VMEM((local // 2, span * SUB), F32))
        scratch.append(pltpu.VMEM((local // 2, 2 * span * SUB), BF16))
    in_specs = [column, column, whole(b), whole(c), whole(decays)]
    args, aliases = [x, dy, b, c, decays], {}
    if before is not None:
        part, scaled, out_part, map_part = before
        in_specs += [tokens, tokens, pl.BlockSpec(memory_space=pl.ANY), pl.BlockSpec(memory_space=pl.ANY)]
        args += [out_part, map_part, part, scaled]
        aliases = {7: 0, 8: 1}
    return pl.pallas_call(
        functools.partial(local_kernel, first_tile, before is not None),
        grid=(count,),
        in_specs=in_specs,
        out_specs=(column, pl.BlockSpec((2, 2, local, TILE), lambda j: (0, 0, 0, first_tile + j)), tokens, tokens),
        out_shape=(
            jax.ShapeDtypeStruct((local, width), F32),
            jax.ShapeDtypeStruct((2, 2, local, width), BF16),
            jax.ShapeDtypeStruct((local, N), F32),
            jax.ShapeDtypeStruct((local, N), F32),
        ),
        scratch_shapes=scratch,
        input_output_aliases=aliases,
        compiler_params=PARAMS,
        name="local_part",
        cost_estimate=pl.CostEstimate(
            flops=40 * local * N * TILE * count, bytes_accessed=8 * local * TILE * count, transcendentals=0
        ),
    )(*args)


def map_kernel(count, ranks, scaled_ref, carry_ref, out_before_ref, map_before_ref, *refs):
    messages, (out_ref, map_ref) = refs[:-2], refs[-2:]
    step = pl.program_id(0)

    @pl.when(step == 0)
    def _():
        out_ref[...] = out_before_ref[...]
        map_ref[...] = map_before_ref[...]

    for i, sum_ref in enumerate((map_ref, out_ref)):
        carry = halves(carry_ref[1 - i])
        both = dot(scaled_ref[i, 0], stacked(*carry), NT)
        sum_ref[...] += both[:, :N] + (both[:, N:] + dot(scaled_ref[i, 1], carry[0], NT))

    if messages:

        @pl.when(step == count - 1)
        def _():
            rows = messages[0].shape[1]
            for r, message in enumerate(messages):
                at = pl.ds(pl.multiple_of(((lax.axis_index("head") + r) % ranks) * rows, rows), rows)
                message[0] = out_ref[at, :]
                message[1] = map_ref[at, :]


def map_terms(half, scaled, carry, out_before, map_before, ranks=0):
    local, width = scaled.shape[2], carry.shape[2]
    tile = min(512, width)
    count = width // tile
    whole = lambda a: pl.BlockSpec(a.shape, lambda j: (0,) * len(a.shape))
    tokens = jax.ShapeDtypeStruct((local, N), F32)
    if ranks:
        out_shape = [jax.ShapeDtypeStruct((2, local // ranks, N), F32)] * ranks
        scratch = [pltpu.VMEM((local, N), F32), pltpu.VMEM((local, N), F32)]
    else:
        out_shape, scratch = [tokens, tokens], []
    return pl.pallas_call(
        functools.partial(map_kernel, count, ranks),
        grid=(count,),
        in_specs=[
            pl.BlockSpec((2, 2, local, tile), lambda j: (0, 0, 0, place(half) * count + j)),
            pl.BlockSpec((2, N, tile), lambda j: (0, 0, j)),
            whole(tokens),
            whole(tokens),
        ],
        out_specs=[whole(shape) for shape in out_shape],
        scratch_shapes=scratch,
        out_shape=out_shape,
        compiler_params=PARAMS,
        name="map_terms",
        cost_estimate=pl.CostEstimate(flops=12 * local * N * width, bytes_accessed=8 * local * width, transcendentals=0),
    )(scaled, carry, out_before, map_before)


def input_kernel(count, part_ref, suf_ref, b_ref, own_ref, other_ref, input_ref):
    tile = part_ref.shape[1]
    step = pl.program_id(0)
    after = spread(suf_ref[...], step * (tile // P_SIZE), tile)
    grad = jnp.where(step // count == place(CORE), own_ref[0], other_ref[0])
    input_ref[...] = (part_ref[...] + after * dot12(b_ref[...], halves(grad))).astype(BF16)


def input_terms(part, suf, b, own, other):
    local, width = part.shape
    count = width // 2 // TILE
    whole = lambda a: pl.BlockSpec(a.shape, lambda j: (0, 0))
    column = pl.BlockSpec((local, TILE), lambda j: (0, j))
    carry = pl.BlockSpec((1, N, TILE), lambda j: (1, 0, j % count))
    return pl.pallas_call(
        functools.partial(input_kernel, count),
        grid=(2 * count,),
        in_specs=[column, whole(suf), whole(b), carry, carry],
        out_specs=column,
        out_shape=jax.ShapeDtypeStruct((local, width), BF16),
        compiler_params=PARAMS,
        name="input_terms",
        cost_estimate=pl.CostEstimate(flops=4 * local * N * width, bytes_accessed=8 * local * width, transcendentals=0),
    )(part, suf, b, own, other)


def swap_cores(v, length):
    return lax.ppermute(v, "seq", [(i, i ^ 1) for i in range(length)])


def turned(v, axis, length, by):
    return lax.ppermute(v, axis, [(i, (i + by) % length) for i in range(length)])


def per_device(mixer_input, output_grad, input_map, output_map, decays):
    length, ranks = lax.axis_size("seq"), lax.axis_size("head")
    chips = length // 2
    args = mixer_input, output_grad, input_map, output_map
    sent, _, _ = totals(OTHER, *args, decays, FIRST)
    recv = swap_cores(sent, length)
    mine, _, suf = totals(CORE, *args, decays, PARAMS)
    tiles = mixer_input.shape[1] // TILE
    if chips == 4:
        ahead = tiles * 3 // 4
        own, back, *others = first_phase(length, mine, recv)
        result = local_part(0, ahead, *args, decays)
        others, result = lax.optimization_barrier((others, result))
        cross, same = second_phase(own, back, *others)
        others += [crossed(cross, length, 4), crossed(same, length, 2)]
        result, _, _ = lax.optimization_barrier((result, cross, same))
        result = local_part(ahead, tiles - ahead, *args, decays, result)
        others, result = lax.optimization_barrier((others, result))
        own, peer = carried4(mine, recv, *others)
    else:
        messages = chip_totals(chips, mine, recv)
        others = [turned(message, "seq", length, 2 * r) for r, message in enumerate(messages, 1)]
        result = local_part(0, tiles, *args, decays)
        own, peer = carried(chips, mine, recv, others)
    part, scaled, out_part, map_part = result
    other = swap_cores(peer, length)
    out_part, map_part = map_terms(CORE, scaled, own, out_part, map_part)
    shares = map_terms(OTHER, scaled, other, out_part, map_part, ranks)
    total = shares[0]
    own, other, shares = lax.optimization_barrier((own, other, shares))
    for r in range(1, ranks):
        total = total + turned(shares[r], "head", ranks, r)
    input_grad = input_terms(part, suf, input_map, own, other)
    return input_grad, total[1], total[0]


def solution(mesh):
    in_specs = (
        P("seq", "head"),
        P("seq", "head"),
        P("seq", None),
        P("seq", None),
        P("head", "seq"),
    )
    out_specs = (P("seq", "head"), P(("seq", "head"), None), P(("seq", "head"), None))
    return jax.shard_map(
        per_device, mesh=mesh, in_specs=in_specs, out_specs=out_specs, check_vma=False
    )
```

```python
import functools

import jax
import jax.numpy as jnp
from jax import lax
from jax.experimental import pallas as pl
from jax.experimental.pallas import tpu as pltpu
from jax.sharding import PartitionSpec as P

P_SIZE = 64
N = 128
SUB = 64
TILE = 256
EXTRA = 8
PARTS = 4
LANES = 128
CORE, OTHER = range(2)
PARAMS = pltpu.CompilerParams(vmem_limit_bytes=24 * 1024 * 1024)
FIRST = pltpu.CompilerParams(vmem_limit_bytes=56 * 1024 * 1024)
F32 = jnp.float32
BF16 = jnp.bfloat16

NN = (((1,), (0,)), ((), ()))
NT = (((1,), (1,)), ((), ()))


def dot(a, b, dims=NN):
    return lax.dot_general(a, b, dims, preferred_element_type=F32)


def halves(v):
    hi = v.astype(BF16)
    return hi, (v - hi.astype(F32)).astype(BF16)


def dot21(pair, b, dims=NN):
    return dot(pair[0], b, dims) + dot(pair[1], b, dims)


def dot12(a, pair, dims=NN):
    return dot(a, pair[0], dims) + dot(a, pair[1], dims)


def dot22(p, q, dims=NN):
    return dot(p[0], q[0], dims) + (dot(p[0], q[1], dims) + dot(p[1], q[0], dims))


def thirds(v):
    hi = v.astype(BF16)
    rest = v - hi.astype(F32)
    mid = rest.astype(BF16)
    return hi, mid, (rest - mid.astype(F32)).astype(BF16)


def spread(by_head, first, width):
    lanes = lax.broadcasted_iota(jnp.int32, by_head.shape, 1)
    step = LANES // P_SIZE
    shift = P_SIZE.bit_length() - 1
    taken = [
        jnp.take_along_axis(by_head, first + step * k + (lanes >> shift), axis=1) for k in range(width // LANES)
    ]
    return jnp.concatenate(taken, axis=1)


def place(half):
    core = lax.axis_index("seq") % 2
    return core if half == CORE else 1 - core


def stacked(*parts):
    return jnp.concatenate(parts, axis=0)


def transposed(v):
    return v.astype(F32).T.astype(BF16)


def log_parts(decays):
    return jnp.concatenate([part.astype(F32) for part in thirds(jnp.log(decays))], axis=0).astype(BF16)


def summed_logs(logs, table):
    heads = logs.shape[0] // 3
    sums = dot(logs, table.astype(F32).astype(BF16))
    return sums[:heads] + (sums[heads : 2 * heads] + sums[2 * heads :])


def by_token(v):
    rest = jnp.zeros((LANES - v.shape[0], v.shape[1]), F32)
    return jnp.concatenate([v, rest], axis=0).T


def packed(v):
    parts = [part.astype(F32) for part in thirds(v)]
    rest = jnp.zeros((LANES - 3 * v.shape[0], v.shape[1]), F32)
    return jnp.concatenate(parts + [rest], axis=0).T.astype(BF16)


def spread_table(heads, first, width):
    rows = lax.broadcasted_iota(jnp.int32, (heads, width), 0)
    columns = lax.broadcasted_iota(jnp.int32, (heads, width), 1)
    offset = columns - (rows - first) * P_SIZE
    picked = ((offset >= 0) & (offset < P_SIZE)).astype(F32)
    rest = jnp.zeros((LANES - 3 * heads, width), F32)
    return jnp.concatenate([picked, picked, picked, rest], axis=0).astype(BF16)


def device_factors(decays, ref):
    local = decays.shape[1]
    logs = log_parts(decays)
    rows = lax.broadcasted_iota(jnp.int32, (local, local), 0)
    columns = lax.broadcasted_iota(jnp.int32, (local, local), 1)
    ref[:, :LANES] = packed(jnp.exp(summed_logs(logs, rows <= columns)))
    ref[:, LANES:] = packed(jnp.exp(summed_logs(logs, rows > columns)))


def totals_kernel(heads, count, half, made, *refs):
    x_refs, dy_refs, (b_ref, c_ref) = refs[:PARTS], refs[PARTS : 2 * PARTS], refs[2 * PARTS : 2 * PARTS + 2]
    refs = refs[2 * PARTS + 2 :]
    if made:
        factor_ref, out_ref, bt_ref, ct_ref = refs
    else:
        decays_ref, out_ref, factor_ref, bt_ref, ct_ref = refs
    step = pl.program_id(0)

    @pl.when(step == 0)
    def _():
        bt_ref[...] = transposed(b_ref[...])
        ct_ref[...] = transposed(c_ref[...])
        if not made:
            device_factors(decays_ref[...], factor_ref)

    tile = x_refs[0].shape[1]
    table = spread_table(heads, (place(half) * count + step) * (tile // P_SIZE), tile)
    before = dot(factor_ref[:, :LANES], table)
    after = dot(factor_ref[:, LANES:], table)
    ended = before[before.shape[0] - 1 :, :]
    for i, (sources, factor, other) in enumerate(((x_refs, after, bt_ref), (dy_refs, before, ct_ref))):
        source = stacked(*[ref[...].astype(F32) for ref in sources])
        out_ref[i, :N, :] = dot12(other[...], halves(source * factor))
        out_ref[i, N:, :] = jnp.broadcast_to(ended, (EXTRA, tile))


def totals(half, x, dy, b, c, decays=None, factors=None):
    local, width = x.shape
    count = width // 2 // TILE
    whole = lambda a: pl.BlockSpec(a.shape, lambda j: (0, 0))
    columns = [
        pl.BlockSpec((local // PARTS, TILE), functools.partial(lambda part, j: (part, place(half) * count + j), part))
        for part in range(PARTS)
    ]
    factor = jax.ShapeDtypeStruct((local, 2 * LANES), BF16)
    made = factors is not None
    last = factors if made else decays
    out_specs = [pl.BlockSpec((2, N + EXTRA, TILE), lambda j: (0, 0, j))]
    out_shape = [jax.ShapeDtypeStruct((2, N + EXTRA, width // 2), F32)]
    if not made:
        out_specs.append(whole(factor))
        out_shape.append(factor)
    return pl.pallas_call(
        functools.partial(totals_kernel, width // P_SIZE, count, half, made),
        grid=(count,),
        in_specs=columns + columns + [whole(b), whole(c), whole(last)],
        out_specs=out_specs,
        scratch_shapes=[pltpu.VMEM((N, local), BF16), pltpu.VMEM((N, local), BF16)],
        out_shape=out_shape,
        compiler_params=PARAMS if made else FIRST,
        name="state_totals",
        cost_estimate=pl.CostEstimate(flops=8 * local * N * width // 2, bytes_accessed=4 * local * width, transcendentals=0),
    )(*[x] * PARTS, *[dy] * PARTS, b, c, last)


def ordered(core, mine, recv):
    return jnp.where(core == 0, mine, recv), jnp.where(core == 0, recv, mine)


def chip_kernel(chips, mine_ref, recv_ref, *out_refs):
    core, chip = place(CORE), lax.axis_index("seq") // 2
    early, late = ordered(core, mine_ref[0], recv_ref[0])
    early_decay, late_decay = early[N : N + 1], late[N : N + 1]
    both = jnp.broadcast_to(early_decay * late_decay, (EXTRA, early.shape[1]))
    state = late_decay * early[:N] + late[:N]
    early, late = ordered(core, mine_ref[1], recv_ref[1])
    grad = early[:N] + early_decay * late[:N]
    for r, out_ref in enumerate(out_refs, 1):
        out_ref[:N, :] = jnp.where(chip + r < chips, state, grad)
        out_ref[N:, :] = both


def chip_totals(chips, mine, recv):
    width = mine.shape[2]
    tile = min(512, width)
    block = pl.BlockSpec((2, N + EXTRA, tile), lambda j: (0, 0, j))
    out = pl.BlockSpec((N + EXTRA, tile), lambda j: (0, j))
    shape = jax.ShapeDtypeStruct((N + EXTRA, width), F32)
    return pl.pallas_call(
        functools.partial(chip_kernel, chips),
        grid=(width // tile,),
        in_specs=[block, block],
        out_specs=[out] * (chips - 1),
        out_shape=[shape] * (chips - 1),
        compiler_params=PARAMS,
        name="chip_totals",
        cost_estimate=pl.CostEstimate(flops=6 * N * width, bytes_accessed=24 * N * width, transcendentals=0),
    )(mine, recv)


def sides():
    chip = lax.axis_index("seq") // 2
    return chip < 2, (chip == 1) | (chip == 2)


def first_kernel(mine_ref, recv_ref, same_ref, cross_ref, back_ref, decay_ref):
    left, inner = sides()
    core = place(CORE)
    width = mine_ref.shape[2] // 2
    early, late = ordered(core, mine_ref[0], recv_ref[0])
    early_decay, late_decay = early[N : N + 1], late[N : N + 1]
    state = late_decay * early[:N] + late[:N]
    decay = early_decay * late_decay
    early, late = ordered(core, mine_ref[1], recv_ref[1])
    grad = early[:N] + early_decay * late[:N]
    out, back = jnp.where(left, state, grad), jnp.where(left, grad, state)
    same_ref[:N, :] = out[:, :width]
    same_ref[N : 2 * N, :] = jnp.where(inner, back[:, :width], out[:, width:])
    rows = lax.broadcasted_iota(jnp.int32, (EXTRA, width), 0)
    same_ref[2 * N :, :] = jnp.where(rows == 0, decay[:, :width], decay[:, width:])
    cross_ref[...] = out[:, width:]
    back_ref[...] = back[:, width:]
    decay_ref[...] = jnp.broadcast_to(decay[:, width:], (EXTRA, width))


def second_kernel(own_ref, back_ref, same_ref, cross_ref, decay_ref, cross2_ref, same2_ref):
    _, inner = sides()
    own, other = own_ref[:N, :], same_ref[:N, :]
    own_decay, other_decay = own_ref[2 * N : 2 * N + 1, :], same_ref[2 * N : 2 * N + 1, :]
    cross2_ref[...] = jnp.where(inner, own + own_decay * other, other + other_decay * own)
    weight = own_ref[2 * N + 1 : 2 * N + 2, :] * decay_ref[:1, :]
    same2_ref[...] = jnp.where(inner, back_ref[...] + weight * cross_ref[...], cross_ref[...])


def plain_call(kernel, name, out_shape, *args):
    whole = lambda a: pl.BlockSpec(a.shape, lambda j: (0,) * len(a.shape))
    size = sum(a.size for a in args)
    return pl.pallas_call(
        kernel,
        grid=(1,),
        in_specs=[whole(a) for a in args],
        out_specs=[whole(a) for a in out_shape],
        out_shape=out_shape,
        compiler_params=PARAMS,
        name=name,
        cost_estimate=pl.CostEstimate(flops=8 * size, bytes_accessed=4 * size, transcendentals=0),
    )(*args)


def crossed(v, length, bit):
    return lax.ppermute(v, "seq", [(i, i ^ bit) for i in range(length)])


def first_phase(length, mine, recv):
    half = mine.shape[2] // 2
    shapes = [jax.ShapeDtypeStruct((rows, half), F32) for rows in (2 * N + EXTRA, N, N, EXTRA)]
    own, cross, back, decay = plain_call(first_kernel, "first_messages", shapes, mine, recv)
    return own, back, crossed(own, length, 2), crossed(cross, length, 4), crossed(decay, length, 6)


def second_phase(own, back, same, cross, decay):
    shape = jax.ShapeDtypeStruct(back.shape, F32)
    return plain_call(second_kernel, "second_messages", [shape, shape], own, back, same, cross, decay)


def carried4_kernel(mine_ref, recv_ref, same_ref, cross_ref, decay_ref, cross2_ref, same2_ref, own_ref, peer_ref):
    left, inner = sides()
    width = cross_ref.shape[1]
    decay_a, decay_b = same_ref[2 * N : 2 * N + 1, :], same_ref[2 * N + 1 : 2 * N + 2, :]
    for part in range(2):
        at = slice(part * width, (part + 1) * width)
        out = jnp.where(inner, same_ref[part * N : (part + 1) * N, :], 0.0)
        if part == 0:
            back = jnp.where(inner, cross2_ref[...], same_ref[N : 2 * N, :] + decay_a * cross2_ref[...])
        else:
            back = same2_ref[...] + jnp.where(inner, decay_ref[:1, :], decay_b) * cross_ref[...]
        carried_cores(
            place(CORE), jnp.where(left, out, back), jnp.where(left, back, out), mine_ref, recv_ref, own_ref, peer_ref, at
        )


def carried4(mine, recv, *others):
    shape = jax.ShapeDtypeStruct((2, N, mine.shape[2]), F32)
    return plain_call(carried4_kernel, "carried_in", [shape, shape], mine, recv, *others)


def carried_cores(core, state, grad, mine_ref, recv_ref, own_ref, peer_ref, at):
    early, late = ordered(core, mine_ref[0, :, at], recv_ref[0, :, at])
    at_late = early[N : N + 1] * state + early[:N]
    own_ref[0, :, at] = jnp.where(core == 0, state, at_late)
    peer_ref[0, :, at] = jnp.where(core == 0, at_late, state)
    early, late = ordered(core, mine_ref[1, :, at], recv_ref[1, :, at])
    at_early = late[:N] + late[N : N + 1] * grad
    own_ref[1, :, at] = jnp.where(core == 0, at_early, grad)
    peer_ref[1, :, at] = jnp.where(core == 0, grad, at_early)


def carried_kernel(chips, mine_ref, recv_ref, *refs):
    others, (own_ref, peer_ref) = refs[:-2], refs[-2:]
    core, chip = place(CORE), lax.axis_index("seq") // 2
    state = grad = jnp.zeros((N, own_ref.shape[2]), F32)
    state_weight = grad_weight = jnp.ones((1, own_ref.shape[2]), F32)
    for r, ref in enumerate(others, 1):
        earlier = chip >= r
        state = jnp.where(earlier, state + state_weight * ref[:N, :], state)
        state_weight = state_weight * ref[N : N + 1, :]
    for r in range(1, chips):
        later = chip + r < chips
        ref = others[chips - r - 1]
        grad = jnp.where(later, grad + grad_weight * ref[:N, :], grad)
        grad_weight = grad_weight * ref[N : N + 1, :]
    carried_cores(core, state, grad, mine_ref, recv_ref, own_ref, peer_ref, slice(None))


def carried(chips, mine, recv, others):
    width = mine.shape[2]
    tile = min(512, width)
    pair = pl.BlockSpec((2, N + EXTRA, tile), lambda j: (0, 0, j))
    other = pl.BlockSpec((N + EXTRA, tile), lambda j: (0, j))
    out = pl.BlockSpec((2, N, tile), lambda j: (0, 0, j))
    shape = jax.ShapeDtypeStruct((2, N, width), F32)
    return pl.pallas_call(
        functools.partial(carried_kernel, chips),
        grid=(width // tile,),
        in_specs=[pair, pair] + [other] * len(others),
        out_specs=(out, out),
        out_shape=(shape, shape),
        compiler_params=PARAMS,
        name="carried_in",
        cost_estimate=pl.CostEstimate(flops=20 * N * width, bytes_accessed=44 * N * width, transcendentals=0),
    )(mine, recv, *others)


def blocks(chunks):
    span = 2
    while span < chunks:
        yield span, [at for at in range(span, chunks, 2 * span)]
        span *= 2


def row_bounds(chunks):
    middles = [k * SUB + SUB // 2 + 1 for k in range(chunks)]
    for span in [1] + [span for span, _ in blocks(chunks)]:
        for k, middle in enumerate(middles):
            boundary = (k // span + 1 - (k // span) % 2) * span * SUB
            yield min(boundary, middle), max(boundary, middle)
    yield from ((0, middle) for middle in middles)
    yield from ((middle, chunks * SUB) for middle in middles)


def local_factors(decays, lift_ref, drop_ref, rows_ref):
    local = decays.shape[1]
    logs = log_parts(decays)
    rows = lax.broadcasted_iota(jnp.int32, (local, local), 0)
    columns = lax.broadcasted_iota(jnp.int32, (local, local), 1)
    middle = (columns & -SUB) + SUB // 2
    later = (rows > middle) & (rows <= columns)
    sooner = (rows > columns) & (rows <= middle)
    offset = summed_logs(logs, later.astype(F32) - sooner.astype(F32))
    lift_ref[...] = by_token(jnp.exp(offset))
    drop_ref[...] = by_token(jnp.exp(-offset))
    lane = lax.broadcasted_iota(jnp.int32, (1, LANES), 1)
    first = last = jnp.zeros((1, LANES), jnp.int32)
    for i, (start, end) in enumerate(row_bounds(local // SUB)):
        first, last = jnp.where(lane == i, start, first), jnp.where(lane == i, end, last)
    rows = lax.broadcasted_iota(jnp.int32, (local, LANES), 0)
    decay = by_token(jnp.exp(summed_logs(logs, (rows >= first) & (rows < last))))
    rows_ref[...] = decay[: rows_ref.shape[0]]


def score_parts(b, c, ref, at, times, ahead=None):
    score = dot(b, c, NT)
    if ahead is not None:
        rows = lax.broadcasted_iota(jnp.int32, score.shape, 0)
        columns = lax.broadcasted_iota(jnp.int32, score.shape, 1)
        score = jnp.where(rows <= columns + ahead, score, 0.0)
    hi, lo = halves(score)
    width = score.shape[1]
    ref[at, :width] = hi
    ref[at, width : 2 * width] = lo
    if times == 3:
        ref[at, 2 * width :] = hi


def added_up(v):
    width = v.shape[1] // 2
    return v[:, :width] + v[:, width:]


def local_kernel(first_tile, continued, *refs):
    x_ref, dy_ref, b_ref, c_ref, decays_ref = refs[:5]
    refs = refs[5:]
    if continued:
        out_before_ref, map_before_ref = refs[:2]
        refs = refs[4:]
    part_ref, scaled_ref, out_ref, map_ref = refs[:4]
    lift_ref, drop_ref, rows_ref, full_ref, dys_ref, xs_ref, back_ref, sums_ref, even_ref, odd_ref = refs[4:14]
    level_refs = refs[14:]
    local, tile = x_ref.shape
    chunks = local // SUB
    step = pl.program_id(0)
    levels = [(span, at, level_refs[2 * i], level_refs[2 * i + 1]) for i, (span, at) in enumerate(blocks(chunks))]

    @pl.when(step == 0)
    def _():
        local_factors(decays_ref[...], lift_ref, drop_ref, rows_ref)
        sums_ref[...] = jnp.zeros(sums_ref.shape, F32)
        for k in range(0, chunks, 2):
            pair, even, odd = pl.ds(k * SUB, 2 * SUB), pl.ds(k * SUB, SUB), pl.ds((k + 1) * SUB, SUB)
            score_parts(b_ref[even, :], c_ref[even, :], even_ref, pl.ds(k // 2 * SUB, SUB), 3, 0)
            score_parts(b_ref[pair, :], c_ref[odd, :], odd_ref, pair, 3, SUB)
        for span, boundaries, mixed_ref, scores_ref in levels:
            mixed_ref[...] = jnp.zeros(mixed_ref.shape, F32)
            size = span * SUB
            for i, boundary in enumerate(boundaries):
                before, after = pl.ds((boundary - span) * SUB, size), pl.ds(boundary * SUB, size)
                score_parts(b_ref[before, :], c_ref[after, :], scores_ref, pl.ds(i * size, size), 2)

    first = (first_tile + step) * (tile // P_SIZE)
    dys_ref[...] = dy_ref[...].astype(F32) * spread(lift_ref[...], first, tile)
    back_ref[...] = spread(drop_ref[...], first, tile)
    xs_ref[...] = x_ref[...].astype(F32) * back_ref[...]
    row = spread(rows_ref[...], first, tile)
    factor = lambda kind, k: row[kind * chunks + k : kind * chunks + k + 1]

    for k in range(0, chunks, 2):
        even, odd, pair = pl.ds(k * SUB, SUB), pl.ds((k + 1) * SUB, SUB), pl.ds(k * SUB, 2 * SUB)
        dys, xs = halves(dys_ref[even, :]), halves(xs_ref[even, :])
        sums_ref[even, :] += dot(dys[0], stacked(*xs), NT)
        sums_ref[even, :SUB] += dot(dys[1], xs[0], NT)
        gained_even = dot(even_ref[pl.ds(k // 2 * SUB, SUB), :], stacked(dys[0], dys[0], dys[1]))
        joint = factor(0, k) * factor(0, k + 1)
        crossing = halves(xs_ref[even, :] * joint)
        dys, xs = halves(dys_ref[odd, :]), halves(xs_ref[odd, :])
        high = stacked(xs[0], crossing[0])
        both = dot(dys[0], stacked(high, xs[1], crossing[1]), NT)
        sums_ref[odd, :] += added_up(both) + dot(dys[1], high, NT)
        gained_odd = dot(odd_ref[pair, :], stacked(dys[0], dys[0], dys[1]))
        part_ref[even, :] = back_ref[even, :] * (gained_even + joint * gained_odd[:SUB])
        part_ref[odd, :] = back_ref[odd, :] * gained_odd[SUB:]

    for level, (span, boundaries, mixed_ref, scores_ref) in enumerate(levels, 1):
        size = span * SUB
        for i, boundary in enumerate(boundaries):
            at = pl.ds(i * size, size)
            take = lambda ref, start: halves(
                stacked(*[ref[k * SUB : (k + 1) * SUB, :] * factor(level, k) for k in range(start, start + span)])
            )
            dys, xs = take(dys_ref, boundary), take(xs_ref, boundary - span)
            both = dot(dys[0], stacked(*xs), NT)
            mixed_ref[at, :] += added_up(both) + dot(dys[1], xs[0], NT)
            gained = dot(scores_ref[at, :], stacked(dys[0], dys[0])) + dot(scores_ref[at, :size], dys[1])
            for q in range(span):
                k = boundary - span + q
                rows = pl.ds(k * SUB, SUB)
                part_ref[rows, :] += (back_ref[rows, :] * factor(level, k)) * gained[q * SUB : (q + 1) * SUB]

    for k in range(chunks):
        at = pl.ds(k * SUB, SUB)
        kind = len(levels) + 1
        scaled_ref[1, 0, at, :], scaled_ref[1, 1, at, :] = halves(dys_ref[at, :] * factor(kind, k))
        scaled_ref[0, 0, at, :], scaled_ref[0, 1, at, :] = halves(xs_ref[at, :] * factor(kind + 1, k))

    @pl.when(step == pl.num_programs(0) - 1)
    def _():
        full_ref[...] = jnp.zeros(full_ref.shape, F32)
        rows = lax.broadcasted_iota(jnp.int32, (SUB, SUB), 0)
        columns = lax.broadcasted_iota(jnp.int32, (SUB, SUB), 1)
        for k in range(0, chunks, 2):
            even, odd = pl.ds(k * SUB, SUB), pl.ds((k + 1) * SUB, SUB)
            full_ref[even, k * SUB : (k + 1) * SUB] = jnp.where(rows >= columns, added_up(sums_ref[even, :]), 0.0)
            full_ref[odd, (k + 1) * SUB : (k + 2) * SUB] = jnp.where(rows >= columns, sums_ref[odd, :SUB], 0.0)
            full_ref[odd, k * SUB : (k + 1) * SUB] = sums_ref[odd, SUB:]
        for span, boundaries, mixed_ref, _ in levels:
            size = span * SUB
            for i, boundary in enumerate(boundaries):
                block = mixed_ref[pl.ds(i * size, size), :]
                full_ref[pl.ds(boundary * SUB, size), (boundary - span) * SUB : boundary * SUB] = block
        map_ref[...] = map_before_ref[...] if continued else jnp.zeros(map_ref.shape, F32)
        for k in range(0, local, LANES):
            at = pl.ds(k, LANES)
            mixed = full_ref[at, :]
            gained = dot21(halves(mixed), b_ref[...])
            out_ref[at, :] = out_before_ref[at, :] + gained if continued else gained
            map_ref[...] += dot21(halves(mixed.T), c_ref[at, :])


def local_part(first_tile, count, x, dy, b, c, decays, before=None):
    local, width = x.shape
    chunks = local // SUB
    whole = lambda a: pl.BlockSpec(a.shape, lambda j: (0, 0))
    column = pl.BlockSpec((local, TILE), lambda j: (0, first_tile + j))
    tokens = pl.BlockSpec((local, N), lambda j: (0, 0))
    scratch = [
        pltpu.VMEM((local, LANES), F32),
        pltpu.VMEM((local, LANES), F32),
        pltpu.VMEM((-(-len(list(row_bounds(chunks))) // 8) * 8, LANES), F32),
        pltpu.VMEM((local, local), F32),
        pltpu.VMEM((local, TILE), F32),
        pltpu.VMEM((local, TILE), F32),
        pltpu.VMEM((local, TILE), F32),
        pltpu.VMEM((local, 2 * SUB), F32),
        pltpu.VMEM((local // 2, 3 * SUB), BF16),
        pltpu.VMEM((local, 3 * SUB), BF16),
    ]
    for span, _ in blocks(chunks):
        scratch.append(pltpu.VMEM((local // 2, span * SUB), F32))
        scratch.append(pltpu.VMEM((local // 2, 2 * span * SUB), BF16))
    in_specs = [column, column, whole(b), whole(c), whole(decays)]
    args, aliases = [x, dy, b, c, decays], {}
    if before is not None:
        part, scaled, out_part, map_part = before
        in_specs += [tokens, tokens, pl.BlockSpec(memory_space=pl.ANY), pl.BlockSpec(memory_space=pl.ANY)]
        args += [out_part, map_part, part, scaled]
        aliases = {7: 0, 8: 1}
    return pl.pallas_call(
        functools.partial(local_kernel, first_tile, before is not None),
        grid=(count,),
        in_specs=in_specs,
        out_specs=(column, pl.BlockSpec((2, 2, local, TILE), lambda j: (0, 0, 0, first_tile + j)), tokens, tokens),
        out_shape=(
            jax.ShapeDtypeStruct((local, width), F32),
            jax.ShapeDtypeStruct((2, 2, local, width), BF16),
            jax.ShapeDtypeStruct((local, N), F32),
            jax.ShapeDtypeStruct((local, N), F32),
        ),
        scratch_shapes=scratch,
        input_output_aliases=aliases,
        compiler_params=PARAMS,
        name="local_part",
        cost_estimate=pl.CostEstimate(
            flops=40 * local * N * TILE * count, bytes_accessed=8 * local * TILE * count, transcendentals=0
        ),
    )(*args)


def map_kernel(count, ranks, scaled_ref, carry_ref, out_before_ref, map_before_ref, *refs):
    messages, (out_ref, map_ref) = refs[:-2], refs[-2:]
    step = pl.program_id(0)

    @pl.when(step == 0)
    def _():
        out_ref[...] = out_before_ref[...]
        map_ref[...] = map_before_ref[...]

    for i, sum_ref in enumerate((map_ref, out_ref)):
        carry = halves(carry_ref[1 - i])
        both = dot(scaled_ref[i, 0], stacked(*carry), NT)
        sum_ref[...] += both[:, :N] + (both[:, N:] + dot(scaled_ref[i, 1], carry[0], NT))

    if messages:

        @pl.when(step == count - 1)
        def _():
            rows = messages[0].shape[1]
            for r, message in enumerate(messages):
                at = pl.ds(pl.multiple_of(((lax.axis_index("head") + r) % ranks) * rows, rows), rows)
                message[0] = out_ref[at, :]
                message[1] = map_ref[at, :]


def map_terms(half, scaled, carry, out_before, map_before, ranks=0):
    local, width = scaled.shape[2], carry.shape[2]
    tile = min(512, width)
    count = width // tile
    whole = lambda a: pl.BlockSpec(a.shape, lambda j: (0,) * len(a.shape))
    tokens = jax.ShapeDtypeStruct((local, N), F32)
    if ranks:
        out_shape = [jax.ShapeDtypeStruct((2, local // ranks, N), F32)] * ranks
        scratch = [pltpu.VMEM((local, N), F32), pltpu.VMEM((local, N), F32)]
    else:
        out_shape, scratch = [tokens, tokens], []
    return pl.pallas_call(
        functools.partial(map_kernel, count, ranks),
        grid=(count,),
        in_specs=[
            pl.BlockSpec((2, 2, local, tile), lambda j: (0, 0, 0, place(half) * count + j)),
            pl.BlockSpec((2, N, tile), lambda j: (0, 0, j)),
            whole(tokens),
            whole(tokens),
        ],
        out_specs=[whole(shape) for shape in out_shape],
        scratch_shapes=scratch,
        out_shape=out_shape,
        compiler_params=PARAMS,
        name="map_terms",
        cost_estimate=pl.CostEstimate(flops=12 * local * N * width, bytes_accessed=8 * local * width, transcendentals=0),
    )(scaled, carry, out_before, map_before)


def input_kernel(heads, count, part_ref, suf_ref, b_ref, own_ref, other_ref, input_ref):
    tile = part_ref.shape[1]
    step = pl.program_id(0)
    after = dot(suf_ref[...], spread_table(heads, step * (tile // P_SIZE), tile))
    grad = jnp.where(step // count == place(CORE), own_ref[0], other_ref[0])
    input_ref[...] = (part_ref[...] + after * dot12(b_ref[...], halves(grad))).astype(BF16)


def input_terms(part, factors, b, own, other):
    local, width = part.shape
    count = width // 2 // TILE
    whole = lambda a: pl.BlockSpec(a.shape, lambda j: (0, 0))
    column = pl.BlockSpec((local, TILE), lambda j: (0, j))
    carry = pl.BlockSpec((1, N, TILE), lambda j: (1, 0, j % count))
    return pl.pallas_call(
        functools.partial(input_kernel, width // P_SIZE, count),
        grid=(2 * count,),
        in_specs=[column, pl.BlockSpec((local, LANES), lambda j: (0, 1)), whole(b), carry, carry],
        out_specs=column,
        out_shape=jax.ShapeDtypeStruct((local, width), BF16),
        compiler_params=PARAMS,
        name="input_terms",
        cost_estimate=pl.CostEstimate(flops=4 * local * N * width, bytes_accessed=8 * local * width, transcendentals=0),
    )(part, factors, b, own, other)


def swap_cores(v, length):
    return lax.ppermute(v, "seq", [(i, i ^ 1) for i in range(length)])


def turned(v, axis, length, by):
    return lax.ppermute(v, axis, [(i, (i + by) % length) for i in range(length)])


def per_device(mixer_input, output_grad, input_map, output_map, decays):
    length, ranks = lax.axis_size("seq"), lax.axis_size("head")
    chips = length // 2
    args = mixer_input, output_grad, input_map, output_map
    sent, factors = totals(OTHER, *args, decays=decays)
    recv = swap_cores(sent, length)
    (mine,) = totals(CORE, *args, factors=factors)
    tiles = mixer_input.shape[1] // TILE
    if chips == 4:
        ahead = tiles * 3 // 4
        own, back, *others = first_phase(length, mine, recv)
        result = local_part(0, ahead, *args, decays)
        others, result = lax.optimization_barrier((others, result))
        cross, same = second_phase(own, back, *others)
        others += [crossed(cross, length, 4), crossed(same, length, 2)]
        result, _, _ = lax.optimization_barrier((result, cross, same))
        result = local_part(ahead, tiles - ahead, *args, decays, result)
        others, result = lax.optimization_barrier((others, result))
        own, peer = carried4(mine, recv, *others)
    else:
        messages = chip_totals(chips, mine, recv)
        others = [turned(message, "seq", length, 2 * r) for r, message in enumerate(messages, 1)]
        result = local_part(0, tiles, *args, decays)
        own, peer = carried(chips, mine, recv, others)
    part, scaled, out_part, map_part = result
    other = swap_cores(peer, length)
    out_part, map_part = map_terms(CORE, scaled, own, out_part, map_part)
    shares = map_terms(OTHER, scaled, other, out_part, map_part, ranks)
    total = shares[0]
    own, other, shares = lax.optimization_barrier((own, other, shares))
    for r in range(1, ranks):
        total = total + turned(shares[r], "head", ranks, r)
    input_grad = input_terms(part, factors, input_map, own, other)
    return input_grad, total[1], total[0]


def solution(mesh):
    in_specs = (
        P("seq", "head"),
        P("seq", "head"),
        P("seq", None),
        P("seq", None),
        P("head", "seq"),
    )
    out_specs = (P("seq", "head"), P(("seq", "head"), None), P(("seq", "head"), None))
    return jax.shard_map(
        per_device, mesh=mesh, in_specs=in_specs, out_specs=out_specs, check_vma=False
    )
```

```python
import functools

import jax
import jax.numpy as jnp
from jax import lax
from jax.experimental import pallas as pl
from jax.experimental.pallas import tpu as pltpu
from jax.sharding import PartitionSpec as P

P_SIZE = 64
N = 128
SUB = 64
TILE = 256
WIDE = 512
EXTRA = 8
PARTS = 4
LANES = 128
CORE, OTHER = range(2)
PARAMS = pltpu.CompilerParams(vmem_limit_bytes=24 * 1024 * 1024)
FIRST = pltpu.CompilerParams(vmem_limit_bytes=52 * 1024 * 1024)
F32 = jnp.float32
BF16 = jnp.bfloat16

NN = (((1,), (0,)), ((), ()))
NT = (((1,), (1,)), ((), ()))


def dot(a, b, dims=NN):
    return lax.dot_general(a, b, dims, preferred_element_type=F32)


def halves(v):
    hi = v.astype(BF16)
    return hi, (v - hi.astype(F32)).astype(BF16)


def dot21(pair, b, dims=NN):
    return dot(pair[0], b, dims) + dot(pair[1], b, dims)


def dot12(a, pair, dims=NN):
    return dot(a, pair[0], dims) + dot(a, pair[1], dims)


def dot22(p, q, dims=NN):
    return dot(p[0], q[0], dims) + (dot(p[0], q[1], dims) + dot(p[1], q[0], dims))


def thirds(v):
    hi = v.astype(BF16)
    rest = v - hi.astype(F32)
    mid = rest.astype(BF16)
    return hi, mid, (rest - mid.astype(F32)).astype(BF16)


def spread(by_head, first, width):
    lanes = lax.broadcasted_iota(jnp.int32, by_head.shape, 1)
    step = LANES // P_SIZE
    shift = P_SIZE.bit_length() - 1
    taken = [
        jnp.take_along_axis(by_head, first + step * k + (lanes >> shift), axis=1) for k in range(width // LANES)
    ]
    return jnp.concatenate(taken, axis=1)


def place(half):
    core = lax.axis_index("seq") % 2
    return core if half == CORE else 1 - core


def stacked(*parts):
    return jnp.concatenate(parts, axis=0)


def transposed(v):
    return v.astype(F32).T.astype(BF16)


def log_parts(decays):
    return jnp.concatenate([part.astype(F32) for part in thirds(jnp.log(decays))], axis=0).astype(BF16)


def summed_logs(logs, table):
    heads = logs.shape[0] // 3
    sums = dot(logs, table.astype(F32).astype(BF16))
    return sums[:heads] + (sums[heads : 2 * heads] + sums[2 * heads :])


def by_token(v):
    rest = jnp.zeros((LANES - v.shape[0], v.shape[1]), F32)
    return jnp.concatenate([v, rest], axis=0).T


def packed(v):
    parts = [part.astype(F32) for part in thirds(v)]
    rest = jnp.zeros((LANES - 3 * v.shape[0], v.shape[1]), F32)
    return jnp.concatenate(parts + [rest], axis=0).T.astype(BF16)


def spread_table(heads, first, width):
    rows = lax.broadcasted_iota(jnp.int32, (heads, width), 0)
    columns = lax.broadcasted_iota(jnp.int32, (heads, width), 1)
    offset = columns - (rows - first) * P_SIZE
    picked = ((offset >= 0) & (offset < P_SIZE)).astype(F32)
    rest = jnp.zeros((LANES - 3 * heads, width), F32)
    return jnp.concatenate([picked, picked, picked, rest], axis=0).astype(BF16)


def device_factors(decays, ref):
    local = decays.shape[1]
    logs = log_parts(decays)
    rows = lax.broadcasted_iota(jnp.int32, (local, local), 0)
    columns = lax.broadcasted_iota(jnp.int32, (local, local), 1)
    ref[:, :LANES] = packed(jnp.exp(summed_logs(logs, rows <= columns)))
    ref[:, LANES:] = packed(jnp.exp(summed_logs(logs, rows > columns)))


def totals_kernel(heads, count, half, made, *refs):
    x_refs, dy_refs, (b_ref, c_ref) = refs[:PARTS], refs[PARTS : 2 * PARTS], refs[2 * PARTS : 2 * PARTS + 2]
    refs = refs[2 * PARTS + 2 :]
    if made:
        factor_ref, out_ref, bt_ref, ct_ref = refs
    else:
        decays_ref, out_ref, factor_ref, bt_ref, ct_ref = refs
    step = pl.program_id(0)

    @pl.when(step == 0)
    def _():
        bt_ref[...] = transposed(b_ref[...])
        ct_ref[...] = transposed(c_ref[...])
        if not made:
            device_factors(decays_ref[...], factor_ref)

    tile = x_refs[0].shape[1]
    table = spread_table(heads, (place(half) * count + step) * (tile // P_SIZE), tile)
    before = dot(factor_ref[:, :LANES], table)
    after = dot(factor_ref[:, LANES:], table)
    ended = before[before.shape[0] - 1 :, :]
    for i, (sources, factor, other) in enumerate(((x_refs, after, bt_ref), (dy_refs, before, ct_ref))):
        source = stacked(*[ref[...].astype(F32) for ref in sources])
        out_ref[i, :N, :] = dot12(other[...], halves(source * factor))
        out_ref[i, N:, :] = jnp.broadcast_to(ended, (EXTRA, tile))


def totals(half, x, dy, b, c, decays=None, factors=None):
    local, width = x.shape
    count = width // 2 // TILE
    whole = lambda a: pl.BlockSpec(a.shape, lambda j: (0, 0))
    columns = [
        pl.BlockSpec((local // PARTS, TILE), functools.partial(lambda part, j: (part, place(half) * count + j), part))
        for part in range(PARTS)
    ]
    factor = jax.ShapeDtypeStruct((local, 2 * LANES), BF16)
    made = factors is not None
    last = factors if made else decays
    out_specs = [pl.BlockSpec((2, N + EXTRA, TILE), lambda j: (0, 0, j))]
    out_shape = [jax.ShapeDtypeStruct((2, N + EXTRA, width // 2), F32)]
    if not made:
        out_specs.append(whole(factor))
        out_shape.append(factor)
    return pl.pallas_call(
        functools.partial(totals_kernel, width // P_SIZE, count, half, made),
        grid=(count,),
        in_specs=columns + columns + [whole(b), whole(c), whole(last)],
        out_specs=out_specs,
        scratch_shapes=[pltpu.VMEM((N, local), BF16), pltpu.VMEM((N, local), BF16)],
        out_shape=out_shape,
        compiler_params=PARAMS if made else FIRST,
        name="state_totals",
        cost_estimate=pl.CostEstimate(flops=8 * local * N * width // 2, bytes_accessed=4 * local * width, transcendentals=0),
    )(*[x] * PARTS, *[dy] * PARTS, b, c, last)


def ordered(core, mine, recv):
    return jnp.where(core == 0, mine, recv), jnp.where(core == 0, recv, mine)


def chip_kernel(chips, mine_ref, recv_ref, *out_refs):
    core, chip = place(CORE), lax.axis_index("seq") // 2
    early, late = ordered(core, mine_ref[0], recv_ref[0])
    early_decay, late_decay = early[N : N + 1], late[N : N + 1]
    both = jnp.broadcast_to(early_decay * late_decay, (EXTRA, early.shape[1]))
    state = late_decay * early[:N] + late[:N]
    early, late = ordered(core, mine_ref[1], recv_ref[1])
    grad = early[:N] + early_decay * late[:N]
    for r, out_ref in enumerate(out_refs, 1):
        out_ref[:N, :] = jnp.where(chip + r < chips, state, grad)
        out_ref[N:, :] = both


def chip_totals(chips, mine, recv):
    width = mine.shape[2]
    tile = min(512, width)
    block = pl.BlockSpec((2, N + EXTRA, tile), lambda j: (0, 0, j))
    out = pl.BlockSpec((N + EXTRA, tile), lambda j: (0, j))
    shape = jax.ShapeDtypeStruct((N + EXTRA, width), F32)
    return pl.pallas_call(
        functools.partial(chip_kernel, chips),
        grid=(width // tile,),
        in_specs=[block, block],
        out_specs=[out] * (chips - 1),
        out_shape=[shape] * (chips - 1),
        compiler_params=PARAMS,
        name="chip_totals",
        cost_estimate=pl.CostEstimate(flops=6 * N * width, bytes_accessed=24 * N * width, transcendentals=0),
    )(mine, recv)


def sides():
    chip = lax.axis_index("seq") // 2
    return chip < 2, (chip == 1) | (chip == 2)


def first_kernel(mine_ref, recv_ref, same_ref, cross_ref, back_ref, decay_ref):
    left, inner = sides()
    core = place(CORE)
    width = mine_ref.shape[2] // 2
    early, late = ordered(core, mine_ref[0], recv_ref[0])
    early_decay, late_decay = early[N : N + 1], late[N : N + 1]
    state = late_decay * early[:N] + late[:N]
    decay = early_decay * late_decay
    early, late = ordered(core, mine_ref[1], recv_ref[1])
    grad = early[:N] + early_decay * late[:N]
    out, back = jnp.where(left, state, grad), jnp.where(left, grad, state)
    same_ref[:N, :] = out[:, :width]
    same_ref[N : 2 * N, :] = jnp.where(inner, back[:, :width], out[:, width:])
    rows = lax.broadcasted_iota(jnp.int32, (EXTRA, width), 0)
    same_ref[2 * N :, :] = jnp.where(rows == 0, decay[:, :width], decay[:, width:])
    cross_ref[...] = out[:, width:]
    back_ref[...] = back[:, width:]
    decay_ref[...] = jnp.broadcast_to(decay[:, width:], (EXTRA, width))


def second_kernel(own_ref, back_ref, same_ref, cross_ref, decay_ref, cross2_ref, same2_ref):
    _, inner = sides()
    own, other = own_ref[:N, :], same_ref[:N, :]
    own_decay, other_decay = own_ref[2 * N : 2 * N + 1, :], same_ref[2 * N : 2 * N + 1, :]
    cross2_ref[...] = jnp.where(inner, own + own_decay * other, other + other_decay * own)
    weight = own_ref[2 * N + 1 : 2 * N + 2, :] * decay_ref[:1, :]
    same2_ref[...] = jnp.where(inner, back_ref[...] + weight * cross_ref[...], cross_ref[...])


def plain_call(kernel, name, out_shape, *args):
    whole = lambda a: pl.BlockSpec(a.shape, lambda j: (0,) * len(a.shape))
    size = sum(a.size for a in args)
    return pl.pallas_call(
        kernel,
        grid=(1,),
        in_specs=[whole(a) for a in args],
        out_specs=[whole(a) for a in out_shape],
        out_shape=out_shape,
        compiler_params=PARAMS,
        name=name,
        cost_estimate=pl.CostEstimate(flops=8 * size, bytes_accessed=4 * size, transcendentals=0),
    )(*args)


def crossed(v, length, bit):
    return lax.ppermute(v, "seq", [(i, i ^ bit) for i in range(length)])


def first_phase(length, mine, recv):
    half = mine.shape[2] // 2
    shapes = [jax.ShapeDtypeStruct((rows, half), F32) for rows in (2 * N + EXTRA, N, N, EXTRA)]
    own, cross, back, decay = plain_call(first_kernel, "first_messages", shapes, mine, recv)
    return own, back, crossed(own, length, 2), crossed(cross, length, 4), crossed(decay, length, 6)


def second_phase(own, back, same, cross, decay):
    shape = jax.ShapeDtypeStruct(back.shape, F32)
    return plain_call(second_kernel, "second_messages", [shape, shape], own, back, same, cross, decay)


def carried4_kernel(mine_ref, recv_ref, same_ref, cross_ref, decay_ref, cross2_ref, same2_ref, own_ref, peer_ref):
    left, inner = sides()
    width = cross_ref.shape[1]
    decay_a, decay_b = same_ref[2 * N : 2 * N + 1, :], same_ref[2 * N + 1 : 2 * N + 2, :]
    for part in range(2):
        at = slice(part * width, (part + 1) * width)
        out = jnp.where(inner, same_ref[part * N : (part + 1) * N, :], 0.0)
        if part == 0:
            back = jnp.where(inner, cross2_ref[...], same_ref[N : 2 * N, :] + decay_a * cross2_ref[...])
        else:
            back = same2_ref[...] + jnp.where(inner, decay_ref[:1, :], decay_b) * cross_ref[...]
        carried_cores(
            place(CORE), jnp.where(left, out, back), jnp.where(left, back, out), mine_ref, recv_ref, own_ref, peer_ref, at
        )


def carried4(mine, recv, *others):
    shape = jax.ShapeDtypeStruct((2, N, mine.shape[2]), F32)
    return plain_call(carried4_kernel, "carried_in", [shape, shape], mine, recv, *others)


def carried_cores(core, state, grad, mine_ref, recv_ref, own_ref, peer_ref, at):
    early, late = ordered(core, mine_ref[0, :, at], recv_ref[0, :, at])
    at_late = early[N : N + 1] * state + early[:N]
    own_ref[0, :, at] = jnp.where(core == 0, state, at_late)
    peer_ref[0, :, at] = jnp.where(core == 0, at_late, state)
    early, late = ordered(core, mine_ref[1, :, at], recv_ref[1, :, at])
    at_early = late[:N] + late[N : N + 1] * grad
    own_ref[1, :, at] = jnp.where(core == 0, at_early, grad)
    peer_ref[1, :, at] = jnp.where(core == 0, grad, at_early)


def carried_kernel(chips, mine_ref, recv_ref, *refs):
    others, (own_ref, peer_ref) = refs[:-2], refs[-2:]
    core, chip = place(CORE), lax.axis_index("seq") // 2
    state = grad = jnp.zeros((N, own_ref.shape[2]), F32)
    state_weight = grad_weight = jnp.ones((1, own_ref.shape[2]), F32)
    for r, ref in enumerate(others, 1):
        earlier = chip >= r
        state = jnp.where(earlier, state + state_weight * ref[:N, :], state)
        state_weight = state_weight * ref[N : N + 1, :]
    for r in range(1, chips):
        later = chip + r < chips
        ref = others[chips - r - 1]
        grad = jnp.where(later, grad + grad_weight * ref[:N, :], grad)
        grad_weight = grad_weight * ref[N : N + 1, :]
    carried_cores(core, state, grad, mine_ref, recv_ref, own_ref, peer_ref, slice(None))


def carried(chips, mine, recv, others):
    width = mine.shape[2]
    tile = min(512, width)
    pair = pl.BlockSpec((2, N + EXTRA, tile), lambda j: (0, 0, j))
    other = pl.BlockSpec((N + EXTRA, tile), lambda j: (0, j))
    out = pl.BlockSpec((2, N, tile), lambda j: (0, 0, j))
    shape = jax.ShapeDtypeStruct((2, N, width), F32)
    return pl.pallas_call(
        functools.partial(carried_kernel, chips),
        grid=(width // tile,),
        in_specs=[pair, pair] + [other] * len(others),
        out_specs=(out, out),
        out_shape=(shape, shape),
        compiler_params=PARAMS,
        name="carried_in",
        cost_estimate=pl.CostEstimate(flops=20 * N * width, bytes_accessed=44 * N * width, transcendentals=0),
    )(mine, recv, *others)


def blocks(chunks):
    span = 2
    while span < chunks:
        yield span, [at for at in range(span, chunks, 2 * span)]
        span *= 2


def row_bounds(chunks):
    middles = [k * SUB + SUB // 2 + 1 for k in range(chunks)]
    for span in [1] + [span for span, _ in blocks(chunks)]:
        for k, middle in enumerate(middles):
            boundary = (k // span + 1 - (k // span) % 2) * span * SUB
            yield min(boundary, middle), max(boundary, middle)
    yield from ((0, middle) for middle in middles)
    yield from ((middle, chunks * SUB) for middle in middles)


def local_factors(decays, lift_ref, drop_ref, rows_ref):
    local = decays.shape[1]
    logs = log_parts(decays)
    rows = lax.broadcasted_iota(jnp.int32, (local, local), 0)
    columns = lax.broadcasted_iota(jnp.int32, (local, local), 1)
    middle = (columns & -SUB) + SUB // 2
    later = (rows > middle) & (rows <= columns)
    sooner = (rows > columns) & (rows <= middle)
    offset = summed_logs(logs, later.astype(F32) - sooner.astype(F32))
    lift_ref[...] = by_token(jnp.exp(offset))
    drop_ref[...] = by_token(jnp.exp(-offset))
    lane = lax.broadcasted_iota(jnp.int32, (1, LANES), 1)
    first = last = jnp.zeros((1, LANES), jnp.int32)
    for i, (start, end) in enumerate(row_bounds(local // SUB)):
        first, last = jnp.where(lane == i, start, first), jnp.where(lane == i, end, last)
    rows = lax.broadcasted_iota(jnp.int32, (local, LANES), 0)
    decay = by_token(jnp.exp(summed_logs(logs, (rows >= first) & (rows < last))))
    rows_ref[...] = decay[: rows_ref.shape[0]]


def score_parts(b, c, ref, at, times, ahead=None):
    score = dot(b, c, NT)
    if ahead is not None:
        rows = lax.broadcasted_iota(jnp.int32, score.shape, 0)
        columns = lax.broadcasted_iota(jnp.int32, score.shape, 1)
        score = jnp.where(rows <= columns + ahead, score, 0.0)
    hi, lo = halves(score)
    width = score.shape[1]
    ref[at, :width] = hi
    ref[at, width : 2 * width] = lo
    if times == 3:
        ref[at, 2 * width :] = hi


def added_up(v):
    width = v.shape[1] // 2
    return v[:, :width] + v[:, width:]


def local_kernel(first_tile, continued, *refs):
    x_ref, dy_ref, b_ref, c_ref, decays_ref = refs[:5]
    refs = refs[5:]
    if continued:
        out_before_ref, map_before_ref = refs[:2]
        refs = refs[4:]
    part_ref, scaled_ref, out_ref, map_ref = refs[:4]
    lift_ref, drop_ref, rows_ref, full_ref, dys_ref, xs_ref, back_ref, sums_ref, even_ref, odd_ref = refs[4:14]
    level_refs = refs[14:]
    local, tile = x_ref.shape
    chunks = local // SUB
    step = pl.program_id(0)
    levels = [(span, at, level_refs[2 * i], level_refs[2 * i + 1]) for i, (span, at) in enumerate(blocks(chunks))]

    @pl.when(step == 0)
    def _():
        local_factors(decays_ref[...], lift_ref, drop_ref, rows_ref)
        sums_ref[...] = jnp.zeros(sums_ref.shape, F32)
        for k in range(0, chunks, 2):
            pair, even, odd = pl.ds(k * SUB, 2 * SUB), pl.ds(k * SUB, SUB), pl.ds((k + 1) * SUB, SUB)
            score_parts(b_ref[even, :], c_ref[even, :], even_ref, pl.ds(k // 2 * SUB, SUB), 3, 0)
            score_parts(b_ref[pair, :], c_ref[odd, :], odd_ref, pair, 3, SUB)
        for span, boundaries, mixed_ref, scores_ref in levels:
            mixed_ref[...] = jnp.zeros(mixed_ref.shape, F32)
            size = span * SUB
            for i, boundary in enumerate(boundaries):
                before, after = pl.ds((boundary - span) * SUB, size), pl.ds(boundary * SUB, size)
                score_parts(b_ref[before, :], c_ref[after, :], scores_ref, pl.ds(i * size, size), 2)

    first = (first_tile + step) * (tile // P_SIZE)
    dys_ref[...] = dy_ref[...].astype(F32) * spread(lift_ref[...], first, tile)
    back_ref[...] = spread(drop_ref[...], first, tile)
    xs_ref[...] = x_ref[...].astype(F32) * back_ref[...]
    row = spread(rows_ref[...], first, tile)
    factor = lambda kind, k: row[kind * chunks + k : kind * chunks + k + 1]

    for k in range(0, chunks, 2):
        even, odd, pair = pl.ds(k * SUB, SUB), pl.ds((k + 1) * SUB, SUB), pl.ds(k * SUB, 2 * SUB)
        dys, xs = halves(dys_ref[even, :]), halves(xs_ref[even, :])
        sums_ref[even, :] += dot(dys[0], stacked(*xs), NT)
        sums_ref[even, :SUB] += dot(dys[1], xs[0], NT)
        gained_even = dot(even_ref[pl.ds(k // 2 * SUB, SUB), :], stacked(dys[0], dys[0], dys[1]))
        joint = factor(0, k) * factor(0, k + 1)
        crossing = halves(xs_ref[even, :] * joint)
        dys, xs = halves(dys_ref[odd, :]), halves(xs_ref[odd, :])
        high = stacked(xs[0], crossing[0])
        both = dot(dys[0], stacked(high, xs[1], crossing[1]), NT)
        sums_ref[odd, :] += added_up(both) + dot(dys[1], high, NT)
        gained_odd = dot(odd_ref[pair, :], stacked(dys[0], dys[0], dys[1]))
        part_ref[even, :] = back_ref[even, :] * (gained_even + joint * gained_odd[:SUB])
        part_ref[odd, :] = back_ref[odd, :] * gained_odd[SUB:]

    for level, (span, boundaries, mixed_ref, scores_ref) in enumerate(levels, 1):
        size = span * SUB
        for i, boundary in enumerate(boundaries):
            at = pl.ds(i * size, size)
            take = lambda ref, start: halves(
                stacked(*[ref[k * SUB : (k + 1) * SUB, :] * factor(level, k) for k in range(start, start + span)])
            )
            dys, xs = take(dys_ref, boundary), take(xs_ref, boundary - span)
            both = dot(dys[0], stacked(*xs), NT)
            mixed_ref[at, :] += added_up(both) + dot(dys[1], xs[0], NT)
            gained = dot(scores_ref[at, :], stacked(dys[0], dys[0])) + dot(scores_ref[at, :size], dys[1])
            for q in range(span):
                k = boundary - span + q
                rows = pl.ds(k * SUB, SUB)
                part_ref[rows, :] += (back_ref[rows, :] * factor(level, k)) * gained[q * SUB : (q + 1) * SUB]

    for k in range(chunks):
        at = pl.ds(k * SUB, SUB)
        kind = len(levels) + 1
        scaled_ref[1, 0, at, :], scaled_ref[1, 1, at, :] = halves(dys_ref[at, :] * factor(kind, k))
        scaled_ref[0, 0, at, :], scaled_ref[0, 1, at, :] = halves(xs_ref[at, :] * factor(kind + 1, k))

    @pl.when(step == pl.num_programs(0) - 1)
    def _():
        full_ref[...] = jnp.zeros(full_ref.shape, F32)
        rows = lax.broadcasted_iota(jnp.int32, (SUB, SUB), 0)
        columns = lax.broadcasted_iota(jnp.int32, (SUB, SUB), 1)
        for k in range(0, chunks, 2):
            even, odd = pl.ds(k * SUB, SUB), pl.ds((k + 1) * SUB, SUB)
            full_ref[even, k * SUB : (k + 1) * SUB] = jnp.where(rows >= columns, added_up(sums_ref[even, :]), 0.0)
            full_ref[odd, (k + 1) * SUB : (k + 2) * SUB] = jnp.where(rows >= columns, sums_ref[odd, :SUB], 0.0)
            full_ref[odd, k * SUB : (k + 1) * SUB] = sums_ref[odd, SUB:]
        for span, boundaries, mixed_ref, _ in levels:
            size = span * SUB
            for i, boundary in enumerate(boundaries):
                block = mixed_ref[pl.ds(i * size, size), :]
                full_ref[pl.ds(boundary * SUB, size), (boundary - span) * SUB : boundary * SUB] = block
        map_ref[...] = map_before_ref[...] if continued else jnp.zeros(map_ref.shape, F32)
        for k in range(0, local, LANES):
            at = pl.ds(k, LANES)
            mixed = full_ref[at, :]
            gained = dot21(halves(mixed), b_ref[...])
            out_ref[at, :] = out_before_ref[at, :] + gained if continued else gained
            map_ref[...] += dot21(halves(mixed.T), c_ref[at, :])


def local_part(first_tile, count, x, dy, b, c, decays, before=None):
    local, width = x.shape
    chunks = local // SUB
    whole = lambda a: pl.BlockSpec(a.shape, lambda j: (0, 0))
    column = pl.BlockSpec((local, WIDE), lambda j: (0, first_tile + j))
    tokens = pl.BlockSpec((local, N), lambda j: (0, 0))
    scratch = [
        pltpu.VMEM((local, LANES), F32),
        pltpu.VMEM((local, LANES), F32),
        pltpu.VMEM((-(-len(list(row_bounds(chunks))) // 8) * 8, LANES), F32),
        pltpu.VMEM((local, local), F32),
        pltpu.VMEM((local, WIDE), F32),
        pltpu.VMEM((local, WIDE), F32),
        pltpu.VMEM((local, WIDE), F32),
        pltpu.VMEM((local, 2 * SUB), F32),
        pltpu.VMEM((local // 2, 3 * SUB), BF16),
        pltpu.VMEM((local, 3 * SUB), BF16),
    ]
    for span, _ in blocks(chunks):
        scratch.append(pltpu.VMEM((local // 2, span * SUB), F32))
        scratch.append(pltpu.VMEM((local // 2, 2 * span * SUB), BF16))
    in_specs = [column, column, whole(b), whole(c), whole(decays)]
    args, aliases = [x, dy, b, c, decays], {}
    if before is not None:
        part, scaled, out_part, map_part = before
        in_specs += [tokens, tokens, pl.BlockSpec(memory_space=pl.ANY), pl.BlockSpec(memory_space=pl.ANY)]
        args += [out_part, map_part, part, scaled]
        aliases = {7: 0, 8: 1}
    return pl.pallas_call(
        functools.partial(local_kernel, first_tile, before is not None),
        grid=(count,),
        in_specs=in_specs,
        out_specs=(column, pl.BlockSpec((2, 2, local, WIDE), lambda j: (0, 0, 0, first_tile + j)), tokens, tokens),
        out_shape=(
            jax.ShapeDtypeStruct((local, width), F32),
            jax.ShapeDtypeStruct((2, 2, local, width), BF16),
            jax.ShapeDtypeStruct((local, N), F32),
            jax.ShapeDtypeStruct((local, N), F32),
        ),
        scratch_shapes=scratch,
        input_output_aliases=aliases,
        compiler_params=PARAMS,
        name="local_part",
        cost_estimate=pl.CostEstimate(
            flops=40 * local * N * WIDE * count, bytes_accessed=8 * local * WIDE * count, transcendentals=0
        ),
    )(*args)


def map_kernel(count, ranks, scaled_ref, carry_ref, out_before_ref, map_before_ref, *refs):
    messages, (out_ref, map_ref) = refs[:-2], refs[-2:]
    step = pl.program_id(0)

    @pl.when(step == 0)
    def _():
        out_ref[...] = out_before_ref[...]
        map_ref[...] = map_before_ref[...]

    for i, sum_ref in enumerate((map_ref, out_ref)):
        carry = halves(carry_ref[1 - i])
        both = dot(scaled_ref[i, 0], stacked(*carry), NT)
        sum_ref[...] += both[:, :N] + (both[:, N:] + dot(scaled_ref[i, 1], carry[0], NT))

    if messages:

        @pl.when(step == count - 1)
        def _():
            rows = messages[0].shape[1]
            for r, message in enumerate(messages):
                at = pl.ds(pl.multiple_of(((lax.axis_index("head") + r) % ranks) * rows, rows), rows)
                message[0] = out_ref[at, :]
                message[1] = map_ref[at, :]


def map_terms(half, scaled, carry, out_before, map_before, ranks=0):
    local, width = scaled.shape[2], carry.shape[2]
    tile = min(WIDE, width)
    count = width // tile
    whole = lambda a: pl.BlockSpec(a.shape, lambda j: (0,) * len(a.shape))
    tokens = jax.ShapeDtypeStruct((local, N), F32)
    if ranks:
        out_shape = [jax.ShapeDtypeStruct((2, local // ranks, N), F32)] * ranks
        scratch = [pltpu.VMEM((local, N), F32), pltpu.VMEM((local, N), F32)]
    else:
        out_shape, scratch = [tokens, tokens], []
    return pl.pallas_call(
        functools.partial(map_kernel, count, ranks),
        grid=(count,),
        in_specs=[
            pl.BlockSpec((2, 2, local, tile), lambda j: (0, 0, 0, place(half) * count + j)),
            pl.BlockSpec((2, N, tile), lambda j: (0, 0, j)),
            whole(tokens),
            whole(tokens),
        ],
        out_specs=[whole(shape) for shape in out_shape],
        scratch_shapes=scratch,
        out_shape=out_shape,
        compiler_params=PARAMS,
        name="map_terms",
        cost_estimate=pl.CostEstimate(flops=12 * local * N * width, bytes_accessed=8 * local * width, transcendentals=0),
    )(scaled, carry, out_before, map_before)


def input_kernel(heads, count, part_ref, suf_ref, b_ref, own_ref, other_ref, input_ref):
    tile = part_ref.shape[1]
    step = pl.program_id(0)
    after = dot(suf_ref[...], spread_table(heads, step * (tile // P_SIZE), tile))
    grad = jnp.where(step // count == place(CORE), own_ref[0], other_ref[0])
    input_ref[...] = (part_ref[...] + after * dot12(b_ref[...], halves(grad))).astype(BF16)


def input_terms(part, factors, b, own, other):
    local, width = part.shape
    count = width // 2 // WIDE
    whole = lambda a: pl.BlockSpec(a.shape, lambda j: (0, 0))
    column = pl.BlockSpec((local, WIDE), lambda j: (0, j))
    carry = pl.BlockSpec((1, N, WIDE), lambda j: (1, 0, j % count))
    return pl.pallas_call(
        functools.partial(input_kernel, width // P_SIZE, count),
        grid=(2 * count,),
        in_specs=[column, pl.BlockSpec((local, LANES), lambda j: (0, 1)), whole(b), carry, carry],
        out_specs=column,
        out_shape=jax.ShapeDtypeStruct((local, width), BF16),
        compiler_params=PARAMS,
        name="input_terms",
        cost_estimate=pl.CostEstimate(flops=4 * local * N * width, bytes_accessed=8 * local * width, transcendentals=0),
    )(part, factors, b, own, other)


def sums_kernel(*refs):
    shares, (map_ref, out_ref) = refs[:-2], refs[-2:]
    for i, ref in enumerate((out_ref, map_ref)):
        ref[...] = functools.reduce(lambda a, b: a + b, [share[i] for share in shares])


def swap_cores(v, length):
    return lax.ppermute(v, "seq", [(i, i ^ 1) for i in range(length)])


def turned(v, axis, length, by):
    return lax.ppermute(v, axis, [(i, (i + by) % length) for i in range(length)])


def per_device(mixer_input, output_grad, input_map, output_map, decays):
    length, ranks = lax.axis_size("seq"), lax.axis_size("head")
    chips = length // 2
    args = mixer_input, output_grad, input_map, output_map
    sent, factors = totals(OTHER, *args, decays=decays)
    recv = swap_cores(sent, length)
    (mine,) = totals(CORE, *args, factors=factors)
    tiles = mixer_input.shape[1] // WIDE
    if chips == 4:
        ahead = tiles * 3 // 4
        own, back, *others = first_phase(length, mine, recv)
        result = local_part(0, ahead, *args, decays)
        others, result = lax.optimization_barrier((others, result))
        cross, same = second_phase(own, back, *others)
        others += [crossed(cross, length, 4), crossed(same, length, 2)]
        result, _, _ = lax.optimization_barrier((result, cross, same))
        result = local_part(ahead, tiles - ahead, *args, decays, result)
        others, result = lax.optimization_barrier((others, result))
        own, peer = carried4(mine, recv, *others)
    else:
        messages = chip_totals(chips, mine, recv)
        others = [turned(message, "seq", length, 2 * r) for r, message in enumerate(messages, 1)]
        result = local_part(0, tiles, *args, decays)
        own, peer = carried(chips, mine, recv, others)
    part, scaled, out_part, map_part = result
    other = swap_cores(peer, length)
    out_part, map_part = map_terms(CORE, scaled, own, out_part, map_part)
    shares = map_terms(OTHER, scaled, other, out_part, map_part, ranks)
    own, other, shares = lax.optimization_barrier((own, other, shares))
    sums = [shares[0]] + [turned(shares[r], "head", ranks, r) for r in range(1, ranks)]
    input_grad = input_terms(part, factors, input_map, own, other)
    shape = jax.ShapeDtypeStruct(shares[0].shape[1:], F32)
    input_map_grad, output_map_grad = plain_call(sums_kernel, "head_sums", [shape, shape], *sums)
    return input_grad, input_map_grad, output_map_grad


def solution(mesh):
    in_specs = (
        P("seq", "head"),
        P("seq", "head"),
        P("seq", None),
        P("seq", None),
        P("head", "seq"),
    )
    out_specs = (P("seq", "head"), P(("seq", "head"), None), P(("seq", "head"), None))
    return jax.shard_map(
        per_device, mesh=mesh, in_specs=in_specs, out_specs=out_specs, check_vma=False
    )
```

```python
import functools

import jax
import jax.numpy as jnp
from jax import lax
from jax.experimental import pallas as pl
from jax.experimental.pallas import tpu as pltpu
from jax.sharding import PartitionSpec as P

P_SIZE = 64
N = 128
SUB = 64
TILE = 256
WIDE = 512
EXTRA = 8
PARTS = 4
LANES = 128
CORE, OTHER = range(2)
PARAMS = pltpu.CompilerParams(vmem_limit_bytes=24 * 1024 * 1024)
FIRST = pltpu.CompilerParams(vmem_limit_bytes=56 * 1024 * 1024)
F32 = jnp.float32
BF16 = jnp.bfloat16

NN = (((1,), (0,)), ((), ()))
NT = (((1,), (1,)), ((), ()))


def dot(a, b, dims=NN):
    return lax.dot_general(a, b, dims, preferred_element_type=F32)


def halves(v):
    hi = v.astype(BF16)
    return hi, (v - hi.astype(F32)).astype(BF16)


def dot21(pair, b, dims=NN):
    return dot(pair[0], b, dims) + dot(pair[1], b, dims)


def dot12(a, pair, dims=NN):
    return dot(a, pair[0], dims) + dot(a, pair[1], dims)


def dot22(p, q, dims=NN):
    return dot(p[0], q[0], dims) + (dot(p[0], q[1], dims) + dot(p[1], q[0], dims))


def thirds(v):
    hi = v.astype(BF16)
    rest = v - hi.astype(F32)
    mid = rest.astype(BF16)
    return hi, mid, (rest - mid.astype(F32)).astype(BF16)


def spread(by_head, first, width):
    lanes = lax.broadcasted_iota(jnp.int32, by_head.shape, 1)
    step = LANES // P_SIZE
    shift = P_SIZE.bit_length() - 1
    taken = [
        jnp.take_along_axis(by_head, first + step * k + (lanes >> shift), axis=1) for k in range(width // LANES)
    ]
    return jnp.concatenate(taken, axis=1)


def place(half):
    core = lax.axis_index("seq") % 2
    return core if half == CORE else 1 - core


def stacked(*parts):
    return jnp.concatenate(parts, axis=0)


def transposed(v):
    return v.astype(F32).T.astype(BF16)


def log_parts(decays):
    return jnp.concatenate([part.astype(F32) for part in thirds(jnp.log(decays))], axis=0).astype(BF16)


def summed_logs(logs, table):
    heads = logs.shape[0] // 3
    sums = dot(logs, table.astype(F32).astype(BF16))
    return sums[:heads] + (sums[heads : 2 * heads] + sums[2 * heads :])


def by_token(v):
    rest = jnp.zeros((LANES - v.shape[0], v.shape[1]), F32)
    return jnp.concatenate([v, rest], axis=0).T


def packed(v):
    parts = [part.astype(F32) for part in thirds(v)]
    rest = jnp.zeros((LANES - 3 * v.shape[0], v.shape[1]), F32)
    return jnp.concatenate(parts + [rest], axis=0).T.astype(BF16)


def spread_table(heads, first, width):
    rows = lax.broadcasted_iota(jnp.int32, (heads, width), 0)
    columns = lax.broadcasted_iota(jnp.int32, (heads, width), 1)
    offset = columns - (rows - first) * P_SIZE
    picked = ((offset >= 0) & (offset < P_SIZE)).astype(F32)
    rest = jnp.zeros((LANES - 3 * heads, width), F32)
    return jnp.concatenate([picked, picked, picked, rest], axis=0).astype(BF16)


def device_factors(decays, ref):
    local = decays.shape[1]
    logs = log_parts(decays)
    rows = lax.broadcasted_iota(jnp.int32, (local, local), 0)
    columns = lax.broadcasted_iota(jnp.int32, (local, local), 1)
    ref[:, :LANES] = packed(jnp.exp(summed_logs(logs, rows <= columns)))
    ref[:, LANES:] = packed(jnp.exp(summed_logs(logs, rows > columns)))


def totals_kernel(heads, count, half, made, *refs):
    x_refs, dy_refs, (b_ref, c_ref) = refs[:PARTS], refs[PARTS : 2 * PARTS], refs[2 * PARTS : 2 * PARTS + 2]
    refs = refs[2 * PARTS + 2 :]
    if made:
        factor_ref, out_ref, bt_ref, ct_ref = refs
    else:
        decays_ref, out_ref, factor_ref, bt_ref, ct_ref = refs
    step = pl.program_id(0)

    @pl.when(step == 0)
    def _():
        bt_ref[...] = transposed(b_ref[...])
        ct_ref[...] = transposed(c_ref[...])
        if not made:
            device_factors(decays_ref[...], factor_ref)

    tile = x_refs[0].shape[1]
    table = spread_table(heads, (place(half) * count + step) * (tile // P_SIZE), tile)
    before = dot(factor_ref[:, :LANES], table)
    after = dot(factor_ref[:, LANES:], table)
    ended = before[before.shape[0] - 1 :, :]
    for i, (sources, factor, other) in enumerate(((x_refs, after, bt_ref), (dy_refs, before, ct_ref))):
        source = stacked(*[ref[...].astype(F32) for ref in sources])
        out_ref[i, :N, :] = dot12(other[...], halves(source * factor))
        out_ref[i, N:, :] = jnp.broadcast_to(ended, (EXTRA, tile))


def totals(half, x, dy, b, c, decays=None, factors=None):
    local, width = x.shape
    count = width // 2 // TILE
    whole = lambda a: pl.BlockSpec(a.shape, lambda j: (0, 0))
    columns = [
        pl.BlockSpec((local // PARTS, TILE), functools.partial(lambda part, j: (part, place(half) * count + j), part))
        for part in range(PARTS)
    ]
    factor = jax.ShapeDtypeStruct((local, 2 * LANES), BF16)
    made = factors is not None
    last = factors if made else decays
    out_specs = [pl.BlockSpec((2, N + EXTRA, TILE), lambda j: (0, 0, j))]
    out_shape = [jax.ShapeDtypeStruct((2, N + EXTRA, width // 2), F32)]
    if not made:
        out_specs.append(whole(factor))
        out_shape.append(factor)
    return pl.pallas_call(
        functools.partial(totals_kernel, width // P_SIZE, count, half, made),
        grid=(count,),
        in_specs=columns + columns + [whole(b), whole(c), whole(last)],
        out_specs=out_specs,
        scratch_shapes=[pltpu.VMEM((N, local), BF16), pltpu.VMEM((N, local), BF16)],
        out_shape=out_shape,
        compiler_params=PARAMS if made else FIRST,
        name="state_totals",
        cost_estimate=pl.CostEstimate(flops=8 * local * N * width // 2, bytes_accessed=4 * local * width, transcendentals=0),
    )(*[x] * PARTS, *[dy] * PARTS, b, c, last)


def ordered(core, mine, recv):
    return jnp.where(core == 0, mine, recv), jnp.where(core == 0, recv, mine)


def chip_kernel(chips, mine_ref, recv_ref, *out_refs):
    core, chip = place(CORE), lax.axis_index("seq") // 2
    early, late = ordered(core, mine_ref[0], recv_ref[0])
    early_decay, late_decay = early[N : N + 1], late[N : N + 1]
    both = jnp.broadcast_to(early_decay * late_decay, (EXTRA, early.shape[1]))
    state = late_decay * early[:N] + late[:N]
    early, late = ordered(core, mine_ref[1], recv_ref[1])
    grad = early[:N] + early_decay * late[:N]
    for r, out_ref in enumerate(out_refs, 1):
        out_ref[:N, :] = jnp.where(chip + r < chips, state, grad)
        out_ref[N:, :] = both


def chip_totals(chips, mine, recv):
    width = mine.shape[2]
    tile = min(512, width)
    block = pl.BlockSpec((2, N + EXTRA, tile), lambda j: (0, 0, j))
    out = pl.BlockSpec((N + EXTRA, tile), lambda j: (0, j))
    shape = jax.ShapeDtypeStruct((N + EXTRA, width), F32)
    return pl.pallas_call(
        functools.partial(chip_kernel, chips),
        grid=(width // tile,),
        in_specs=[block, block],
        out_specs=[out] * (chips - 1),
        out_shape=[shape] * (chips - 1),
        compiler_params=PARAMS,
        name="chip_totals",
        cost_estimate=pl.CostEstimate(flops=6 * N * width, bytes_accessed=24 * N * width, transcendentals=0),
    )(mine, recv)


def sides():
    chip = lax.axis_index("seq") // 2
    return chip < 2, (chip == 1) | (chip == 2)


def first_kernel(mine_ref, recv_ref, same_ref, later_ref, cross_ref, back_ref, decay_ref):
    left, inner = sides()
    core = place(CORE)
    width = mine_ref.shape[2] // 2
    early, late = ordered(core, mine_ref[0], recv_ref[0])
    early_decay, late_decay = early[N : N + 1], late[N : N + 1]
    state = late_decay * early[:N] + late[:N]
    decay = early_decay * late_decay
    early, late = ordered(core, mine_ref[1], recv_ref[1])
    grad = early[:N] + early_decay * late[:N]
    out, back = jnp.where(left, state, grad), jnp.where(left, grad, state)
    same_ref[:N, :] = out[:, :width]
    later_ref[...] = jnp.where(inner, back[:, :width], out[:, width:])
    rows = lax.broadcasted_iota(jnp.int32, (EXTRA, width), 0)
    same_ref[N:, :] = jnp.where(rows == 0, decay[:, :width], decay[:, width:])
    cross_ref[...] = out[:, width:]
    back_ref[...] = back[:, width:]
    decay_ref[...] = jnp.broadcast_to(decay[:, width:], (EXTRA, width))


def second_kernel(own_ref, back_ref, same_ref, cross_ref, decay_ref, cross2_ref, same2_ref):
    _, inner = sides()
    own, other = own_ref[:N, :], same_ref[:N, :]
    own_decay, other_decay = own_ref[N : N + 1, :], same_ref[N : N + 1, :]
    cross2_ref[...] = jnp.where(inner, own + own_decay * other, other + other_decay * own)
    weight = own_ref[N + 1 : N + 2, :] * decay_ref[:1, :]
    same2_ref[...] = jnp.where(inner, back_ref[...] + weight * cross_ref[...], cross_ref[...])


def plain_call(kernel, name, out_shape, *args):
    whole = lambda a: pl.BlockSpec(a.shape, lambda j: (0,) * len(a.shape))
    size = sum(a.size for a in args)
    return pl.pallas_call(
        kernel,
        grid=(1,),
        in_specs=[whole(a) for a in args],
        out_specs=[whole(a) for a in out_shape],
        out_shape=out_shape,
        compiler_params=PARAMS,
        name=name,
        cost_estimate=pl.CostEstimate(flops=8 * size, bytes_accessed=4 * size, transcendentals=0),
    )(*args)


def crossed(v, length, bit):
    return lax.ppermute(v, "seq", [(i, i ^ bit) for i in range(length)])


def first_phase(length, mine, recv):
    half = mine.shape[2] // 2
    shapes = [jax.ShapeDtypeStruct((rows, half), F32) for rows in (N + EXTRA, N, N, N, EXTRA)]
    own, later, cross, back, decay = plain_call(first_kernel, "first_messages", shapes, mine, recv)
    same, cross, decay = crossed(own, length, 2), crossed(cross, length, 4), crossed(decay, length, 6)
    return own, back, same, cross, decay, crossed(later, length, 2)


def second_phase(own, back, same, cross, decay):
    shape = jax.ShapeDtypeStruct(back.shape, F32)
    return plain_call(second_kernel, "second_messages", [shape, shape], own, back, same, cross, decay)


def carried4_kernel(
    mine_ref, recv_ref, same_ref, cross_ref, decay_ref, later_ref, cross2_ref, same2_ref, own_ref, peer_ref
):
    left, inner = sides()
    width = cross_ref.shape[1]
    decay_a, decay_b = same_ref[N : N + 1, :], same_ref[N + 1 : N + 2, :]
    for part in range(2):
        at = slice(part * width, (part + 1) * width)
        out = jnp.where(inner, later_ref[...] if part else same_ref[:N, :], 0.0)
        if part == 0:
            back = jnp.where(inner, cross2_ref[...], later_ref[...] + decay_a * cross2_ref[...])
        else:
            back = same2_ref[...] + jnp.where(inner, decay_ref[:1, :], decay_b) * cross_ref[...]
        carried_cores(
            place(CORE), jnp.where(left, out, back), jnp.where(left, back, out), mine_ref, recv_ref, own_ref, peer_ref, at
        )


def carried4(mine, recv, *others):
    shape = jax.ShapeDtypeStruct((2, N, mine.shape[2]), F32)
    return plain_call(carried4_kernel, "carried_in", [shape, shape], mine, recv, *others)


def carried_cores(core, state, grad, mine_ref, recv_ref, own_ref, peer_ref, at):
    early, late = ordered(core, mine_ref[0, :, at], recv_ref[0, :, at])
    at_late = early[N : N + 1] * state + early[:N]
    own_ref[0, :, at] = jnp.where(core == 0, state, at_late)
    peer_ref[0, :, at] = jnp.where(core == 0, at_late, state)
    early, late = ordered(core, mine_ref[1, :, at], recv_ref[1, :, at])
    at_early = late[:N] + late[N : N + 1] * grad
    own_ref[1, :, at] = jnp.where(core == 0, at_early, grad)
    peer_ref[1, :, at] = jnp.where(core == 0, grad, at_early)


def carried_kernel(chips, mine_ref, recv_ref, *refs):
    others, (own_ref, peer_ref) = refs[:-2], refs[-2:]
    core, chip = place(CORE), lax.axis_index("seq") // 2
    state = grad = jnp.zeros((N, own_ref.shape[2]), F32)
    state_weight = grad_weight = jnp.ones((1, own_ref.shape[2]), F32)
    for r, ref in enumerate(others, 1):
        earlier = chip >= r
        state = jnp.where(earlier, state + state_weight * ref[:N, :], state)
        state_weight = state_weight * ref[N : N + 1, :]
    for r in range(1, chips):
        later = chip + r < chips
        ref = others[chips - r - 1]
        grad = jnp.where(later, grad + grad_weight * ref[:N, :], grad)
        grad_weight = grad_weight * ref[N : N + 1, :]
    carried_cores(core, state, grad, mine_ref, recv_ref, own_ref, peer_ref, slice(None))


def carried(chips, mine, recv, others):
    width = mine.shape[2]
    tile = min(512, width)
    pair = pl.BlockSpec((2, N + EXTRA, tile), lambda j: (0, 0, j))
    other = pl.BlockSpec((N + EXTRA, tile), lambda j: (0, j))
    out = pl.BlockSpec((2, N, tile), lambda j: (0, 0, j))
    shape = jax.ShapeDtypeStruct((2, N, width), F32)
    return pl.pallas_call(
        functools.partial(carried_kernel, chips),
        grid=(width // tile,),
        in_specs=[pair, pair] + [other] * len(others),
        out_specs=(out, out),
        out_shape=(shape, shape),
        compiler_params=PARAMS,
        name="carried_in",
        cost_estimate=pl.CostEstimate(flops=20 * N * width, bytes_accessed=44 * N * width, transcendentals=0),
    )(mine, recv, *others)


def blocks(chunks):
    span = 2
    while span < chunks:
        yield span, [at for at in range(span, chunks, 2 * span)]
        span *= 2


def row_bounds(chunks):
    middles = [k * SUB + SUB // 2 + 1 for k in range(chunks)]
    for span in [1] + [span for span, _ in blocks(chunks)]:
        for k, middle in enumerate(middles):
            boundary = (k // span + 1 - (k // span) % 2) * span * SUB
            yield min(boundary, middle), max(boundary, middle)
    yield from ((0, middle) for middle in middles)
    yield from ((middle, chunks * SUB) for middle in middles)


def local_factors(decays, lift_ref, drop_ref, rows_ref):
    local = decays.shape[1]
    logs = log_parts(decays)
    rows = lax.broadcasted_iota(jnp.int32, (local, local), 0)
    columns = lax.broadcasted_iota(jnp.int32, (local, local), 1)
    middle = (columns & -SUB) + SUB // 2
    later = (rows > middle) & (rows <= columns)
    sooner = (rows > columns) & (rows <= middle)
    offset = summed_logs(logs, later.astype(F32) - sooner.astype(F32))
    lift_ref[...] = by_token(jnp.exp(offset))
    drop_ref[...] = by_token(jnp.exp(-offset))
    lane = lax.broadcasted_iota(jnp.int32, (1, LANES), 1)
    first = last = jnp.zeros((1, LANES), jnp.int32)
    for i, (start, end) in enumerate(row_bounds(local // SUB)):
        first, last = jnp.where(lane == i, start, first), jnp.where(lane == i, end, last)
    rows = lax.broadcasted_iota(jnp.int32, (local, LANES), 0)
    decay = by_token(jnp.exp(summed_logs(logs, (rows >= first) & (rows < last))))
    rows_ref[...] = decay[: rows_ref.shape[0]]


def score_parts(b, c, ref, at, times, ahead=None):
    score = dot(b, c, NT)
    if ahead is not None:
        rows = lax.broadcasted_iota(jnp.int32, score.shape, 0)
        columns = lax.broadcasted_iota(jnp.int32, score.shape, 1)
        score = jnp.where(rows <= columns + ahead, score, 0.0)
    hi, lo = halves(score)
    width = score.shape[1]
    ref[at, :width] = hi
    ref[at, width : 2 * width] = lo
    if times == 3:
        ref[at, 2 * width :] = hi


def added_up(v):
    width = v.shape[1] // 2
    return v[:, :width] + v[:, width:]


def local_kernel(first_tile, continued, *refs):
    x_ref, dy_ref, b_ref, c_ref, decays_ref = refs[:5]
    refs = refs[5:]
    if continued:
        out_before_ref, map_before_ref = refs[:2]
        refs = refs[4:]
    part_ref, scaled_ref, out_ref, map_ref = refs[:4]
    lift_ref, drop_ref, rows_ref, full_ref, dys_ref, xs_ref, back_ref, sums_ref, even_ref, odd_ref = refs[4:14]
    level_refs = refs[14:]
    local, tile = x_ref.shape
    chunks = local // SUB
    step = pl.program_id(0)
    levels = [(span, at, level_refs[2 * i], level_refs[2 * i + 1]) for i, (span, at) in enumerate(blocks(chunks))]

    @pl.when(step == 0)
    def _():
        local_factors(decays_ref[...], lift_ref, drop_ref, rows_ref)
        sums_ref[...] = jnp.zeros(sums_ref.shape, F32)
        for k in range(0, chunks, 2):
            pair, even, odd = pl.ds(k * SUB, 2 * SUB), pl.ds(k * SUB, SUB), pl.ds((k + 1) * SUB, SUB)
            score_parts(b_ref[even, :], c_ref[even, :], even_ref, pl.ds(k // 2 * SUB, SUB), 3, 0)
            score_parts(b_ref[pair, :], c_ref[odd, :], odd_ref, pair, 3, SUB)
        for span, boundaries, mixed_ref, scores_ref in levels:
            mixed_ref[...] = jnp.zeros(mixed_ref.shape, F32)
            size = span * SUB
            for i, boundary in enumerate(boundaries):
                before, after = pl.ds((boundary - span) * SUB, size), pl.ds(boundary * SUB, size)
                score_parts(b_ref[before, :], c_ref[after, :], scores_ref, pl.ds(i * size, size), 2)

    first = (first_tile + step) * (tile // P_SIZE)
    dys_ref[...] = dy_ref[...].astype(F32) * spread(lift_ref[...], first, tile)
    back_ref[...] = spread(drop_ref[...], first, tile)
    xs_ref[...] = x_ref[...].astype(F32) * back_ref[...]
    row = spread(rows_ref[...], first, tile)
    factor = lambda kind, k: row[kind * chunks + k : kind * chunks + k + 1]

    for k in range(0, chunks, 2):
        even, odd, pair = pl.ds(k * SUB, SUB), pl.ds((k + 1) * SUB, SUB), pl.ds(k * SUB, 2 * SUB)
        dys, xs = halves(dys_ref[even, :]), halves(xs_ref[even, :])
        sums_ref[even, :] += dot(dys[0], stacked(*xs), NT)
        sums_ref[even, :SUB] += dot(dys[1], xs[0], NT)
        gained_even = dot(even_ref[pl.ds(k // 2 * SUB, SUB), :], stacked(dys[0], dys[0], dys[1]))
        joint = factor(0, k) * factor(0, k + 1)
        crossing = halves(xs_ref[even, :] * joint)
        dys, xs = halves(dys_ref[odd, :]), halves(xs_ref[odd, :])
        high = stacked(xs[0], crossing[0])
        both = dot(dys[0], stacked(high, xs[1], crossing[1]), NT)
        sums_ref[odd, :] += added_up(both) + dot(dys[1], high, NT)
        gained_odd = dot(odd_ref[pair, :], stacked(dys[0], dys[0], dys[1]))
        part_ref[even, :] = back_ref[even, :] * (gained_even + joint * gained_odd[:SUB])
        part_ref[odd, :] = back_ref[odd, :] * gained_odd[SUB:]

    for level, (span, boundaries, mixed_ref, scores_ref) in enumerate(levels, 1):
        size = span * SUB
        for i, boundary in enumerate(boundaries):
            at = pl.ds(i * size, size)
            take = lambda ref, start: halves(
                stacked(*[ref[k * SUB : (k + 1) * SUB, :] * factor(level, k) for k in range(start, start + span)])
            )
            dys, xs = take(dys_ref, boundary), take(xs_ref, boundary - span)
            both = dot(dys[0], stacked(*xs), NT)
            mixed_ref[at, :] += added_up(both) + dot(dys[1], xs[0], NT)
            gained = dot(scores_ref[at, :], stacked(dys[0], dys[0])) + dot(scores_ref[at, :size], dys[1])
            for q in range(span):
                k = boundary - span + q
                rows = pl.ds(k * SUB, SUB)
                part_ref[rows, :] += (back_ref[rows, :] * factor(level, k)) * gained[q * SUB : (q + 1) * SUB]

    for k in range(chunks):
        at = pl.ds(k * SUB, SUB)
        kind = len(levels) + 1
        scaled_ref[1, 0, at, :], scaled_ref[1, 1, at, :] = halves(dys_ref[at, :] * factor(kind, k))
        scaled_ref[0, 0, at, :], scaled_ref[0, 1, at, :] = halves(xs_ref[at, :] * factor(kind + 1, k))

    @pl.when(step == pl.num_programs(0) - 1)
    def _():
        full_ref[...] = jnp.zeros(full_ref.shape, F32)
        rows = lax.broadcasted_iota(jnp.int32, (SUB, SUB), 0)
        columns = lax.broadcasted_iota(jnp.int32, (SUB, SUB), 1)
        for k in range(0, chunks, 2):
            even, odd = pl.ds(k * SUB, SUB), pl.ds((k + 1) * SUB, SUB)
            full_ref[even, k * SUB : (k + 1) * SUB] = jnp.where(rows >= columns, added_up(sums_ref[even, :]), 0.0)
            full_ref[odd, (k + 1) * SUB : (k + 2) * SUB] = jnp.where(rows >= columns, sums_ref[odd, :SUB], 0.0)
            full_ref[odd, k * SUB : (k + 1) * SUB] = sums_ref[odd, SUB:]
        for span, boundaries, mixed_ref, _ in levels:
            size = span * SUB
            for i, boundary in enumerate(boundaries):
                block = mixed_ref[pl.ds(i * size, size), :]
                full_ref[pl.ds(boundary * SUB, size), (boundary - span) * SUB : boundary * SUB] = block
        map_ref[...] = map_before_ref[...] if continued else jnp.zeros(map_ref.shape, F32)
        for k in range(0, local, LANES):
            at = pl.ds(k, LANES)
            mixed = full_ref[at, :]
            gained = dot21(halves(mixed), b_ref[...])
            out_ref[at, :] = out_before_ref[at, :] + gained if continued else gained
            map_ref[...] += dot21(halves(mixed.T), c_ref[at, :])


def local_part(first_tile, count, x, dy, b, c, decays, before=None):
    local, width = x.shape
    chunks = local // SUB
    whole = lambda a: pl.BlockSpec(a.shape, lambda j: (0, 0))
    column = pl.BlockSpec((local, WIDE), lambda j: (0, first_tile + j))
    tokens = pl.BlockSpec((local, N), lambda j: (0, 0))
    scratch = [
        pltpu.VMEM((local, LANES), F32),
        pltpu.VMEM((local, LANES), F32),
        pltpu.VMEM((-(-len(list(row_bounds(chunks))) // 8) * 8, LANES), F32),
        pltpu.VMEM((local, local), F32),
        pltpu.VMEM((local, WIDE), F32),
        pltpu.VMEM((local, WIDE), F32),
        pltpu.VMEM((local, WIDE), F32),
        pltpu.VMEM((local, 2 * SUB), F32),
        pltpu.VMEM((local // 2, 3 * SUB), BF16),
        pltpu.VMEM((local, 3 * SUB), BF16),
    ]
    for span, _ in blocks(chunks):
        scratch.append(pltpu.VMEM((local // 2, span * SUB), F32))
        scratch.append(pltpu.VMEM((local // 2, 2 * span * SUB), BF16))
    in_specs = [column, column, whole(b), whole(c), whole(decays)]
    args, aliases = [x, dy, b, c, decays], {}
    if before is not None:
        part, scaled, out_part, map_part = before
        in_specs += [tokens, tokens, pl.BlockSpec(memory_space=pl.ANY), pl.BlockSpec(memory_space=pl.ANY)]
        args += [out_part, map_part, part, scaled]
        aliases = {7: 0, 8: 1}
    return pl.pallas_call(
        functools.partial(local_kernel, first_tile, before is not None),
        grid=(count,),
        in_specs=in_specs,
        out_specs=(column, pl.BlockSpec((2, 2, local, WIDE), lambda j: (0, 0, 0, first_tile + j)), tokens, tokens),
        out_shape=(
            jax.ShapeDtypeStruct((local, width), F32),
            jax.ShapeDtypeStruct((2, 2, local, width), BF16),
            jax.ShapeDtypeStruct((local, N), F32),
            jax.ShapeDtypeStruct((local, N), F32),
        ),
        scratch_shapes=scratch,
        input_output_aliases=aliases,
        compiler_params=PARAMS,
        name="local_part",
        cost_estimate=pl.CostEstimate(
            flops=40 * local * N * WIDE * count, bytes_accessed=8 * local * WIDE * count, transcendentals=0
        ),
    )(*args)


def map_kernel(count, ranks, scaled_ref, carry_ref, out_before_ref, map_before_ref, *refs):
    messages, (out_ref, map_ref) = refs[:-2], refs[-2:]
    step = pl.program_id(0)

    @pl.when(step == 0)
    def _():
        out_ref[...] = out_before_ref[...]
        map_ref[...] = map_before_ref[...]

    for i, sum_ref in enumerate((map_ref, out_ref)):
        carry = halves(carry_ref[1 - i])
        both = dot(scaled_ref[i, 0], stacked(*carry), NT)
        sum_ref[...] += both[:, :N] + (both[:, N:] + dot(scaled_ref[i, 1], carry[0], NT))

    if messages:

        @pl.when(step == count - 1)
        def _():
            rows = messages[0].shape[1]
            for r, message in enumerate(messages):
                at = pl.ds(pl.multiple_of(((lax.axis_index("head") + r) % ranks) * rows, rows), rows)
                message[0] = out_ref[at, :]
                message[1] = map_ref[at, :]


def map_terms(half, scaled, carry, out_before, map_before, ranks=0):
    local, width = scaled.shape[2], carry.shape[2]
    tile = min(WIDE, width)
    count = width // tile
    whole = lambda a: pl.BlockSpec(a.shape, lambda j: (0,) * len(a.shape))
    tokens = jax.ShapeDtypeStruct((local, N), F32)
    if ranks:
        out_shape = [jax.ShapeDtypeStruct((2, local // ranks, N), F32)] * ranks
        scratch = [pltpu.VMEM((local, N), F32), pltpu.VMEM((local, N), F32)]
    else:
        out_shape, scratch = [tokens, tokens], []
    return pl.pallas_call(
        functools.partial(map_kernel, count, ranks),
        grid=(count,),
        in_specs=[
            pl.BlockSpec((2, 2, local, tile), lambda j: (0, 0, 0, place(half) * count + j)),
            pl.BlockSpec((2, N, tile), lambda j: (0, 0, j)),
            whole(tokens),
            whole(tokens),
        ],
        out_specs=[whole(shape) for shape in out_shape],
        scratch_shapes=scratch,
        out_shape=out_shape,
        compiler_params=PARAMS,
        name="map_terms",
        cost_estimate=pl.CostEstimate(flops=12 * local * N * width, bytes_accessed=8 * local * width, transcendentals=0),
    )(scaled, carry, out_before, map_before)


def input_kernel(heads, count, part_ref, suf_ref, b_ref, own_ref, other_ref, input_ref):
    tile = part_ref.shape[1]
    step = pl.program_id(0)
    after = dot(suf_ref[...], spread_table(heads, step * (tile // P_SIZE), tile))
    grad = jnp.where(step // count == place(CORE), own_ref[0], other_ref[0])
    input_ref[...] = (part_ref[...] + after * dot12(b_ref[...], halves(grad))).astype(BF16)


def input_terms(part, factors, b, own, other):
    local, width = part.shape
    count = width // 2 // WIDE
    whole = lambda a: pl.BlockSpec(a.shape, lambda j: (0, 0))
    column = pl.BlockSpec((local, WIDE), lambda j: (0, j))
    carry = pl.BlockSpec((1, N, WIDE), lambda j: (1, 0, j % count))
    return pl.pallas_call(
        functools.partial(input_kernel, width // P_SIZE, count),
        grid=(2 * count,),
        in_specs=[column, pl.BlockSpec((local, LANES), lambda j: (0, 1)), whole(b), carry, carry],
        out_specs=column,
        out_shape=jax.ShapeDtypeStruct((local, width), BF16),
        compiler_params=PARAMS,
        name="input_terms",
        cost_estimate=pl.CostEstimate(flops=4 * local * N * width, bytes_accessed=8 * local * width, transcendentals=0),
    )(part, factors, b, own, other)


def sums_kernel(*refs):
    shares, (map_ref, out_ref) = refs[:-2], refs[-2:]
    for i, ref in enumerate((out_ref, map_ref)):
        ref[...] = functools.reduce(lambda a, b: a + b, [share[i] for share in shares])


def swap_cores(v, length):
    return lax.ppermute(v, "seq", [(i, i ^ 1) for i in range(length)])


def turned(v, axis, length, by):
    return lax.ppermute(v, axis, [(i, (i + by) % length) for i in range(length)])


def per_device(mixer_input, output_grad, input_map, output_map, decays):
    length, ranks = lax.axis_size("seq"), lax.axis_size("head")
    chips = length // 2
    args = mixer_input, output_grad, input_map, output_map
    sent, factors = totals(OTHER, *args, decays=decays)
    recv = swap_cores(sent, length)
    (mine,) = totals(CORE, *args, factors=factors)
    tiles = mixer_input.shape[1] // WIDE
    if chips == 4:
        ahead = tiles // 2
        own, back, *others, later = first_phase(length, mine, recv)
        result = local_part(0, ahead, *args, decays)
        others, result = lax.optimization_barrier((others, result))
        cross, same = second_phase(own, back, *others)
        crossing = [crossed(cross, length, 4), crossed(same, length, 2)]
        result, later, _, _ = lax.optimization_barrier((result, later, cross, same))
        result = local_part(ahead, tiles - ahead, *args, decays, result)
        others, result = lax.optimization_barrier((others + [later] + crossing, result))
        own, peer = carried4(mine, recv, *others)
    else:
        messages = chip_totals(chips, mine, recv)
        others = [turned(message, "seq", length, 2 * r) for r, message in enumerate(messages, 1)]
        result = local_part(0, tiles, *args, decays)
        own, peer = carried(chips, mine, recv, others)
    part, scaled, out_part, map_part = result
    other = swap_cores(peer, length)
    out_part, map_part = map_terms(CORE, scaled, own, out_part, map_part)
    shares = map_terms(OTHER, scaled, other, out_part, map_part, ranks)
    own, other, shares = lax.optimization_barrier((own, other, shares))
    sums = [shares[0]] + [turned(shares[r], "head", ranks, r) for r in range(1, ranks)]
    input_grad = input_terms(part, factors, input_map, own, other)
    shape = jax.ShapeDtypeStruct(shares[0].shape[1:], F32)
    input_map_grad, output_map_grad = plain_call(sums_kernel, "head_sums", [shape, shape], *sums)
    return input_grad, input_map_grad, output_map_grad


def solution(mesh):
    in_specs = (
        P("seq", "head"),
        P("seq", "head"),
        P("seq", None),
        P("seq", None),
        P("head", "seq"),
    )
    out_specs = (P("seq", "head"), P(("seq", "head"), None), P(("seq", "head"), None))
    return jax.shard_map(
        per_device, mesh=mesh, in_specs=in_specs, out_specs=out_specs, check_vma=False
    )
```

```python
import functools

import jax
import jax.numpy as jnp
from jax import lax
from jax.experimental import pallas as pl
from jax.experimental.pallas import tpu as pltpu
from jax.sharding import PartitionSpec as P

P_SIZE = 64
N = 128
SUB = 64
TILE = 256
WIDE = 512
EXTRA = 8
LANES = 128
CORE, OTHER = range(2)
PARAMS = pltpu.CompilerParams(vmem_limit_bytes=24 * 1024 * 1024)
FIRST = pltpu.CompilerParams(vmem_limit_bytes=56 * 1024 * 1024)
F32 = jnp.float32
BF16 = jnp.bfloat16

NN = (((1,), (0,)), ((), ()))
NT = (((1,), (1,)), ((), ()))


def dot(a, b, dims=NN):
    return lax.dot_general(a, b, dims, preferred_element_type=F32)


def halves(v):
    hi = v.astype(BF16)
    return hi, (v - hi.astype(F32)).astype(BF16)


def dot21(pair, b, dims=NN):
    return dot(pair[0], b, dims) + dot(pair[1], b, dims)


def dot12(a, pair, dims=NN):
    return dot(a, pair[0], dims) + dot(a, pair[1], dims)


def dot22(p, q, dims=NN):
    return dot(p[0], q[0], dims) + (dot(p[0], q[1], dims) + dot(p[1], q[0], dims))


def thirds(v):
    hi = v.astype(BF16)
    rest = v - hi.astype(F32)
    mid = rest.astype(BF16)
    return hi, mid, (rest - mid.astype(F32)).astype(BF16)


def spread(by_head, first, width):
    lanes = lax.broadcasted_iota(jnp.int32, by_head.shape, 1)
    step = LANES // P_SIZE
    shift = P_SIZE.bit_length() - 1
    taken = [
        jnp.take_along_axis(by_head, first + step * k + (lanes >> shift), axis=1) for k in range(width // LANES)
    ]
    return jnp.concatenate(taken, axis=1)


def place(half):
    core = lax.axis_index("seq") % 2
    return core if half == CORE else 1 - core


def stacked(*parts):
    return jnp.concatenate(parts, axis=0)


def transposed(v):
    return v.astype(F32).T.astype(BF16)


def log_parts(decays):
    return jnp.concatenate([part.astype(F32) for part in thirds(jnp.log(decays))], axis=0).astype(BF16)


def summed_logs(logs, table):
    heads = logs.shape[0] // 3
    sums = dot(logs, table.astype(F32).astype(BF16))
    return sums[:heads] + (sums[heads : 2 * heads] + sums[2 * heads :])


def by_token(v):
    rest = jnp.zeros((LANES - v.shape[0], v.shape[1]), F32)
    return jnp.concatenate([v, rest], axis=0).T


def packed(v):
    parts = [part.astype(F32) for part in thirds(v)]
    rest = jnp.zeros((LANES - 3 * v.shape[0], v.shape[1]), F32)
    return jnp.concatenate(parts + [rest], axis=0).T.astype(BF16)


def spread_table(heads, first, width):
    rows = lax.broadcasted_iota(jnp.int32, (heads, width), 0)
    columns = lax.broadcasted_iota(jnp.int32, (heads, width), 1)
    offset = columns - (rows - first) * P_SIZE
    picked = ((offset >= 0) & (offset < P_SIZE)).astype(F32)
    rest = jnp.zeros((LANES - 3 * heads, width), F32)
    return jnp.concatenate([picked, picked, picked, rest], axis=0).astype(BF16)


def device_factors(decays, ref):
    local = decays.shape[1]
    logs = log_parts(decays)
    rows = lax.broadcasted_iota(jnp.int32, (local, local), 0)
    columns = lax.broadcasted_iota(jnp.int32, (local, local), 1)
    ref[:, :LANES] = packed(jnp.exp(summed_logs(logs, rows <= columns)))
    ref[:, LANES:] = packed(jnp.exp(summed_logs(logs, rows > columns)))


def tile_totals(heads, first, x, dy, bt_ref, ct_ref, factor_ref, out_ref):
    tile = x.shape[1]
    table = spread_table(heads, first, tile)
    before = dot(factor_ref[:, :LANES], table)
    after = dot(factor_ref[:, LANES:], table)
    ended = jnp.broadcast_to(before[before.shape[0] - 1 :, :], (EXTRA, tile))
    for i, (source, factor, other) in enumerate(((x, after, bt_ref), (dy, before, ct_ref))):
        out_ref[i, :N, :] = dot12(other[...], halves(source.astype(F32) * factor))
        out_ref[i, N:, :] = ended


def other_kernel(
    heads, x_ref, dy_ref, b_ref, c_ref, decays_ref, out_ref, factor_ref, x_buf, dy_buf, out_buf, bt_ref, ct_ref, arrived, sent
):
    count, _, tile = x_buf.shape
    base = place(OTHER) * count
    loads = []
    for k in range(count):
        columns = pl.ds(pl.multiple_of((base + k) * tile, tile), tile)
        for i, (source, buf) in enumerate(((x_ref, x_buf), (dy_ref, dy_buf))):
            loads.append(pltpu.make_async_copy(source.at[:, columns], buf.at[k], arrived.at[i, k]))
            loads[-1].start()
    bt_ref[...] = transposed(b_ref[...])
    ct_ref[...] = transposed(c_ref[...])
    device_factors(decays_ref[...], factor_ref)
    stores = []
    for k in range(count):
        loads[2 * k].wait()
        loads[2 * k + 1].wait()
        first = (base + k) * (tile // P_SIZE)
        tile_totals(heads, first, x_buf[k], dy_buf[k], bt_ref, ct_ref, factor_ref, out_buf.at[k])
        stores.append(pltpu.make_async_copy(out_buf.at[k], out_ref.at[:, :, pl.ds(k * tile, tile)], sent.at[k]))
        stores[-1].start()
    for store in stores:
        store.wait()


def other_totals(x, dy, b, c, decays):
    local, width = x.shape
    count = width // 2 // TILE
    anywhere = pl.BlockSpec(memory_space=pl.ANY)
    whole = lambda a: pl.BlockSpec(a.shape, lambda j: (0, 0))
    factor = jax.ShapeDtypeStruct((local, 2 * LANES), BF16)
    return pl.pallas_call(
        functools.partial(other_kernel, width // P_SIZE),
        grid=(1,),
        in_specs=[anywhere, anywhere, whole(b), whole(c), whole(decays)],
        out_specs=[anywhere, whole(factor)],
        out_shape=[jax.ShapeDtypeStruct((2, N + EXTRA, width // 2), F32), factor],
        scratch_shapes=[
            pltpu.VMEM((count, local, TILE), BF16),
            pltpu.VMEM((count, local, TILE), BF16),
            pltpu.VMEM((count, 2, N + EXTRA, TILE), F32),
            pltpu.VMEM((N, local), BF16),
            pltpu.VMEM((N, local), BF16),
            pltpu.SemaphoreType.DMA((2, count)),
            pltpu.SemaphoreType.DMA((count,)),
        ],
        compiler_params=FIRST,
        name="other_totals",
        cost_estimate=pl.CostEstimate(flops=8 * local * N * width // 2, bytes_accessed=4 * local * width, transcendentals=0),
    )(x, dy, b, c, decays)


def own_kernel(heads, count, x_ref, dy_ref, b_ref, c_ref, factor_ref, out_ref, bt_ref, ct_ref):
    step = pl.program_id(0)

    @pl.when(step == 0)
    def _():
        bt_ref[...] = transposed(b_ref[...])
        ct_ref[...] = transposed(c_ref[...])

    first = (place(CORE) * count + step) * (x_ref.shape[1] // P_SIZE)
    tile_totals(heads, first, x_ref[...], dy_ref[...], bt_ref, ct_ref, factor_ref, out_ref)


def own_totals(x, dy, b, c, factors):
    local, width = x.shape
    tile = min(WIDE, width // 2)
    count = width // 2 // tile
    whole = lambda a: pl.BlockSpec(a.shape, lambda j: (0, 0))
    column = pl.BlockSpec((local, tile), lambda j: (0, place(CORE) * count + j))
    return pl.pallas_call(
        functools.partial(own_kernel, width // P_SIZE, count),
        grid=(count,),
        in_specs=[column, column, whole(b), whole(c), whole(factors)],
        out_specs=pl.BlockSpec((2, N + EXTRA, tile), lambda j: (0, 0, j)),
        scratch_shapes=[pltpu.VMEM((N, local), BF16), pltpu.VMEM((N, local), BF16)],
        out_shape=jax.ShapeDtypeStruct((2, N + EXTRA, width // 2), F32),
        compiler_params=PARAMS,
        name="own_totals",
        cost_estimate=pl.CostEstimate(flops=8 * local * N * width // 2, bytes_accessed=4 * local * width, transcendentals=0),
    )(x, dy, b, c, factors)


def ordered(core, mine, recv):
    return jnp.where(core == 0, mine, recv), jnp.where(core == 0, recv, mine)


def chip_kernel(chips, mine_ref, recv_ref, *out_refs):
    core, chip = place(CORE), lax.axis_index("seq") // 2
    early, late = ordered(core, mine_ref[0], recv_ref[0])
    early_decay, late_decay = early[N : N + 1], late[N : N + 1]
    both = jnp.broadcast_to(early_decay * late_decay, (EXTRA, early.shape[1]))
    state = late_decay * early[:N] + late[:N]
    early, late = ordered(core, mine_ref[1], recv_ref[1])
    grad = early[:N] + early_decay * late[:N]
    for r, out_ref in enumerate(out_refs, 1):
        out_ref[:N, :] = jnp.where(chip + r < chips, state, grad)
        out_ref[N:, :] = both


def chip_totals(chips, mine, recv):
    width = mine.shape[2]
    tile = min(512, width)
    block = pl.BlockSpec((2, N + EXTRA, tile), lambda j: (0, 0, j))
    out = pl.BlockSpec((N + EXTRA, tile), lambda j: (0, j))
    shape = jax.ShapeDtypeStruct((N + EXTRA, width), F32)
    return pl.pallas_call(
        functools.partial(chip_kernel, chips),
        grid=(width // tile,),
        in_specs=[block, block],
        out_specs=[out] * (chips - 1),
        out_shape=[shape] * (chips - 1),
        compiler_params=PARAMS,
        name="chip_totals",
        cost_estimate=pl.CostEstimate(flops=6 * N * width, bytes_accessed=24 * N * width, transcendentals=0),
    )(mine, recv)


def sides():
    chip = lax.axis_index("seq") // 2
    return chip < 2, (chip == 1) | (chip == 2)


def first_kernel(mine_ref, recv_ref, same_ref, later_ref, cross_ref, back_ref, decay_ref):
    left, inner = sides()
    core = place(CORE)
    width = mine_ref.shape[2] // 2
    early, late = ordered(core, mine_ref[0], recv_ref[0])
    early_decay, late_decay = early[N : N + 1], late[N : N + 1]
    state = late_decay * early[:N] + late[:N]
    decay = early_decay * late_decay
    early, late = ordered(core, mine_ref[1], recv_ref[1])
    grad = early[:N] + early_decay * late[:N]
    out, back = jnp.where(left, state, grad), jnp.where(left, grad, state)
    same_ref[:N, :] = out[:, :width]
    later_ref[...] = jnp.where(inner, back[:, :width], out[:, width:])
    rows = lax.broadcasted_iota(jnp.int32, (EXTRA, width), 0)
    same_ref[N:, :] = jnp.where(rows == 0, decay[:, :width], decay[:, width:])
    cross_ref[...] = out[:, width:]
    back_ref[...] = back[:, width:]
    decay_ref[...] = jnp.broadcast_to(decay[:, width:], (EXTRA, width))


def second_kernel(own_ref, back_ref, same_ref, cross_ref, decay_ref, cross2_ref, same2_ref):
    _, inner = sides()
    own, other = own_ref[:N, :], same_ref[:N, :]
    own_decay, other_decay = own_ref[N : N + 1, :], same_ref[N : N + 1, :]
    cross2_ref[...] = jnp.where(inner, own + own_decay * other, other + other_decay * own)
    weight = own_ref[N + 1 : N + 2, :] * decay_ref[:1, :]
    same2_ref[...] = jnp.where(inner, back_ref[...] + weight * cross_ref[...], cross_ref[...])


def plain_call(kernel, name, out_shape, *args):
    whole = lambda a: pl.BlockSpec(a.shape, lambda j: (0,) * len(a.shape))
    size = sum(a.size for a in args)
    return pl.pallas_call(
        kernel,
        grid=(1,),
        in_specs=[whole(a) for a in args],
        out_specs=[whole(a) for a in out_shape],
        out_shape=out_shape,
        compiler_params=PARAMS,
        name=name,
        cost_estimate=pl.CostEstimate(flops=8 * size, bytes_accessed=4 * size, transcendentals=0),
    )(*args)


def crossed(v, length, bit):
    return lax.ppermute(v, "seq", [(i, i ^ bit) for i in range(length)])


def first_phase(length, mine, recv):
    half = mine.shape[2] // 2
    shapes = [jax.ShapeDtypeStruct((rows, half), F32) for rows in (N + EXTRA, N, N, N, EXTRA)]
    own, later, cross, back, decay = plain_call(first_kernel, "first_messages", shapes, mine, recv)
    same, cross, decay = crossed(own, length, 2), crossed(cross, length, 4), crossed(decay, length, 6)
    return own, back, same, cross, decay, crossed(later, length, 2)


def second_phase(own, back, same, cross, decay):
    shape = jax.ShapeDtypeStruct(back.shape, F32)
    return plain_call(second_kernel, "second_messages", [shape, shape], own, back, same, cross, decay)


def carried4_kernel(
    mine_ref, recv_ref, same_ref, cross_ref, decay_ref, later_ref, cross2_ref, same2_ref, own_ref, peer_ref
):
    left, inner = sides()
    width = cross_ref.shape[1]
    decay_a, decay_b = same_ref[N : N + 1, :], same_ref[N + 1 : N + 2, :]
    for part in range(2):
        at = slice(part * width, (part + 1) * width)
        out = jnp.where(inner, later_ref[...] if part else same_ref[:N, :], 0.0)
        if part == 0:
            back = jnp.where(inner, cross2_ref[...], later_ref[...] + decay_a * cross2_ref[...])
        else:
            back = same2_ref[...] + jnp.where(inner, decay_ref[:1, :], decay_b) * cross_ref[...]
        carried_cores(
            place(CORE), jnp.where(left, out, back), jnp.where(left, back, out), mine_ref, recv_ref, own_ref, peer_ref, at
        )


def carried4(mine, recv, *others):
    shape = jax.ShapeDtypeStruct((2, N, mine.shape[2]), F32)
    return plain_call(carried4_kernel, "carried_in", [shape, shape], mine, recv, *others)


def carried_cores(core, state, grad, mine_ref, recv_ref, own_ref, peer_ref, at):
    early, late = ordered(core, mine_ref[0, :, at], recv_ref[0, :, at])
    at_late = early[N : N + 1] * state + early[:N]
    own_ref[0, :, at] = jnp.where(core == 0, state, at_late)
    peer_ref[0, :, at] = jnp.where(core == 0, at_late, state)
    early, late = ordered(core, mine_ref[1, :, at], recv_ref[1, :, at])
    at_early = late[:N] + late[N : N + 1] * grad
    own_ref[1, :, at] = jnp.where(core == 0, at_early, grad)
    peer_ref[1, :, at] = jnp.where(core == 0, grad, at_early)


def carried_kernel(chips, mine_ref, recv_ref, *refs):
    others, (own_ref, peer_ref) = refs[:-2], refs[-2:]
    core, chip = place(CORE), lax.axis_index("seq") // 2
    state = grad = jnp.zeros((N, own_ref.shape[2]), F32)
    state_weight = grad_weight = jnp.ones((1, own_ref.shape[2]), F32)
    for r, ref in enumerate(others, 1):
        earlier = chip >= r
        state = jnp.where(earlier, state + state_weight * ref[:N, :], state)
        state_weight = state_weight * ref[N : N + 1, :]
    for r in range(1, chips):
        later = chip + r < chips
        ref = others[chips - r - 1]
        grad = jnp.where(later, grad + grad_weight * ref[:N, :], grad)
        grad_weight = grad_weight * ref[N : N + 1, :]
    carried_cores(core, state, grad, mine_ref, recv_ref, own_ref, peer_ref, slice(None))


def carried(chips, mine, recv, others):
    width = mine.shape[2]
    tile = min(512, width)
    pair = pl.BlockSpec((2, N + EXTRA, tile), lambda j: (0, 0, j))
    other = pl.BlockSpec((N + EXTRA, tile), lambda j: (0, j))
    out = pl.BlockSpec((2, N, tile), lambda j: (0, 0, j))
    shape = jax.ShapeDtypeStruct((2, N, width), F32)
    return pl.pallas_call(
        functools.partial(carried_kernel, chips),
        grid=(width // tile,),
        in_specs=[pair, pair] + [other] * len(others),
        out_specs=(out, out),
        out_shape=(shape, shape),
        compiler_params=PARAMS,
        name="carried_in",
        cost_estimate=pl.CostEstimate(flops=20 * N * width, bytes_accessed=44 * N * width, transcendentals=0),
    )(mine, recv, *others)


def blocks(chunks):
    span = 2
    while span < chunks:
        yield span, [at for at in range(span, chunks, 2 * span)]
        span *= 2


def row_bounds(chunks):
    middles = [k * SUB + SUB // 2 + 1 for k in range(chunks)]
    for span in [1] + [span for span, _ in blocks(chunks)]:
        for k, middle in enumerate(middles):
            boundary = (k // span + 1 - (k // span) % 2) * span * SUB
            yield min(boundary, middle), max(boundary, middle)
    yield from ((0, middle) for middle in middles)
    yield from ((middle, chunks * SUB) for middle in middles)


def local_factors(decays, lift_ref, drop_ref, rows_ref):
    local = decays.shape[1]
    logs = log_parts(decays)
    rows = lax.broadcasted_iota(jnp.int32, (local, local), 0)
    columns = lax.broadcasted_iota(jnp.int32, (local, local), 1)
    middle = (columns & -SUB) + SUB // 2
    later = (rows > middle) & (rows <= columns)
    sooner = (rows > columns) & (rows <= middle)
    offset = summed_logs(logs, later.astype(F32) - sooner.astype(F32))
    lift_ref[...] = by_token(jnp.exp(offset))
    drop_ref[...] = by_token(jnp.exp(-offset))
    lane = lax.broadcasted_iota(jnp.int32, (1, LANES), 1)
    first = last = jnp.zeros((1, LANES), jnp.int32)
    for i, (start, end) in enumerate(row_bounds(local // SUB)):
        first, last = jnp.where(lane == i, start, first), jnp.where(lane == i, end, last)
    rows = lax.broadcasted_iota(jnp.int32, (local, LANES), 0)
    decay = by_token(jnp.exp(summed_logs(logs, (rows >= first) & (rows < last))))
    rows_ref[...] = decay[: rows_ref.shape[0]]


def score_parts(b, c, ref, at, times, ahead=None):
    score = dot(b, c, NT)
    if ahead is not None:
        rows = lax.broadcasted_iota(jnp.int32, score.shape, 0)
        columns = lax.broadcasted_iota(jnp.int32, score.shape, 1)
        score = jnp.where(rows <= columns + ahead, score, 0.0)
    hi, lo = halves(score)
    width = score.shape[1]
    ref[at, :width] = hi
    ref[at, width : 2 * width] = lo
    if times == 3:
        ref[at, 2 * width :] = hi


def added_up(v):
    width = v.shape[1] // 2
    return v[:, :width] + v[:, width:]


def local_kernel(first_tile, continued, *refs):
    x_ref, dy_ref, b_ref, c_ref, decays_ref = refs[:5]
    refs = refs[5:]
    if continued:
        out_before_ref, map_before_ref = refs[:2]
        refs = refs[4:]
    part_ref, scaled_ref, out_ref, map_ref = refs[:4]
    lift_ref, drop_ref, rows_ref, full_ref, dys_ref, xs_ref, back_ref, sums_ref, even_ref, odd_ref = refs[4:14]
    level_refs = refs[14:]
    local, tile = x_ref.shape
    chunks = local // SUB
    step = pl.program_id(0)
    levels = [(span, at, level_refs[2 * i], level_refs[2 * i + 1]) for i, (span, at) in enumerate(blocks(chunks))]

    @pl.when(step == 0)
    def _():
        local_factors(decays_ref[...], lift_ref, drop_ref, rows_ref)
        sums_ref[...] = jnp.zeros(sums_ref.shape, F32)
        for k in range(0, chunks, 2):
            pair, even, odd = pl.ds(k * SUB, 2 * SUB), pl.ds(k * SUB, SUB), pl.ds((k + 1) * SUB, SUB)
            score_parts(b_ref[even, :], c_ref[even, :], even_ref, pl.ds(k // 2 * SUB, SUB), 3, 0)
            score_parts(b_ref[pair, :], c_ref[odd, :], odd_ref, pair, 3, SUB)
        for span, boundaries, mixed_ref, scores_ref in levels:
            mixed_ref[...] = jnp.zeros(mixed_ref.shape, F32)
            size = span * SUB
            for i, boundary in enumerate(boundaries):
                before, after = pl.ds((boundary - span) * SUB, size), pl.ds(boundary * SUB, size)
                score_parts(b_ref[before, :], c_ref[after, :], scores_ref, pl.ds(i * size, size), 2)

    first = (first_tile + step) * (tile // P_SIZE)
    dys_ref[...] = dy_ref[...].astype(F32) * spread(lift_ref[...], first, tile)
    back_ref[...] = spread(drop_ref[...], first, tile)
    xs_ref[...] = x_ref[...].astype(F32) * back_ref[...]
    row = spread(rows_ref[...], first, tile)
    factor = lambda kind, k: row[kind * chunks + k : kind * chunks + k + 1]

    for k in range(0, chunks, 2):
        even, odd, pair = pl.ds(k * SUB, SUB), pl.ds((k + 1) * SUB, SUB), pl.ds(k * SUB, 2 * SUB)
        dys, xs = halves(dys_ref[even, :]), halves(xs_ref[even, :])
        sums_ref[even, :] += dot(dys[0], stacked(*xs), NT)
        sums_ref[even, :SUB] += dot(dys[1], xs[0], NT)
        gained_even = dot(even_ref[pl.ds(k // 2 * SUB, SUB), :], stacked(dys[0], dys[0], dys[1]))
        joint = factor(0, k) * factor(0, k + 1)
        crossing = halves(xs_ref[even, :] * joint)
        dys, xs = halves(dys_ref[odd, :]), halves(xs_ref[odd, :])
        high = stacked(xs[0], crossing[0])
        both = dot(dys[0], stacked(high, xs[1], crossing[1]), NT)
        sums_ref[odd, :] += added_up(both) + dot(dys[1], high, NT)
        gained_odd = dot(odd_ref[pair, :], stacked(dys[0], dys[0], dys[1]))
        part_ref[even, :] = back_ref[even, :] * (gained_even + joint * gained_odd[:SUB])
        part_ref[odd, :] = back_ref[odd, :] * gained_odd[SUB:]

    for level, (span, boundaries, mixed_ref, scores_ref) in enumerate(levels, 1):
        size = span * SUB
        for i, boundary in enumerate(boundaries):
            at = pl.ds(i * size, size)
            take = lambda ref, start: halves(
                stacked(*[ref[k * SUB : (k + 1) * SUB, :] * factor(level, k) for k in range(start, start + span)])
            )
            dys, xs = take(dys_ref, boundary), take(xs_ref, boundary - span)
            both = dot(dys[0], stacked(*xs), NT)
            mixed_ref[at, :] += added_up(both) + dot(dys[1], xs[0], NT)
            gained = dot(scores_ref[at, :], stacked(dys[0], dys[0])) + dot(scores_ref[at, :size], dys[1])
            for q in range(span):
                k = boundary - span + q
                rows = pl.ds(k * SUB, SUB)
                part_ref[rows, :] += (back_ref[rows, :] * factor(level, k)) * gained[q * SUB : (q + 1) * SUB]

    for k in range(chunks):
        at = pl.ds(k * SUB, SUB)
        kind = len(levels) + 1
        scaled_ref[1, 0, at, :], scaled_ref[1, 1, at, :] = halves(dys_ref[at, :] * factor(kind, k))
        scaled_ref[0, 0, at, :], scaled_ref[0, 1, at, :] = halves(xs_ref[at, :] * factor(kind + 1, k))

    @pl.when(step == pl.num_programs(0) - 1)
    def _():
        full_ref[...] = jnp.zeros(full_ref.shape, F32)
        rows = lax.broadcasted_iota(jnp.int32, (SUB, SUB), 0)
        columns = lax.broadcasted_iota(jnp.int32, (SUB, SUB), 1)
        for k in range(0, chunks, 2):
            even, odd = pl.ds(k * SUB, SUB), pl.ds((k + 1) * SUB, SUB)
            full_ref[even, k * SUB : (k + 1) * SUB] = jnp.where(rows >= columns, added_up(sums_ref[even, :]), 0.0)
            full_ref[odd, (k + 1) * SUB : (k + 2) * SUB] = jnp.where(rows >= columns, sums_ref[odd, :SUB], 0.0)
            full_ref[odd, k * SUB : (k + 1) * SUB] = sums_ref[odd, SUB:]
        for span, boundaries, mixed_ref, _ in levels:
            size = span * SUB
            for i, boundary in enumerate(boundaries):
                block = mixed_ref[pl.ds(i * size, size), :]
                full_ref[pl.ds(boundary * SUB, size), (boundary - span) * SUB : boundary * SUB] = block
        map_ref[...] = map_before_ref[...] if continued else jnp.zeros(map_ref.shape, F32)
        for k in range(0, local, LANES):
            at = pl.ds(k, LANES)
            mixed = full_ref[at, :]
            gained = dot21(halves(mixed), b_ref[...])
            out_ref[at, :] = out_before_ref[at, :] + gained if continued else gained
            map_ref[...] += dot21(halves(mixed.T), c_ref[at, :])


def local_part(first_tile, count, x, dy, b, c, decays, before=None):
    local, width = x.shape
    chunks = local // SUB
    whole = lambda a: pl.BlockSpec(a.shape, lambda j: (0, 0))
    column = pl.BlockSpec((local, WIDE), lambda j: (0, first_tile + j))
    tokens = pl.BlockSpec((local, N), lambda j: (0, 0))
    scratch = [
        pltpu.VMEM((local, LANES), F32),
        pltpu.VMEM((local, LANES), F32),
        pltpu.VMEM((-(-len(list(row_bounds(chunks))) // 8) * 8, LANES), F32),
        pltpu.VMEM((local, local), F32),
        pltpu.VMEM((local, WIDE), F32),
        pltpu.VMEM((local, WIDE), F32),
        pltpu.VMEM((local, WIDE), F32),
        pltpu.VMEM((local, 2 * SUB), F32),
        pltpu.VMEM((local // 2, 3 * SUB), BF16),
        pltpu.VMEM((local, 3 * SUB), BF16),
    ]
    for span, _ in blocks(chunks):
        scratch.append(pltpu.VMEM((local // 2, span * SUB), F32))
        scratch.append(pltpu.VMEM((local // 2, 2 * span * SUB), BF16))
    in_specs = [column, column, whole(b), whole(c), whole(decays)]
    args, aliases = [x, dy, b, c, decays], {}
    if before is not None:
        part, scaled, out_part, map_part = before
        in_specs += [tokens, tokens, pl.BlockSpec(memory_space=pl.ANY), pl.BlockSpec(memory_space=pl.ANY)]
        args += [out_part, map_part, part, scaled]
        aliases = {7: 0, 8: 1}
    return pl.pallas_call(
        functools.partial(local_kernel, first_tile, before is not None),
        grid=(count,),
        in_specs=in_specs,
        out_specs=(column, pl.BlockSpec((2, 2, local, WIDE), lambda j: (0, 0, 0, first_tile + j)), tokens, tokens),
        out_shape=(
            jax.ShapeDtypeStruct((local, width), F32),
            jax.ShapeDtypeStruct((2, 2, local, width), BF16),
            jax.ShapeDtypeStruct((local, N), F32),
            jax.ShapeDtypeStruct((local, N), F32),
        ),
        scratch_shapes=scratch,
        input_output_aliases=aliases,
        compiler_params=PARAMS,
        name="local_part",
        cost_estimate=pl.CostEstimate(
            flops=40 * local * N * WIDE * count, bytes_accessed=8 * local * WIDE * count, transcendentals=0
        ),
    )(*args)


def map_kernel(count, ranks, scaled_ref, carry_ref, out_before_ref, map_before_ref, *refs):
    messages, (out_ref, map_ref) = refs[:-2], refs[-2:]
    step = pl.program_id(0)

    @pl.when(step == 0)
    def _():
        out_ref[...] = out_before_ref[...]
        map_ref[...] = map_before_ref[...]

    for i, sum_ref in enumerate((map_ref, out_ref)):
        carry = halves(carry_ref[1 - i])
        both = dot(scaled_ref[i, 0], stacked(*carry), NT)
        sum_ref[...] += both[:, :N] + (both[:, N:] + dot(scaled_ref[i, 1], carry[0], NT))

    if messages:

        @pl.when(step == count - 1)
        def _():
            rows = messages[0].shape[1]
            for r, message in enumerate(messages):
                at = pl.ds(pl.multiple_of(((lax.axis_index("head") + r) % ranks) * rows, rows), rows)
                message[0] = out_ref[at, :]
                message[1] = map_ref[at, :]


def map_terms(half, scaled, carry, out_before, map_before, ranks=0):
    local, width = scaled.shape[2], carry.shape[2]
    tile = min(WIDE, width)
    count = width // tile
    whole = lambda a: pl.BlockSpec(a.shape, lambda j: (0,) * len(a.shape))
    tokens = jax.ShapeDtypeStruct((local, N), F32)
    if ranks:
        out_shape = [jax.ShapeDtypeStruct((2, local // ranks, N), F32)] * ranks
        scratch = [pltpu.VMEM((local, N), F32), pltpu.VMEM((local, N), F32)]
    else:
        out_shape, scratch = [tokens, tokens], []
    return pl.pallas_call(
        functools.partial(map_kernel, count, ranks),
        grid=(count,),
        in_specs=[
            pl.BlockSpec((2, 2, local, tile), lambda j: (0, 0, 0, place(half) * count + j)),
            pl.BlockSpec((2, N, tile), lambda j: (0, 0, j)),
            whole(tokens),
            whole(tokens),
        ],
        out_specs=[whole(shape) for shape in out_shape],
        scratch_shapes=scratch,
        out_shape=out_shape,
        compiler_params=PARAMS,
        name="map_terms",
        cost_estimate=pl.CostEstimate(flops=12 * local * N * width, bytes_accessed=8 * local * width, transcendentals=0),
    )(scaled, carry, out_before, map_before)


def input_kernel(heads, count, part_ref, suf_ref, b_ref, own_ref, other_ref, input_ref):
    tile = part_ref.shape[1]
    step = pl.program_id(0)
    after = dot(suf_ref[...], spread_table(heads, step * (tile // P_SIZE), tile))
    grad = jnp.where(step // count == place(CORE), own_ref[0], other_ref[0])
    input_ref[...] = (part_ref[...] + after * dot12(b_ref[...], halves(grad))).astype(BF16)


def input_terms(part, factors, b, own, other):
    local, width = part.shape
    count = width // 2 // WIDE
    whole = lambda a: pl.BlockSpec(a.shape, lambda j: (0, 0))
    column = pl.BlockSpec((local, WIDE), lambda j: (0, j))
    carry = pl.BlockSpec((1, N, WIDE), lambda j: (1, 0, j % count))
    return pl.pallas_call(
        functools.partial(input_kernel, width // P_SIZE, count),
        grid=(2 * count,),
        in_specs=[column, pl.BlockSpec((local, LANES), lambda j: (0, 1)), whole(b), carry, carry],
        out_specs=column,
        out_shape=jax.ShapeDtypeStruct((local, width), BF16),
        compiler_params=PARAMS,
        name="input_terms",
        cost_estimate=pl.CostEstimate(flops=4 * local * N * width, bytes_accessed=8 * local * width, transcendentals=0),
    )(part, factors, b, own, other)


def sums_kernel(*refs):
    shares, (map_ref, out_ref) = refs[:-2], refs[-2:]
    for i, ref in enumerate((out_ref, map_ref)):
        ref[...] = functools.reduce(lambda a, b: a + b, [share[i] for share in shares])


def swap_cores(v, length):
    return lax.ppermute(v, "seq", [(i, i ^ 1) for i in range(length)])


def turned(v, axis, length, by):
    return lax.ppermute(v, axis, [(i, (i + by) % length) for i in range(length)])


def per_device(mixer_input, output_grad, input_map, output_map, decays):
    length, ranks = lax.axis_size("seq"), lax.axis_size("head")
    chips = length // 2
    args = mixer_input, output_grad, input_map, output_map
    sent, factors = other_totals(*args, decays)
    recv = swap_cores(sent, length)
    mine = own_totals(*args, factors)
    tiles = mixer_input.shape[1] // WIDE
    if chips == 4:
        ahead = tiles // 2
        own, back, *others, later = first_phase(length, mine, recv)
        result = local_part(0, ahead, *args, decays)
        others, result = lax.optimization_barrier((others, result))
        cross, same = second_phase(own, back, *others)
        crossing = [crossed(cross, length, 4), crossed(same, length, 2)]
        result, later, _, _ = lax.optimization_barrier((result, later, cross, same))
        result = local_part(ahead, tiles - ahead, *args, decays, result)
        others, result = lax.optimization_barrier((others + [later] + crossing, result))
        own, peer = carried4(mine, recv, *others)
    else:
        messages = chip_totals(chips, mine, recv)
        others = [turned(message, "seq", length, 2 * r) for r, message in enumerate(messages, 1)]
        result = local_part(0, tiles, *args, decays)
        own, peer = carried(chips, mine, recv, others)
    part, scaled, out_part, map_part = result
    other = swap_cores(peer, length)
    out_part, map_part = map_terms(CORE, scaled, own, out_part, map_part)
    shares = map_terms(OTHER, scaled, other, out_part, map_part, ranks)
    own, other, shares = lax.optimization_barrier((own, other, shares))
    sums = [shares[0]] + [turned(shares[r], "head", ranks, r) for r in range(1, ranks)]
    input_grad = input_terms(part, factors, input_map, own, other)
    shape = jax.ShapeDtypeStruct(shares[0].shape[1:], F32)
    input_map_grad, output_map_grad = plain_call(sums_kernel, "head_sums", [shape, shape], *sums)
    return input_grad, input_map_grad, output_map_grad


def solution(mesh):
    in_specs = (
        P("seq", "head"),
        P("seq", "head"),
        P("seq", None),
        P("seq", None),
        P("head", "seq"),
    )
    out_specs = (P("seq", "head"), P(("seq", "head"), None), P(("seq", "head"), None))
    return jax.shard_map(
        per_device, mesh=mesh, in_specs=in_specs, out_specs=out_specs, check_vma=False
    )
```

```python
import functools

import jax
import jax.numpy as jnp
from jax import lax
from jax.experimental import pallas as pl
from jax.experimental.pallas import tpu as pltpu
from jax.sharding import PartitionSpec as P

P_SIZE = 64
N = 128
SUB = 64
TILE = 256
WIDE = 512
EXTRA = 8
LANES = 128
CORE, OTHER = range(2)
PARAMS = pltpu.CompilerParams(vmem_limit_bytes=24 * 1024 * 1024)
FIRST = pltpu.CompilerParams(vmem_limit_bytes=56 * 1024 * 1024)
F32 = jnp.float32
BF16 = jnp.bfloat16

NN = (((1,), (0,)), ((), ()))
NT = (((1,), (1,)), ((), ()))


def dot(a, b, dims=NN):
    return lax.dot_general(a, b, dims, preferred_element_type=F32)


def halves(v):
    hi = v.astype(BF16)
    return hi, (v - hi.astype(F32)).astype(BF16)


def dot21(pair, b, dims=NN):
    return dot(pair[0], b, dims) + dot(pair[1], b, dims)


def dot12(a, pair, dims=NN):
    return dot(a, pair[0], dims) + dot(a, pair[1], dims)


def dot22(p, q, dims=NN):
    return dot(p[0], q[0], dims) + (dot(p[0], q[1], dims) + dot(p[1], q[0], dims))


def thirds(v):
    hi = v.astype(BF16)
    rest = v - hi.astype(F32)
    mid = rest.astype(BF16)
    return hi, mid, (rest - mid.astype(F32)).astype(BF16)


def spread(by_head, first, width):
    lanes = lax.broadcasted_iota(jnp.int32, by_head.shape, 1)
    step = LANES // P_SIZE
    shift = P_SIZE.bit_length() - 1
    taken = [
        jnp.take_along_axis(by_head, first + step * k + (lanes >> shift), axis=1) for k in range(width // LANES)
    ]
    return jnp.concatenate(taken, axis=1)


def place(half):
    core = lax.axis_index("seq") % 2
    return core if half == CORE else 1 - core


def stacked(*parts):
    return jnp.concatenate(parts, axis=0)


def transposed(v):
    return v.astype(F32).T.astype(BF16)


def log_parts(decays):
    return jnp.concatenate([part.astype(F32) for part in thirds(jnp.log(decays))], axis=0).astype(BF16)


def summed_logs(logs, table):
    heads = logs.shape[0] // 3
    sums = dot(logs, table.astype(F32).astype(BF16))
    return sums[:heads] + (sums[heads : 2 * heads] + sums[2 * heads :])


def block_sums(logs, table):
    blocks_of = [logs[:, k : k + LANES] for k in range(0, logs.shape[1], LANES)]
    return [summed_logs(block, table) for block in blocks_of]


def by_token(v):
    rest = jnp.zeros((LANES - v.shape[0], v.shape[1]), F32)
    return jnp.concatenate([v, rest], axis=0).T


def packed(v):
    parts = [part.astype(F32) for part in thirds(v)]
    rest = jnp.zeros((LANES - 3 * v.shape[0], v.shape[1]), F32)
    return jnp.concatenate(parts + [rest], axis=0).T.astype(BF16)


def spread_table(heads, first, width):
    rows = lax.broadcasted_iota(jnp.int32, (heads, width), 0)
    columns = lax.broadcasted_iota(jnp.int32, (heads, width), 1)
    offset = columns - (rows - first) * P_SIZE
    picked = ((offset >= 0) & (offset < P_SIZE)).astype(F32)
    rest = jnp.zeros((LANES - 3 * heads, width), F32)
    return jnp.concatenate([picked, picked, picked, rest], axis=0).astype(BF16)


def device_factors(decays, ref):
    logs = log_parts(decays)
    rows = lax.broadcasted_iota(jnp.int32, (LANES, LANES), 0)
    columns = lax.broadcasted_iota(jnp.int32, (LANES, LANES), 1)
    before, after = block_sums(logs, rows <= columns), block_sums(logs, rows > columns)
    totals_of = [block[:, LANES - 1 :] for block in before]
    ahead = behind = jnp.zeros(totals_of[0].shape, F32)
    for k, total in enumerate(totals_of):
        before[k] = before[k] + ahead
        ahead = ahead + total
    for k in reversed(range(len(totals_of))):
        after[k] = after[k] + behind
        behind = behind + totals_of[k]
    ref[:, :LANES] = packed(jnp.exp(jnp.concatenate(before, axis=1)))
    ref[:, LANES:] = packed(jnp.exp(jnp.concatenate(after, axis=1)))


def tile_totals(heads, first, x, dy, bt_ref, ct_ref, factor_ref, out_ref):
    tile = x.shape[1]
    table = spread_table(heads, first, tile)
    before = dot(factor_ref[:, :LANES], table)
    after = dot(factor_ref[:, LANES:], table)
    ended = jnp.broadcast_to(before[before.shape[0] - 1 :, :], (EXTRA, tile))
    for i, (source, factor, other) in enumerate(((x, after, bt_ref), (dy, before, ct_ref))):
        out_ref[i, :N, :] = dot12(other[...], halves(source.astype(F32) * factor))
        out_ref[i, N:, :] = ended


def other_kernel(
    heads, x_ref, dy_ref, b_ref, c_ref, decays_ref, out_ref, factor_ref, x_buf, dy_buf, out_buf, bt_ref, ct_ref, arrived, sent
):
    count, _, tile = x_buf.shape
    base = place(OTHER) * count
    loads = []
    for k in range(count):
        columns = pl.ds(pl.multiple_of((base + k) * tile, tile), tile)
        for i, (source, buf) in enumerate(((x_ref, x_buf), (dy_ref, dy_buf))):
            loads.append(pltpu.make_async_copy(source.at[:, columns], buf.at[k], arrived.at[i, k]))
            loads[-1].start()
    bt_ref[...] = transposed(b_ref[...])
    ct_ref[...] = transposed(c_ref[...])
    device_factors(decays_ref[...], factor_ref)
    stores = []
    for k in range(count):
        loads[2 * k].wait()
        loads[2 * k + 1].wait()
        first = (base + k) * (tile // P_SIZE)
        tile_totals(heads, first, x_buf[k], dy_buf[k], bt_ref, ct_ref, factor_ref, out_buf.at[k])
        stores.append(pltpu.make_async_copy(out_buf.at[k], out_ref.at[:, :, pl.ds(k * tile, tile)], sent.at[k]))
        stores[-1].start()
    for store in stores:
        store.wait()


def other_totals(x, dy, b, c, decays):
    local, width = x.shape
    count = width // 2 // TILE
    anywhere = pl.BlockSpec(memory_space=pl.ANY)
    whole = lambda a: pl.BlockSpec(a.shape, lambda j: (0, 0))
    factor = jax.ShapeDtypeStruct((local, 2 * LANES), BF16)
    return pl.pallas_call(
        functools.partial(other_kernel, width // P_SIZE),
        grid=(1,),
        in_specs=[anywhere, anywhere, whole(b), whole(c), whole(decays)],
        out_specs=[anywhere, whole(factor)],
        out_shape=[jax.ShapeDtypeStruct((2, N + EXTRA, width // 2), F32), factor],
        scratch_shapes=[
            pltpu.VMEM((count, local, TILE), BF16),
            pltpu.VMEM((count, local, TILE), BF16),
            pltpu.VMEM((count, 2, N + EXTRA, TILE), F32),
            pltpu.VMEM((N, local), BF16),
            pltpu.VMEM((N, local), BF16),
            pltpu.SemaphoreType.DMA((2, count)),
            pltpu.SemaphoreType.DMA((count,)),
        ],
        compiler_params=FIRST,
        name="other_totals",
        cost_estimate=pl.CostEstimate(flops=8 * local * N * width // 2, bytes_accessed=4 * local * width, transcendentals=0),
    )(x, dy, b, c, decays)


def own_kernel(heads, count, x_ref, dy_ref, b_ref, c_ref, factor_ref, out_ref, bt_ref, ct_ref):
    step = pl.program_id(0)

    @pl.when(step == 0)
    def _():
        bt_ref[...] = transposed(b_ref[...])
        ct_ref[...] = transposed(c_ref[...])

    first = (place(CORE) * count + step) * (x_ref.shape[1] // P_SIZE)
    tile_totals(heads, first, x_ref[...], dy_ref[...], bt_ref, ct_ref, factor_ref, out_ref)


def own_totals(x, dy, b, c, factors):
    local, width = x.shape
    tile = min(WIDE, width // 2)
    count = width // 2 // tile
    whole = lambda a: pl.BlockSpec(a.shape, lambda j: (0, 0))
    column = pl.BlockSpec((local, tile), lambda j: (0, place(CORE) * count + j))
    return pl.pallas_call(
        functools.partial(own_kernel, width // P_SIZE, count),
        grid=(count,),
        in_specs=[column, column, whole(b), whole(c), whole(factors)],
        out_specs=pl.BlockSpec((2, N + EXTRA, tile), lambda j: (0, 0, j)),
        scratch_shapes=[pltpu.VMEM((N, local), BF16), pltpu.VMEM((N, local), BF16)],
        out_shape=jax.ShapeDtypeStruct((2, N + EXTRA, width // 2), F32),
        compiler_params=PARAMS,
        name="own_totals",
        cost_estimate=pl.CostEstimate(flops=8 * local * N * width // 2, bytes_accessed=4 * local * width, transcendentals=0),
    )(x, dy, b, c, factors)


def ordered(core, mine, recv):
    return jnp.where(core == 0, mine, recv), jnp.where(core == 0, recv, mine)


def chip_kernel(chips, mine_ref, recv_ref, *out_refs):
    core, chip = place(CORE), lax.axis_index("seq") // 2
    early, late = ordered(core, mine_ref[0], recv_ref[0])
    early_decay, late_decay = early[N : N + 1], late[N : N + 1]
    both = jnp.broadcast_to(early_decay * late_decay, (EXTRA, early.shape[1]))
    state = late_decay * early[:N] + late[:N]
    early, late = ordered(core, mine_ref[1], recv_ref[1])
    grad = early[:N] + early_decay * late[:N]
    for r, out_ref in enumerate(out_refs, 1):
        out_ref[:N, :] = jnp.where(chip + r < chips, state, grad)
        out_ref[N:, :] = both


def chip_totals(chips, mine, recv):
    width = mine.shape[2]
    tile = min(512, width)
    block = pl.BlockSpec((2, N + EXTRA, tile), lambda j: (0, 0, j))
    out = pl.BlockSpec((N + EXTRA, tile), lambda j: (0, j))
    shape = jax.ShapeDtypeStruct((N + EXTRA, width), F32)
    return pl.pallas_call(
        functools.partial(chip_kernel, chips),
        grid=(width // tile,),
        in_specs=[block, block],
        out_specs=[out] * (chips - 1),
        out_shape=[shape] * (chips - 1),
        compiler_params=PARAMS,
        name="chip_totals",
        cost_estimate=pl.CostEstimate(flops=6 * N * width, bytes_accessed=24 * N * width, transcendentals=0),
    )(mine, recv)


def sides():
    chip = lax.axis_index("seq") // 2
    return chip < 2, (chip == 1) | (chip == 2)


def first_kernel(mine_ref, recv_ref, same_ref, later_ref, cross_ref, back_ref, decay_ref):
    left, inner = sides()
    core = place(CORE)
    width = mine_ref.shape[2] // 2
    early, late = ordered(core, mine_ref[0], recv_ref[0])
    early_decay, late_decay = early[N : N + 1], late[N : N + 1]
    state = late_decay * early[:N] + late[:N]
    decay = early_decay * late_decay
    early, late = ordered(core, mine_ref[1], recv_ref[1])
    grad = early[:N] + early_decay * late[:N]
    out, back = jnp.where(left, state, grad), jnp.where(left, grad, state)
    same_ref[:N, :] = out[:, :width]
    later_ref[...] = jnp.where(inner, back[:, :width], out[:, width:])
    rows = lax.broadcasted_iota(jnp.int32, (EXTRA, width), 0)
    same_ref[N:, :] = jnp.where(rows == 0, decay[:, :width], decay[:, width:])
    cross_ref[...] = out[:, width:]
    back_ref[...] = back[:, width:]
    decay_ref[...] = jnp.broadcast_to(decay[:, width:], (EXTRA, width))


def second_kernel(own_ref, back_ref, same_ref, cross_ref, decay_ref, cross2_ref, same2_ref):
    _, inner = sides()
    own, other = own_ref[:N, :], same_ref[:N, :]
    own_decay, other_decay = own_ref[N : N + 1, :], same_ref[N : N + 1, :]
    cross2_ref[...] = jnp.where(inner, own + own_decay * other, other + other_decay * own)
    weight = own_ref[N + 1 : N + 2, :] * decay_ref[:1, :]
    same2_ref[...] = jnp.where(inner, back_ref[...] + weight * cross_ref[...], cross_ref[...])


def plain_call(kernel, name, out_shape, *args):
    whole = lambda a: pl.BlockSpec(a.shape, lambda j: (0,) * len(a.shape))
    size = sum(a.size for a in args)
    return pl.pallas_call(
        kernel,
        grid=(1,),
        in_specs=[whole(a) for a in args],
        out_specs=[whole(a) for a in out_shape],
        out_shape=out_shape,
        compiler_params=PARAMS,
        name=name,
        cost_estimate=pl.CostEstimate(flops=8 * size, bytes_accessed=4 * size, transcendentals=0),
    )(*args)


def crossed(v, length, bit):
    return lax.ppermute(v, "seq", [(i, i ^ bit) for i in range(length)])


def first_phase(length, mine, recv):
    half = mine.shape[2] // 2
    shapes = [jax.ShapeDtypeStruct((rows, half), F32) for rows in (N + EXTRA, N, N, N, EXTRA)]
    own, later, cross, back, decay = plain_call(first_kernel, "first_messages", shapes, mine, recv)
    same, cross, decay = crossed(own, length, 2), crossed(cross, length, 4), crossed(decay, length, 6)
    return own, back, same, cross, decay, crossed(later, length, 2)


def second_phase(own, back, same, cross, decay):
    shape = jax.ShapeDtypeStruct(back.shape, F32)
    return plain_call(second_kernel, "second_messages", [shape, shape], own, back, same, cross, decay)


def carried4_kernel(
    mine_ref, recv_ref, same_ref, cross_ref, decay_ref, later_ref, cross2_ref, same2_ref, own_ref, peer_ref
):
    left, inner = sides()
    width = cross_ref.shape[1]
    decay_a, decay_b = same_ref[N : N + 1, :], same_ref[N + 1 : N + 2, :]
    for part in range(2):
        at = slice(part * width, (part + 1) * width)
        out = jnp.where(inner, later_ref[...] if part else same_ref[:N, :], 0.0)
        if part == 0:
            back = jnp.where(inner, cross2_ref[...], later_ref[...] + decay_a * cross2_ref[...])
        else:
            back = same2_ref[...] + jnp.where(inner, decay_ref[:1, :], decay_b) * cross_ref[...]
        carried_cores(
            place(CORE), jnp.where(left, out, back), jnp.where(left, back, out), mine_ref, recv_ref, own_ref, peer_ref, at
        )


def carried4(mine, recv, *others):
    shape = jax.ShapeDtypeStruct((2, N, mine.shape[2]), F32)
    return plain_call(carried4_kernel, "carried_in", [shape, shape], mine, recv, *others)


def carried_cores(core, state, grad, mine_ref, recv_ref, own_ref, peer_ref, at):
    early, late = ordered(core, mine_ref[0, :, at], recv_ref[0, :, at])
    at_late = early[N : N + 1] * state + early[:N]
    own_ref[0, :, at] = jnp.where(core == 0, state, at_late)
    peer_ref[0, :, at] = jnp.where(core == 0, at_late, state)
    early, late = ordered(core, mine_ref[1, :, at], recv_ref[1, :, at])
    at_early = late[:N] + late[N : N + 1] * grad
    own_ref[1, :, at] = jnp.where(core == 0, at_early, grad)
    peer_ref[1, :, at] = jnp.where(core == 0, grad, at_early)


def carried_kernel(chips, mine_ref, recv_ref, *refs):
    others, (own_ref, peer_ref) = refs[:-2], refs[-2:]
    core, chip = place(CORE), lax.axis_index("seq") // 2
    state = grad = jnp.zeros((N, own_ref.shape[2]), F32)
    state_weight = grad_weight = jnp.ones((1, own_ref.shape[2]), F32)
    for r, ref in enumerate(others, 1):
        earlier = chip >= r
        state = jnp.where(earlier, state + state_weight * ref[:N, :], state)
        state_weight = state_weight * ref[N : N + 1, :]
    for r in range(1, chips):
        later = chip + r < chips
        ref = others[chips - r - 1]
        grad = jnp.where(later, grad + grad_weight * ref[:N, :], grad)
        grad_weight = grad_weight * ref[N : N + 1, :]
    carried_cores(core, state, grad, mine_ref, recv_ref, own_ref, peer_ref, slice(None))


def carried(chips, mine, recv, others):
    width = mine.shape[2]
    tile = min(512, width)
    pair = pl.BlockSpec((2, N + EXTRA, tile), lambda j: (0, 0, j))
    other = pl.BlockSpec((N + EXTRA, tile), lambda j: (0, j))
    out = pl.BlockSpec((2, N, tile), lambda j: (0, 0, j))
    shape = jax.ShapeDtypeStruct((2, N, width), F32)
    return pl.pallas_call(
        functools.partial(carried_kernel, chips),
        grid=(width // tile,),
        in_specs=[pair, pair] + [other] * len(others),
        out_specs=(out, out),
        out_shape=(shape, shape),
        compiler_params=PARAMS,
        name="carried_in",
        cost_estimate=pl.CostEstimate(flops=20 * N * width, bytes_accessed=44 * N * width, transcendentals=0),
    )(mine, recv, *others)


def blocks(chunks):
    span = 2
    while span < chunks:
        yield span, [at for at in range(span, chunks, 2 * span)]
        span *= 2


def row_bounds(chunks):
    middles = [k * SUB + SUB // 2 + 1 for k in range(chunks)]
    for span in [1] + [span for span, _ in blocks(chunks)]:
        for k, middle in enumerate(middles):
            boundary = (k // span + 1 - (k // span) % 2) * span * SUB
            yield min(boundary, middle), max(boundary, middle)
    yield from ((0, middle) for middle in middles)
    yield from ((middle, chunks * SUB) for middle in middles)


def local_factors(decays, lift_ref, drop_ref, rows_ref):
    local = decays.shape[1]
    logs = log_parts(decays)
    rows = lax.broadcasted_iota(jnp.int32, (LANES, LANES), 0)
    columns = lax.broadcasted_iota(jnp.int32, (LANES, LANES), 1)
    middle = (columns & -SUB) + SUB // 2
    later = (rows > middle) & (rows <= columns)
    sooner = (rows > columns) & (rows <= middle)
    offset = jnp.concatenate(block_sums(logs, later.astype(F32) - sooner.astype(F32)), axis=1)
    lift_ref[...] = by_token(jnp.exp(offset))
    drop_ref[...] = by_token(jnp.exp(-offset))
    lane = lax.broadcasted_iota(jnp.int32, (1, LANES), 1)
    first = last = jnp.zeros((1, LANES), jnp.int32)
    for i, (start, end) in enumerate(row_bounds(local // SUB)):
        first, last = jnp.where(lane == i, start, first), jnp.where(lane == i, end, last)
    rows = lax.broadcasted_iota(jnp.int32, (local, LANES), 0)
    decay = by_token(jnp.exp(summed_logs(logs, (rows >= first) & (rows < last))))
    rows_ref[...] = decay[: rows_ref.shape[0]]


def score_parts(b, c, ref, at, times, ahead=None):
    score = dot(b, c, NT)
    if ahead is not None:
        rows = lax.broadcasted_iota(jnp.int32, score.shape, 0)
        columns = lax.broadcasted_iota(jnp.int32, score.shape, 1)
        score = jnp.where(rows <= columns + ahead, score, 0.0)
    hi, lo = halves(score)
    width = score.shape[1]
    ref[at, :width] = hi
    ref[at, width : 2 * width] = lo
    if times == 3:
        ref[at, 2 * width :] = hi


def added_up(v):
    width = v.shape[1] // 2
    return v[:, :width] + v[:, width:]


def local_kernel(first_tile, continued, *refs):
    x_ref, dy_ref, b_ref, c_ref, decays_ref = refs[:5]
    refs = refs[5:]
    if continued:
        out_before_ref, map_before_ref = refs[:2]
        refs = refs[4:]
    part_ref, scaled_ref, out_ref, map_ref = refs[:4]
    lift_ref, drop_ref, rows_ref, full_ref, dys_ref, xs_ref, back_ref, sums_ref, even_ref, odd_ref = refs[4:14]
    level_refs = refs[14:]
    local, tile = x_ref.shape
    chunks = local // SUB
    step = pl.program_id(0)
    levels = [(span, at, level_refs[2 * i], level_refs[2 * i + 1]) for i, (span, at) in enumerate(blocks(chunks))]

    @pl.when(step == 0)
    def _():
        local_factors(decays_ref[...], lift_ref, drop_ref, rows_ref)
        sums_ref[...] = jnp.zeros(sums_ref.shape, F32)
        for k in range(0, chunks, 2):
            pair, even, odd = pl.ds(k * SUB, 2 * SUB), pl.ds(k * SUB, SUB), pl.ds((k + 1) * SUB, SUB)
            score_parts(b_ref[even, :], c_ref[even, :], even_ref, pl.ds(k // 2 * SUB, SUB), 3, 0)
            score_parts(b_ref[pair, :], c_ref[odd, :], odd_ref, pair, 3, SUB)
        for span, boundaries, mixed_ref, scores_ref in levels:
            mixed_ref[...] = jnp.zeros(mixed_ref.shape, F32)
            size = span * SUB
            for i, boundary in enumerate(boundaries):
                before, after = pl.ds((boundary - span) * SUB, size), pl.ds(boundary * SUB, size)
                score_parts(b_ref[before, :], c_ref[after, :], scores_ref, pl.ds(i * size, size), 2)

    first = (first_tile + step) * (tile // P_SIZE)
    dys_ref[...] = dy_ref[...].astype(F32) * spread(lift_ref[...], first, tile)
    back_ref[...] = spread(drop_ref[...], first, tile)
    xs_ref[...] = x_ref[...].astype(F32) * back_ref[...]
    row = spread(rows_ref[...], first, tile)
    factor = lambda kind, k: row[kind * chunks + k : kind * chunks + k + 1]

    for k in range(0, chunks, 2):
        even, odd, pair = pl.ds(k * SUB, SUB), pl.ds((k + 1) * SUB, SUB), pl.ds(k * SUB, 2 * SUB)
        dys, xs = halves(dys_ref[even, :]), halves(xs_ref[even, :])
        sums_ref[even, :] += dot(dys[0], stacked(*xs), NT)
        sums_ref[even, :SUB] += dot(dys[1], xs[0], NT)
        gained_even = dot(even_ref[pl.ds(k // 2 * SUB, SUB), :], stacked(dys[0], dys[0], dys[1]))
        crossing = halves((xs_ref[even, :] * factor(0, k)) * factor(0, k + 1))
        dys, xs = halves(dys_ref[odd, :]), halves(xs_ref[odd, :])
        high = stacked(xs[0], crossing[0])
        both = dot(dys[0], stacked(high, xs[1], crossing[1]), NT)
        sums_ref[odd, :] += added_up(both) + dot(dys[1], high, NT)
        gained_odd = dot(odd_ref[pair, :], stacked(dys[0], dys[0], dys[1]))
        ahead = (back_ref[even, :] * factor(0, k)) * (factor(0, k + 1) * gained_odd[:SUB])
        part_ref[even, :] = back_ref[even, :] * gained_even + ahead
        part_ref[odd, :] = back_ref[odd, :] * gained_odd[SUB:]

    for level, (span, boundaries, mixed_ref, scores_ref) in enumerate(levels, 1):
        size = span * SUB
        for i, boundary in enumerate(boundaries):
            at = pl.ds(i * size, size)
            take = lambda ref, start: halves(
                stacked(*[ref[k * SUB : (k + 1) * SUB, :] * factor(level, k) for k in range(start, start + span)])
            )
            dys, xs = take(dys_ref, boundary), take(xs_ref, boundary - span)
            both = dot(dys[0], stacked(*xs), NT)
            mixed_ref[at, :] += added_up(both) + dot(dys[1], xs[0], NT)
            gained = dot(scores_ref[at, :], stacked(dys[0], dys[0])) + dot(scores_ref[at, :size], dys[1])
            for q in range(span):
                k = boundary - span + q
                rows = pl.ds(k * SUB, SUB)
                part_ref[rows, :] += (back_ref[rows, :] * factor(level, k)) * gained[q * SUB : (q + 1) * SUB]

    for k in range(chunks):
        at = pl.ds(k * SUB, SUB)
        kind = len(levels) + 1
        scaled_ref[1, 0, at, :], scaled_ref[1, 1, at, :] = halves(dys_ref[at, :] * factor(kind, k))
        scaled_ref[0, 0, at, :], scaled_ref[0, 1, at, :] = halves(xs_ref[at, :] * factor(kind + 1, k))

    @pl.when(step == pl.num_programs(0) - 1)
    def _():
        full_ref[...] = jnp.zeros(full_ref.shape, F32)
        rows = lax.broadcasted_iota(jnp.int32, (SUB, SUB), 0)
        columns = lax.broadcasted_iota(jnp.int32, (SUB, SUB), 1)
        for k in range(0, chunks, 2):
            even, odd = pl.ds(k * SUB, SUB), pl.ds((k + 1) * SUB, SUB)
            full_ref[even, k * SUB : (k + 1) * SUB] = jnp.where(rows >= columns, added_up(sums_ref[even, :]), 0.0)
            full_ref[odd, (k + 1) * SUB : (k + 2) * SUB] = jnp.where(rows >= columns, sums_ref[odd, :SUB], 0.0)
            full_ref[odd, k * SUB : (k + 1) * SUB] = sums_ref[odd, SUB:]
        for span, boundaries, mixed_ref, _ in levels:
            size = span * SUB
            for i, boundary in enumerate(boundaries):
                block = mixed_ref[pl.ds(i * size, size), :]
                full_ref[pl.ds(boundary * SUB, size), (boundary - span) * SUB : boundary * SUB] = block
        map_ref[...] = map_before_ref[...] if continued else jnp.zeros(map_ref.shape, F32)
        for k in range(0, local, LANES):
            at = pl.ds(k, LANES)
            mixed = full_ref[at, :]
            gained = dot21(halves(mixed), b_ref[...])
            out_ref[at, :] = out_before_ref[at, :] + gained if continued else gained
            map_ref[...] += dot21(halves(mixed.T), c_ref[at, :])


def local_part(first_tile, count, x, dy, b, c, decays, before=None):
    local, width = x.shape
    chunks = local // SUB
    whole = lambda a: pl.BlockSpec(a.shape, lambda j: (0, 0))
    column = pl.BlockSpec((local, WIDE), lambda j: (0, first_tile + j))
    tokens = pl.BlockSpec((local, N), lambda j: (0, 0))
    scratch = [
        pltpu.VMEM((local, LANES), F32),
        pltpu.VMEM((local, LANES), F32),
        pltpu.VMEM((-(-len(list(row_bounds(chunks))) // 8) * 8, LANES), F32),
        pltpu.VMEM((local, local), F32),
        pltpu.VMEM((local, WIDE), F32),
        pltpu.VMEM((local, WIDE), F32),
        pltpu.VMEM((local, WIDE), F32),
        pltpu.VMEM((local, 2 * SUB), F32),
        pltpu.VMEM((local // 2, 3 * SUB), BF16),
        pltpu.VMEM((local, 3 * SUB), BF16),
    ]
    for span, _ in blocks(chunks):
        scratch.append(pltpu.VMEM((local // 2, span * SUB), F32))
        scratch.append(pltpu.VMEM((local // 2, 2 * span * SUB), BF16))
    in_specs = [column, column, whole(b), whole(c), whole(decays)]
    args, aliases = [x, dy, b, c, decays], {}
    if before is not None:
        part, scaled, out_part, map_part = before
        in_specs += [tokens, tokens, pl.BlockSpec(memory_space=pl.ANY), pl.BlockSpec(memory_space=pl.ANY)]
        args += [out_part, map_part, part, scaled]
        aliases = {7: 0, 8: 1}
    return pl.pallas_call(
        functools.partial(local_kernel, first_tile, before is not None),
        grid=(count,),
        in_specs=in_specs,
        out_specs=(column, pl.BlockSpec((2, 2, local, WIDE), lambda j: (0, 0, 0, first_tile + j)), tokens, tokens),
        out_shape=(
            jax.ShapeDtypeStruct((local, width), F32),
            jax.ShapeDtypeStruct((2, 2, local, width), BF16),
            jax.ShapeDtypeStruct((local, N), F32),
            jax.ShapeDtypeStruct((local, N), F32),
        ),
        scratch_shapes=scratch,
        input_output_aliases=aliases,
        compiler_params=PARAMS,
        name="local_part",
        cost_estimate=pl.CostEstimate(
            flops=40 * local * N * WIDE * count, bytes_accessed=8 * local * WIDE * count, transcendentals=0
        ),
    )(*args)


def map_kernel(count, ranks, scaled_ref, carry_ref, out_before_ref, map_before_ref, *refs):
    messages, (out_ref, map_ref) = refs[:-2], refs[-2:]
    step = pl.program_id(0)

    @pl.when(step == 0)
    def _():
        out_ref[...] = out_before_ref[...]
        map_ref[...] = map_before_ref[...]

    for i, sum_ref in enumerate((map_ref, out_ref)):
        carry = halves(carry_ref[1 - i])
        both = dot(scaled_ref[i, 0], stacked(*carry), NT)
        sum_ref[...] += both[:, :N] + (both[:, N:] + dot(scaled_ref[i, 1], carry[0], NT))

    if messages:

        @pl.when(step == count - 1)
        def _():
            rows = messages[0].shape[1]
            for r, message in enumerate(messages):
                at = pl.ds(pl.multiple_of(((lax.axis_index("head") + r) % ranks) * rows, rows), rows)
                message[0] = out_ref[at, :]
                message[1] = map_ref[at, :]


def map_terms(half, scaled, carry, out_before, map_before, ranks=0):
    local, width = scaled.shape[2], carry.shape[2]
    tile = min(WIDE, width)
    count = width // tile
    whole = lambda a: pl.BlockSpec(a.shape, lambda j: (0,) * len(a.shape))
    tokens = jax.ShapeDtypeStruct((local, N), F32)
    if ranks:
        out_shape = [jax.ShapeDtypeStruct((2, local // ranks, N), F32)] * ranks
        scratch = [pltpu.VMEM((local, N), F32), pltpu.VMEM((local, N), F32)]
    else:
        out_shape, scratch = [tokens, tokens], []
    return pl.pallas_call(
        functools.partial(map_kernel, count, ranks),
        grid=(count,),
        in_specs=[
            pl.BlockSpec((2, 2, local, tile), lambda j: (0, 0, 0, place(half) * count + j)),
            pl.BlockSpec((2, N, tile), lambda j: (0, 0, j)),
            whole(tokens),
            whole(tokens),
        ],
        out_specs=[whole(shape) for shape in out_shape],
        scratch_shapes=scratch,
        out_shape=out_shape,
        compiler_params=PARAMS,
        name="map_terms",
        cost_estimate=pl.CostEstimate(flops=12 * local * N * width, bytes_accessed=8 * local * width, transcendentals=0),
    )(scaled, carry, out_before, map_before)


def input_kernel(heads, count, part_ref, suf_ref, b_ref, own_ref, other_ref, input_ref):
    tile = part_ref.shape[1]
    step = pl.program_id(0)
    after = dot(suf_ref[...], spread_table(heads, step * (tile // P_SIZE), tile))
    grad = jnp.where(step // count == place(CORE), own_ref[0], other_ref[0])
    input_ref[...] = (part_ref[...] + after * dot12(b_ref[...], halves(grad))).astype(BF16)


def input_terms(part, factors, b, own, other):
    local, width = part.shape
    count = width // 2 // WIDE
    whole = lambda a: pl.BlockSpec(a.shape, lambda j: (0, 0))
    column = pl.BlockSpec((local, WIDE), lambda j: (0, j))
    carry = pl.BlockSpec((1, N, WIDE), lambda j: (1, 0, j % count))
    return pl.pallas_call(
        functools.partial(input_kernel, width // P_SIZE, count),
        grid=(2 * count,),
        in_specs=[column, pl.BlockSpec((local, LANES), lambda j: (0, 1)), whole(b), carry, carry],
        out_specs=column,
        out_shape=jax.ShapeDtypeStruct((local, width), BF16),
        compiler_params=PARAMS,
        name="input_terms",
        cost_estimate=pl.CostEstimate(flops=4 * local * N * width, bytes_accessed=8 * local * width, transcendentals=0),
    )(part, factors, b, own, other)


def sums_kernel(*refs):
    shares, (map_ref, out_ref) = refs[:-2], refs[-2:]
    for i, ref in enumerate((out_ref, map_ref)):
        ref[...] = functools.reduce(lambda a, b: a + b, [share[i] for share in shares])


def swap_cores(v, length):
    return lax.ppermute(v, "seq", [(i, i ^ 1) for i in range(length)])


def turned(v, axis, length, by):
    return lax.ppermute(v, axis, [(i, (i + by) % length) for i in range(length)])


def per_device(mixer_input, output_grad, input_map, output_map, decays):
    length, ranks = lax.axis_size("seq"), lax.axis_size("head")
    chips = length // 2
    args = mixer_input, output_grad, input_map, output_map
    sent, factors = other_totals(*args, decays)
    recv = swap_cores(sent, length)
    mine = own_totals(*args, factors)
    tiles = mixer_input.shape[1] // WIDE
    if chips == 4:
        ahead = tiles // 2
        own, back, *others, later = first_phase(length, mine, recv)
        result = local_part(0, ahead, *args, decays)
        others, result = lax.optimization_barrier((others, result))
        cross, same = second_phase(own, back, *others)
        crossing = [crossed(cross, length, 4), crossed(same, length, 2)]
        result, later, _, _ = lax.optimization_barrier((result, later, cross, same))
        result = local_part(ahead, tiles - ahead, *args, decays, result)
        others, result = lax.optimization_barrier((others + [later] + crossing, result))
        own, peer = carried4(mine, recv, *others)
    else:
        messages = chip_totals(chips, mine, recv)
        others = [turned(message, "seq", length, 2 * r) for r, message in enumerate(messages, 1)]
        result = local_part(0, tiles, *args, decays)
        own, peer = carried(chips, mine, recv, others)
    part, scaled, out_part, map_part = result
    other = swap_cores(peer, length)
    out_part, map_part = map_terms(CORE, scaled, own, out_part, map_part)
    shares = map_terms(OTHER, scaled, other, out_part, map_part, ranks)
    own, other, shares = lax.optimization_barrier((own, other, shares))
    sums = [shares[0]] + [turned(shares[r], "head", ranks, r) for r in range(1, ranks)]
    input_grad = input_terms(part, factors, input_map, own, other)
    shape = jax.ShapeDtypeStruct(shares[0].shape[1:], F32)
    input_map_grad, output_map_grad = plain_call(sums_kernel, "head_sums", [shape, shape], *sums)
    return input_grad, input_map_grad, output_map_grad


def solution(mesh):
    in_specs = (
        P("seq", "head"),
        P("seq", "head"),
        P("seq", None),
        P("seq", None),
        P("head", "seq"),
    )
    out_specs = (P("seq", "head"), P(("seq", "head"), None), P(("seq", "head"), None))
    return jax.shard_map(
        per_device, mesh=mesh, in_specs=in_specs, out_specs=out_specs, check_vma=False
    )
```

```python
import functools

import jax
import jax.numpy as jnp
from jax import lax
from jax.experimental import pallas as pl
from jax.experimental.pallas import tpu as pltpu
from jax.sharding import PartitionSpec as P

P_SIZE = 64
N = 128
SUB = 64
TILE = 256
WIDE = 512
EXTRA = 8
LANES = 128
CORE, OTHER = range(2)
PARAMS = pltpu.CompilerParams(vmem_limit_bytes=24 * 1024 * 1024)
FIRST = pltpu.CompilerParams(vmem_limit_bytes=60 * 1024 * 1024)
F32 = jnp.float32
BF16 = jnp.bfloat16

NN = (((1,), (0,)), ((), ()))
NT = (((1,), (1,)), ((), ()))


def dot(a, b, dims=NN):
    return lax.dot_general(a, b, dims, preferred_element_type=F32)


def halves(v):
    hi = v.astype(BF16)
    return hi, (v - hi.astype(F32)).astype(BF16)


def dot21(pair, b, dims=NN):
    return dot(pair[0], b, dims) + dot(pair[1], b, dims)


def dot12(a, pair, dims=NN):
    return dot(a, pair[0], dims) + dot(a, pair[1], dims)


def dot22(p, q, dims=NN):
    return dot(p[0], q[0], dims) + (dot(p[0], q[1], dims) + dot(p[1], q[0], dims))


def thirds(v):
    hi = v.astype(BF16)
    rest = v - hi.astype(F32)
    mid = rest.astype(BF16)
    return hi, mid, (rest - mid.astype(F32)).astype(BF16)


def spread(by_head, first, width):
    lanes = lax.broadcasted_iota(jnp.int32, by_head.shape, 1)
    step = LANES // P_SIZE
    shift = P_SIZE.bit_length() - 1
    taken = [
        jnp.take_along_axis(by_head, first + step * k + (lanes >> shift), axis=1) for k in range(width // LANES)
    ]
    return jnp.concatenate(taken, axis=1)


def place(half):
    core = lax.axis_index("seq") % 2
    return core if half == CORE else 1 - core


def stacked(*parts):
    return jnp.concatenate(parts, axis=0)


def transposed(v):
    return v.astype(F32).T.astype(BF16)


def log_parts(decays):
    return jnp.concatenate([part.astype(F32) for part in thirds(jnp.log(decays))], axis=0).astype(BF16)


def summed_logs(logs, table):
    heads = logs.shape[0] // 3
    sums = dot(logs, table.astype(F32).astype(BF16))
    return sums[:heads] + (sums[heads : 2 * heads] + sums[2 * heads :])


def block_sums(logs, table):
    blocks_of = [logs[:, k : k + LANES] for k in range(0, logs.shape[1], LANES)]
    return [summed_logs(block, table) for block in blocks_of]


def by_token(v):
    rest = jnp.zeros((LANES - v.shape[0], v.shape[1]), F32)
    return jnp.concatenate([v, rest], axis=0).T


def packed(v):
    parts = [part.astype(F32) for part in thirds(v)]
    rest = jnp.zeros((LANES - 3 * v.shape[0], v.shape[1]), F32)
    return jnp.concatenate(parts + [rest], axis=0).T.astype(BF16)


def spread_table(heads, first, width):
    rows = lax.broadcasted_iota(jnp.int32, (heads, width), 0)
    columns = lax.broadcasted_iota(jnp.int32, (heads, width), 1)
    offset = columns - (rows - first) * P_SIZE
    picked = ((offset >= 0) & (offset < P_SIZE)).astype(F32)
    rest = jnp.zeros((LANES - 3 * heads, width), F32)
    return jnp.concatenate([picked, picked, picked, rest], axis=0).astype(BF16)


def device_factors(decays, ref):
    logs = log_parts(decays)
    rows = lax.broadcasted_iota(jnp.int32, (LANES, LANES), 0)
    columns = lax.broadcasted_iota(jnp.int32, (LANES, LANES), 1)
    before, after = block_sums(logs, rows <= columns), block_sums(logs, rows > columns)
    totals_of = [block[:, LANES - 1 :] for block in before]
    ahead = behind = jnp.zeros(totals_of[0].shape, F32)
    for k, total in enumerate(totals_of):
        before[k] = before[k] + ahead
        ahead = ahead + total
    for k in reversed(range(len(totals_of))):
        after[k] = after[k] + behind
        behind = behind + totals_of[k]
    ref[:, :LANES] = packed(jnp.exp(jnp.concatenate(before, axis=1)))
    ref[:, LANES:] = packed(jnp.exp(jnp.concatenate(after, axis=1)))


def tile_totals(heads, first, x, dy, bt_ref, ct_ref, factor_ref, out_ref):
    tile = x.shape[1]
    table = spread_table(heads, first, tile)
    before = dot(factor_ref[:, :LANES], table)
    after = dot(factor_ref[:, LANES:], table)
    ended = jnp.broadcast_to(before[before.shape[0] - 1 :, :], (EXTRA, tile))
    for i, (source, factor, other) in enumerate(((x, after, bt_ref), (dy, before, ct_ref))):
        out_ref[i, :N, :] = dot12(other[...], halves(source.astype(F32) * factor))
        out_ref[i, N:, :] = ended


def totals_kernel(
    heads, x_ref, dy_ref, b_ref, c_ref, decays_ref, other_ref, own_ref, factor_ref,
    x_buf, dy_buf, out_buf, b_buf, c_buf, decays_buf, bt_ref, ct_ref, arrived, small, sent,
):
    tiles, _, tile = x_buf.shape
    count = tiles // 2
    smalls = [
        pltpu.make_async_copy(source, buf, small.at[i])
        for i, (source, buf) in enumerate(((decays_ref, decays_buf), (b_ref, b_buf), (c_ref, c_buf)))
    ]
    for load in smalls:
        load.start()
    first_tile = [place(half) * count + k for half in (OTHER, CORE) for k in range(count)]
    loads = []
    for k in range(tiles):
        columns = pl.ds(pl.multiple_of(first_tile[k] * tile, tile), tile)
        for i, (source, buf) in enumerate(((x_ref, x_buf), (dy_ref, dy_buf))):
            loads.append(pltpu.make_async_copy(source.at[:, columns], buf.at[k], arrived.at[i, k]))
            loads[-1].start()
    smalls[0].wait()
    device_factors(decays_buf[...], factor_ref)
    smalls[1].wait()
    smalls[2].wait()
    bt_ref[...] = transposed(b_buf[...])
    ct_ref[...] = transposed(c_buf[...])
    stores = []
    for k in range(tiles):
        loads[2 * k].wait()
        loads[2 * k + 1].wait()
        first = first_tile[k] * (tile // P_SIZE)
        tile_totals(heads, first, x_buf[k], dy_buf[k], bt_ref, ct_ref, factor_ref, out_buf.at[k])
        target = own_ref if k >= count else other_ref
        columns = pl.ds(k % count * tile, tile)
        stores.append(pltpu.make_async_copy(out_buf.at[k], target.at[:, :, columns], sent.at[k]))
        stores[-1].start()
    for store in stores:
        store.wait()


def totals(x, dy, b, c, decays):
    local, width = x.shape
    tiles = width // TILE
    anywhere = pl.BlockSpec(memory_space=pl.ANY)
    factor = jax.ShapeDtypeStruct((local, 2 * LANES), BF16)
    half = jax.ShapeDtypeStruct((2, N + EXTRA, width // 2), F32)
    return pl.pallas_call(
        functools.partial(totals_kernel, width // P_SIZE),
        grid=(1,),
        in_specs=[anywhere] * 5,
        out_specs=[anywhere, anywhere, pl.BlockSpec(factor.shape, lambda j: (0, 0))],
        out_shape=[half, half, factor],
        scratch_shapes=[
            pltpu.VMEM((tiles, local, TILE), BF16),
            pltpu.VMEM((tiles, local, TILE), BF16),
            pltpu.VMEM((tiles, 2, N + EXTRA, TILE), F32),
            pltpu.VMEM(b.shape, BF16),
            pltpu.VMEM(c.shape, BF16),
            pltpu.VMEM(decays.shape, F32),
            pltpu.VMEM((N, local), BF16),
            pltpu.VMEM((N, local), BF16),
            pltpu.SemaphoreType.DMA((2, tiles)),
            pltpu.SemaphoreType.DMA((3,)),
            pltpu.SemaphoreType.DMA((tiles,)),
        ],
        compiler_params=FIRST,
        name="state_totals",
        cost_estimate=pl.CostEstimate(flops=8 * local * N * width, bytes_accessed=4 * local * width, transcendentals=0),
    )(x, dy, b, c, decays)


def ordered(core, mine, recv):
    return jnp.where(core == 0, mine, recv), jnp.where(core == 0, recv, mine)


def chip_kernel(chips, mine_ref, recv_ref, *out_refs):
    core, chip = place(CORE), lax.axis_index("seq") // 2
    early, late = ordered(core, mine_ref[0], recv_ref[0])
    early_decay, late_decay = early[N : N + 1], late[N : N + 1]
    both = jnp.broadcast_to(early_decay * late_decay, (EXTRA, early.shape[1]))
    state = late_decay * early[:N] + late[:N]
    early, late = ordered(core, mine_ref[1], recv_ref[1])
    grad = early[:N] + early_decay * late[:N]
    for r, out_ref in enumerate(out_refs, 1):
        out_ref[:N, :] = jnp.where(chip + r < chips, state, grad)
        out_ref[N:, :] = both


def chip_totals(chips, mine, recv):
    width = mine.shape[2]
    tile = min(512, width)
    block = pl.BlockSpec((2, N + EXTRA, tile), lambda j: (0, 0, j))
    out = pl.BlockSpec((N + EXTRA, tile), lambda j: (0, j))
    shape = jax.ShapeDtypeStruct((N + EXTRA, width), F32)
    return pl.pallas_call(
        functools.partial(chip_kernel, chips),
        grid=(width // tile,),
        in_specs=[block, block],
        out_specs=[out] * (chips - 1),
        out_shape=[shape] * (chips - 1),
        compiler_params=PARAMS,
        name="chip_totals",
        cost_estimate=pl.CostEstimate(flops=6 * N * width, bytes_accessed=24 * N * width, transcendentals=0),
    )(mine, recv)


def sides():
    chip = lax.axis_index("seq") // 2
    return chip < 2, (chip == 1) | (chip == 2)


def first_kernel(mine_ref, recv_ref, same_ref, later_ref, cross_ref, back_ref, decay_ref):
    left, inner = sides()
    core = place(CORE)
    width = mine_ref.shape[2] // 2
    early, late = ordered(core, mine_ref[0], recv_ref[0])
    early_decay, late_decay = early[N : N + 1], late[N : N + 1]
    state = late_decay * early[:N] + late[:N]
    decay = early_decay * late_decay
    early, late = ordered(core, mine_ref[1], recv_ref[1])
    grad = early[:N] + early_decay * late[:N]
    out, back = jnp.where(left, state, grad), jnp.where(left, grad, state)
    same_ref[:N, :] = out[:, :width]
    later_ref[...] = jnp.where(inner, back[:, :width], out[:, width:])
    rows = lax.broadcasted_iota(jnp.int32, (EXTRA, width), 0)
    same_ref[N:, :] = jnp.where(rows == 0, decay[:, :width], decay[:, width:])
    cross_ref[...] = out[:, width:]
    back_ref[...] = back[:, width:]
    decay_ref[...] = jnp.broadcast_to(decay[:, width:], (EXTRA, width))


def second_kernel(own_ref, back_ref, same_ref, cross_ref, decay_ref, cross2_ref, same2_ref):
    _, inner = sides()
    own, other = own_ref[:N, :], same_ref[:N, :]
    own_decay, other_decay = own_ref[N : N + 1, :], same_ref[N : N + 1, :]
    cross2_ref[...] = jnp.where(inner, own + own_decay * other, other + other_decay * own)
    weight = own_ref[N + 1 : N + 2, :] * decay_ref[:1, :]
    same2_ref[...] = jnp.where(inner, back_ref[...] + weight * cross_ref[...], cross_ref[...])


def plain_call(kernel, name, out_shape, *args):
    whole = lambda a: pl.BlockSpec(a.shape, lambda j: (0,) * len(a.shape))
    size = sum(a.size for a in args)
    return pl.pallas_call(
        kernel,
        grid=(1,),
        in_specs=[whole(a) for a in args],
        out_specs=[whole(a) for a in out_shape],
        out_shape=out_shape,
        compiler_params=PARAMS,
        name=name,
        cost_estimate=pl.CostEstimate(flops=8 * size, bytes_accessed=4 * size, transcendentals=0),
    )(*args)


def crossed(v, length, bit):
    return lax.ppermute(v, "seq", [(i, i ^ bit) for i in range(length)])


def copy_kernel(from_ref, to_ref):
    to_ref[...] = from_ref[...]


def nearer(v):
    tile = min(WIDE, v.shape[2])
    block = pl.BlockSpec((2, N + EXTRA, tile), lambda j: (0, 0, j))
    return pl.pallas_call(
        copy_kernel,
        grid=(v.shape[2] // tile,),
        in_specs=[block],
        out_specs=block,
        out_shape=jax.ShapeDtypeStruct(v.shape, F32),
        compiler_params=PARAMS,
        name="nearer",
        cost_estimate=pl.CostEstimate(flops=v.size, bytes_accessed=8 * v.size, transcendentals=0),
    )(v)


def first_phase(length, mine, recv):
    half = mine.shape[2] // 2
    shapes = [jax.ShapeDtypeStruct((rows, half), F32) for rows in (N + EXTRA, N, N, N, EXTRA)]
    own, later, cross, back, decay = plain_call(first_kernel, "first_messages", shapes, mine, recv)
    same, cross, decay = crossed(own, length, 2), crossed(cross, length, 4), crossed(decay, length, 6)
    return own, back, same, cross, decay, crossed(later, length, 2)


def second_phase(own, back, same, cross, decay):
    shape = jax.ShapeDtypeStruct(back.shape, F32)
    return plain_call(second_kernel, "second_messages", [shape, shape], own, back, same, cross, decay)


def carried4_kernel(
    mine_ref, recv_ref, same_ref, cross_ref, decay_ref, later_ref, cross2_ref, same2_ref, own_ref, peer_ref
):
    left, inner = sides()
    width = cross_ref.shape[1]
    decay_a, decay_b = same_ref[N : N + 1, :], same_ref[N + 1 : N + 2, :]
    for part in range(2):
        at = slice(part * width, (part + 1) * width)
        out = jnp.where(inner, later_ref[...] if part else same_ref[:N, :], 0.0)
        if part == 0:
            back = jnp.where(inner, cross2_ref[...], later_ref[...] + decay_a * cross2_ref[...])
        else:
            back = same2_ref[...] + jnp.where(inner, decay_ref[:1, :], decay_b) * cross_ref[...]
        carried_cores(
            place(CORE), jnp.where(left, out, back), jnp.where(left, back, out), mine_ref, recv_ref, own_ref, peer_ref, at
        )


def carried4(mine, recv, *others):
    shape = jax.ShapeDtypeStruct((2, N, mine.shape[2]), F32)
    return plain_call(carried4_kernel, "carried_in", [shape, shape], mine, recv, *others)


def carried_cores(core, state, grad, mine_ref, recv_ref, own_ref, peer_ref, at):
    early, late = ordered(core, mine_ref[0, :, at], recv_ref[0, :, at])
    at_late = early[N : N + 1] * state + early[:N]
    own_ref[0, :, at] = jnp.where(core == 0, state, at_late)
    peer_ref[0, :, at] = jnp.where(core == 0, at_late, state)
    early, late = ordered(core, mine_ref[1, :, at], recv_ref[1, :, at])
    at_early = late[:N] + late[N : N + 1] * grad
    own_ref[1, :, at] = jnp.where(core == 0, at_early, grad)
    peer_ref[1, :, at] = jnp.where(core == 0, grad, at_early)


def carried_kernel(chips, mine_ref, recv_ref, *refs):
    others, (own_ref, peer_ref) = refs[:-2], refs[-2:]
    core, chip = place(CORE), lax.axis_index("seq") // 2
    state = grad = jnp.zeros((N, own_ref.shape[2]), F32)
    state_weight = grad_weight = jnp.ones((1, own_ref.shape[2]), F32)
    for r, ref in enumerate(others, 1):
        earlier = chip >= r
        state = jnp.where(earlier, state + state_weight * ref[:N, :], state)
        state_weight = state_weight * ref[N : N + 1, :]
    for r in range(1, chips):
        later = chip + r < chips
        ref = others[chips - r - 1]
        grad = jnp.where(later, grad + grad_weight * ref[:N, :], grad)
        grad_weight = grad_weight * ref[N : N + 1, :]
    carried_cores(core, state, grad, mine_ref, recv_ref, own_ref, peer_ref, slice(None))


def carried(chips, mine, recv, others):
    width = mine.shape[2]
    tile = min(512, width)
    pair = pl.BlockSpec((2, N + EXTRA, tile), lambda j: (0, 0, j))
    other = pl.BlockSpec((N + EXTRA, tile), lambda j: (0, j))
    out = pl.BlockSpec((2, N, tile), lambda j: (0, 0, j))
    shape = jax.ShapeDtypeStruct((2, N, width), F32)
    return pl.pallas_call(
        functools.partial(carried_kernel, chips),
        grid=(width // tile,),
        in_specs=[pair, pair] + [other] * len(others),
        out_specs=(out, out),
        out_shape=(shape, shape),
        compiler_params=PARAMS,
        name="carried_in",
        cost_estimate=pl.CostEstimate(flops=20 * N * width, bytes_accessed=44 * N * width, transcendentals=0),
    )(mine, recv, *others)


def blocks(chunks):
    span = 2
    while span < chunks:
        yield span, [at for at in range(span, chunks, 2 * span)]
        span *= 2


def row_bounds(chunks):
    middles = [k * SUB + SUB // 2 + 1 for k in range(chunks)]
    for span in [1] + [span for span, _ in blocks(chunks)]:
        for k, middle in enumerate(middles):
            boundary = (k // span + 1 - (k // span) % 2) * span * SUB
            yield min(boundary, middle), max(boundary, middle)
    yield from ((0, middle) for middle in middles)
    yield from ((middle, chunks * SUB) for middle in middles)


def local_factors(decays, lift_ref, drop_ref, rows_ref):
    local = decays.shape[1]
    logs = log_parts(decays)
    rows = lax.broadcasted_iota(jnp.int32, (LANES, LANES), 0)
    columns = lax.broadcasted_iota(jnp.int32, (LANES, LANES), 1)
    middle = (columns & -SUB) + SUB // 2
    later = (rows > middle) & (rows <= columns)
    sooner = (rows > columns) & (rows <= middle)
    offset = jnp.concatenate(block_sums(logs, later.astype(F32) - sooner.astype(F32)), axis=1)
    lift_ref[...] = by_token(jnp.exp(offset))
    drop_ref[...] = by_token(jnp.exp(-offset))
    lane = lax.broadcasted_iota(jnp.int32, (1, LANES), 1)
    first = last = jnp.zeros((1, LANES), jnp.int32)
    for i, (start, end) in enumerate(row_bounds(local // SUB)):
        first, last = jnp.where(lane == i, start, first), jnp.where(lane == i, end, last)
    rows = lax.broadcasted_iota(jnp.int32, (local, LANES), 0)
    decay = by_token(jnp.exp(summed_logs(logs, (rows >= first) & (rows < last))))
    rows_ref[...] = decay[: rows_ref.shape[0]]


def score_parts(b, c, ref, at, times, ahead=None):
    score = dot(b, c, NT)
    if ahead is not None:
        rows = lax.broadcasted_iota(jnp.int32, score.shape, 0)
        columns = lax.broadcasted_iota(jnp.int32, score.shape, 1)
        score = jnp.where(rows <= columns + ahead, score, 0.0)
    hi, lo = halves(score)
    width = score.shape[1]
    ref[at, :width] = hi
    ref[at, width : 2 * width] = lo
    if times == 3:
        ref[at, 2 * width :] = hi


def added_up(v):
    width = v.shape[1] // 2
    return v[:, :width] + v[:, width:]


def local_kernel(first_tile, continued, *refs):
    x_ref, dy_ref, b_ref, c_ref, decays_ref = refs[:5]
    refs = refs[5:]
    if continued:
        out_before_ref, map_before_ref = refs[:2]
        refs = refs[4:]
    part_ref, scaled_ref, out_ref, map_ref = refs[:4]
    lift_ref, drop_ref, rows_ref, full_ref, dys_ref, xs_ref, back_ref, sums_ref, even_ref, odd_ref = refs[4:14]
    level_refs = refs[14:]
    local, tile = x_ref.shape
    chunks = local // SUB
    step = pl.program_id(0)
    levels = [(span, at, level_refs[2 * i], level_refs[2 * i + 1]) for i, (span, at) in enumerate(blocks(chunks))]

    @pl.when(step == 0)
    def _():
        local_factors(decays_ref[...], lift_ref, drop_ref, rows_ref)
        sums_ref[...] = jnp.zeros(sums_ref.shape, F32)
        for k in range(0, chunks, 2):
            pair, even, odd = pl.ds(k * SUB, 2 * SUB), pl.ds(k * SUB, SUB), pl.ds((k + 1) * SUB, SUB)
            score_parts(b_ref[even, :], c_ref[even, :], even_ref, pl.ds(k // 2 * SUB, SUB), 3, 0)
            score_parts(b_ref[pair, :], c_ref[odd, :], odd_ref, pair, 3, SUB)
        for span, boundaries, mixed_ref, scores_ref in levels:
            mixed_ref[...] = jnp.zeros(mixed_ref.shape, F32)
            size = span * SUB
            for i, boundary in enumerate(boundaries):
                before, after = pl.ds((boundary - span) * SUB, size), pl.ds(boundary * SUB, size)
                score_parts(b_ref[before, :], c_ref[after, :], scores_ref, pl.ds(i * size, size), 2)

    first = (first_tile + step) * (tile // P_SIZE)
    dys_ref[...] = dy_ref[...].astype(F32) * spread(lift_ref[...], first, tile)
    back_ref[...] = spread(drop_ref[...], first, tile)
    xs_ref[...] = x_ref[...].astype(F32) * back_ref[...]
    row = spread(rows_ref[...], first, tile)
    factor = lambda kind, k: row[kind * chunks + k : kind * chunks + k + 1]

    for k in range(0, chunks, 2):
        even, odd, pair = pl.ds(k * SUB, SUB), pl.ds((k + 1) * SUB, SUB), pl.ds(k * SUB, 2 * SUB)
        dys, xs = halves(dys_ref[even, :]), halves(xs_ref[even, :])
        sums_ref[even, :] += dot(dys[0], stacked(*xs), NT)
        sums_ref[even, :SUB] += dot(dys[1], xs[0], NT)
        gained_even = dot(even_ref[pl.ds(k // 2 * SUB, SUB), :], stacked(dys[0], dys[0], dys[1]))
        crossing = halves((xs_ref[even, :] * factor(0, k)) * factor(0, k + 1))
        dys, xs = halves(dys_ref[odd, :]), halves(xs_ref[odd, :])
        high = stacked(xs[0], crossing[0])
        both = dot(dys[0], stacked(high, xs[1], crossing[1]), NT)
        sums_ref[odd, :] += added_up(both) + dot(dys[1], high, NT)
        gained_odd = dot(odd_ref[pair, :], stacked(dys[0], dys[0], dys[1]))
        ahead = (back_ref[even, :] * factor(0, k)) * (factor(0, k + 1) * gained_odd[:SUB])
        part_ref[even, :] = back_ref[even, :] * gained_even + ahead
        part_ref[odd, :] = back_ref[odd, :] * gained_odd[SUB:]

    for level, (span, boundaries, mixed_ref, scores_ref) in enumerate(levels, 1):
        size = span * SUB
        for i, boundary in enumerate(boundaries):
            at = pl.ds(i * size, size)
            take = lambda ref, start: halves(
                stacked(*[ref[k * SUB : (k + 1) * SUB, :] * factor(level, k) for k in range(start, start + span)])
            )
            dys, xs = take(dys_ref, boundary), take(xs_ref, boundary - span)
            both = dot(dys[0], stacked(*xs), NT)
            mixed_ref[at, :] += added_up(both) + dot(dys[1], xs[0], NT)
            gained = dot(scores_ref[at, :], stacked(dys[0], dys[0])) + dot(scores_ref[at, :size], dys[1])
            for q in range(span):
                k = boundary - span + q
                rows = pl.ds(k * SUB, SUB)
                part_ref[rows, :] += (back_ref[rows, :] * factor(level, k)) * gained[q * SUB : (q + 1) * SUB]

    for k in range(chunks):
        at = pl.ds(k * SUB, SUB)
        kind = len(levels) + 1
        scaled_ref[1, 0, at, :], scaled_ref[1, 1, at, :] = halves(dys_ref[at, :] * factor(kind, k))
        scaled_ref[0, 0, at, :], scaled_ref[0, 1, at, :] = halves(xs_ref[at, :] * factor(kind + 1, k))

    @pl.when(step == pl.num_programs(0) - 1)
    def _():
        full_ref[...] = jnp.zeros(full_ref.shape, F32)
        rows = lax.broadcasted_iota(jnp.int32, (SUB, SUB), 0)
        columns = lax.broadcasted_iota(jnp.int32, (SUB, SUB), 1)
        for k in range(0, chunks, 2):
            even, odd = pl.ds(k * SUB, SUB), pl.ds((k + 1) * SUB, SUB)
            full_ref[even, k * SUB : (k + 1) * SUB] = jnp.where(rows >= columns, added_up(sums_ref[even, :]), 0.0)
            full_ref[odd, (k + 1) * SUB : (k + 2) * SUB] = jnp.where(rows >= columns, sums_ref[odd, :SUB], 0.0)
            full_ref[odd, k * SUB : (k + 1) * SUB] = sums_ref[odd, SUB:]
        for span, boundaries, mixed_ref, _ in levels:
            size = span * SUB
            for i, boundary in enumerate(boundaries):
                block = mixed_ref[pl.ds(i * size, size), :]
                full_ref[pl.ds(boundary * SUB, size), (boundary - span) * SUB : boundary * SUB] = block
        map_ref[...] = map_before_ref[...] if continued else jnp.zeros(map_ref.shape, F32)
        for k in range(0, local, LANES):
            at = pl.ds(k, LANES)
            mixed = full_ref[at, :]
            gained = dot21(halves(mixed), b_ref[...])
            out_ref[at, :] = out_before_ref[at, :] + gained if continued else gained
            map_ref[...] += dot21(halves(mixed.T), c_ref[at, :])


def local_part(first_tile, count, x, dy, b, c, decays, before=None):
    local, width = x.shape
    chunks = local // SUB
    whole = lambda a: pl.BlockSpec(a.shape, lambda j: (0, 0))
    column = pl.BlockSpec((local, WIDE), lambda j: (0, first_tile + j))
    tokens = pl.BlockSpec((local, N), lambda j: (0, 0))
    scratch = [
        pltpu.VMEM((local, LANES), F32),
        pltpu.VMEM((local, LANES), F32),
        pltpu.VMEM((-(-len(list(row_bounds(chunks))) // 8) * 8, LANES), F32),
        pltpu.VMEM((local, local), F32),
        pltpu.VMEM((local, WIDE), F32),
        pltpu.VMEM((local, WIDE), F32),
        pltpu.VMEM((local, WIDE), F32),
        pltpu.VMEM((local, 2 * SUB), F32),
        pltpu.VMEM((local // 2, 3 * SUB), BF16),
        pltpu.VMEM((local, 3 * SUB), BF16),
    ]
    for span, _ in blocks(chunks):
        scratch.append(pltpu.VMEM((local // 2, span * SUB), F32))
        scratch.append(pltpu.VMEM((local // 2, 2 * span * SUB), BF16))
    in_specs = [column, column, whole(b), whole(c), whole(decays)]
    args, aliases = [x, dy, b, c, decays], {}
    if before is not None:
        part, scaled, out_part, map_part = before
        in_specs += [tokens, tokens, pl.BlockSpec(memory_space=pl.ANY), pl.BlockSpec(memory_space=pl.ANY)]
        args += [out_part, map_part, part, scaled]
        aliases = {7: 0, 8: 1}
    return pl.pallas_call(
        functools.partial(local_kernel, first_tile, before is not None),
        grid=(count,),
        in_specs=in_specs,
        out_specs=(column, pl.BlockSpec((2, 2, local, WIDE), lambda j: (0, 0, 0, first_tile + j)), tokens, tokens),
        out_shape=(
            jax.ShapeDtypeStruct((local, width), F32),
            jax.ShapeDtypeStruct((2, 2, local, width), BF16),
            jax.ShapeDtypeStruct((local, N), F32),
            jax.ShapeDtypeStruct((local, N), F32),
        ),
        scratch_shapes=scratch,
        input_output_aliases=aliases,
        compiler_params=PARAMS,
        name="local_part",
        cost_estimate=pl.CostEstimate(
            flops=40 * local * N * WIDE * count, bytes_accessed=8 * local * WIDE * count, transcendentals=0
        ),
    )(*args)


def map_kernel(count, ranks, scaled_ref, carry_ref, out_before_ref, map_before_ref, *refs):
    messages, (out_ref, map_ref) = refs[:-2], refs[-2:]
    step = pl.program_id(0)

    @pl.when(step == 0)
    def _():
        out_ref[...] = out_before_ref[...]
        map_ref[...] = map_before_ref[...]

    for i, sum_ref in enumerate((map_ref, out_ref)):
        carry = halves(carry_ref[1 - i])
        both = dot(scaled_ref[i, 0], stacked(*carry), NT)
        sum_ref[...] += both[:, :N] + (both[:, N:] + dot(scaled_ref[i, 1], carry[0], NT))

    if messages:

        @pl.when(step == count - 1)
        def _():
            rows = messages[0].shape[1]
            for r, message in enumerate(messages):
                at = pl.ds(pl.multiple_of(((lax.axis_index("head") + r) % ranks) * rows, rows), rows)
                message[0] = out_ref[at, :]
                message[1] = map_ref[at, :]


def map_terms(half, scaled, carry, out_before, map_before, ranks=0):
    local, width = scaled.shape[2], carry.shape[2]
    tile = min(WIDE, width)
    count = width // tile
    whole = lambda a: pl.BlockSpec(a.shape, lambda j: (0,) * len(a.shape))
    tokens = jax.ShapeDtypeStruct((local, N), F32)
    if ranks:
        out_shape = [jax.ShapeDtypeStruct((2, local // ranks, N), F32)] * ranks
        scratch = [pltpu.VMEM((local, N), F32), pltpu.VMEM((local, N), F32)]
    else:
        out_shape, scratch = [tokens, tokens], []
    return pl.pallas_call(
        functools.partial(map_kernel, count, ranks),
        grid=(count,),
        in_specs=[
            pl.BlockSpec((2, 2, local, tile), lambda j: (0, 0, 0, place(half) * count + j)),
            pl.BlockSpec((2, N, tile), lambda j: (0, 0, j)),
            whole(tokens),
            whole(tokens),
        ],
        out_specs=[whole(shape) for shape in out_shape],
        scratch_shapes=scratch,
        out_shape=out_shape,
        compiler_params=PARAMS,
        name="map_terms",
        cost_estimate=pl.CostEstimate(flops=12 * local * N * width, bytes_accessed=8 * local * width, transcendentals=0),
    )(scaled, carry, out_before, map_before)


def input_kernel(heads, count, part_ref, suf_ref, b_ref, own_ref, other_ref, input_ref):
    tile = part_ref.shape[1]
    step = pl.program_id(0)
    after = dot(suf_ref[...], spread_table(heads, step * (tile // P_SIZE), tile))
    grad = jnp.where(step // count == place(CORE), own_ref[0], other_ref[0])
    input_ref[...] = (part_ref[...] + after * dot12(b_ref[...], halves(grad))).astype(BF16)


def input_terms(part, factors, b, own, other):
    local, width = part.shape
    count = width // 2 // WIDE
    whole = lambda a: pl.BlockSpec(a.shape, lambda j: (0, 0))
    column = pl.BlockSpec((local, WIDE), lambda j: (0, j))
    carry = pl.BlockSpec((1, N, WIDE), lambda j: (1, 0, j % count))
    return pl.pallas_call(
        functools.partial(input_kernel, width // P_SIZE, count),
        grid=(2 * count,),
        in_specs=[column, pl.BlockSpec((local, LANES), lambda j: (0, 1)), whole(b), carry, carry],
        out_specs=column,
        out_shape=jax.ShapeDtypeStruct((local, width), BF16),
        compiler_params=PARAMS,
        name="input_terms",
        cost_estimate=pl.CostEstimate(flops=4 * local * N * width, bytes_accessed=8 * local * width, transcendentals=0),
    )(part, factors, b, own, other)


def sums_kernel(*refs):
    shares, (map_ref, out_ref) = refs[:-2], refs[-2:]
    for i, ref in enumerate((out_ref, map_ref)):
        ref[...] = functools.reduce(lambda a, b: a + b, [share[i] for share in shares])


def swap_cores(v, length):
    return lax.ppermute(v, "seq", [(i, i ^ 1) for i in range(length)])


def turned(v, axis, length, by):
    return lax.ppermute(v, axis, [(i, (i + by) % length) for i in range(length)])


def per_device(mixer_input, output_grad, input_map, output_map, decays):
    length, ranks = lax.axis_size("seq"), lax.axis_size("head")
    chips = length // 2
    args = mixer_input, output_grad, input_map, output_map
    sent, mine, factors = totals(*args, decays)
    recv = swap_cores(sent, length)
    mine = nearer(mine)
    tiles = mixer_input.shape[1] // WIDE
    if chips == 4:
        ahead = tiles // 2
        own, back, *others, later = first_phase(length, mine, recv)
        result = local_part(0, ahead, *args, decays)
        others, result = lax.optimization_barrier((others, result))
        cross, same = second_phase(own, back, *others)
        crossing = [crossed(cross, length, 4), crossed(same, length, 2)]
        result, later, _, _ = lax.optimization_barrier((result, later, cross, same))
        result = local_part(ahead, tiles - ahead, *args, decays, result)
        others, result = lax.optimization_barrier((others + [later] + crossing, result))
        own, peer = carried4(mine, recv, *others)
    else:
        messages = chip_totals(chips, mine, recv)
        others = [turned(message, "seq", length, 2 * r) for r, message in enumerate(messages, 1)]
        result = local_part(0, tiles, *args, decays)
        own, peer = carried(chips, mine, recv, others)
    part, scaled, out_part, map_part = result
    other = swap_cores(peer, length)
    out_part, map_part = map_terms(CORE, scaled, own, out_part, map_part)
    shares = map_terms(OTHER, scaled, other, out_part, map_part, ranks)
    own, other, shares = lax.optimization_barrier((own, other, shares))
    sums = [shares[0]] + [turned(shares[r], "head", ranks, r) for r in range(1, ranks)]
    input_grad = input_terms(part, factors, input_map, own, other)
    shape = jax.ShapeDtypeStruct(shares[0].shape[1:], F32)
    input_map_grad, output_map_grad = plain_call(sums_kernel, "head_sums", [shape, shape], *sums)
    return input_grad, input_map_grad, output_map_grad


def solution(mesh):
    in_specs = (
        P("seq", "head"),
        P("seq", "head"),
        P("seq", None),
        P("seq", None),
        P("head", "seq"),
    )
    out_specs = (P("seq", "head"), P(("seq", "head"), None), P(("seq", "head"), None))
    return jax.shard_map(
        per_device, mesh=mesh, in_specs=in_specs, out_specs=out_specs, check_vma=False
    )
```

```python
import functools

import jax
import jax.numpy as jnp
from jax import lax
from jax.experimental import pallas as pl
from jax.experimental.pallas import tpu as pltpu
from jax.sharding import PartitionSpec as P

P_SIZE = 64
N = 128
SUB = 64
TILE = 256
WIDE = 512
EXTRA = 8
PARTS = 4
LANES = 128
CORE, OTHER = range(2)
PARAMS = pltpu.CompilerParams(vmem_limit_bytes=24 * 1024 * 1024)
FIRST = pltpu.CompilerParams(vmem_limit_bytes=56 * 1024 * 1024)
F32 = jnp.float32
BF16 = jnp.bfloat16

NN = (((1,), (0,)), ((), ()))
NT = (((1,), (1,)), ((), ()))


def dot(a, b, dims=NN):
    return lax.dot_general(a, b, dims, preferred_element_type=F32)


def halves(v):
    hi = v.astype(BF16)
    return hi, (v - hi.astype(F32)).astype(BF16)


def dot21(pair, b, dims=NN):
    return dot(pair[0], b, dims) + dot(pair[1], b, dims)


def dot12(a, pair, dims=NN):
    return dot(a, pair[0], dims) + dot(a, pair[1], dims)


def dot22(p, q, dims=NN):
    return dot(p[0], q[0], dims) + (dot(p[0], q[1], dims) + dot(p[1], q[0], dims))


def thirds(v):
    hi = v.astype(BF16)
    rest = v - hi.astype(F32)
    mid = rest.astype(BF16)
    return hi, mid, (rest - mid.astype(F32)).astype(BF16)


def spread(by_head, first, width):
    lanes = lax.broadcasted_iota(jnp.int32, by_head.shape, 1)
    step = LANES // P_SIZE
    shift = P_SIZE.bit_length() - 1
    taken = [
        jnp.take_along_axis(by_head, first + step * k + (lanes >> shift), axis=1) for k in range(width // LANES)
    ]
    return jnp.concatenate(taken, axis=1)


def place(half):
    core = lax.axis_index("seq") % 2
    return core if half == CORE else 1 - core


def stacked(*parts):
    return jnp.concatenate(parts, axis=0)


def transposed(v):
    return v.astype(F32).T.astype(BF16)


def log_parts(decays):
    return jnp.concatenate([part.astype(F32) for part in thirds(jnp.log(decays))], axis=0).astype(BF16)


def summed_logs(logs, table):
    heads = logs.shape[0] // 3
    sums = dot(logs, table.astype(F32).astype(BF16))
    return sums[:heads] + (sums[heads : 2 * heads] + sums[2 * heads :])


def block_sums(logs, table):
    blocks_of = [logs[:, k : k + LANES] for k in range(0, logs.shape[1], LANES)]
    return [summed_logs(block, table) for block in blocks_of]


def by_token(v):
    rest = jnp.zeros((LANES - v.shape[0], v.shape[1]), F32)
    return jnp.concatenate([v, rest], axis=0).T


def packed(v):
    parts = [part.astype(F32) for part in thirds(v)]
    rest = jnp.zeros((LANES - 3 * v.shape[0], v.shape[1]), F32)
    return jnp.concatenate(parts + [rest], axis=0).T.astype(BF16)


def spread_table(heads, first, width):
    rows = lax.broadcasted_iota(jnp.int32, (heads, width), 0)
    columns = lax.broadcasted_iota(jnp.int32, (heads, width), 1)
    offset = columns - (rows - first) * P_SIZE
    picked = ((offset >= 0) & (offset < P_SIZE)).astype(F32)
    rest = jnp.zeros((LANES - 3 * heads, width), F32)
    return jnp.concatenate([picked, picked, picked, rest], axis=0).astype(BF16)


def device_factors(decays, ref):
    logs = log_parts(decays)
    rows = lax.broadcasted_iota(jnp.int32, (LANES, LANES), 0)
    columns = lax.broadcasted_iota(jnp.int32, (LANES, LANES), 1)
    before, after = block_sums(logs, rows <= columns), block_sums(logs, rows > columns)
    totals_of = [block[:, LANES - 1 :] for block in before]
    ahead = behind = jnp.zeros(totals_of[0].shape, F32)
    for k, total in enumerate(totals_of):
        before[k] = before[k] + ahead
        ahead = ahead + total
    for k in reversed(range(len(totals_of))):
        after[k] = after[k] + behind
        behind = behind + totals_of[k]
    ref[:, :LANES] = packed(jnp.exp(jnp.concatenate(before, axis=1)))
    ref[:, LANES:] = packed(jnp.exp(jnp.concatenate(after, axis=1)))


def tile_totals(heads, first, x, dy, bt_ref, ct_ref, factor_ref, out_ref):
    tile = x.shape[1]
    table = spread_table(heads, first, tile)
    before = dot(factor_ref[:, :LANES], table)
    after = dot(factor_ref[:, LANES:], table)
    ended = jnp.broadcast_to(before[before.shape[0] - 1 :, :], (EXTRA, tile))
    for i, (source, factor, other) in enumerate(((x, after, bt_ref), (dy, before, ct_ref))):
        out_ref[i, :N, :] = dot12(other[...], halves(source.astype(F32) * factor))
        out_ref[i, N:, :] = ended


def other_kernel(
    heads, x_ref, dy_ref, b_ref, c_ref, decays_ref, out_ref, factor_ref,
    x_buf, dy_buf, out_buf, b_buf, c_buf, decays_buf, bt_ref, ct_ref, arrived, small, sent,
):
    local, width = x_buf.shape
    count, _, _, tile = out_buf.shape
    smalls = [
        pltpu.make_async_copy(source, buf, small.at[i])
        for i, (source, buf) in enumerate(((decays_ref, decays_buf), (b_ref, b_buf), (c_ref, c_buf)))
    ]
    for load in smalls:
        load.start()
    columns = pl.ds(pl.multiple_of(place(OTHER) * width, width), width)
    loads = []
    for i, (source, buf) in enumerate(((x_ref, x_buf), (dy_ref, dy_buf))):
        for k in range(PARTS):
            rows = pl.ds(k * (local // PARTS), local // PARTS)
            loads.append(pltpu.make_async_copy(source.at[rows, columns], buf.at[rows, :], arrived.at[i, k]))
            loads[-1].start()
    smalls[0].wait()
    device_factors(decays_buf[...], factor_ref)
    smalls[1].wait()
    smalls[2].wait()
    bt_ref[...] = transposed(b_buf[...])
    ct_ref[...] = transposed(c_buf[...])
    for load in loads:
        load.wait()
    stores = []
    for k in range(count):
        first = (place(OTHER) * count + k) * (tile // P_SIZE)
        x, dy = x_buf[:, k * tile : (k + 1) * tile], dy_buf[:, k * tile : (k + 1) * tile]
        tile_totals(heads, first, x, dy, bt_ref, ct_ref, factor_ref, out_buf.at[k])
        stores.append(pltpu.make_async_copy(out_buf.at[k], out_ref.at[:, :, pl.ds(k * tile, tile)], sent.at[k]))
        stores[-1].start()
    for store in stores:
        store.wait()


def other_totals(x, dy, b, c, decays):
    local, width = x.shape
    tile = min(WIDE, width // 2)
    count = width // 2 // tile
    anywhere = pl.BlockSpec(memory_space=pl.ANY)
    factor = jax.ShapeDtypeStruct((local, 2 * LANES), BF16)
    return pl.pallas_call(
        functools.partial(other_kernel, width // P_SIZE),
        grid=(1,),
        in_specs=[anywhere] * 5,
        out_specs=[anywhere, pl.BlockSpec(factor.shape, lambda j: (0, 0))],
        out_shape=[jax.ShapeDtypeStruct((2, N + EXTRA, width // 2), F32), factor],
        scratch_shapes=[
            pltpu.VMEM((local, width // 2), BF16),
            pltpu.VMEM((local, width // 2), BF16),
            pltpu.VMEM((count, 2, N + EXTRA, tile), F32),
            pltpu.VMEM(b.shape, BF16),
            pltpu.VMEM(c.shape, BF16),
            pltpu.VMEM(decays.shape, F32),
            pltpu.VMEM((N, local), BF16),
            pltpu.VMEM((N, local), BF16),
            pltpu.SemaphoreType.DMA((2, PARTS)),
            pltpu.SemaphoreType.DMA((3,)),
            pltpu.SemaphoreType.DMA((count,)),
        ],
        compiler_params=FIRST,
        name="other_totals",
        cost_estimate=pl.CostEstimate(flops=8 * local * N * width // 2, bytes_accessed=4 * local * width, transcendentals=0),
    )(x, dy, b, c, decays)


def own_kernel(heads, count, x_ref, dy_ref, b_ref, c_ref, factor_ref, out_ref, bt_ref, ct_ref):
    step = pl.program_id(0)

    @pl.when(step == 0)
    def _():
        bt_ref[...] = transposed(b_ref[...])
        ct_ref[...] = transposed(c_ref[...])

    first = (place(CORE) * count + step) * (x_ref.shape[1] // P_SIZE)
    tile_totals(heads, first, x_ref[...], dy_ref[...], bt_ref, ct_ref, factor_ref, out_ref)


def own_totals(x, dy, b, c, factors):
    local, width = x.shape
    tile = min(WIDE, width // 2)
    count = width // 2 // tile
    whole = lambda a: pl.BlockSpec(a.shape, lambda j: (0, 0))
    column = pl.BlockSpec((local, tile), lambda j: (0, place(CORE) * count + j))
    return pl.pallas_call(
        functools.partial(own_kernel, width // P_SIZE, count),
        grid=(count,),
        in_specs=[column, column, whole(b), whole(c), whole(factors)],
        out_specs=pl.BlockSpec((2, N + EXTRA, tile), lambda j: (0, 0, j)),
        scratch_shapes=[pltpu.VMEM((N, local), BF16), pltpu.VMEM((N, local), BF16)],
        out_shape=jax.ShapeDtypeStruct((2, N + EXTRA, width // 2), F32),
        compiler_params=PARAMS,
        name="own_totals",
        cost_estimate=pl.CostEstimate(flops=8 * local * N * width // 2, bytes_accessed=4 * local * width, transcendentals=0),
    )(x, dy, b, c, factors)


def ordered(core, mine, recv):
    return jnp.where(core == 0, mine, recv), jnp.where(core == 0, recv, mine)


def chip_kernel(chips, mine_ref, recv_ref, *out_refs):
    core, chip = place(CORE), lax.axis_index("seq") // 2
    early, late = ordered(core, mine_ref[0], recv_ref[0])
    early_decay, late_decay = early[N : N + 1], late[N : N + 1]
    both = jnp.broadcast_to(early_decay * late_decay, (EXTRA, early.shape[1]))
    state = late_decay * early[:N] + late[:N]
    early, late = ordered(core, mine_ref[1], recv_ref[1])
    grad = early[:N] + early_decay * late[:N]
    for r, out_ref in enumerate(out_refs, 1):
        out_ref[:N, :] = jnp.where(chip + r < chips, state, grad)
        out_ref[N:, :] = both


def chip_totals(chips, mine, recv):
    width = mine.shape[2]
    tile = min(512, width)
    block = pl.BlockSpec((2, N + EXTRA, tile), lambda j: (0, 0, j))
    out = pl.BlockSpec((N + EXTRA, tile), lambda j: (0, j))
    shape = jax.ShapeDtypeStruct((N + EXTRA, width), F32)
    return pl.pallas_call(
        functools.partial(chip_kernel, chips),
        grid=(width // tile,),
        in_specs=[block, block],
        out_specs=[out] * (chips - 1),
        out_shape=[shape] * (chips - 1),
        compiler_params=PARAMS,
        name="chip_totals",
        cost_estimate=pl.CostEstimate(flops=6 * N * width, bytes_accessed=24 * N * width, transcendentals=0),
    )(mine, recv)


def sides():
    chip = lax.axis_index("seq") // 2
    return chip < 2, (chip == 1) | (chip == 2)


def first_kernel(mine_ref, recv_ref, same_ref, later_ref, cross_ref, back_ref, decay_ref):
    left, inner = sides()
    core = place(CORE)
    width = mine_ref.shape[2] // 2
    early, late = ordered(core, mine_ref[0], recv_ref[0])
    early_decay, late_decay = early[N : N + 1], late[N : N + 1]
    state = late_decay * early[:N] + late[:N]
    decay = early_decay * late_decay
    early, late = ordered(core, mine_ref[1], recv_ref[1])
    grad = early[:N] + early_decay * late[:N]
    out, back = jnp.where(left, state, grad), jnp.where(left, grad, state)
    same_ref[:N, :] = out[:, :width]
    later_ref[...] = jnp.where(inner, back[:, :width], out[:, width:])
    rows = lax.broadcasted_iota(jnp.int32, (EXTRA, width), 0)
    same_ref[N:, :] = jnp.where(rows == 0, decay[:, :width], decay[:, width:])
    cross_ref[...] = out[:, width:]
    back_ref[...] = back[:, width:]
    decay_ref[...] = jnp.broadcast_to(decay[:, width:], (EXTRA, width))


def second_kernel(own_ref, back_ref, same_ref, cross_ref, decay_ref, cross2_ref, same2_ref):
    _, inner = sides()
    own, other = own_ref[:N, :], same_ref[:N, :]
    own_decay, other_decay = own_ref[N : N + 1, :], same_ref[N : N + 1, :]
    cross2_ref[...] = jnp.where(inner, own + own_decay * other, other + other_decay * own)
    weight = own_ref[N + 1 : N + 2, :] * decay_ref[:1, :]
    same2_ref[...] = jnp.where(inner, back_ref[...] + weight * cross_ref[...], cross_ref[...])


def plain_call(kernel, name, out_shape, *args):
    whole = lambda a: pl.BlockSpec(a.shape, lambda j: (0,) * len(a.shape))
    size = sum(a.size for a in args)
    return pl.pallas_call(
        kernel,
        grid=(1,),
        in_specs=[whole(a) for a in args],
        out_specs=[whole(a) for a in out_shape],
        out_shape=out_shape,
        compiler_params=PARAMS,
        name=name,
        cost_estimate=pl.CostEstimate(flops=8 * size, bytes_accessed=4 * size, transcendentals=0),
    )(*args)


def crossed(v, length, bit):
    return lax.ppermute(v, "seq", [(i, i ^ bit) for i in range(length)])


def first_phase(length, mine, recv):
    half = mine.shape[2] // 2
    shapes = [jax.ShapeDtypeStruct((rows, half), F32) for rows in (N + EXTRA, N, N, N, EXTRA)]
    own, later, cross, back, decay = plain_call(first_kernel, "first_messages", shapes, mine, recv)
    same, cross, decay = crossed(own, length, 2), crossed(cross, length, 4), crossed(decay, length, 6)
    return own, back, same, cross, decay, crossed(later, length, 2)


def second_phase(own, back, same, cross, decay):
    shape = jax.ShapeDtypeStruct(back.shape, F32)
    return plain_call(second_kernel, "second_messages", [shape, shape], own, back, same, cross, decay)


def carried4_kernel(
    mine_ref, recv_ref, same_ref, cross_ref, decay_ref, later_ref, cross2_ref, same2_ref, own_ref, peer_ref
):
    left, inner = sides()
    width = cross_ref.shape[1]
    decay_a, decay_b = same_ref[N : N + 1, :], same_ref[N + 1 : N + 2, :]
    for part in range(2):
        at = slice(part * width, (part + 1) * width)
        out = jnp.where(inner, later_ref[...] if part else same_ref[:N, :], 0.0)
        if part == 0:
            back = jnp.where(inner, cross2_ref[...], later_ref[...] + decay_a * cross2_ref[...])
        else:
            back = same2_ref[...] + jnp.where(inner, decay_ref[:1, :], decay_b) * cross_ref[...]
        carried_cores(
            place(CORE), jnp.where(left, out, back), jnp.where(left, back, out), mine_ref, recv_ref, own_ref, peer_ref, at
        )


def carried4(mine, recv, *others):
    shape = jax.ShapeDtypeStruct((2, N, mine.shape[2]), F32)
    return plain_call(carried4_kernel, "carried_in", [shape, shape], mine, recv, *others)


def carried_cores(core, state, grad, mine_ref, recv_ref, own_ref, peer_ref, at):
    early, late = ordered(core, mine_ref[0, :, at], recv_ref[0, :, at])
    at_late = early[N : N + 1] * state + early[:N]
    own_ref[0, :, at] = jnp.where(core == 0, state, at_late)
    peer_ref[0, :, at] = jnp.where(core == 0, at_late, state)
    early, late = ordered(core, mine_ref[1, :, at], recv_ref[1, :, at])
    at_early = late[:N] + late[N : N + 1] * grad
    own_ref[1, :, at] = jnp.where(core == 0, at_early, grad)
    peer_ref[1, :, at] = jnp.where(core == 0, grad, at_early)


def carried_kernel(chips, mine_ref, recv_ref, *refs):
    others, (own_ref, peer_ref) = refs[:-2], refs[-2:]
    core, chip = place(CORE), lax.axis_index("seq") // 2
    state = grad = jnp.zeros((N, own_ref.shape[2]), F32)
    state_weight = grad_weight = jnp.ones((1, own_ref.shape[2]), F32)
    for r, ref in enumerate(others, 1):
        earlier = chip >= r
        state = jnp.where(earlier, state + state_weight * ref[:N, :], state)
        state_weight = state_weight * ref[N : N + 1, :]
    for r in range(1, chips):
        later = chip + r < chips
        ref = others[chips - r - 1]
        grad = jnp.where(later, grad + grad_weight * ref[:N, :], grad)
        grad_weight = grad_weight * ref[N : N + 1, :]
    carried_cores(core, state, grad, mine_ref, recv_ref, own_ref, peer_ref, slice(None))


def carried(chips, mine, recv, others):
    width = mine.shape[2]
    tile = min(512, width)
    pair = pl.BlockSpec((2, N + EXTRA, tile), lambda j: (0, 0, j))
    other = pl.BlockSpec((N + EXTRA, tile), lambda j: (0, j))
    out = pl.BlockSpec((2, N, tile), lambda j: (0, 0, j))
    shape = jax.ShapeDtypeStruct((2, N, width), F32)
    return pl.pallas_call(
        functools.partial(carried_kernel, chips),
        grid=(width // tile,),
        in_specs=[pair, pair] + [other] * len(others),
        out_specs=(out, out),
        out_shape=(shape, shape),
        compiler_params=PARAMS,
        name="carried_in",
        cost_estimate=pl.CostEstimate(flops=20 * N * width, bytes_accessed=44 * N * width, transcendentals=0),
    )(mine, recv, *others)


def blocks(chunks):
    span = 2
    while span < chunks:
        yield span, [at for at in range(span, chunks, 2 * span)]
        span *= 2


def row_bounds(chunks):
    middles = [k * SUB + SUB // 2 + 1 for k in range(chunks)]
    for span in [1] + [span for span, _ in blocks(chunks)]:
        for k, middle in enumerate(middles):
            boundary = (k // span + 1 - (k // span) % 2) * span * SUB
            yield min(boundary, middle), max(boundary, middle)
    yield from ((0, middle) for middle in middles)
    yield from ((middle, chunks * SUB) for middle in middles)


def local_factors(decays, lift_ref, drop_ref, rows_ref):
    local = decays.shape[1]
    logs = log_parts(decays)
    rows = lax.broadcasted_iota(jnp.int32, (LANES, LANES), 0)
    columns = lax.broadcasted_iota(jnp.int32, (LANES, LANES), 1)
    middle = (columns & -SUB) + SUB // 2
    later = (rows > middle) & (rows <= columns)
    sooner = (rows > columns) & (rows <= middle)
    offset = jnp.concatenate(block_sums(logs, later.astype(F32) - sooner.astype(F32)), axis=1)
    lift_ref[...] = by_token(jnp.exp(offset))
    drop_ref[...] = by_token(jnp.exp(-offset))
    lane = lax.broadcasted_iota(jnp.int32, (1, LANES), 1)
    first = last = jnp.zeros((1, LANES), jnp.int32)
    for i, (start, end) in enumerate(row_bounds(local // SUB)):
        first, last = jnp.where(lane == i, start, first), jnp.where(lane == i, end, last)
    rows = lax.broadcasted_iota(jnp.int32, (local, LANES), 0)
    decay = by_token(jnp.exp(summed_logs(logs, (rows >= first) & (rows < last))))
    rows_ref[...] = decay[: rows_ref.shape[0]]


def score_parts(b, c, ref, at, times, ahead=None):
    score = dot(b, c, NT)
    if ahead is not None:
        rows = lax.broadcasted_iota(jnp.int32, score.shape, 0)
        columns = lax.broadcasted_iota(jnp.int32, score.shape, 1)
        score = jnp.where(rows <= columns + ahead, score, 0.0)
    hi, lo = halves(score)
    width = score.shape[1]
    ref[at, :width] = hi
    ref[at, width : 2 * width] = lo
    if times == 3:
        ref[at, 2 * width :] = hi


def added_up(v):
    width = v.shape[1] // 2
    return v[:, :width] + v[:, width:]


def local_kernel(first_tile, continued, *refs):
    x_ref, dy_ref, b_ref, c_ref, decays_ref = refs[:5]
    refs = refs[5:]
    if continued:
        out_before_ref, map_before_ref = refs[:2]
        refs = refs[4:]
    part_ref, scaled_ref, out_ref, map_ref = refs[:4]
    lift_ref, drop_ref, rows_ref, full_ref, dys_ref, xs_ref, back_ref, sums_ref, even_ref, odd_ref = refs[4:14]
    level_refs = refs[14:]
    local, tile = x_ref.shape
    chunks = local // SUB
    step = pl.program_id(0)
    levels = [(span, at, level_refs[2 * i], level_refs[2 * i + 1]) for i, (span, at) in enumerate(blocks(chunks))]

    @pl.when(step == 0)
    def _():
        local_factors(decays_ref[...], lift_ref, drop_ref, rows_ref)
        sums_ref[...] = jnp.zeros(sums_ref.shape, F32)
        for k in range(0, chunks, 2):
            pair, even, odd = pl.ds(k * SUB, 2 * SUB), pl.ds(k * SUB, SUB), pl.ds((k + 1) * SUB, SUB)
            score_parts(b_ref[even, :], c_ref[even, :], even_ref, pl.ds(k // 2 * SUB, SUB), 3, 0)
            score_parts(b_ref[pair, :], c_ref[odd, :], odd_ref, pair, 3, SUB)
        for span, boundaries, mixed_ref, scores_ref in levels:
            mixed_ref[...] = jnp.zeros(mixed_ref.shape, F32)
            size = span * SUB
            for i, boundary in enumerate(boundaries):
                before, after = pl.ds((boundary - span) * SUB, size), pl.ds(boundary * SUB, size)
                score_parts(b_ref[before, :], c_ref[after, :], scores_ref, pl.ds(i * size, size), 2)

    first = (first_tile + step) * (tile // P_SIZE)
    dys_ref[...] = dy_ref[...].astype(F32) * spread(lift_ref[...], first, tile)
    back_ref[...] = spread(drop_ref[...], first, tile)
    xs_ref[...] = x_ref[...].astype(F32) * back_ref[...]
    row = spread(rows_ref[...], first, tile)
    factor = lambda kind, k: row[kind * chunks + k : kind * chunks + k + 1]

    for k in range(0, chunks, 2):
        even, odd, pair = pl.ds(k * SUB, SUB), pl.ds((k + 1) * SUB, SUB), pl.ds(k * SUB, 2 * SUB)
        dys, xs = halves(dys_ref[even, :]), halves(xs_ref[even, :])
        sums_ref[even, :] += dot(dys[0], stacked(*xs), NT)
        sums_ref[even, :SUB] += dot(dys[1], xs[0], NT)
        gained_even = dot(even_ref[pl.ds(k // 2 * SUB, SUB), :], stacked(dys[0], dys[0], dys[1]))
        crossing = halves((xs_ref[even, :] * factor(0, k)) * factor(0, k + 1))
        dys, xs = halves(dys_ref[odd, :]), halves(xs_ref[odd, :])
        high = stacked(xs[0], crossing[0])
        both = dot(dys[0], stacked(high, xs[1], crossing[1]), NT)
        sums_ref[odd, :] += added_up(both) + dot(dys[1], high, NT)
        gained_odd = dot(odd_ref[pair, :], stacked(dys[0], dys[0], dys[1]))
        ahead = (back_ref[even, :] * factor(0, k)) * (factor(0, k + 1) * gained_odd[:SUB])
        part_ref[even, :] = back_ref[even, :] * gained_even + ahead
        part_ref[odd, :] = back_ref[odd, :] * gained_odd[SUB:]

    for level, (span, boundaries, mixed_ref, scores_ref) in enumerate(levels, 1):
        size = span * SUB
        for i, boundary in enumerate(boundaries):
            at = pl.ds(i * size, size)
            take = lambda ref, start: halves(
                stacked(*[ref[k * SUB : (k + 1) * SUB, :] * factor(level, k) for k in range(start, start + span)])
            )
            dys, xs = take(dys_ref, boundary), take(xs_ref, boundary - span)
            both = dot(dys[0], stacked(*xs), NT)
            mixed_ref[at, :] += added_up(both) + dot(dys[1], xs[0], NT)
            gained = dot(scores_ref[at, :], stacked(dys[0], dys[0])) + dot(scores_ref[at, :size], dys[1])
            for q in range(span):
                k = boundary - span + q
                rows = pl.ds(k * SUB, SUB)
                part_ref[rows, :] += (back_ref[rows, :] * factor(level, k)) * gained[q * SUB : (q + 1) * SUB]

    for k in range(chunks):
        at = pl.ds(k * SUB, SUB)
        kind = len(levels) + 1
        scaled_ref[1, 0, at, :], scaled_ref[1, 1, at, :] = halves(dys_ref[at, :] * factor(kind, k))
        scaled_ref[0, 0, at, :], scaled_ref[0, 1, at, :] = halves(xs_ref[at, :] * factor(kind + 1, k))

    @pl.when(step == pl.num_programs(0) - 1)
    def _():
        full_ref[...] = jnp.zeros(full_ref.shape, F32)
        rows = lax.broadcasted_iota(jnp.int32, (SUB, SUB), 0)
        columns = lax.broadcasted_iota(jnp.int32, (SUB, SUB), 1)
        for k in range(0, chunks, 2):
            even, odd = pl.ds(k * SUB, SUB), pl.ds((k + 1) * SUB, SUB)
            full_ref[even, k * SUB : (k + 1) * SUB] = jnp.where(rows >= columns, added_up(sums_ref[even, :]), 0.0)
            full_ref[odd, (k + 1) * SUB : (k + 2) * SUB] = jnp.where(rows >= columns, sums_ref[odd, :SUB], 0.0)
            full_ref[odd, k * SUB : (k + 1) * SUB] = sums_ref[odd, SUB:]
        for span, boundaries, mixed_ref, _ in levels:
            size = span * SUB
            for i, boundary in enumerate(boundaries):
                block = mixed_ref[pl.ds(i * size, size), :]
                full_ref[pl.ds(boundary * SUB, size), (boundary - span) * SUB : boundary * SUB] = block
        map_ref[...] = map_before_ref[...] if continued else jnp.zeros(map_ref.shape, F32)
        for k in range(0, local, LANES):
            at = pl.ds(k, LANES)
            mixed = full_ref[at, :]
            gained = dot21(halves(mixed), b_ref[...])
            out_ref[at, :] = out_before_ref[at, :] + gained if continued else gained
            map_ref[...] += dot21(halves(mixed.T), c_ref[at, :])


def local_part(first_tile, count, x, dy, b, c, decays, before=None):
    local, width = x.shape
    chunks = local // SUB
    whole = lambda a: pl.BlockSpec(a.shape, lambda j: (0, 0))
    column = pl.BlockSpec((local, WIDE), lambda j: (0, first_tile + j))
    tokens = pl.BlockSpec((local, N), lambda j: (0, 0))
    scratch = [
        pltpu.VMEM((local, LANES), F32),
        pltpu.VMEM((local, LANES), F32),
        pltpu.VMEM((-(-len(list(row_bounds(chunks))) // 8) * 8, LANES), F32),
        pltpu.VMEM((local, local), F32),
        pltpu.VMEM((local, WIDE), F32),
        pltpu.VMEM((local, WIDE), F32),
        pltpu.VMEM((local, WIDE), F32),
        pltpu.VMEM((local, 2 * SUB), F32),
        pltpu.VMEM((local // 2, 3 * SUB), BF16),
        pltpu.VMEM((local, 3 * SUB), BF16),
    ]
    for span, _ in blocks(chunks):
        scratch.append(pltpu.VMEM((local // 2, span * SUB), F32))
        scratch.append(pltpu.VMEM((local // 2, 2 * span * SUB), BF16))
    in_specs = [column, column, whole(b), whole(c), whole(decays)]
    args, aliases = [x, dy, b, c, decays], {}
    if before is not None:
        part, scaled, out_part, map_part = before
        in_specs += [tokens, tokens, pl.BlockSpec(memory_space=pl.ANY), pl.BlockSpec(memory_space=pl.ANY)]
        args += [out_part, map_part, part, scaled]
        aliases = {7: 0, 8: 1}
    return pl.pallas_call(
        functools.partial(local_kernel, first_tile, before is not None),
        grid=(count,),
        in_specs=in_specs,
        out_specs=(column, pl.BlockSpec((2, 2, local, WIDE), lambda j: (0, 0, 0, first_tile + j)), tokens, tokens),
        out_shape=(
            jax.ShapeDtypeStruct((local, width), F32),
            jax.ShapeDtypeStruct((2, 2, local, width), BF16),
            jax.ShapeDtypeStruct((local, N), F32),
            jax.ShapeDtypeStruct((local, N), F32),
        ),
        scratch_shapes=scratch,
        input_output_aliases=aliases,
        compiler_params=PARAMS,
        name="local_part",
        cost_estimate=pl.CostEstimate(
            flops=40 * local * N * WIDE * count, bytes_accessed=8 * local * WIDE * count, transcendentals=0
        ),
    )(*args)


def map_kernel(count, ranks, scaled_ref, carry_ref, out_before_ref, map_before_ref, *refs):
    messages, (out_ref, map_ref) = refs[:-2], refs[-2:]
    step = pl.program_id(0)

    @pl.when(step == 0)
    def _():
        out_ref[...] = out_before_ref[...]
        map_ref[...] = map_before_ref[...]

    for i, sum_ref in enumerate((map_ref, out_ref)):
        carry = halves(carry_ref[1 - i])
        both = dot(scaled_ref[i, 0], stacked(*carry), NT)
        sum_ref[...] += both[:, :N] + (both[:, N:] + dot(scaled_ref[i, 1], carry[0], NT))

    if messages:

        @pl.when(step == count - 1)
        def _():
            rows = messages[0].shape[1]
            for r, message in enumerate(messages):
                at = pl.ds(pl.multiple_of(((lax.axis_index("head") + r) % ranks) * rows, rows), rows)
                message[0] = out_ref[at, :]
                message[1] = map_ref[at, :]


def map_terms(half, scaled, carry, out_before, map_before, ranks=0):
    local, width = scaled.shape[2], carry.shape[2]
    tile = min(WIDE, width)
    count = width // tile
    whole = lambda a: pl.BlockSpec(a.shape, lambda j: (0,) * len(a.shape))
    tokens = jax.ShapeDtypeStruct((local, N), F32)
    if ranks:
        out_shape = [jax.ShapeDtypeStruct((2, local // ranks, N), F32)] * ranks
        scratch = [pltpu.VMEM((local, N), F32), pltpu.VMEM((local, N), F32)]
    else:
        out_shape, scratch = [tokens, tokens], []
    return pl.pallas_call(
        functools.partial(map_kernel, count, ranks),
        grid=(count,),
        in_specs=[
            pl.BlockSpec((2, 2, local, tile), lambda j: (0, 0, 0, place(half) * count + j)),
            pl.BlockSpec((2, N, tile), lambda j: (0, 0, j)),
            whole(tokens),
            whole(tokens),
        ],
        out_specs=[whole(shape) for shape in out_shape],
        scratch_shapes=scratch,
        out_shape=out_shape,
        compiler_params=PARAMS,
        name="map_terms",
        cost_estimate=pl.CostEstimate(flops=12 * local * N * width, bytes_accessed=8 * local * width, transcendentals=0),
    )(scaled, carry, out_before, map_before)


def input_kernel(heads, count, part_ref, suf_ref, b_ref, own_ref, other_ref, input_ref):
    tile = part_ref.shape[1]
    step = pl.program_id(0)
    after = dot(suf_ref[...], spread_table(heads, step * (tile // P_SIZE), tile))
    grad = jnp.where(step // count == place(CORE), own_ref[0], other_ref[0])
    input_ref[...] = (part_ref[...] + after * dot12(b_ref[...], halves(grad))).astype(BF16)


def input_terms(part, factors, b, own, other):
    local, width = part.shape
    count = width // 2 // WIDE
    whole = lambda a: pl.BlockSpec(a.shape, lambda j: (0, 0))
    column = pl.BlockSpec((local, WIDE), lambda j: (0, j))
    carry = pl.BlockSpec((1, N, WIDE), lambda j: (1, 0, j % count))
    return pl.pallas_call(
        functools.partial(input_kernel, width // P_SIZE, count),
        grid=(2 * count,),
        in_specs=[column, pl.BlockSpec((local, LANES), lambda j: (0, 1)), whole(b), carry, carry],
        out_specs=column,
        out_shape=jax.ShapeDtypeStruct((local, width), BF16),
        compiler_params=PARAMS,
        name="input_terms",
        cost_estimate=pl.CostEstimate(flops=4 * local * N * width, bytes_accessed=8 * local * width, transcendentals=0),
    )(part, factors, b, own, other)


def sums_kernel(*refs):
    shares, (map_ref, out_ref) = refs[:-2], refs[-2:]
    for i, ref in enumerate((out_ref, map_ref)):
        ref[...] = functools.reduce(lambda a, b: a + b, [share[i] for share in shares])


def swap_cores(v, length):
    return lax.ppermute(v, "seq", [(i, i ^ 1) for i in range(length)])


def turned(v, axis, length, by):
    return lax.ppermute(v, axis, [(i, (i + by) % length) for i in range(length)])


def per_device(mixer_input, output_grad, input_map, output_map, decays):
    length, ranks = lax.axis_size("seq"), lax.axis_size("head")
    chips = length // 2
    args = mixer_input, output_grad, input_map, output_map
    sent, factors = other_totals(*args, decays)
    recv = swap_cores(sent, length)
    mine = own_totals(*args, factors)
    tiles = mixer_input.shape[1] // WIDE
    if chips == 4:
        ahead = tiles // 2
        own, back, *others, later = first_phase(length, mine, recv)
        result = local_part(0, ahead, *args, decays)
        others, result = lax.optimization_barrier((others, result))
        cross, same = second_phase(own, back, *others)
        crossing = [crossed(cross, length, 4), crossed(same, length, 2)]
        result, later, _, _ = lax.optimization_barrier((result, later, cross, same))
        result = local_part(ahead, tiles - ahead, *args, decays, result)
        others, result = lax.optimization_barrier((others + [later] + crossing, result))
        own, peer = carried4(mine, recv, *others)
    else:
        messages = chip_totals(chips, mine, recv)
        others = [turned(message, "seq", length, 2 * r) for r, message in enumerate(messages, 1)]
        result = local_part(0, tiles, *args, decays)
        own, peer = carried(chips, mine, recv, others)
    part, scaled, out_part, map_part = result
    other = swap_cores(peer, length)
    out_part, map_part = map_terms(CORE, scaled, own, out_part, map_part)
    shares = map_terms(OTHER, scaled, other, out_part, map_part, ranks)
    own, other, shares = lax.optimization_barrier((own, other, shares))
    sums = [shares[0]] + [turned(shares[r], "head", ranks, r) for r in range(1, ranks)]
    input_grad = input_terms(part, factors, input_map, own, other)
    shape = jax.ShapeDtypeStruct(shares[0].shape[1:], F32)
    input_map_grad, output_map_grad = plain_call(sums_kernel, "head_sums", [shape, shape], *sums)
    return input_grad, input_map_grad, output_map_grad


def solution(mesh):
    in_specs = (
        P("seq", "head"),
        P("seq", "head"),
        P("seq", None),
        P("seq", None),
        P("head", "seq"),
    )
    out_specs = (P("seq", "head"), P(("seq", "head"), None), P(("seq", "head"), None))
    return jax.shard_map(
        per_device, mesh=mesh, in_specs=in_specs, out_specs=out_specs, check_vma=False
    )
```

```python
import functools

import jax
import jax.numpy as jnp
from jax import lax
from jax.experimental import pallas as pl
from jax.experimental.pallas import tpu as pltpu
from jax.sharding import PartitionSpec as P

P_SIZE = 64
N = 128
SUB = 64
TILE = 256
WIDE = 512
EXTRA = 8
PARTS = 4
LANES = 128
CORE, OTHER = range(2)
PARAMS = pltpu.CompilerParams(vmem_limit_bytes=24 * 1024 * 1024)
FIRST = pltpu.CompilerParams(vmem_limit_bytes=56 * 1024 * 1024)
F32 = jnp.float32
BF16 = jnp.bfloat16

NN = (((1,), (0,)), ((), ()))
NT = (((1,), (1,)), ((), ()))


def dot(a, b, dims=NN):
    return lax.dot_general(a, b, dims, preferred_element_type=F32)


def halves(v):
    hi = v.astype(BF16)
    return hi, (v - hi.astype(F32)).astype(BF16)


def dot21(pair, b, dims=NN):
    return dot(pair[0], b, dims) + dot(pair[1], b, dims)


def dot12(a, pair, dims=NN):
    return dot(a, pair[0], dims) + dot(a, pair[1], dims)


def dot22(p, q, dims=NN):
    return dot(p[0], q[0], dims) + (dot(p[0], q[1], dims) + dot(p[1], q[0], dims))


def thirds(v):
    hi = v.astype(BF16)
    rest = v - hi.astype(F32)
    mid = rest.astype(BF16)
    return hi, mid, (rest - mid.astype(F32)).astype(BF16)


def spread(by_head, first, width):
    lanes = lax.broadcasted_iota(jnp.int32, by_head.shape, 1)
    step = LANES // P_SIZE
    shift = P_SIZE.bit_length() - 1
    taken = [
        jnp.take_along_axis(by_head, first + step * k + (lanes >> shift), axis=1) for k in range(width // LANES)
    ]
    return jnp.concatenate(taken, axis=1)


def place(half):
    core = lax.axis_index("seq") % 2
    return core if half == CORE else 1 - core


def stacked(*parts):
    return jnp.concatenate(parts, axis=0)


def transposed(v):
    return v.astype(F32).T.astype(BF16)


def log_parts(decays):
    return jnp.concatenate([part.astype(F32) for part in thirds(jnp.log(decays))], axis=0).astype(BF16)


def summed_logs(logs, table):
    heads = logs.shape[0] // 3
    sums = dot(logs, table.astype(F32).astype(BF16))
    return sums[:heads] + (sums[heads : 2 * heads] + sums[2 * heads :])


def block_sums(logs, table):
    blocks_of = [logs[:, k : k + LANES] for k in range(0, logs.shape[1], LANES)]
    return [summed_logs(block, table) for block in blocks_of]


def by_token(v):
    rest = jnp.zeros((LANES - v.shape[0], v.shape[1]), F32)
    return jnp.concatenate([v, rest], axis=0).T


def packed(v):
    parts = [part.astype(F32) for part in thirds(v)]
    rest = jnp.zeros((LANES - 3 * v.shape[0], v.shape[1]), F32)
    return jnp.concatenate(parts + [rest], axis=0).T.astype(BF16)


def spread_table(heads, first, width):
    rows = lax.broadcasted_iota(jnp.int32, (heads, width), 0)
    columns = lax.broadcasted_iota(jnp.int32, (heads, width), 1)
    offset = columns - (rows - first) * P_SIZE
    picked = ((offset >= 0) & (offset < P_SIZE)).astype(F32)
    rest = jnp.zeros((LANES - 3 * heads, width), F32)
    return jnp.concatenate([picked, picked, picked, rest], axis=0).astype(BF16)


def device_factors(decays, ref):
    logs = log_parts(decays)
    rows = lax.broadcasted_iota(jnp.int32, (LANES, LANES), 0)
    columns = lax.broadcasted_iota(jnp.int32, (LANES, LANES), 1)
    before, after = block_sums(logs, rows <= columns), block_sums(logs, rows > columns)
    totals_of = [block[:, LANES - 1 :] for block in before]
    ahead = behind = jnp.zeros(totals_of[0].shape, F32)
    for k, total in enumerate(totals_of):
        before[k] = before[k] + ahead
        ahead = ahead + total
    for k in reversed(range(len(totals_of))):
        after[k] = after[k] + behind
        behind = behind + totals_of[k]
    ref[:, :LANES] = packed(jnp.exp(jnp.concatenate(before, axis=1)))
    ref[:, LANES:] = packed(jnp.exp(jnp.concatenate(after, axis=1)))


def tile_totals(heads, first, x, dy, bt_ref, ct_ref, factor_ref, out_ref):
    tile = x.shape[1]
    table = spread_table(heads, first, tile)
    before = dot(factor_ref[:, :LANES], table)
    after = dot(factor_ref[:, LANES:], table)
    ended = jnp.broadcast_to(before[before.shape[0] - 1 :, :], (EXTRA, tile))
    for i, (source, factor, other) in enumerate(((x, after, bt_ref), (dy, before, ct_ref))):
        out_ref[i, :N, :] = dot12(other[...], halves(source.astype(F32) * factor))
        out_ref[i, N:, :] = ended


def other_kernel(
    heads, x_ref, dy_ref, b_ref, c_ref, decays_ref, out_ref, factor_ref,
    x_buf, dy_buf, out_buf, b_buf, c_buf, decays_buf, bt_ref, ct_ref, arrived, small, sent,
):
    local, width = x_buf.shape
    count, _, _, tile = out_buf.shape
    smalls = [
        pltpu.make_async_copy(source, buf, small.at[i])
        for i, (source, buf) in enumerate(((decays_ref, decays_buf), (b_ref, b_buf), (c_ref, c_buf)))
    ]
    for load in smalls:
        load.start()
    columns = pl.ds(pl.multiple_of(place(OTHER) * width, width), width)
    loads = []
    for i, (source, buf) in enumerate(((x_ref, x_buf), (dy_ref, dy_buf))):
        for k in range(PARTS):
            rows = pl.ds(k * (local // PARTS), local // PARTS)
            loads.append(pltpu.make_async_copy(source.at[rows, columns], buf.at[rows, :], arrived.at[i, k]))
            loads[-1].start()
    smalls[0].wait()
    device_factors(decays_buf[...], factor_ref)
    smalls[1].wait()
    smalls[2].wait()
    bt_ref[...] = transposed(b_buf[...])
    ct_ref[...] = transposed(c_buf[...])
    for load in loads:
        load.wait()
    stores = []
    for k in range(count):
        first = (place(OTHER) * count + k) * (tile // P_SIZE)
        x, dy = x_buf[:, k * tile : (k + 1) * tile], dy_buf[:, k * tile : (k + 1) * tile]
        tile_totals(heads, first, x, dy, bt_ref, ct_ref, factor_ref, out_buf.at[k])
        stores.append(pltpu.make_async_copy(out_buf.at[k], out_ref.at[:, :, pl.ds(k * tile, tile)], sent.at[k]))
        stores[-1].start()
    for store in stores:
        store.wait()


def other_totals(x, dy, b, c, decays):
    local, width = x.shape
    tile = min(WIDE, width // 2)
    count = width // 2 // tile
    anywhere = pl.BlockSpec(memory_space=pl.ANY)
    factor = jax.ShapeDtypeStruct((local, 2 * LANES), BF16)
    return pl.pallas_call(
        functools.partial(other_kernel, width // P_SIZE),
        grid=(1,),
        in_specs=[anywhere] * 5,
        out_specs=[anywhere, pl.BlockSpec(factor.shape, lambda j: (0, 0))],
        out_shape=[jax.ShapeDtypeStruct((2, N + EXTRA, width // 2), F32), factor],
        scratch_shapes=[
            pltpu.VMEM((local, width // 2), BF16),
            pltpu.VMEM((local, width // 2), BF16),
            pltpu.VMEM((count, 2, N + EXTRA, tile), F32),
            pltpu.VMEM(b.shape, BF16),
            pltpu.VMEM(c.shape, BF16),
            pltpu.VMEM(decays.shape, F32),
            pltpu.VMEM((N, local), BF16),
            pltpu.VMEM((N, local), BF16),
            pltpu.SemaphoreType.DMA((2, PARTS)),
            pltpu.SemaphoreType.DMA((3,)),
            pltpu.SemaphoreType.DMA((count,)),
        ],
        compiler_params=FIRST,
        name="other_totals",
        cost_estimate=pl.CostEstimate(flops=8 * local * N * width // 2, bytes_accessed=4 * local * width, transcendentals=0),
    )(x, dy, b, c, decays)


def own_kernel(heads, count, x_ref, dy_ref, b_ref, c_ref, decays_ref, out_ref, bt_ref, ct_ref, factor_ref):
    step = pl.program_id(0)

    @pl.when(step == 0)
    def _():
        bt_ref[...] = transposed(b_ref[...])
        ct_ref[...] = transposed(c_ref[...])
        device_factors(decays_ref[...], factor_ref)

    first = (place(CORE) * count + step) * (x_ref.shape[1] // P_SIZE)
    tile_totals(heads, first, x_ref[...], dy_ref[...], bt_ref, ct_ref, factor_ref, out_ref)


def own_totals(x, dy, b, c, decays):
    local, width = x.shape
    tile = min(WIDE, width // 2)
    count = width // 2 // tile
    whole = lambda a: pl.BlockSpec(a.shape, lambda j: (0, 0))
    column = pl.BlockSpec((local, tile), lambda j: (0, place(CORE) * count + j))
    return pl.pallas_call(
        functools.partial(own_kernel, width // P_SIZE, count),
        grid=(count,),
        in_specs=[column, column, whole(b), whole(c), whole(decays)],
        out_specs=pl.BlockSpec((2, N + EXTRA, tile), lambda j: (0, 0, j)),
        scratch_shapes=[
            pltpu.VMEM((N, local), BF16),
            pltpu.VMEM((N, local), BF16),
            pltpu.VMEM((local, 2 * LANES), BF16),
        ],
        out_shape=jax.ShapeDtypeStruct((2, N + EXTRA, width // 2), F32),
        compiler_params=PARAMS,
        name="own_totals",
        cost_estimate=pl.CostEstimate(flops=8 * local * N * width // 2, bytes_accessed=4 * local * width, transcendentals=0),
    )(x, dy, b, c, decays)


def ordered(core, mine, recv):
    return jnp.where(core == 0, mine, recv), jnp.where(core == 0, recv, mine)


def chip_kernel(chips, mine_ref, recv_ref, *out_refs):
    core, chip = place(CORE), lax.axis_index("seq") // 2
    early, late = ordered(core, mine_ref[0], recv_ref[0])
    early_decay, late_decay = early[N : N + 1], late[N : N + 1]
    both = jnp.broadcast_to(early_decay * late_decay, (EXTRA, early.shape[1]))
    state = late_decay * early[:N] + late[:N]
    early, late = ordered(core, mine_ref[1], recv_ref[1])
    grad = early[:N] + early_decay * late[:N]
    for r, out_ref in enumerate(out_refs, 1):
        out_ref[:N, :] = jnp.where(chip + r < chips, state, grad)
        out_ref[N:, :] = both


def chip_totals(chips, mine, recv):
    width = mine.shape[2]
    tile = min(512, width)
    block = pl.BlockSpec((2, N + EXTRA, tile), lambda j: (0, 0, j))
    out = pl.BlockSpec((N + EXTRA, tile), lambda j: (0, j))
    shape = jax.ShapeDtypeStruct((N + EXTRA, width), F32)
    return pl.pallas_call(
        functools.partial(chip_kernel, chips),
        grid=(width // tile,),
        in_specs=[block, block],
        out_specs=[out] * (chips - 1),
        out_shape=[shape] * (chips - 1),
        compiler_params=PARAMS,
        name="chip_totals",
        cost_estimate=pl.CostEstimate(flops=6 * N * width, bytes_accessed=24 * N * width, transcendentals=0),
    )(mine, recv)


def sides():
    chip = lax.axis_index("seq") // 2
    return chip < 2, (chip == 1) | (chip == 2)


def first_kernel(mine_ref, recv_ref, same_ref, later_ref, cross_ref, back_ref, decay_ref):
    left, inner = sides()
    core = place(CORE)
    width = mine_ref.shape[2] // 2
    early, late = ordered(core, mine_ref[0], recv_ref[0])
    early_decay, late_decay = early[N : N + 1], late[N : N + 1]
    state = late_decay * early[:N] + late[:N]
    decay = early_decay * late_decay
    early, late = ordered(core, mine_ref[1], recv_ref[1])
    grad = early[:N] + early_decay * late[:N]
    out, back = jnp.where(left, state, grad), jnp.where(left, grad, state)
    same_ref[:N, :] = out[:, :width]
    later_ref[...] = jnp.where(inner, back[:, :width], out[:, width:])
    rows = lax.broadcasted_iota(jnp.int32, (EXTRA, width), 0)
    same_ref[N:, :] = jnp.where(rows == 0, decay[:, :width], decay[:, width:])
    cross_ref[...] = out[:, width:]
    back_ref[...] = back[:, width:]
    decay_ref[...] = jnp.broadcast_to(decay[:, width:], (EXTRA, width))


def second_kernel(own_ref, back_ref, same_ref, cross_ref, decay_ref, cross2_ref, same2_ref):
    _, inner = sides()
    own, other = own_ref[:N, :], same_ref[:N, :]
    own_decay, other_decay = own_ref[N : N + 1, :], same_ref[N : N + 1, :]
    cross2_ref[...] = jnp.where(inner, own + own_decay * other, other + other_decay * own)
    weight = own_ref[N + 1 : N + 2, :] * decay_ref[:1, :]
    same2_ref[...] = jnp.where(inner, back_ref[...] + weight * cross_ref[...], cross_ref[...])


def plain_call(kernel, name, out_shape, *args):
    whole = lambda a: pl.BlockSpec(a.shape, lambda j: (0,) * len(a.shape))
    size = sum(a.size for a in args)
    return pl.pallas_call(
        kernel,
        grid=(1,),
        in_specs=[whole(a) for a in args],
        out_specs=[whole(a) for a in out_shape],
        out_shape=out_shape,
        compiler_params=PARAMS,
        name=name,
        cost_estimate=pl.CostEstimate(flops=8 * size, bytes_accessed=4 * size, transcendentals=0),
    )(*args)


def crossed(v, length, bit):
    return lax.ppermute(v, "seq", [(i, i ^ bit) for i in range(length)])


def first_phase(length, mine, recv):
    half = mine.shape[2] // 2
    shapes = [jax.ShapeDtypeStruct((rows, half), F32) for rows in (N + EXTRA, N, N, N, EXTRA)]
    own, later, cross, back, decay = plain_call(first_kernel, "first_messages", shapes, mine, recv)
    same, cross, decay = crossed(own, length, 2), crossed(cross, length, 4), crossed(decay, length, 6)
    return own, back, same, cross, decay, crossed(later, length, 2)


def second_phase(own, back, same, cross, decay):
    shape = jax.ShapeDtypeStruct(back.shape, F32)
    return plain_call(second_kernel, "second_messages", [shape, shape], own, back, same, cross, decay)


def carried4_kernel(
    mine_ref, recv_ref, same_ref, cross_ref, decay_ref, later_ref, cross2_ref, same2_ref, own_ref, peer_ref
):
    left, inner = sides()
    width = cross_ref.shape[1]
    decay_a, decay_b = same_ref[N : N + 1, :], same_ref[N + 1 : N + 2, :]
    for part in range(2):
        at = slice(part * width, (part + 1) * width)
        out = jnp.where(inner, later_ref[...] if part else same_ref[:N, :], 0.0)
        if part == 0:
            back = jnp.where(inner, cross2_ref[...], later_ref[...] + decay_a * cross2_ref[...])
        else:
            back = same2_ref[...] + jnp.where(inner, decay_ref[:1, :], decay_b) * cross_ref[...]
        carried_cores(
            place(CORE), jnp.where(left, out, back), jnp.where(left, back, out), mine_ref, recv_ref, own_ref, peer_ref, at
        )


def carried4(mine, recv, *others):
    shape = jax.ShapeDtypeStruct((2, N, mine.shape[2]), F32)
    return plain_call(carried4_kernel, "carried_in", [shape, shape], mine, recv, *others)


def carried_cores(core, state, grad, mine_ref, recv_ref, own_ref, peer_ref, at):
    early, late = ordered(core, mine_ref[0, :, at], recv_ref[0, :, at])
    at_late = early[N : N + 1] * state + early[:N]
    own_ref[0, :, at] = jnp.where(core == 0, state, at_late)
    peer_ref[0, :, at] = jnp.where(core == 0, at_late, state)
    early, late = ordered(core, mine_ref[1, :, at], recv_ref[1, :, at])
    at_early = late[:N] + late[N : N + 1] * grad
    own_ref[1, :, at] = jnp.where(core == 0, at_early, grad)
    peer_ref[1, :, at] = jnp.where(core == 0, grad, at_early)


def carried_kernel(chips, mine_ref, recv_ref, *refs):
    others, (own_ref, peer_ref) = refs[:-2], refs[-2:]
    core, chip = place(CORE), lax.axis_index("seq") // 2
    state = grad = jnp.zeros((N, own_ref.shape[2]), F32)
    state_weight = grad_weight = jnp.ones((1, own_ref.shape[2]), F32)
    for r, ref in enumerate(others, 1):
        earlier = chip >= r
        state = jnp.where(earlier, state + state_weight * ref[:N, :], state)
        state_weight = state_weight * ref[N : N + 1, :]
    for r in range(1, chips):
        later = chip + r < chips
        ref = others[chips - r - 1]
        grad = jnp.where(later, grad + grad_weight * ref[:N, :], grad)
        grad_weight = grad_weight * ref[N : N + 1, :]
    carried_cores(core, state, grad, mine_ref, recv_ref, own_ref, peer_ref, slice(None))


def carried(chips, mine, recv, others):
    width = mine.shape[2]
    tile = min(512, width)
    pair = pl.BlockSpec((2, N + EXTRA, tile), lambda j: (0, 0, j))
    other = pl.BlockSpec((N + EXTRA, tile), lambda j: (0, j))
    out = pl.BlockSpec((2, N, tile), lambda j: (0, 0, j))
    shape = jax.ShapeDtypeStruct((2, N, width), F32)
    return pl.pallas_call(
        functools.partial(carried_kernel, chips),
        grid=(width // tile,),
        in_specs=[pair, pair] + [other] * len(others),
        out_specs=(out, out),
        out_shape=(shape, shape),
        compiler_params=PARAMS,
        name="carried_in",
        cost_estimate=pl.CostEstimate(flops=20 * N * width, bytes_accessed=44 * N * width, transcendentals=0),
    )(mine, recv, *others)


def blocks(chunks):
    span = 2
    while span < chunks:
        yield span, [at for at in range(span, chunks, 2 * span)]
        span *= 2


def row_bounds(chunks):
    middles = [k * SUB + SUB // 2 + 1 for k in range(chunks)]
    for span in [1] + [span for span, _ in blocks(chunks)]:
        for k, middle in enumerate(middles):
            boundary = (k // span + 1 - (k // span) % 2) * span * SUB
            yield min(boundary, middle), max(boundary, middle)
    yield from ((0, middle) for middle in middles)
    yield from ((middle, chunks * SUB) for middle in middles)


def local_factors(decays, lift_ref, drop_ref, rows_ref):
    local = decays.shape[1]
    logs = log_parts(decays)
    rows = lax.broadcasted_iota(jnp.int32, (LANES, LANES), 0)
    columns = lax.broadcasted_iota(jnp.int32, (LANES, LANES), 1)
    middle = (columns & -SUB) + SUB // 2
    later = (rows > middle) & (rows <= columns)
    sooner = (rows > columns) & (rows <= middle)
    offset = jnp.concatenate(block_sums(logs, later.astype(F32) - sooner.astype(F32)), axis=1)
    lift_ref[...] = by_token(jnp.exp(offset))
    drop_ref[...] = by_token(jnp.exp(-offset))
    lane = lax.broadcasted_iota(jnp.int32, (1, LANES), 1)
    first = last = jnp.zeros((1, LANES), jnp.int32)
    for i, (start, end) in enumerate(row_bounds(local // SUB)):
        first, last = jnp.where(lane == i, start, first), jnp.where(lane == i, end, last)
    rows = lax.broadcasted_iota(jnp.int32, (local, LANES), 0)
    decay = by_token(jnp.exp(summed_logs(logs, (rows >= first) & (rows < last))))
    rows_ref[...] = decay[: rows_ref.shape[0]]


def score_parts(b, c, ref, at, times, ahead=None):
    score = dot(b, c, NT)
    if ahead is not None:
        rows = lax.broadcasted_iota(jnp.int32, score.shape, 0)
        columns = lax.broadcasted_iota(jnp.int32, score.shape, 1)
        score = jnp.where(rows <= columns + ahead, score, 0.0)
    hi, lo = halves(score)
    width = score.shape[1]
    ref[at, :width] = hi
    ref[at, width : 2 * width] = lo
    if times == 3:
        ref[at, 2 * width :] = hi


def added_up(v):
    width = v.shape[1] // 2
    return v[:, :width] + v[:, width:]


def local_kernel(first_tile, continued, *refs):
    x_ref, dy_ref, b_ref, c_ref, decays_ref = refs[:5]
    refs = refs[5:]
    if continued:
        out_before_ref, map_before_ref = refs[:2]
        refs = refs[4:]
    part_ref, scaled_ref, out_ref, map_ref = refs[:4]
    lift_ref, drop_ref, rows_ref, full_ref, dys_ref, xs_ref, back_ref, sums_ref, even_ref, odd_ref = refs[4:14]
    level_refs = refs[14:]
    local, tile = x_ref.shape
    chunks = local // SUB
    step = pl.program_id(0)
    levels = [(span, at, level_refs[2 * i], level_refs[2 * i + 1]) for i, (span, at) in enumerate(blocks(chunks))]

    @pl.when(step == 0)
    def _():
        local_factors(decays_ref[...], lift_ref, drop_ref, rows_ref)
        sums_ref[...] = jnp.zeros(sums_ref.shape, F32)
        for k in range(0, chunks, 2):
            pair, even, odd = pl.ds(k * SUB, 2 * SUB), pl.ds(k * SUB, SUB), pl.ds((k + 1) * SUB, SUB)
            score_parts(b_ref[even, :], c_ref[even, :], even_ref, pl.ds(k // 2 * SUB, SUB), 3, 0)
            score_parts(b_ref[pair, :], c_ref[odd, :], odd_ref, pair, 3, SUB)
        for span, boundaries, mixed_ref, scores_ref in levels:
            mixed_ref[...] = jnp.zeros(mixed_ref.shape, F32)
            size = span * SUB
            for i, boundary in enumerate(boundaries):
                before, after = pl.ds((boundary - span) * SUB, size), pl.ds(boundary * SUB, size)
                score_parts(b_ref[before, :], c_ref[after, :], scores_ref, pl.ds(i * size, size), 2)

    first = (first_tile + step) * (tile // P_SIZE)
    dys_ref[...] = dy_ref[...].astype(F32) * spread(lift_ref[...], first, tile)
    back_ref[...] = spread(drop_ref[...], first, tile)
    xs_ref[...] = x_ref[...].astype(F32) * back_ref[...]
    row = spread(rows_ref[...], first, tile)
    factor = lambda kind, k: row[kind * chunks + k : kind * chunks + k + 1]

    for k in range(0, chunks, 2):
        even, odd, pair = pl.ds(k * SUB, SUB), pl.ds((k + 1) * SUB, SUB), pl.ds(k * SUB, 2 * SUB)
        dys, xs = halves(dys_ref[even, :]), halves(xs_ref[even, :])
        sums_ref[even, :] += dot(dys[0], stacked(*xs), NT)
        sums_ref[even, :SUB] += dot(dys[1], xs[0], NT)
        gained_even = dot(even_ref[pl.ds(k // 2 * SUB, SUB), :], stacked(dys[0], dys[0], dys[1]))
        crossing = halves((xs_ref[even, :] * factor(0, k)) * factor(0, k + 1))
        dys, xs = halves(dys_ref[odd, :]), halves(xs_ref[odd, :])
        high = stacked(xs[0], crossing[0])
        both = dot(dys[0], stacked(high, xs[1], crossing[1]), NT)
        sums_ref[odd, :] += added_up(both) + dot(dys[1], high, NT)
        gained_odd = dot(odd_ref[pair, :], stacked(dys[0], dys[0], dys[1]))
        ahead = (back_ref[even, :] * factor(0, k)) * (factor(0, k + 1) * gained_odd[:SUB])
        part_ref[even, :] = back_ref[even, :] * gained_even + ahead
        part_ref[odd, :] = back_ref[odd, :] * gained_odd[SUB:]

    for level, (span, boundaries, mixed_ref, scores_ref) in enumerate(levels, 1):
        size = span * SUB
        for i, boundary in enumerate(boundaries):
            at = pl.ds(i * size, size)
            take = lambda ref, start: halves(
                stacked(*[ref[k * SUB : (k + 1) * SUB, :] * factor(level, k) for k in range(start, start + span)])
            )
            dys, xs = take(dys_ref, boundary), take(xs_ref, boundary - span)
            both = dot(dys[0], stacked(*xs), NT)
            mixed_ref[at, :] += added_up(both) + dot(dys[1], xs[0], NT)
            gained = dot(scores_ref[at, :], stacked(dys[0], dys[0])) + dot(scores_ref[at, :size], dys[1])
            for q in range(span):
                k = boundary - span + q
                rows = pl.ds(k * SUB, SUB)
                part_ref[rows, :] += (back_ref[rows, :] * factor(level, k)) * gained[q * SUB : (q + 1) * SUB]

    for k in range(chunks):
        at = pl.ds(k * SUB, SUB)
        kind = len(levels) + 1
        scaled_ref[1, 0, at, :], scaled_ref[1, 1, at, :] = halves(dys_ref[at, :] * factor(kind, k))
        scaled_ref[0, 0, at, :], scaled_ref[0, 1, at, :] = halves(xs_ref[at, :] * factor(kind + 1, k))

    @pl.when(step == pl.num_programs(0) - 1)
    def _():
        full_ref[...] = jnp.zeros(full_ref.shape, F32)
        rows = lax.broadcasted_iota(jnp.int32, (SUB, SUB), 0)
        columns = lax.broadcasted_iota(jnp.int32, (SUB, SUB), 1)
        for k in range(0, chunks, 2):
            even, odd = pl.ds(k * SUB, SUB), pl.ds((k + 1) * SUB, SUB)
            full_ref[even, k * SUB : (k + 1) * SUB] = jnp.where(rows >= columns, added_up(sums_ref[even, :]), 0.0)
            full_ref[odd, (k + 1) * SUB : (k + 2) * SUB] = jnp.where(rows >= columns, sums_ref[odd, :SUB], 0.0)
            full_ref[odd, k * SUB : (k + 1) * SUB] = sums_ref[odd, SUB:]
        for span, boundaries, mixed_ref, _ in levels:
            size = span * SUB
            for i, boundary in enumerate(boundaries):
                block = mixed_ref[pl.ds(i * size, size), :]
                full_ref[pl.ds(boundary * SUB, size), (boundary - span) * SUB : boundary * SUB] = block
        map_ref[...] = map_before_ref[...] if continued else jnp.zeros(map_ref.shape, F32)
        for k in range(0, local, LANES):
            at = pl.ds(k, LANES)
            mixed = full_ref[at, :]
            gained = dot21(halves(mixed), b_ref[...])
            out_ref[at, :] = out_before_ref[at, :] + gained if continued else gained
            map_ref[...] += dot21(halves(mixed.T), c_ref[at, :])


def local_part(first_tile, count, x, dy, b, c, decays, before=None):
    local, width = x.shape
    chunks = local // SUB
    whole = lambda a: pl.BlockSpec(a.shape, lambda j: (0, 0))
    column = pl.BlockSpec((local, WIDE), lambda j: (0, first_tile + j))
    tokens = pl.BlockSpec((local, N), lambda j: (0, 0))
    scratch = [
        pltpu.VMEM((local, LANES), F32),
        pltpu.VMEM((local, LANES), F32),
        pltpu.VMEM((-(-len(list(row_bounds(chunks))) // 8) * 8, LANES), F32),
        pltpu.VMEM((local, local), F32),
        pltpu.VMEM((local, WIDE), F32),
        pltpu.VMEM((local, WIDE), F32),
        pltpu.VMEM((local, WIDE), F32),
        pltpu.VMEM((local, 2 * SUB), F32),
        pltpu.VMEM((local // 2, 3 * SUB), BF16),
        pltpu.VMEM((local, 3 * SUB), BF16),
    ]
    for span, _ in blocks(chunks):
        scratch.append(pltpu.VMEM((local // 2, span * SUB), F32))
        scratch.append(pltpu.VMEM((local // 2, 2 * span * SUB), BF16))
    in_specs = [column, column, whole(b), whole(c), whole(decays)]
    args, aliases = [x, dy, b, c, decays], {}
    if before is not None:
        part, scaled, out_part, map_part = before
        in_specs += [tokens, tokens, pl.BlockSpec(memory_space=pl.ANY), pl.BlockSpec(memory_space=pl.ANY)]
        args += [out_part, map_part, part, scaled]
        aliases = {7: 0, 8: 1}
    return pl.pallas_call(
        functools.partial(local_kernel, first_tile, before is not None),
        grid=(count,),
        in_specs=in_specs,
        out_specs=(column, pl.BlockSpec((2, 2, local, WIDE), lambda j: (0, 0, 0, first_tile + j)), tokens, tokens),
        out_shape=(
            jax.ShapeDtypeStruct((local, width), F32),
            jax.ShapeDtypeStruct((2, 2, local, width), BF16),
            jax.ShapeDtypeStruct((local, N), F32),
            jax.ShapeDtypeStruct((local, N), F32),
        ),
        scratch_shapes=scratch,
        input_output_aliases=aliases,
        compiler_params=PARAMS,
        name="local_part",
        cost_estimate=pl.CostEstimate(
            flops=40 * local * N * WIDE * count, bytes_accessed=8 * local * WIDE * count, transcendentals=0
        ),
    )(*args)


def map_kernel(count, ranks, scaled_ref, carry_ref, out_before_ref, map_before_ref, *refs):
    messages, (out_ref, map_ref) = refs[:-2], refs[-2:]
    step = pl.program_id(0)

    @pl.when(step == 0)
    def _():
        out_ref[...] = out_before_ref[...]
        map_ref[...] = map_before_ref[...]

    for i, sum_ref in enumerate((map_ref, out_ref)):
        carry = halves(carry_ref[1 - i])
        both = dot(scaled_ref[i, 0], stacked(*carry), NT)
        sum_ref[...] += both[:, :N] + (both[:, N:] + dot(scaled_ref[i, 1], carry[0], NT))

    if messages:

        @pl.when(step == count - 1)
        def _():
            rows = messages[0].shape[1]
            for r, message in enumerate(messages):
                at = pl.ds(pl.multiple_of(((lax.axis_index("head") + r) % ranks) * rows, rows), rows)
                message[0] = out_ref[at, :]
                message[1] = map_ref[at, :]


def map_terms(half, scaled, carry, out_before, map_before, ranks=0):
    local, width = scaled.shape[2], carry.shape[2]
    tile = min(WIDE, width)
    count = width // tile
    whole = lambda a: pl.BlockSpec(a.shape, lambda j: (0,) * len(a.shape))
    tokens = jax.ShapeDtypeStruct((local, N), F32)
    if ranks:
        out_shape = [jax.ShapeDtypeStruct((2, local // ranks, N), F32)] * ranks
        scratch = [pltpu.VMEM((local, N), F32), pltpu.VMEM((local, N), F32)]
    else:
        out_shape, scratch = [tokens, tokens], []
    return pl.pallas_call(
        functools.partial(map_kernel, count, ranks),
        grid=(count,),
        in_specs=[
            pl.BlockSpec((2, 2, local, tile), lambda j: (0, 0, 0, place(half) * count + j)),
            pl.BlockSpec((2, N, tile), lambda j: (0, 0, j)),
            whole(tokens),
            whole(tokens),
        ],
        out_specs=[whole(shape) for shape in out_shape],
        scratch_shapes=scratch,
        out_shape=out_shape,
        compiler_params=PARAMS,
        name="map_terms",
        cost_estimate=pl.CostEstimate(flops=12 * local * N * width, bytes_accessed=8 * local * width, transcendentals=0),
    )(scaled, carry, out_before, map_before)


def input_kernel(heads, count, part_ref, suf_ref, b_ref, own_ref, other_ref, input_ref):
    tile = part_ref.shape[1]
    step = pl.program_id(0)
    after = dot(suf_ref[...], spread_table(heads, step * (tile // P_SIZE), tile))
    grad = jnp.where(step // count == place(CORE), own_ref[0], other_ref[0])
    input_ref[...] = (part_ref[...] + after * dot12(b_ref[...], halves(grad))).astype(BF16)


def input_terms(part, factors, b, own, other):
    local, width = part.shape
    count = width // 2 // WIDE
    whole = lambda a: pl.BlockSpec(a.shape, lambda j: (0, 0))
    column = pl.BlockSpec((local, WIDE), lambda j: (0, j))
    carry = pl.BlockSpec((1, N, WIDE), lambda j: (1, 0, j % count))
    return pl.pallas_call(
        functools.partial(input_kernel, width // P_SIZE, count),
        grid=(2 * count,),
        in_specs=[column, pl.BlockSpec((local, LANES), lambda j: (0, 1)), whole(b), carry, carry],
        out_specs=column,
        out_shape=jax.ShapeDtypeStruct((local, width), BF16),
        compiler_params=PARAMS,
        name="input_terms",
        cost_estimate=pl.CostEstimate(flops=4 * local * N * width, bytes_accessed=8 * local * width, transcendentals=0),
    )(part, factors, b, own, other)


def sums_kernel(*refs):
    shares, (map_ref, out_ref) = refs[:-2], refs[-2:]
    for i, ref in enumerate((out_ref, map_ref)):
        ref[...] = functools.reduce(lambda a, b: a + b, [share[i] for share in shares])


def swap_cores(v, length):
    return lax.ppermute(v, "seq", [(i, i ^ 1) for i in range(length)])


def turned(v, axis, length, by):
    return lax.ppermute(v, axis, [(i, (i + by) % length) for i in range(length)])


def per_device(mixer_input, output_grad, input_map, output_map, decays):
    length, ranks = lax.axis_size("seq"), lax.axis_size("head")
    chips = length // 2
    args = mixer_input, output_grad, input_map, output_map
    sent, factors = other_totals(*args, decays)
    recv = swap_cores(sent, length)
    mine = own_totals(*args, decays)
    tiles = mixer_input.shape[1] // WIDE
    if chips == 4:
        ahead = tiles // 2
        own, back, *others, later = first_phase(length, mine, recv)
        result = local_part(0, ahead, *args, decays)
        others, result = lax.optimization_barrier((others, result))
        cross, same = second_phase(own, back, *others)
        crossing = [crossed(cross, length, 4), crossed(same, length, 2)]
        result, later, _, _ = lax.optimization_barrier((result, later, cross, same))
        result = local_part(ahead, tiles - ahead, *args, decays, result)
        others, result = lax.optimization_barrier((others + [later] + crossing, result))
        own, peer = carried4(mine, recv, *others)
    else:
        messages = chip_totals(chips, mine, recv)
        others = [turned(message, "seq", length, 2 * r) for r, message in enumerate(messages, 1)]
        result = local_part(0, tiles, *args, decays)
        own, peer = carried(chips, mine, recv, others)
    part, scaled, out_part, map_part = result
    other = swap_cores(peer, length)
    out_part, map_part = map_terms(CORE, scaled, own, out_part, map_part)
    shares = map_terms(OTHER, scaled, other, out_part, map_part, ranks)
    own, other, shares = lax.optimization_barrier((own, other, shares))
    sums = [shares[0]] + [turned(shares[r], "head", ranks, r) for r in range(1, ranks)]
    input_grad = input_terms(part, factors, input_map, own, other)
    shape = jax.ShapeDtypeStruct(shares[0].shape[1:], F32)
    input_map_grad, output_map_grad = plain_call(sums_kernel, "head_sums", [shape, shape], *sums)
    return input_grad, input_map_grad, output_map_grad


def solution(mesh):
    in_specs = (
        P("seq", "head"),
        P("seq", "head"),
        P("seq", None),
        P("seq", None),
        P("head", "seq"),
    )
    out_specs = (P("seq", "head"), P(("seq", "head"), None), P(("seq", "head"), None))
    return jax.shard_map(
        per_device, mesh=mesh, in_specs=in_specs, out_specs=out_specs, check_vma=False
    )
```

```python
import functools

import jax
import jax.numpy as jnp
from jax import lax
from jax.experimental import pallas as pl
from jax.experimental.pallas import tpu as pltpu
from jax.sharding import PartitionSpec as P

P_SIZE = 64
N = 128
SUB = 64
TILE = 256
WIDE = 512
EXTRA = 8
PARTS = 4
LANES = 128
CORE, OTHER = range(2)
PARAMS = pltpu.CompilerParams(vmem_limit_bytes=24 * 1024 * 1024)
FIRST = pltpu.CompilerParams(vmem_limit_bytes=56 * 1024 * 1024)
F32 = jnp.float32
BF16 = jnp.bfloat16

NN = (((1,), (0,)), ((), ()))
NT = (((1,), (1,)), ((), ()))


def dot(a, b, dims=NN):
    return lax.dot_general(a, b, dims, preferred_element_type=F32)


def halves(v):
    hi = v.astype(BF16)
    return hi, (v - hi.astype(F32)).astype(BF16)


def dot21(pair, b, dims=NN):
    return dot(pair[0], b, dims) + dot(pair[1], b, dims)


def dot12(a, pair, dims=NN):
    return dot(a, pair[0], dims) + dot(a, pair[1], dims)


def dot22(p, q, dims=NN):
    return dot(p[0], q[0], dims) + (dot(p[0], q[1], dims) + dot(p[1], q[0], dims))


def thirds(v):
    hi = v.astype(BF16)
    rest = v - hi.astype(F32)
    mid = rest.astype(BF16)
    return hi, mid, (rest - mid.astype(F32)).astype(BF16)


def spread(by_head, first, width):
    lanes = lax.broadcasted_iota(jnp.int32, by_head.shape, 1)
    step = LANES // P_SIZE
    shift = P_SIZE.bit_length() - 1
    taken = [
        jnp.take_along_axis(by_head, first + step * k + (lanes >> shift), axis=1) for k in range(width // LANES)
    ]
    return jnp.concatenate(taken, axis=1)


def place(half):
    core = lax.axis_index("seq") % 2
    return core if half == CORE else 1 - core


def stacked(*parts):
    return jnp.concatenate(parts, axis=0)


def transposed(v):
    return v.astype(F32).T.astype(BF16)


def log_parts(decays):
    return jnp.concatenate([part.astype(F32) for part in thirds(jnp.log(decays))], axis=0).astype(BF16)


def summed_logs(logs, table):
    heads = logs.shape[0] // 3
    sums = dot(logs, table.astype(F32).astype(BF16))
    return sums[:heads] + (sums[heads : 2 * heads] + sums[2 * heads :])


def block_sums(logs, table):
    blocks_of = [logs[:, k : k + LANES] for k in range(0, logs.shape[1], LANES)]
    return [summed_logs(block, table) for block in blocks_of]


def by_token(v):
    rest = jnp.zeros((LANES - v.shape[0], v.shape[1]), F32)
    return jnp.concatenate([v, rest], axis=0).T


def packed(v):
    parts = [part.astype(F32) for part in thirds(v)]
    rest = jnp.zeros((LANES - 3 * v.shape[0], v.shape[1]), F32)
    return jnp.concatenate(parts + [rest], axis=0).T.astype(BF16)


def spread_table(heads, first, width):
    rows = lax.broadcasted_iota(jnp.int32, (heads, width), 0)
    columns = lax.broadcasted_iota(jnp.int32, (heads, width), 1)
    offset = columns - (rows - first) * P_SIZE
    picked = ((offset >= 0) & (offset < P_SIZE)).astype(F32)
    rest = jnp.zeros((LANES - 3 * heads, width), F32)
    return jnp.concatenate([picked, picked, picked, rest], axis=0).astype(BF16)


def device_factors(decays, ref):
    logs = log_parts(decays)
    rows = lax.broadcasted_iota(jnp.int32, (LANES, LANES), 0)
    columns = lax.broadcasted_iota(jnp.int32, (LANES, LANES), 1)
    before, after = block_sums(logs, rows <= columns), block_sums(logs, rows > columns)
    totals_of = [block[:, LANES - 1 :] for block in before]
    ahead = behind = jnp.zeros(totals_of[0].shape, F32)
    for k, total in enumerate(totals_of):
        before[k] = before[k] + ahead
        ahead = ahead + total
    for k in reversed(range(len(totals_of))):
        after[k] = after[k] + behind
        behind = behind + totals_of[k]
    ref[:, :LANES] = packed(jnp.exp(jnp.concatenate(before, axis=1)))
    ref[:, LANES:] = packed(jnp.exp(jnp.concatenate(after, axis=1)))


def tile_totals(heads, first, x, dy, bt_ref, ct_ref, factor_ref, out_ref):
    tile = x.shape[1]
    table = spread_table(heads, first, tile)
    before = dot(factor_ref[:, :LANES], table)
    after = dot(factor_ref[:, LANES:], table)
    ended = jnp.broadcast_to(before[before.shape[0] - 1 :, :], (EXTRA, tile))
    for i, (source, factor, other) in enumerate(((x, after, bt_ref), (dy, before, ct_ref))):
        out_ref[i, :N, :] = dot12(other[...], halves(source.astype(F32) * factor))
        out_ref[i, N:, :] = ended


def other_kernel(
    heads, x_ref, dy_ref, b_ref, c_ref, decays_ref, out_ref, factor_ref,
    x_buf, dy_buf, out_buf, b_buf, c_buf, decays_buf, bt_ref, ct_ref, arrived, small, sent,
):
    local, width = x_buf.shape
    count, _, _, tile = out_buf.shape
    smalls = [
        pltpu.make_async_copy(source, buf, small.at[i])
        for i, (source, buf) in enumerate(((decays_ref, decays_buf), (b_ref, b_buf), (c_ref, c_buf)))
    ]
    for load in smalls:
        load.start()
    columns = pl.ds(pl.multiple_of(place(OTHER) * width, width), width)
    loads = []
    for i, (source, buf) in enumerate(((x_ref, x_buf), (dy_ref, dy_buf))):
        for k in range(PARTS):
            rows = pl.ds(k * (local // PARTS), local // PARTS)
            loads.append(pltpu.make_async_copy(source.at[rows, columns], buf.at[rows, :], arrived.at[i, k]))
            loads[-1].start()
    smalls[0].wait()
    device_factors(decays_buf[...], factor_ref)
    smalls[1].wait()
    smalls[2].wait()
    bt_ref[...] = transposed(b_buf[...])
    ct_ref[...] = transposed(c_buf[...])
    stores = []

    def store(k, part, index, rows):
        columns = pl.ds(k * tile, tile)
        copy = pltpu.make_async_copy(out_buf.at[k, index, rows], out_ref.at[index, rows, columns], sent.at[k, part])
        copy.start()
        stores.append(copy)

    def factor(k, lanes):
        return dot(factor_ref[:, lanes], spread_table(heads, (place(OTHER) * count + k) * (tile // P_SIZE), tile))

    for load in loads[:PARTS]:
        load.wait()
    for k in range(count):
        scaled = x_buf[:, k * tile : (k + 1) * tile].astype(F32) * factor(k, slice(LANES, None))
        out_buf[k, 0, :N, :] = dot12(bt_ref[...], halves(scaled))
        store(k, 0, 0, pl.ds(0, N))
    for load in loads[PARTS:]:
        load.wait()
    for k in range(count):
        before = factor(k, slice(0, LANES))
        ended = jnp.broadcast_to(before[local - 1 :, :], (EXTRA, tile))
        out_buf[k, 0, N:, :] = ended
        store(k, 1, 0, pl.ds(N, EXTRA))
        scaled = dy_buf[:, k * tile : (k + 1) * tile].astype(F32) * before
        out_buf[k, 1, :N, :] = dot12(ct_ref[...], halves(scaled))
        out_buf[k, 1, N:, :] = ended
        store(k, 2, 1, pl.ds(0, N + EXTRA))
    for copy in stores:
        copy.wait()


def other_totals(x, dy, b, c, decays):
    local, width = x.shape
    tile = min(WIDE, width // 2)
    count = width // 2 // tile
    anywhere = pl.BlockSpec(memory_space=pl.ANY)
    factor = jax.ShapeDtypeStruct((local, 2 * LANES), BF16)
    return pl.pallas_call(
        functools.partial(other_kernel, width // P_SIZE),
        grid=(1,),
        in_specs=[anywhere] * 5,
        out_specs=[anywhere, pl.BlockSpec(factor.shape, lambda j: (0, 0))],
        out_shape=[jax.ShapeDtypeStruct((2, N + EXTRA, width // 2), F32), factor],
        scratch_shapes=[
            pltpu.VMEM((local, width // 2), BF16),
            pltpu.VMEM((local, width // 2), BF16),
            pltpu.VMEM((count, 2, N + EXTRA, tile), F32),
            pltpu.VMEM(b.shape, BF16),
            pltpu.VMEM(c.shape, BF16),
            pltpu.VMEM(decays.shape, F32),
            pltpu.VMEM((N, local), BF16),
            pltpu.VMEM((N, local), BF16),
            pltpu.SemaphoreType.DMA((2, PARTS)),
            pltpu.SemaphoreType.DMA((3,)),
            pltpu.SemaphoreType.DMA((count, 3)),
        ],
        compiler_params=FIRST,
        name="other_totals",
        cost_estimate=pl.CostEstimate(flops=8 * local * N * width // 2, bytes_accessed=4 * local * width, transcendentals=0),
    )(x, dy, b, c, decays)


def own_kernel(heads, count, x_ref, dy_ref, b_ref, c_ref, decays_ref, out_ref, bt_ref, ct_ref, factor_ref):
    step = pl.program_id(0)

    @pl.when(step == 0)
    def _():
        bt_ref[...] = transposed(b_ref[...])
        ct_ref[...] = transposed(c_ref[...])
        device_factors(decays_ref[...], factor_ref)

    first = (place(CORE) * count + step) * (x_ref.shape[1] // P_SIZE)
    tile_totals(heads, first, x_ref[...], dy_ref[...], bt_ref, ct_ref, factor_ref, out_ref)


def own_totals(x, dy, b, c, decays):
    local, width = x.shape
    tile = min(WIDE, width // 2)
    count = width // 2 // tile
    whole = lambda a: pl.BlockSpec(a.shape, lambda j: (0, 0))
    column = pl.BlockSpec((local, tile), lambda j: (0, place(CORE) * count + j))
    return pl.pallas_call(
        functools.partial(own_kernel, width // P_SIZE, count),
        grid=(count,),
        in_specs=[column, column, whole(b), whole(c), whole(decays)],
        out_specs=pl.BlockSpec((2, N + EXTRA, tile), lambda j: (0, 0, j)),
        scratch_shapes=[
            pltpu.VMEM((N, local), BF16),
            pltpu.VMEM((N, local), BF16),
            pltpu.VMEM((local, 2 * LANES), BF16),
        ],
        out_shape=jax.ShapeDtypeStruct((2, N + EXTRA, width // 2), F32),
        compiler_params=PARAMS,
        name="own_totals",
        cost_estimate=pl.CostEstimate(flops=8 * local * N * width // 2, bytes_accessed=4 * local * width, transcendentals=0),
    )(x, dy, b, c, decays)


def ordered(core, mine, recv):
    return jnp.where(core == 0, mine, recv), jnp.where(core == 0, recv, mine)


def chip_kernel(chips, mine_ref, recv_ref, *out_refs):
    core, chip = place(CORE), lax.axis_index("seq") // 2
    early, late = ordered(core, mine_ref[0], recv_ref[0])
    early_decay, late_decay = early[N : N + 1], late[N : N + 1]
    both = jnp.broadcast_to(early_decay * late_decay, (EXTRA, early.shape[1]))
    state = late_decay * early[:N] + late[:N]
    early, late = ordered(core, mine_ref[1], recv_ref[1])
    grad = early[:N] + early_decay * late[:N]
    for r, out_ref in enumerate(out_refs, 1):
        out_ref[:N, :] = jnp.where(chip + r < chips, state, grad)
        out_ref[N:, :] = both


def chip_totals(chips, mine, recv):
    width = mine.shape[2]
    tile = min(512, width)
    block = pl.BlockSpec((2, N + EXTRA, tile), lambda j: (0, 0, j))
    out = pl.BlockSpec((N + EXTRA, tile), lambda j: (0, j))
    shape = jax.ShapeDtypeStruct((N + EXTRA, width), F32)
    return pl.pallas_call(
        functools.partial(chip_kernel, chips),
        grid=(width // tile,),
        in_specs=[block, block],
        out_specs=[out] * (chips - 1),
        out_shape=[shape] * (chips - 1),
        compiler_params=PARAMS,
        name="chip_totals",
        cost_estimate=pl.CostEstimate(flops=6 * N * width, bytes_accessed=24 * N * width, transcendentals=0),
    )(mine, recv)


def sides():
    chip = lax.axis_index("seq") // 2
    return chip < 2, (chip == 1) | (chip == 2)


def first_kernel(mine_ref, recv_ref, same_ref, later_ref, cross_ref, back_ref, decay_ref):
    left, inner = sides()
    core = place(CORE)
    width = mine_ref.shape[2] // 2
    early, late = ordered(core, mine_ref[0], recv_ref[0])
    early_decay, late_decay = early[N : N + 1], late[N : N + 1]
    state = late_decay * early[:N] + late[:N]
    decay = early_decay * late_decay
    early, late = ordered(core, mine_ref[1], recv_ref[1])
    grad = early[:N] + early_decay * late[:N]
    out, back = jnp.where(left, state, grad), jnp.where(left, grad, state)
    same_ref[:N, :] = out[:, :width]
    later_ref[...] = jnp.where(inner, back[:, :width], out[:, width:])
    rows = lax.broadcasted_iota(jnp.int32, (EXTRA, width), 0)
    same_ref[N:, :] = jnp.where(rows == 0, decay[:, :width], decay[:, width:])
    cross_ref[...] = out[:, width:]
    back_ref[...] = back[:, width:]
    decay_ref[...] = jnp.broadcast_to(decay[:, width:], (EXTRA, width))


def second_kernel(own_ref, back_ref, same_ref, cross_ref, decay_ref, cross2_ref, same2_ref):
    _, inner = sides()
    own, other = own_ref[:N, :], same_ref[:N, :]
    own_decay, other_decay = own_ref[N : N + 1, :], same_ref[N : N + 1, :]
    cross2_ref[...] = jnp.where(inner, own + own_decay * other, other + other_decay * own)
    weight = own_ref[N + 1 : N + 2, :] * decay_ref[:1, :]
    same2_ref[...] = jnp.where(inner, back_ref[...] + weight * cross_ref[...], cross_ref[...])


def plain_call(kernel, name, out_shape, *args):
    whole = lambda a: pl.BlockSpec(a.shape, lambda j: (0,) * len(a.shape))
    size = sum(a.size for a in args)
    return pl.pallas_call(
        kernel,
        grid=(1,),
        in_specs=[whole(a) for a in args],
        out_specs=[whole(a) for a in out_shape],
        out_shape=out_shape,
        compiler_params=PARAMS,
        name=name,
        cost_estimate=pl.CostEstimate(flops=8 * size, bytes_accessed=4 * size, transcendentals=0),
    )(*args)


def crossed(v, length, bit):
    return lax.ppermute(v, "seq", [(i, i ^ bit) for i in range(length)])


def first_phase(length, mine, recv):
    half = mine.shape[2] // 2
    shapes = [jax.ShapeDtypeStruct((rows, half), F32) for rows in (N + EXTRA, N, N, N, EXTRA)]
    own, later, cross, back, decay = plain_call(first_kernel, "first_messages", shapes, mine, recv)
    same, cross, decay = crossed(own, length, 2), crossed(cross, length, 4), crossed(decay, length, 6)
    return own, back, same, cross, decay, crossed(later, length, 2)


def second_phase(own, back, same, cross, decay):
    shape = jax.ShapeDtypeStruct(back.shape, F32)
    return plain_call(second_kernel, "second_messages", [shape, shape], own, back, same, cross, decay)


def carried4_kernel(
    mine_ref, recv_ref, same_ref, cross_ref, decay_ref, later_ref, cross2_ref, same2_ref, own_ref, peer_ref
):
    left, inner = sides()
    width = cross_ref.shape[1]
    decay_a, decay_b = same_ref[N : N + 1, :], same_ref[N + 1 : N + 2, :]
    for part in range(2):
        at = slice(part * width, (part + 1) * width)
        out = jnp.where(inner, later_ref[...] if part else same_ref[:N, :], 0.0)
        if part == 0:
            back = jnp.where(inner, cross2_ref[...], later_ref[...] + decay_a * cross2_ref[...])
        else:
            back = same2_ref[...] + jnp.where(inner, decay_ref[:1, :], decay_b) * cross_ref[...]
        carried_cores(
            place(CORE), jnp.where(left, out, back), jnp.where(left, back, out), mine_ref, recv_ref, own_ref, peer_ref, at
        )


def carried4(mine, recv, *others):
    shape = jax.ShapeDtypeStruct((2, N, mine.shape[2]), F32)
    return plain_call(carried4_kernel, "carried_in", [shape, shape], mine, recv, *others)


def carried_cores(core, state, grad, mine_ref, recv_ref, own_ref, peer_ref, at):
    early, late = ordered(core, mine_ref[0, :, at], recv_ref[0, :, at])
    at_late = early[N : N + 1] * state + early[:N]
    own_ref[0, :, at] = jnp.where(core == 0, state, at_late)
    peer_ref[0, :, at] = jnp.where(core == 0, at_late, state)
    early, late = ordered(core, mine_ref[1, :, at], recv_ref[1, :, at])
    at_early = late[:N] + late[N : N + 1] * grad
    own_ref[1, :, at] = jnp.where(core == 0, at_early, grad)
    peer_ref[1, :, at] = jnp.where(core == 0, grad, at_early)


def carried_kernel(chips, mine_ref, recv_ref, *refs):
    others, (own_ref, peer_ref) = refs[:-2], refs[-2:]
    core, chip = place(CORE), lax.axis_index("seq") // 2
    state = grad = jnp.zeros((N, own_ref.shape[2]), F32)
    state_weight = grad_weight = jnp.ones((1, own_ref.shape[2]), F32)
    for r, ref in enumerate(others, 1):
        earlier = chip >= r
        state = jnp.where(earlier, state + state_weight * ref[:N, :], state)
        state_weight = state_weight * ref[N : N + 1, :]
    for r in range(1, chips):
        later = chip + r < chips
        ref = others[chips - r - 1]
        grad = jnp.where(later, grad + grad_weight * ref[:N, :], grad)
        grad_weight = grad_weight * ref[N : N + 1, :]
    carried_cores(core, state, grad, mine_ref, recv_ref, own_ref, peer_ref, slice(None))


def carried(chips, mine, recv, others):
    width = mine.shape[2]
    tile = min(512, width)
    pair = pl.BlockSpec((2, N + EXTRA, tile), lambda j: (0, 0, j))
    other = pl.BlockSpec((N + EXTRA, tile), lambda j: (0, j))
    out = pl.BlockSpec((2, N, tile), lambda j: (0, 0, j))
    shape = jax.ShapeDtypeStruct((2, N, width), F32)
    return pl.pallas_call(
        functools.partial(carried_kernel, chips),
        grid=(width // tile,),
        in_specs=[pair, pair] + [other] * len(others),
        out_specs=(out, out),
        out_shape=(shape, shape),
        compiler_params=PARAMS,
        name="carried_in",
        cost_estimate=pl.CostEstimate(flops=20 * N * width, bytes_accessed=44 * N * width, transcendentals=0),
    )(mine, recv, *others)


def blocks(chunks):
    span = 2
    while span < chunks:
        yield span, [at for at in range(span, chunks, 2 * span)]
        span *= 2


def row_bounds(chunks):
    middles = [k * SUB + SUB // 2 + 1 for k in range(chunks)]
    for span in [1] + [span for span, _ in blocks(chunks)]:
        for k, middle in enumerate(middles):
            boundary = (k // span + 1 - (k // span) % 2) * span * SUB
            yield min(boundary, middle), max(boundary, middle)
    yield from ((0, middle) for middle in middles)
    yield from ((middle, chunks * SUB) for middle in middles)


def local_factors(decays, lift_ref, drop_ref, rows_ref):
    local = decays.shape[1]
    logs = log_parts(decays)
    rows = lax.broadcasted_iota(jnp.int32, (LANES, LANES), 0)
    columns = lax.broadcasted_iota(jnp.int32, (LANES, LANES), 1)
    middle = (columns & -SUB) + SUB // 2
    later = (rows > middle) & (rows <= columns)
    sooner = (rows > columns) & (rows <= middle)
    offset = jnp.concatenate(block_sums(logs, later.astype(F32) - sooner.astype(F32)), axis=1)
    lift_ref[...] = by_token(jnp.exp(offset))
    drop_ref[...] = by_token(jnp.exp(-offset))
    lane = lax.broadcasted_iota(jnp.int32, (1, LANES), 1)
    first = last = jnp.zeros((1, LANES), jnp.int32)
    for i, (start, end) in enumerate(row_bounds(local // SUB)):
        first, last = jnp.where(lane == i, start, first), jnp.where(lane == i, end, last)
    rows = lax.broadcasted_iota(jnp.int32, (local, LANES), 0)
    decay = by_token(jnp.exp(summed_logs(logs, (rows >= first) & (rows < last))))
    rows_ref[...] = decay[: rows_ref.shape[0]]


def score_parts(b, c, ref, at, times, ahead=None):
    score = dot(b, c, NT)
    if ahead is not None:
        rows = lax.broadcasted_iota(jnp.int32, score.shape, 0)
        columns = lax.broadcasted_iota(jnp.int32, score.shape, 1)
        score = jnp.where(rows <= columns + ahead, score, 0.0)
    hi, lo = halves(score)
    width = score.shape[1]
    ref[at, :width] = hi
    ref[at, width : 2 * width] = lo
    if times == 3:
        ref[at, 2 * width :] = hi


def added_up(v):
    width = v.shape[1] // 2
    return v[:, :width] + v[:, width:]


def local_kernel(first_tile, continued, *refs):
    x_ref, dy_ref, b_ref, c_ref, decays_ref = refs[:5]
    refs = refs[5:]
    if continued:
        out_before_ref, map_before_ref = refs[:2]
        refs = refs[4:]
    part_ref, scaled_ref, out_ref, map_ref = refs[:4]
    lift_ref, drop_ref, rows_ref, full_ref, dys_ref, xs_ref, back_ref, sums_ref, even_ref, odd_ref = refs[4:14]
    level_refs = refs[14:]
    local, tile = x_ref.shape
    chunks = local // SUB
    step = pl.program_id(0)
    levels = [(span, at, level_refs[2 * i], level_refs[2 * i + 1]) for i, (span, at) in enumerate(blocks(chunks))]

    @pl.when(step == 0)
    def _():
        local_factors(decays_ref[...], lift_ref, drop_ref, rows_ref)
        sums_ref[...] = jnp.zeros(sums_ref.shape, F32)
        for k in range(0, chunks, 2):
            pair, even, odd = pl.ds(k * SUB, 2 * SUB), pl.ds(k * SUB, SUB), pl.ds((k + 1) * SUB, SUB)
            score_parts(b_ref[even, :], c_ref[even, :], even_ref, pl.ds(k // 2 * SUB, SUB), 3, 0)
            score_parts(b_ref[pair, :], c_ref[odd, :], odd_ref, pair, 3, SUB)
        for span, boundaries, mixed_ref, scores_ref in levels:
            mixed_ref[...] = jnp.zeros(mixed_ref.shape, F32)
            size = span * SUB
            for i, boundary in enumerate(boundaries):
                before, after = pl.ds((boundary - span) * SUB, size), pl.ds(boundary * SUB, size)
                score_parts(b_ref[before, :], c_ref[after, :], scores_ref, pl.ds(i * size, size), 2)

    first = (first_tile + step) * (tile // P_SIZE)
    dys_ref[...] = dy_ref[...].astype(F32) * spread(lift_ref[...], first, tile)
    back_ref[...] = spread(drop_ref[...], first, tile)
    xs_ref[...] = x_ref[...].astype(F32) * back_ref[...]
    row = spread(rows_ref[...], first, tile)
    factor = lambda kind, k: row[kind * chunks + k : kind * chunks + k + 1]

    for k in range(0, chunks, 2):
        even, odd, pair = pl.ds(k * SUB, SUB), pl.ds((k + 1) * SUB, SUB), pl.ds(k * SUB, 2 * SUB)
        dys, xs = halves(dys_ref[even, :]), halves(xs_ref[even, :])
        sums_ref[even, :] += dot(dys[0], stacked(*xs), NT)
        sums_ref[even, :SUB] += dot(dys[1], xs[0], NT)
        gained_even = dot(even_ref[pl.ds(k // 2 * SUB, SUB), :], stacked(dys[0], dys[0], dys[1]))
        crossing = halves((xs_ref[even, :] * factor(0, k)) * factor(0, k + 1))
        dys, xs = halves(dys_ref[odd, :]), halves(xs_ref[odd, :])
        high = stacked(xs[0], crossing[0])
        both = dot(dys[0], stacked(high, xs[1], crossing[1]), NT)
        sums_ref[odd, :] += added_up(both) + dot(dys[1], high, NT)
        gained_odd = dot(odd_ref[pair, :], stacked(dys[0], dys[0], dys[1]))
        ahead = (back_ref[even, :] * factor(0, k)) * (factor(0, k + 1) * gained_odd[:SUB])
        part_ref[even, :] = back_ref[even, :] * gained_even + ahead
        part_ref[odd, :] = back_ref[odd, :] * gained_odd[SUB:]

    for level, (span, boundaries, mixed_ref, scores_ref) in enumerate(levels, 1):
        size = span * SUB
        for i, boundary in enumerate(boundaries):
            at = pl.ds(i * size, size)
            take = lambda ref, start: halves(
                stacked(*[ref[k * SUB : (k + 1) * SUB, :] * factor(level, k) for k in range(start, start + span)])
            )
            dys, xs = take(dys_ref, boundary), take(xs_ref, boundary - span)
            both = dot(dys[0], stacked(*xs), NT)
            mixed_ref[at, :] += added_up(both) + dot(dys[1], xs[0], NT)
            gained = dot(scores_ref[at, :], stacked(dys[0], dys[0])) + dot(scores_ref[at, :size], dys[1])
            for q in range(span):
                k = boundary - span + q
                rows = pl.ds(k * SUB, SUB)
                part_ref[rows, :] += (back_ref[rows, :] * factor(level, k)) * gained[q * SUB : (q + 1) * SUB]

    for k in range(chunks):
        at = pl.ds(k * SUB, SUB)
        kind = len(levels) + 1
        scaled_ref[1, 0, at, :], scaled_ref[1, 1, at, :] = halves(dys_ref[at, :] * factor(kind, k))
        scaled_ref[0, 0, at, :], scaled_ref[0, 1, at, :] = halves(xs_ref[at, :] * factor(kind + 1, k))

    @pl.when(step == pl.num_programs(0) - 1)
    def _():
        full_ref[...] = jnp.zeros(full_ref.shape, F32)
        rows = lax.broadcasted_iota(jnp.int32, (SUB, SUB), 0)
        columns = lax.broadcasted_iota(jnp.int32, (SUB, SUB), 1)
        for k in range(0, chunks, 2):
            even, odd = pl.ds(k * SUB, SUB), pl.ds((k + 1) * SUB, SUB)
            full_ref[even, k * SUB : (k + 1) * SUB] = jnp.where(rows >= columns, added_up(sums_ref[even, :]), 0.0)
            full_ref[odd, (k + 1) * SUB : (k + 2) * SUB] = jnp.where(rows >= columns, sums_ref[odd, :SUB], 0.0)
            full_ref[odd, k * SUB : (k + 1) * SUB] = sums_ref[odd, SUB:]
        for span, boundaries, mixed_ref, _ in levels:
            size = span * SUB
            for i, boundary in enumerate(boundaries):
                block = mixed_ref[pl.ds(i * size, size), :]
                full_ref[pl.ds(boundary * SUB, size), (boundary - span) * SUB : boundary * SUB] = block
        map_ref[...] = map_before_ref[...] if continued else jnp.zeros(map_ref.shape, F32)
        for k in range(0, local, LANES):
            at = pl.ds(k, LANES)
            mixed = full_ref[at, :]
            gained = dot21(halves(mixed), b_ref[...])
            out_ref[at, :] = out_before_ref[at, :] + gained if continued else gained
            map_ref[...] += dot21(halves(mixed.T), c_ref[at, :])


def local_part(first_tile, count, x, dy, b, c, decays, before=None):
    local, width = x.shape
    chunks = local // SUB
    whole = lambda a: pl.BlockSpec(a.shape, lambda j: (0, 0))
    column = pl.BlockSpec((local, WIDE), lambda j: (0, first_tile + j))
    tokens = pl.BlockSpec((local, N), lambda j: (0, 0))
    scratch = [
        pltpu.VMEM((local, LANES), F32),
        pltpu.VMEM((local, LANES), F32),
        pltpu.VMEM((-(-len(list(row_bounds(chunks))) // 8) * 8, LANES), F32),
        pltpu.VMEM((local, local), F32),
        pltpu.VMEM((local, WIDE), F32),
        pltpu.VMEM((local, WIDE), F32),
        pltpu.VMEM((local, WIDE), F32),
        pltpu.VMEM((local, 2 * SUB), F32),
        pltpu.VMEM((local // 2, 3 * SUB), BF16),
        pltpu.VMEM((local, 3 * SUB), BF16),
    ]
    for span, _ in blocks(chunks):
        scratch.append(pltpu.VMEM((local // 2, span * SUB), F32))
        scratch.append(pltpu.VMEM((local // 2, 2 * span * SUB), BF16))
    in_specs = [column, column, whole(b), whole(c), whole(decays)]
    args, aliases = [x, dy, b, c, decays], {}
    if before is not None:
        part, scaled, out_part, map_part = before
        in_specs += [tokens, tokens, pl.BlockSpec(memory_space=pl.ANY), pl.BlockSpec(memory_space=pl.ANY)]
        args += [out_part, map_part, part, scaled]
        aliases = {7: 0, 8: 1}
    return pl.pallas_call(
        functools.partial(local_kernel, first_tile, before is not None),
        grid=(count,),
        in_specs=in_specs,
        out_specs=(column, pl.BlockSpec((2, 2, local, WIDE), lambda j: (0, 0, 0, first_tile + j)), tokens, tokens),
        out_shape=(
            jax.ShapeDtypeStruct((local, width), F32),
            jax.ShapeDtypeStruct((2, 2, local, width), BF16),
            jax.ShapeDtypeStruct((local, N), F32),
            jax.ShapeDtypeStruct((local, N), F32),
        ),
        scratch_shapes=scratch,
        input_output_aliases=aliases,
        compiler_params=PARAMS,
        name="local_part",
        cost_estimate=pl.CostEstimate(
            flops=40 * local * N * WIDE * count, bytes_accessed=8 * local * WIDE * count, transcendentals=0
        ),
    )(*args)


def map_kernel(count, ranks, scaled_ref, carry_ref, out_before_ref, map_before_ref, *refs):
    messages, (out_ref, map_ref) = refs[:-2], refs[-2:]
    step = pl.program_id(0)

    @pl.when(step == 0)
    def _():
        out_ref[...] = out_before_ref[...]
        map_ref[...] = map_before_ref[...]

    for i, sum_ref in enumerate((map_ref, out_ref)):
        carry = halves(carry_ref[1 - i])
        both = dot(scaled_ref[i, 0], stacked(*carry), NT)
        sum_ref[...] += both[:, :N] + (both[:, N:] + dot(scaled_ref[i, 1], carry[0], NT))

    if messages:

        @pl.when(step == count - 1)
        def _():
            rows = messages[0].shape[1]
            for r, message in enumerate(messages):
                at = pl.ds(pl.multiple_of(((lax.axis_index("head") + r) % ranks) * rows, rows), rows)
                message[0] = out_ref[at, :]
                message[1] = map_ref[at, :]


def map_terms(half, scaled, carry, out_before, map_before, ranks=0):
    local, width = scaled.shape[2], carry.shape[2]
    tile = min(WIDE, width)
    count = width // tile
    whole = lambda a: pl.BlockSpec(a.shape, lambda j: (0,) * len(a.shape))
    tokens = jax.ShapeDtypeStruct((local, N), F32)
    if ranks:
        out_shape = [jax.ShapeDtypeStruct((2, local // ranks, N), F32)] * ranks
        scratch = [pltpu.VMEM((local, N), F32), pltpu.VMEM((local, N), F32)]
    else:
        out_shape, scratch = [tokens, tokens], []
    return pl.pallas_call(
        functools.partial(map_kernel, count, ranks),
        grid=(count,),
        in_specs=[
            pl.BlockSpec((2, 2, local, tile), lambda j: (0, 0, 0, place(half) * count + j)),
            pl.BlockSpec((2, N, tile), lambda j: (0, 0, j)),
            whole(tokens),
            whole(tokens),
        ],
        out_specs=[whole(shape) for shape in out_shape],
        scratch_shapes=scratch,
        out_shape=out_shape,
        compiler_params=PARAMS,
        name="map_terms",
        cost_estimate=pl.CostEstimate(flops=12 * local * N * width, bytes_accessed=8 * local * width, transcendentals=0),
    )(scaled, carry, out_before, map_before)


def input_kernel(heads, count, part_ref, suf_ref, b_ref, own_ref, other_ref, input_ref):
    tile = part_ref.shape[1]
    step = pl.program_id(0)
    after = dot(suf_ref[...], spread_table(heads, step * (tile // P_SIZE), tile))
    grad = jnp.where(step // count == place(CORE), own_ref[0], other_ref[0])
    input_ref[...] = (part_ref[...] + after * dot12(b_ref[...], halves(grad))).astype(BF16)


def input_terms(part, factors, b, own, other):
    local, width = part.shape
    count = width // 2 // WIDE
    whole = lambda a: pl.BlockSpec(a.shape, lambda j: (0, 0))
    column = pl.BlockSpec((local, WIDE), lambda j: (0, j))
    carry = pl.BlockSpec((1, N, WIDE), lambda j: (1, 0, j % count))
    return pl.pallas_call(
        functools.partial(input_kernel, width // P_SIZE, count),
        grid=(2 * count,),
        in_specs=[column, pl.BlockSpec((local, LANES), lambda j: (0, 1)), whole(b), carry, carry],
        out_specs=column,
        out_shape=jax.ShapeDtypeStruct((local, width), BF16),
        compiler_params=PARAMS,
        name="input_terms",
        cost_estimate=pl.CostEstimate(flops=4 * local * N * width, bytes_accessed=8 * local * width, transcendentals=0),
    )(part, factors, b, own, other)


def sums_kernel(*refs):
    shares, (map_ref, out_ref) = refs[:-2], refs[-2:]
    for i, ref in enumerate((out_ref, map_ref)):
        ref[...] = functools.reduce(lambda a, b: a + b, [share[i] for share in shares])


def swap_cores(v, length):
    return lax.ppermute(v, "seq", [(i, i ^ 1) for i in range(length)])


def turned(v, axis, length, by):
    return lax.ppermute(v, axis, [(i, (i + by) % length) for i in range(length)])


def per_device(mixer_input, output_grad, input_map, output_map, decays):
    length, ranks = lax.axis_size("seq"), lax.axis_size("head")
    chips = length // 2
    args = mixer_input, output_grad, input_map, output_map
    sent, factors = other_totals(*args, decays)
    recv = swap_cores(sent, length)
    mine = own_totals(*args, decays)
    tiles = mixer_input.shape[1] // WIDE
    if chips == 4:
        ahead = tiles // 2
        own, back, *others, later = first_phase(length, mine, recv)
        result = local_part(0, ahead, *args, decays)
        others, result = lax.optimization_barrier((others, result))
        cross, same = second_phase(own, back, *others)
        crossing = [crossed(cross, length, 4), crossed(same, length, 2)]
        result, later, _, _ = lax.optimization_barrier((result, later, cross, same))
        result = local_part(ahead, tiles - ahead, *args, decays, result)
        others, result = lax.optimization_barrier((others + [later] + crossing, result))
        own, peer = carried4(mine, recv, *others)
    else:
        messages = chip_totals(chips, mine, recv)
        others = [turned(message, "seq", length, 2 * r) for r, message in enumerate(messages, 1)]
        result = local_part(0, tiles, *args, decays)
        own, peer = carried(chips, mine, recv, others)
    part, scaled, out_part, map_part = result
    other = swap_cores(peer, length)
    out_part, map_part = map_terms(CORE, scaled, own, out_part, map_part)
    shares = map_terms(OTHER, scaled, other, out_part, map_part, ranks)
    own, other, shares = lax.optimization_barrier((own, other, shares))
    sums = [shares[0]] + [turned(shares[r], "head", ranks, r) for r in range(1, ranks)]
    input_grad = input_terms(part, factors, input_map, own, other)
    shape = jax.ShapeDtypeStruct(shares[0].shape[1:], F32)
    input_map_grad, output_map_grad = plain_call(sums_kernel, "head_sums", [shape, shape], *sums)
    return input_grad, input_map_grad, output_map_grad


def solution(mesh):
    in_specs = (
        P("seq", "head"),
        P("seq", "head"),
        P("seq", None),
        P("seq", None),
        P("head", "seq"),
    )
    out_specs = (P("seq", "head"), P(("seq", "head"), None), P(("seq", "head"), None))
    return jax.shard_map(
        per_device, mesh=mesh, in_specs=in_specs, out_specs=out_specs, check_vma=False
    )
```

```python
import functools

import jax
import jax.numpy as jnp
from jax import lax
from jax.experimental import pallas as pl
from jax.experimental.pallas import tpu as pltpu
from jax.sharding import PartitionSpec as P

P_SIZE = 64
N = 128
SUB = 64
TILE = 256
WIDE = 512
EXTRA = 8
PARTS = 4
LANES = 128
CORE, OTHER = range(2)
PARAMS = pltpu.CompilerParams(vmem_limit_bytes=24 * 1024 * 1024)
FIRST = pltpu.CompilerParams(vmem_limit_bytes=56 * 1024 * 1024)
F32 = jnp.float32
BF16 = jnp.bfloat16

NN = (((1,), (0,)), ((), ()))
NT = (((1,), (1,)), ((), ()))


def dot(a, b, dims=NN):
    return lax.dot_general(a, b, dims, preferred_element_type=F32)


def halves(v):
    hi = v.astype(BF16)
    return hi, (v - hi.astype(F32)).astype(BF16)


def dot21(pair, b, dims=NN):
    return dot(pair[0], b, dims) + dot(pair[1], b, dims)


def dot12(a, pair, dims=NN):
    return dot(a, pair[0], dims) + dot(a, pair[1], dims)


def dot22(p, q, dims=NN):
    return dot(p[0], q[0], dims) + (dot(p[0], q[1], dims) + dot(p[1], q[0], dims))


def thirds(v):
    hi = v.astype(BF16)
    rest = v - hi.astype(F32)
    mid = rest.astype(BF16)
    return hi, mid, (rest - mid.astype(F32)).astype(BF16)


def spread(by_head, first, width):
    lanes = lax.broadcasted_iota(jnp.int32, by_head.shape, 1)
    step = LANES // P_SIZE
    shift = P_SIZE.bit_length() - 1
    taken = [
        jnp.take_along_axis(by_head, first + step * k + (lanes >> shift), axis=1) for k in range(width // LANES)
    ]
    return jnp.concatenate(taken, axis=1)


def place(half):
    core = lax.axis_index("seq") % 2
    return core if half == CORE else 1 - core


def stacked(*parts):
    return jnp.concatenate(parts, axis=0)


def transposed(v):
    return v.astype(F32).T.astype(BF16)


def log_parts(decays):
    return jnp.concatenate([part.astype(F32) for part in thirds(jnp.log(decays))], axis=0).astype(BF16)


def summed_logs(logs, table):
    heads = logs.shape[0] // 3
    sums = dot(logs, table.astype(F32).astype(BF16))
    return sums[:heads] + (sums[heads : 2 * heads] + sums[2 * heads :])


def block_sums(logs, table):
    blocks_of = [logs[:, k : k + LANES] for k in range(0, logs.shape[1], LANES)]
    return [summed_logs(block, table) for block in blocks_of]


def by_token(v):
    rest = jnp.zeros((LANES - v.shape[0], v.shape[1]), F32)
    return jnp.concatenate([v, rest], axis=0).T


def packed(v):
    parts = [part.astype(F32) for part in thirds(v)]
    rest = jnp.zeros((LANES - 3 * v.shape[0], v.shape[1]), F32)
    return jnp.concatenate(parts + [rest], axis=0).T.astype(BF16)


def spread_table(heads, first, width):
    rows = lax.broadcasted_iota(jnp.int32, (heads, width), 0)
    columns = lax.broadcasted_iota(jnp.int32, (heads, width), 1)
    offset = columns - (rows - first) * P_SIZE
    picked = ((offset >= 0) & (offset < P_SIZE)).astype(F32)
    rest = jnp.zeros((LANES - 3 * heads, width), F32)
    return jnp.concatenate([picked, picked, picked, rest], axis=0).astype(BF16)


def device_factors(decays, ref):
    logs = log_parts(decays)
    rows = lax.broadcasted_iota(jnp.int32, (LANES, LANES), 0)
    columns = lax.broadcasted_iota(jnp.int32, (LANES, LANES), 1)
    before, after = block_sums(logs, rows <= columns), block_sums(logs, rows > columns)
    totals_of = [block[:, LANES - 1 :] for block in before]
    ahead = behind = jnp.zeros(totals_of[0].shape, F32)
    for k, total in enumerate(totals_of):
        before[k] = before[k] + ahead
        ahead = ahead + total
    for k in reversed(range(len(totals_of))):
        after[k] = after[k] + behind
        behind = behind + totals_of[k]
    ref[:, :LANES] = packed(jnp.exp(jnp.concatenate(before, axis=1)))
    ref[:, LANES:] = packed(jnp.exp(jnp.concatenate(after, axis=1)))


def tile_totals(heads, first, x, dy, bt_ref, ct_ref, factor_ref, out_ref):
    tile = x.shape[1]
    table = spread_table(heads, first, tile)
    before = dot(factor_ref[:, :LANES], table)
    after = dot(factor_ref[:, LANES:], table)
    ended = jnp.broadcast_to(before[before.shape[0] - 1 :, :], (EXTRA, tile))
    for i, (source, factor, other) in enumerate(((x, after, bt_ref), (dy, before, ct_ref))):
        out_ref[i, :N, :] = dot12(other[...], halves(source.astype(F32) * factor))
        out_ref[i, N:, :] = ended


def other_kernel(
    heads, x_ref, dy_ref, b_ref, c_ref, decays_ref, out_ref, factor_ref,
    x_buf, dy_buf, out_buf, b_buf, c_buf, decays_buf, bt_ref, ct_ref, arrived, small, sent,
):
    local, width = x_buf.shape
    count, _, _, tile = out_buf.shape
    smalls = [
        pltpu.make_async_copy(source, buf, small.at[i])
        for i, (source, buf) in enumerate(((decays_ref, decays_buf), (b_ref, b_buf), (c_ref, c_buf)))
    ]
    for load in smalls:
        load.start()
    columns = pl.ds(pl.multiple_of(place(OTHER) * width, width), width)
    loads = []
    for i, (source, buf) in enumerate(((x_ref, x_buf), (dy_ref, dy_buf))):
        for k in range(PARTS):
            rows = pl.ds(k * (local // PARTS), local // PARTS)
            loads.append(pltpu.make_async_copy(source.at[rows, columns], buf.at[rows, :], arrived.at[i, k]))
            loads[-1].start()
    smalls[0].wait()
    device_factors(decays_buf[...], factor_ref)
    smalls[1].wait()
    smalls[2].wait()
    bt_ref[...] = transposed(b_buf[...])
    ct_ref[...] = transposed(c_buf[...])
    for load in loads:
        load.wait()
    stores = []
    for k in range(count):
        first = (place(OTHER) * count + k) * (tile // P_SIZE)
        x, dy = x_buf[:, k * tile : (k + 1) * tile], dy_buf[:, k * tile : (k + 1) * tile]
        tile_totals(heads, first, x, dy, bt_ref, ct_ref, factor_ref, out_buf.at[k])
        stores.append(pltpu.make_async_copy(out_buf.at[k], out_ref.at[:, :, pl.ds(k * tile, tile)], sent.at[k]))
        stores[-1].start()
    for store in stores:
        store.wait()


def other_totals(x, dy, b, c, decays):
    local, width = x.shape
    tile = min(WIDE, width // 2)
    count = width // 2 // tile
    anywhere = pl.BlockSpec(memory_space=pl.ANY)
    factor = jax.ShapeDtypeStruct((local, 2 * LANES), BF16)
    return pl.pallas_call(
        functools.partial(other_kernel, width // P_SIZE),
        grid=(1,),
        in_specs=[anywhere] * 5,
        out_specs=[anywhere, pl.BlockSpec(factor.shape, lambda j: (0, 0))],
        out_shape=[jax.ShapeDtypeStruct((2, N + EXTRA, width // 2), F32), factor],
        scratch_shapes=[
            pltpu.VMEM((local, width // 2), BF16),
            pltpu.VMEM((local, width // 2), BF16),
            pltpu.VMEM((count, 2, N + EXTRA, tile), F32),
            pltpu.VMEM(b.shape, BF16),
            pltpu.VMEM(c.shape, BF16),
            pltpu.VMEM(decays.shape, F32),
            pltpu.VMEM((N, local), BF16),
            pltpu.VMEM((N, local), BF16),
            pltpu.SemaphoreType.DMA((2, PARTS)),
            pltpu.SemaphoreType.DMA((3,)),
            pltpu.SemaphoreType.DMA((count,)),
        ],
        compiler_params=FIRST,
        name="other_totals",
        cost_estimate=pl.CostEstimate(flops=8 * local * N * width // 2, bytes_accessed=4 * local * width, transcendentals=0),
    )(x, dy, b, c, decays)


def own_kernel(heads, count, x_ref, dy_ref, b_ref, c_ref, decays_ref, out_ref, bt_ref, ct_ref, factor_ref):
    step = pl.program_id(0)

    @pl.when(step == 0)
    def _():
        bt_ref[...] = transposed(b_ref[...])
        ct_ref[...] = transposed(c_ref[...])
        device_factors(decays_ref[...], factor_ref)

    first = (place(CORE) * count + step) * (x_ref.shape[1] // P_SIZE)
    tile_totals(heads, first, x_ref[...], dy_ref[...], bt_ref, ct_ref, factor_ref, out_ref)


def own_totals(x, dy, b, c, decays):
    local, width = x.shape
    tile = min(WIDE, width // 2)
    count = width // 2 // tile
    whole = lambda a: pl.BlockSpec(a.shape, lambda j: (0, 0))
    column = pl.BlockSpec((local, tile), lambda j: (0, place(CORE) * count + j))
    return pl.pallas_call(
        functools.partial(own_kernel, width // P_SIZE, count),
        grid=(count,),
        in_specs=[column, column, whole(b), whole(c), whole(decays)],
        out_specs=pl.BlockSpec((2, N + EXTRA, tile), lambda j: (0, 0, j)),
        scratch_shapes=[
            pltpu.VMEM((N, local), BF16),
            pltpu.VMEM((N, local), BF16),
            pltpu.VMEM((local, 2 * LANES), BF16),
        ],
        out_shape=jax.ShapeDtypeStruct((2, N + EXTRA, width // 2), F32),
        compiler_params=PARAMS,
        name="own_totals",
        cost_estimate=pl.CostEstimate(flops=8 * local * N * width // 2, bytes_accessed=4 * local * width, transcendentals=0),
    )(x, dy, b, c, decays)


def ordered(core, mine, recv):
    return jnp.where(core == 0, mine, recv), jnp.where(core == 0, recv, mine)


def chip_kernel(chips, mine_ref, recv_ref, *out_refs):
    core, chip = place(CORE), lax.axis_index("seq") // 2
    early, late = ordered(core, mine_ref[0], recv_ref[0])
    early_decay, late_decay = early[N : N + 1], late[N : N + 1]
    both = jnp.broadcast_to(early_decay * late_decay, (EXTRA, early.shape[1]))
    state = late_decay * early[:N] + late[:N]
    early, late = ordered(core, mine_ref[1], recv_ref[1])
    grad = early[:N] + early_decay * late[:N]
    for r, out_ref in enumerate(out_refs, 1):
        out_ref[:N, :] = jnp.where(chip + r < chips, state, grad)
        out_ref[N:, :] = both


def chip_totals(chips, mine, recv):
    width = mine.shape[2]
    tile = min(512, width)
    block = pl.BlockSpec((2, N + EXTRA, tile), lambda j: (0, 0, j))
    out = pl.BlockSpec((N + EXTRA, tile), lambda j: (0, j))
    shape = jax.ShapeDtypeStruct((N + EXTRA, width), F32)
    return pl.pallas_call(
        functools.partial(chip_kernel, chips),
        grid=(width // tile,),
        in_specs=[block, block],
        out_specs=[out] * (chips - 1),
        out_shape=[shape] * (chips - 1),
        compiler_params=PARAMS,
        name="chip_totals",
        cost_estimate=pl.CostEstimate(flops=6 * N * width, bytes_accessed=24 * N * width, transcendentals=0),
    )(mine, recv)


def sides():
    chip = lax.axis_index("seq") // 2
    return chip < 2, (chip == 1) | (chip == 2)


def first_kernel(mine_ref, recv_ref, same_ref, later_ref, cross_ref, back_ref, decay_ref):
    left, inner = sides()
    core = place(CORE)
    width = mine_ref.shape[2] // 2
    early, late = ordered(core, mine_ref[0], recv_ref[0])
    early_decay, late_decay = early[N : N + 1], late[N : N + 1]
    state = late_decay * early[:N] + late[:N]
    decay = early_decay * late_decay
    early, late = ordered(core, mine_ref[1], recv_ref[1])
    grad = early[:N] + early_decay * late[:N]
    out, back = jnp.where(left, state, grad), jnp.where(left, grad, state)
    same_ref[:N, :] = out[:, :width]
    later_ref[...] = jnp.where(inner, back[:, :width], out[:, width:])
    rows = lax.broadcasted_iota(jnp.int32, (EXTRA, width), 0)
    same_ref[N:, :] = jnp.where(rows == 0, decay[:, :width], decay[:, width:])
    cross_ref[...] = out[:, width:]
    back_ref[...] = back[:, width:]
    decay_ref[...] = jnp.broadcast_to(decay[:, width:], (EXTRA, width))


def second_kernel(own_ref, back_ref, same_ref, cross_ref, decay_ref, cross2_ref, same2_ref):
    _, inner = sides()
    own, other = own_ref[:N, :], same_ref[:N, :]
    own_decay, other_decay = own_ref[N : N + 1, :], same_ref[N : N + 1, :]
    cross2_ref[...] = jnp.where(inner, own + own_decay * other, other + other_decay * own)
    weight = own_ref[N + 1 : N + 2, :] * decay_ref[:1, :]
    same2_ref[...] = jnp.where(inner, back_ref[...] + weight * cross_ref[...], cross_ref[...])


def plain_call(kernel, name, out_shape, *args):
    whole = lambda a: pl.BlockSpec(a.shape, lambda j: (0,) * len(a.shape))
    size = sum(a.size for a in args)
    return pl.pallas_call(
        kernel,
        grid=(1,),
        in_specs=[whole(a) for a in args],
        out_specs=[whole(a) for a in out_shape],
        out_shape=out_shape,
        compiler_params=PARAMS,
        name=name,
        cost_estimate=pl.CostEstimate(flops=8 * size, bytes_accessed=4 * size, transcendentals=0),
    )(*args)


def crossed(v, length, bit):
    return lax.ppermute(v, "seq", [(i, i ^ bit) for i in range(length)])


def first_phase(length, mine, recv):
    half = mine.shape[2] // 2
    shapes = [jax.ShapeDtypeStruct((rows, half), F32) for rows in (N + EXTRA, N, N, N, EXTRA)]
    own, later, cross, back, decay = plain_call(first_kernel, "first_messages", shapes, mine, recv)
    same, cross, decay = crossed(own, length, 2), crossed(cross, length, 4), crossed(decay, length, 6)
    return own, back, same, cross, decay, crossed(later, length, 2)


def second_phase(own, back, same, cross, decay):
    shape = jax.ShapeDtypeStruct(back.shape, F32)
    return plain_call(second_kernel, "second_messages", [shape, shape], own, back, same, cross, decay)


def carried4_kernel(
    mine_ref, recv_ref, same_ref, cross_ref, decay_ref, later_ref, cross2_ref, same2_ref, own_ref, peer_ref
):
    left, inner = sides()
    width = cross_ref.shape[1]
    decay_a, decay_b = same_ref[N : N + 1, :], same_ref[N + 1 : N + 2, :]
    for part in range(2):
        at = slice(part * width, (part + 1) * width)
        out = jnp.where(inner, later_ref[...] if part else same_ref[:N, :], 0.0)
        if part == 0:
            back = jnp.where(inner, cross2_ref[...], later_ref[...] + decay_a * cross2_ref[...])
        else:
            back = same2_ref[...] + jnp.where(inner, decay_ref[:1, :], decay_b) * cross_ref[...]
        carried_cores(
            place(CORE), jnp.where(left, out, back), jnp.where(left, back, out), mine_ref, recv_ref, own_ref, peer_ref, at
        )


def carried4(mine, recv, *others):
    shape = jax.ShapeDtypeStruct((2, N, mine.shape[2]), F32)
    return plain_call(carried4_kernel, "carried_in", [shape, shape], mine, recv, *others)


def carried_cores(core, state, grad, mine_ref, recv_ref, own_ref, peer_ref, at):
    early, late = ordered(core, mine_ref[0, :, at], recv_ref[0, :, at])
    at_late = early[N : N + 1] * state + early[:N]
    own_ref[0, :, at] = jnp.where(core == 0, state, at_late)
    peer_ref[0, :, at] = jnp.where(core == 0, at_late, state)
    early, late = ordered(core, mine_ref[1, :, at], recv_ref[1, :, at])
    at_early = late[:N] + late[N : N + 1] * grad
    own_ref[1, :, at] = jnp.where(core == 0, at_early, grad)
    peer_ref[1, :, at] = jnp.where(core == 0, grad, at_early)


def carried_kernel(chips, mine_ref, recv_ref, *refs):
    others, (own_ref, peer_ref) = refs[:-2], refs[-2:]
    core, chip = place(CORE), lax.axis_index("seq") // 2
    state = grad = jnp.zeros((N, own_ref.shape[2]), F32)
    state_weight = grad_weight = jnp.ones((1, own_ref.shape[2]), F32)
    for r, ref in enumerate(others, 1):
        earlier = chip >= r
        state = jnp.where(earlier, state + state_weight * ref[:N, :], state)
        state_weight = state_weight * ref[N : N + 1, :]
    for r in range(1, chips):
        later = chip + r < chips
        ref = others[chips - r - 1]
        grad = jnp.where(later, grad + grad_weight * ref[:N, :], grad)
        grad_weight = grad_weight * ref[N : N + 1, :]
    carried_cores(core, state, grad, mine_ref, recv_ref, own_ref, peer_ref, slice(None))


def carried(chips, mine, recv, others):
    width = mine.shape[2]
    tile = min(512, width)
    pair = pl.BlockSpec((2, N + EXTRA, tile), lambda j: (0, 0, j))
    other = pl.BlockSpec((N + EXTRA, tile), lambda j: (0, j))
    out = pl.BlockSpec((2, N, tile), lambda j: (0, 0, j))
    shape = jax.ShapeDtypeStruct((2, N, width), F32)
    return pl.pallas_call(
        functools.partial(carried_kernel, chips),
        grid=(width // tile,),
        in_specs=[pair, pair] + [other] * len(others),
        out_specs=(out, out),
        out_shape=(shape, shape),
        compiler_params=PARAMS,
        name="carried_in",
        cost_estimate=pl.CostEstimate(flops=20 * N * width, bytes_accessed=44 * N * width, transcendentals=0),
    )(mine, recv, *others)


def blocks(chunks):
    span = 2
    while span < chunks:
        yield span, [at for at in range(span, chunks, 2 * span)]
        span *= 2


def row_bounds(chunks):
    middles = [k * SUB + SUB // 2 + 1 for k in range(chunks)]
    for span in [1] + [span for span, _ in blocks(chunks)]:
        for k, middle in enumerate(middles):
            boundary = (k // span + 1 - (k // span) % 2) * span * SUB
            yield min(boundary, middle), max(boundary, middle)
    yield from ((0, middle) for middle in middles)
    yield from ((middle, chunks * SUB) for middle in middles)


def local_factors(decays, lift_ref, drop_ref, rows_ref):
    local = decays.shape[1]
    logs = log_parts(decays)
    rows = lax.broadcasted_iota(jnp.int32, (LANES, LANES), 0)
    columns = lax.broadcasted_iota(jnp.int32, (LANES, LANES), 1)
    middle = (columns & -SUB) + SUB // 2
    later = (rows > middle) & (rows <= columns)
    sooner = (rows > columns) & (rows <= middle)
    offset = jnp.concatenate(block_sums(logs, later.astype(F32) - sooner.astype(F32)), axis=1)
    lift_ref[...] = by_token(jnp.exp(offset))
    drop_ref[...] = by_token(jnp.exp(-offset))
    lane = lax.broadcasted_iota(jnp.int32, (1, LANES), 1)
    first = last = jnp.zeros((1, LANES), jnp.int32)
    for i, (start, end) in enumerate(row_bounds(local // SUB)):
        first, last = jnp.where(lane == i, start, first), jnp.where(lane == i, end, last)
    rows = lax.broadcasted_iota(jnp.int32, (local, LANES), 0)
    decay = by_token(jnp.exp(summed_logs(logs, (rows >= first) & (rows < last))))
    rows_ref[...] = decay[: rows_ref.shape[0]]


def score_parts(b, c, ref, at, times, ahead=None):
    score = dot(b, c, NT)
    if ahead is not None:
        rows = lax.broadcasted_iota(jnp.int32, score.shape, 0)
        columns = lax.broadcasted_iota(jnp.int32, score.shape, 1)
        score = jnp.where(rows <= columns + ahead, score, 0.0)
    hi, lo = halves(score)
    width = score.shape[1]
    ref[at, :width] = hi
    ref[at, width : 2 * width] = lo
    if times == 3:
        ref[at, 2 * width :] = hi


def added_up(v):
    width = v.shape[1] // 2
    return v[:, :width] + v[:, width:]


def local_kernel(first_tile, continued, *refs):
    x_ref, dy_ref, b_ref, c_ref, decays_ref = refs[:5]
    refs = refs[5:]
    if continued:
        out_before_ref, map_before_ref = refs[:2]
        refs = refs[4:]
    part_ref, scaled_ref, out_ref, map_ref = refs[:4]
    lift_ref, drop_ref, rows_ref, full_ref, dys_ref, xs_ref, back_ref, sums_ref, even_ref, odd_ref = refs[4:14]
    level_refs = refs[14:]
    local, tile = x_ref.shape
    chunks = local // SUB
    step = pl.program_id(0)
    levels = [(span, at, level_refs[2 * i], level_refs[2 * i + 1]) for i, (span, at) in enumerate(blocks(chunks))]

    @pl.when(step == 0)
    def _():
        local_factors(decays_ref[...], lift_ref, drop_ref, rows_ref)
        sums_ref[...] = jnp.zeros(sums_ref.shape, F32)
        for k in range(0, chunks, 2):
            pair, even, odd = pl.ds(k * SUB, 2 * SUB), pl.ds(k * SUB, SUB), pl.ds((k + 1) * SUB, SUB)
            score_parts(b_ref[even, :], c_ref[even, :], even_ref, pl.ds(k // 2 * SUB, SUB), 3, 0)
            score_parts(b_ref[pair, :], c_ref[odd, :], odd_ref, pair, 3, SUB)
        for span, boundaries, mixed_ref, scores_ref in levels:
            mixed_ref[...] = jnp.zeros(mixed_ref.shape, F32)
            size = span * SUB
            for i, boundary in enumerate(boundaries):
                before, after = pl.ds((boundary - span) * SUB, size), pl.ds(boundary * SUB, size)
                score_parts(b_ref[before, :], c_ref[after, :], scores_ref, pl.ds(i * size, size), 2)

    first = (first_tile + step) * (tile // P_SIZE)
    dys_ref[...] = dy_ref[...].astype(F32) * spread(lift_ref[...], first, tile)
    back_ref[...] = spread(drop_ref[...], first, tile)
    xs_ref[...] = x_ref[...].astype(F32) * back_ref[...]
    row = spread(rows_ref[...], first, tile)
    factor = lambda kind, k: row[kind * chunks + k : kind * chunks + k + 1]

    for k in range(0, chunks, 2):
        even, odd, pair = pl.ds(k * SUB, SUB), pl.ds((k + 1) * SUB, SUB), pl.ds(k * SUB, 2 * SUB)
        dys, xs = halves(dys_ref[even, :]), halves(xs_ref[even, :])
        sums_ref[even, :] += dot(dys[0], stacked(*xs), NT)
        sums_ref[even, :SUB] += dot(dys[1], xs[0], NT)
        gained_even = dot(even_ref[pl.ds(k // 2 * SUB, SUB), :], stacked(dys[0], dys[0], dys[1]))
        crossing = halves((xs_ref[even, :] * factor(0, k)) * factor(0, k + 1))
        dys, xs = halves(dys_ref[odd, :]), halves(xs_ref[odd, :])
        high = stacked(xs[0], crossing[0])
        both = dot(dys[0], stacked(high, xs[1], crossing[1]), NT)
        sums_ref[odd, :] += added_up(both) + dot(dys[1], high, NT)
        gained_odd = dot(odd_ref[pair, :], stacked(dys[0], dys[0], dys[1]))
        ahead = (back_ref[even, :] * factor(0, k)) * (factor(0, k + 1) * gained_odd[:SUB])
        part_ref[even, :] = back_ref[even, :] * gained_even + ahead
        part_ref[odd, :] = back_ref[odd, :] * gained_odd[SUB:]

    for level, (span, boundaries, mixed_ref, scores_ref) in enumerate(levels, 1):
        size = span * SUB
        for i, boundary in enumerate(boundaries):
            at = pl.ds(i * size, size)
            take = lambda ref, start: halves(
                stacked(*[ref[k * SUB : (k + 1) * SUB, :] * factor(level, k) for k in range(start, start + span)])
            )
            dys, xs = take(dys_ref, boundary), take(xs_ref, boundary - span)
            both = dot(dys[0], stacked(*xs), NT)
            mixed_ref[at, :] += added_up(both) + dot(dys[1], xs[0], NT)
            gained = dot(scores_ref[at, :], stacked(dys[0], dys[0])) + dot(scores_ref[at, :size], dys[1])
            for q in range(span):
                k = boundary - span + q
                rows = pl.ds(k * SUB, SUB)
                part_ref[rows, :] += (back_ref[rows, :] * factor(level, k)) * gained[q * SUB : (q + 1) * SUB]

    for k in range(chunks):
        at = pl.ds(k * SUB, SUB)
        kind = len(levels) + 1
        scaled_ref[1, 0, at, :], scaled_ref[1, 1, at, :] = halves(dys_ref[at, :] * factor(kind, k))
        scaled_ref[0, 0, at, :], scaled_ref[0, 1, at, :] = halves(xs_ref[at, :] * factor(kind + 1, k))

    @pl.when(step == pl.num_programs(0) - 1)
    def _():
        full_ref[...] = jnp.zeros(full_ref.shape, F32)
        rows = lax.broadcasted_iota(jnp.int32, (SUB, SUB), 0)
        columns = lax.broadcasted_iota(jnp.int32, (SUB, SUB), 1)
        for k in range(0, chunks, 2):
            even, odd = pl.ds(k * SUB, SUB), pl.ds((k + 1) * SUB, SUB)
            full_ref[even, k * SUB : (k + 1) * SUB] = jnp.where(rows >= columns, added_up(sums_ref[even, :]), 0.0)
            full_ref[odd, (k + 1) * SUB : (k + 2) * SUB] = jnp.where(rows >= columns, sums_ref[odd, :SUB], 0.0)
            full_ref[odd, k * SUB : (k + 1) * SUB] = sums_ref[odd, SUB:]
        for span, boundaries, mixed_ref, _ in levels:
            size = span * SUB
            for i, boundary in enumerate(boundaries):
                block = mixed_ref[pl.ds(i * size, size), :]
                full_ref[pl.ds(boundary * SUB, size), (boundary - span) * SUB : boundary * SUB] = block
        map_ref[...] = map_before_ref[...] if continued else jnp.zeros(map_ref.shape, F32)
        for k in range(0, local, LANES):
            at = pl.ds(k, LANES)
            mixed = full_ref[at, :]
            gained = dot21(halves(mixed), b_ref[...])
            out_ref[at, :] = out_before_ref[at, :] + gained if continued else gained
            map_ref[...] += dot21(halves(mixed.T), c_ref[at, :])


def local_part(first_tile, count, x, dy, b, c, decays, before=None):
    local, width = x.shape
    chunks = local // SUB
    whole = lambda a: pl.BlockSpec(a.shape, lambda j: (0, 0))
    column = pl.BlockSpec((local, WIDE), lambda j: (0, first_tile + j))
    tokens = pl.BlockSpec((local, N), lambda j: (0, 0))
    scratch = [
        pltpu.VMEM((local, LANES), F32),
        pltpu.VMEM((local, LANES), F32),
        pltpu.VMEM((-(-len(list(row_bounds(chunks))) // 8) * 8, LANES), F32),
        pltpu.VMEM((local, local), F32),
        pltpu.VMEM((local, WIDE), F32),
        pltpu.VMEM((local, WIDE), F32),
        pltpu.VMEM((local, WIDE), F32),
        pltpu.VMEM((local, 2 * SUB), F32),
        pltpu.VMEM((local // 2, 3 * SUB), BF16),
        pltpu.VMEM((local, 3 * SUB), BF16),
    ]
    for span, _ in blocks(chunks):
        scratch.append(pltpu.VMEM((local // 2, span * SUB), F32))
        scratch.append(pltpu.VMEM((local // 2, 2 * span * SUB), BF16))
    in_specs = [column, column, whole(b), whole(c), whole(decays)]
    args, aliases = [x, dy, b, c, decays], {}
    if before is not None:
        part, scaled, out_part, map_part = before
        in_specs += [tokens, tokens, pl.BlockSpec(memory_space=pl.ANY), pl.BlockSpec(memory_space=pl.ANY)]
        args += [out_part, map_part, part, scaled]
        aliases = {7: 0, 8: 1}
    return pl.pallas_call(
        functools.partial(local_kernel, first_tile, before is not None),
        grid=(count,),
        in_specs=in_specs,
        out_specs=(column, pl.BlockSpec((2, 2, local, WIDE), lambda j: (0, 0, 0, first_tile + j)), tokens, tokens),
        out_shape=(
            jax.ShapeDtypeStruct((local, width), F32),
            jax.ShapeDtypeStruct((2, 2, local, width), BF16),
            jax.ShapeDtypeStruct((local, N), F32),
            jax.ShapeDtypeStruct((local, N), F32),
        ),
        scratch_shapes=scratch,
        input_output_aliases=aliases,
        compiler_params=PARAMS,
        name="local_part",
        cost_estimate=pl.CostEstimate(
            flops=40 * local * N * WIDE * count, bytes_accessed=8 * local * WIDE * count, transcendentals=0
        ),
    )(*args)


def map_kernel(count, ranks, scaled_ref, carry_ref, out_before_ref, map_before_ref, *refs):
    messages, (out_ref, map_ref) = refs[:-2], refs[-2:]
    step = pl.program_id(0)

    @pl.when(step == 0)
    def _():
        out_ref[...] = out_before_ref[...]
        map_ref[...] = map_before_ref[...]

    for i, sum_ref in enumerate((map_ref, out_ref)):
        carry = halves(carry_ref[1 - i])
        both = dot(scaled_ref[i, 0], stacked(*carry), NT)
        sum_ref[...] += both[:, :N] + (both[:, N:] + dot(scaled_ref[i, 1], carry[0], NT))

    if messages:

        @pl.when(step == count - 1)
        def _():
            rows = messages[0].shape[1]
            for r, message in enumerate(messages):
                at = pl.ds(pl.multiple_of(((lax.axis_index("head") + r) % ranks) * rows, rows), rows)
                message[0] = out_ref[at, :]
                message[1] = map_ref[at, :]


def map_terms(half, scaled, carry, out_before, map_before, ranks=0):
    local, width = scaled.shape[2], carry.shape[2]
    tile = min(WIDE, width)
    count = width // tile
    whole = lambda a: pl.BlockSpec(a.shape, lambda j: (0,) * len(a.shape))
    tokens = jax.ShapeDtypeStruct((local, N), F32)
    if ranks:
        out_shape = [jax.ShapeDtypeStruct((2, local // ranks, N), F32)] * ranks
        scratch = [pltpu.VMEM((local, N), F32), pltpu.VMEM((local, N), F32)]
    else:
        out_shape, scratch = [tokens, tokens], []
    return pl.pallas_call(
        functools.partial(map_kernel, count, ranks),
        grid=(count,),
        in_specs=[
            pl.BlockSpec((2, 2, local, tile), lambda j: (0, 0, 0, place(half) * count + j)),
            pl.BlockSpec((2, N, tile), lambda j: (0, 0, j)),
            whole(tokens),
            whole(tokens),
        ],
        out_specs=[whole(shape) for shape in out_shape],
        scratch_shapes=scratch,
        out_shape=out_shape,
        compiler_params=PARAMS,
        name="map_terms",
        cost_estimate=pl.CostEstimate(flops=12 * local * N * width, bytes_accessed=8 * local * width, transcendentals=0),
    )(scaled, carry, out_before, map_before)


def input_kernel(heads, count, part_ref, suf_ref, b_ref, own_ref, other_ref, input_ref):
    tile = part_ref.shape[1]
    step = pl.program_id(0)
    after = dot(suf_ref[...], spread_table(heads, step * (tile // P_SIZE), tile))
    grad = jnp.where(step // count == place(CORE), own_ref[0], other_ref[0])
    input_ref[...] = (part_ref[...] + after * dot12(b_ref[...], halves(grad))).astype(BF16)


def input_terms(part, factors, b, own, other):
    local, width = part.shape
    count = width // 2 // WIDE
    whole = lambda a: pl.BlockSpec(a.shape, lambda j: (0, 0))
    column = pl.BlockSpec((local, WIDE), lambda j: (0, j))
    carry = pl.BlockSpec((1, N, WIDE), lambda j: (1, 0, j % count))
    return pl.pallas_call(
        functools.partial(input_kernel, width // P_SIZE, count),
        grid=(2 * count,),
        in_specs=[column, pl.BlockSpec((local, LANES), lambda j: (0, 1)), whole(b), carry, carry],
        out_specs=column,
        out_shape=jax.ShapeDtypeStruct((local, width), BF16),
        compiler_params=PARAMS,
        name="input_terms",
        cost_estimate=pl.CostEstimate(flops=4 * local * N * width, bytes_accessed=8 * local * width, transcendentals=0),
    )(part, factors, b, own, other)


def sums_kernel(*refs):
    shares, (map_ref, out_ref) = refs[:-2], refs[-2:]
    for i, ref in enumerate((out_ref, map_ref)):
        ref[...] = functools.reduce(lambda a, b: a + b, [share[i] for share in shares])


def swap_cores(v, length):
    return lax.ppermute(v, "seq", [(i, i ^ 1) for i in range(length)])


def turned(v, axis, length, by):
    return lax.ppermute(v, axis, [(i, (i + by) % length) for i in range(length)])


def per_device(mixer_input, output_grad, input_map, output_map, decays):
    length, ranks = lax.axis_size("seq"), lax.axis_size("head")
    chips = length // 2
    args = mixer_input, output_grad, input_map, output_map
    sent, factors = other_totals(*args, decays)
    recv = swap_cores(sent, length)
    mine = own_totals(*args, decays)
    tiles = mixer_input.shape[1] // WIDE
    if chips == 4:
        ahead = tiles // 2
        own, back, *others, later = first_phase(length, mine, recv)
        result = local_part(0, ahead, *args, decays)
        others, result = lax.optimization_barrier((others, result))
        cross, same = second_phase(own, back, *others)
        same = crossed(same, length, 2)
        crossing = [crossed(cross, length, 4), same]
        result, later, _ = lax.optimization_barrier((result, later, cross))
        result = local_part(ahead, tiles - ahead, *args, decays, result)
        others, result = lax.optimization_barrier((others + [later] + crossing, result))
        own, peer = carried4(mine, recv, *others)
    else:
        messages = chip_totals(chips, mine, recv)
        others = [turned(message, "seq", length, 2 * r) for r, message in enumerate(messages, 1)]
        result = local_part(0, tiles, *args, decays)
        own, peer = carried(chips, mine, recv, others)
    part, scaled, out_part, map_part = result
    other = swap_cores(peer, length)
    out_part, map_part = map_terms(CORE, scaled, own, out_part, map_part)
    shares = map_terms(OTHER, scaled, other, out_part, map_part, ranks)
    own, other, shares = lax.optimization_barrier((own, other, shares))
    sums = [shares[0]] + [turned(shares[r], "head", ranks, r) for r in range(1, ranks)]
    input_grad = input_terms(part, factors, input_map, own, other)
    shape = jax.ShapeDtypeStruct(shares[0].shape[1:], F32)
    input_map_grad, output_map_grad = plain_call(sums_kernel, "head_sums", [shape, shape], *sums)
    return input_grad, input_map_grad, output_map_grad


def solution(mesh):
    in_specs = (
        P("seq", "head"),
        P("seq", "head"),
        P("seq", None),
        P("seq", None),
        P("head", "seq"),
    )
    out_specs = (P("seq", "head"), P(("seq", "head"), None), P(("seq", "head"), None))
    return jax.shard_map(
        per_device, mesh=mesh, in_specs=in_specs, out_specs=out_specs, check_vma=False
    )
```
